32 devices in a mesh: dp: 4 (over y, x), ctx: 8 (over z, core).
Axes of the slice: x: 2, y: 2, z: 4, core: 2. Of those that a mesh axis runs over, the one named last changes fastest.
Arguments:
- segment_ids: int32 [8192], P(('dp', 'ctx')), parts along dimension 0, may hold values from 0 to 7, never falling along the last dimension, each value on 1 to 1024 neighbouring positions
- attn_query: bfloat16 [8192, 2048], P(('dp', 'ctx')), parts along dimension 0, may hold values from -96 to 96
- attention_keys: bfloat16 [8192, 256], P(('dp', 'ctx')), parts along dimension 0, may hold values from -8 to 8
- attention_values: bfloat16 [8192, 256], P(('dp', 'ctx')), parts along dimension 0, may hold values from -6 to 6
- attn_gate: bfloat16 [8192, 2048], P(('dp', 'ctx')), parts along dimension 0, may hold values from -8 to 8
- delta_query: bfloat16 [8192, 1024], P(('dp', 'ctx')), parts along dimension 0, may hold values from -400 to 400
- delta_key: bfloat16 [8192, 1024], P(('dp', 'ctx')), parts along dimension 0, may hold values from -400 to 400
- update_rule_payload: bfloat16 [8192, 2048], P(('dp', 'ctx')), parts along dimension 0, may hold values from -400 to 400
- delta_beta: float32 [8192, 16], P(('dp', 'ctx')), parts along dimension 0, may hold values from 0.1 to 0.9
- delta_decay: float32 [8192, 16], P(('dp', 'ctx')), parts along dimension 0, may hold values from -1 to 0
- delta_gate: bfloat16 [8192, 2048], P(('dp', 'ctx')), parts along dimension 0, may hold values from -8 to 8
- norm_gain: float32 [128], replicated, may hold values from 0.5 to 1.5
Outputs:
- attn_mixed: bfloat16 [8192, 2048], P(('dp', 'ctx')), parts along dimension 0
- delta_mixed: bfloat16 [8192, 2048], P(('dp', 'ctx')), parts along dimension 0
The draws below stay inside these ranges and needn't reach their ends.
There are 4 independent parts, one for each index of `dp`. The reference program is written for one: setup_inputs(seed, part) draws one part's arguments, and reference() takes and returns one part's arrays. A program takes and returns all parts, laid end to end along the dimension named above; an argument that names none is the same for every part. Nothing has to cross between parts.
Inputs may be any that keep to these rules, and one draw needn't show every extreme that they name: `segment_ids`: segment ids never fall along the sequence; each of the 8 documents holds 1 to 1024 positions, and one holds exactly 1024.
All inputs are finite; a program needn't handle non-finite values.
Results may differ from the reference program's by a relative error of at most 0.0085.
Values may be sent and summed in bfloat16 or wider, within the bound.
No kernel may reach another device: no remote copies, remote signals or barrier semaphores. Data moves between devices by JAX's collectives and lax.ppermute only.
A program may use at most 256 MiB of HBM per device.

```python
import math
import jax
import jax.numpy as jnp
import numpy as np
from jax import lax

QUERY_HEADS = 8
KEY_VALUE_HEADS = 1
HEAD_WIDTH = 256
ROTARY_ENTRIES = 64
HK = 8
HV = 16
DK = 128
DV = 128
GROUP = 2
DOCS = 8
TOK_DEV = 256
TOKEN_SPAN_TOTAL = 2048


def attention_pair(key):
    query_vector = jax.random.normal(jax.random.fold_in(key, 101), (TOKEN_SPAN_TOTAL, QUERY_HEADS, HEAD_WIDTH), jnp.float32)
    key_rows = jax.random.normal(jax.random.fold_in(key, 102), (TOKEN_SPAN_TOTAL, KEY_VALUE_HEADS, HEAD_WIDTH), jnp.float32)
    return (jnp.clip(query_vector, -96.0, 96.0).reshape(TOKEN_SPAN_TOTAL, QUERY_HEADS * HEAD_WIDTH), jnp.clip(key_rows, -8.0, 8.0).reshape(TOKEN_SPAN_TOTAL, KEY_VALUE_HEADS * HEAD_WIDTH))


def draw_attn_query(key, part):
    return attention_pair(key)[0].astype(jnp.bfloat16)


def draw_attention_keys(key, part):
    return attention_pair(key)[1].astype(jnp.bfloat16)


def scaled_rows(key, width):
    reach = jnp.log(10.0)
    base = jnp.clip(jax.random.normal(jax.random.fold_in(key, 1), (TOKEN_SPAN_TOTAL, width), jnp.float32), -4.5, 4.5)
    row_scale = jnp.exp(jax.random.uniform(jax.random.fold_in(key, 3), (TOKEN_SPAN_TOTAL, 1), jnp.float32, 0.0, reach))
    column_scale = jnp.exp(jax.random.uniform(jax.random.fold_in(key, 4), (1, width), jnp.float32, 0.0, reach))
    return jnp.clip(0.25 * base * row_scale * column_scale, -400.0, 400.0)


def draw_delta_query(key, part):
    return scaled_rows(jax.random.fold_in(key, 201), HK * DK).astype(jnp.bfloat16)


def draw_delta_key(key, part):
    return scaled_rows(jax.random.fold_in(key, 202), HK * DK).astype(jnp.bfloat16)


def draw_update_rule_payload(key, part):
    return scaled_rows(jax.random.fold_in(key, 203), HV * DV).astype(jnp.bfloat16)


def draw_delta_decay(key, part):
    order = jax.random.permutation(jax.random.fold_in(key, 301), HV)
    slow_count = HV // 2
    slow_rate = -0.5 / TOKEN_SPAN_TOTAL
    slow = (order < slow_count)[None, :]
    fast_rate = -1.0 / jax.random.uniform(jax.random.fold_in(key, 302), (1, HV), jnp.float32, 30.0, 50.0)
    rate = jnp.where(slow, slow_rate, fast_rate)
    blocks = TOKEN_SPAN_TOTAL // TOK_DEV
    factor = jnp.exp(jax.random.uniform(jax.random.fold_in(key, 303), (blocks, HV), jnp.float32, jnp.log(0.6), jnp.log(1.3)))
    factor_rows = jnp.repeat(factor, TOK_DEV, axis=0)
    jitter = jax.random.uniform(jax.random.fold_in(key, 304), (TOKEN_SPAN_TOTAL, HV), jnp.float32, 0.5, 1.5)
    episode_offset = jax.random.randint(jax.random.fold_in(key, 305), (2,), 0, TOKEN_SPAN_TOTAL)
    slot_number = jnp.arange(TOKEN_SPAN_TOTAL)
    blocked_pattern = jnp.any(slot_number[:, None] == episode_offset[None, :], axis=1)
    loss = jnp.log(jax.random.uniform(jax.random.fold_in(key, 306), (TOKEN_SPAN_TOTAL, HV), jnp.float32, 0.5, 0.8))
    decay = rate * factor_rows * jitter + jnp.where(blocked_pattern[:, None], loss, 0.0)
    return jnp.clip(decay, -1.0, 0.0)


def level_of(key, dims, split, smallest, high):
    loudness = 1.0
    for position, shards_of in split:
        steps = jax.random.uniform(jax.random.fold_in(jax.random.fold_in(key, 6), position), (shards_of,), jnp.float32, smallest / len(split), high / len(split))
        loudness = loudness * jnp.repeat(jnp.exp(steps), dims[position] // shards_of).reshape((-1,) + (1,) * (len(dims) - 1 - position))
    return loudness


def split_up(amount, total, limit, skew):
    weights = [(1 << 20) // math.isqrt(standing ** skew) + 1 for standing in range(2, amount + 1)]
    surplus, holding = total - limit - (amount - 1), [1] * (amount - 1)
    while surplus > 0:
        movable = [i for i in range(amount - 1) if holding[i] < limit]
        mass, left = sum([weights[i] for i in movable]), surplus
        for i in movable:
            more = min(limit - holding[i], max(1, left * weights[i] // mass), surplus)
            holding[i] = holding[i] + more
            surplus = surplus - more
    return np.array([limit] + holding)


def ragged(rng, number_of, total, bound, skew):
    if number_of == 2:
        one = jax.random.randint(rng, (), max(1, total - bound), min(bound, total - 1) + 1)
        return jnp.stack([one, total - one])
    sizes = jnp.asarray(split_up(number_of, total, bound, skew), jnp.int32)
    pairs = (number_of - 1) // 2
    source_of, receiver = sizes[1:1 + 2 * pairs:2], sizes[2:2 + 2 * pairs:2]
    margin = jnp.minimum(source_of - 1, bound - receiver)
    moved = jax.random.randint(jax.random.fold_in(rng, 1), (pairs,), 0, 1 << 20) % (margin + 1)
    sizes = sizes.at[1:1 + 2 * pairs:2].set(source_of - moved).at[2:2 + 2 * pairs:2].set(receiver + moved)
    return sizes[jax.random.permutation(jax.random.fold_in(rng, 2), number_of)]


def gaussian(own_key, shape, scale, bound, pieces=(), kind=jnp.bfloat16):
    gain = level_of(own_key, shape, pieces, -0.22, 0.18) if pieces else 1.0
    array = jax.random.normal(own_key, shape, jnp.float32) * scale * gain
    return jnp.minimum(jnp.maximum(array, -bound), bound).astype(kind)


def setup_inputs(seed: int = 0, part: int = 0) -> dict:
    streams_of = jax.random.split(jax.random.key(seed), 13)
    own_keys = jax.random.split(jax.random.fold_in(streams_of[12], part), 13)
    segment_ids = jnp.searchsorted(jnp.cumsum(ragged(own_keys[0], DOCS, TOKEN_SPAN_TOTAL, TOKEN_SPAN_TOTAL // 2, 0)), jnp.arange(TOKEN_SPAN_TOTAL), side="right").astype(jnp.int32)
    attn_query = draw_attn_query(jax.random.fold_in(jax.random.fold_in(streams_of[12], part), 71), part)
    attention_keys = draw_attention_keys(jax.random.fold_in(jax.random.fold_in(streams_of[12], part), 71), part)
    attention_values = gaussian(own_keys[3], (TOKEN_SPAN_TOTAL, KEY_VALUE_HEADS * HEAD_WIDTH), 1.0, 6.0, ((0, 8),))
    attn_gate = gaussian(own_keys[4], (TOKEN_SPAN_TOTAL, QUERY_HEADS * HEAD_WIDTH), 1.5, 8.0, ((0, 8),))
    delta_query = draw_delta_query(jax.random.fold_in(jax.random.fold_in(streams_of[12], part), 71), part)
    delta_key = draw_delta_key(jax.random.fold_in(jax.random.fold_in(streams_of[12], part), 71), part)
    update_rule_payload = draw_update_rule_payload(jax.random.fold_in(jax.random.fold_in(streams_of[12], part), 71), part)
    delta_beta = jnp.clip(0.1 + 0.79999997 * jax.random.uniform(own_keys[8], (TOKEN_SPAN_TOTAL, HV), jnp.float32) ** level_of(own_keys[8], (TOKEN_SPAN_TOTAL, HV), ((0, 8),), -0.2, 0.2), 0.1, 0.9)
    delta_decay = draw_delta_decay(jax.random.fold_in(jax.random.fold_in(streams_of[12], part), 71), part)
    delta_gate = gaussian(own_keys[10], (TOKEN_SPAN_TOTAL, HV * DV), 1.5, 8.0, ((0, 8),))
    norm_gain = jnp.clip(1.0 + 0.1 * jax.random.normal(streams_of[11], (DV,), jnp.float32), 0.5, 1.5)
    return dict(segment_ids=segment_ids, attn_query=attn_query, attention_keys=attention_keys, attention_values=attention_values, attn_gate=attn_gate, delta_query=delta_query, delta_key=delta_key, update_rule_payload=update_rule_payload, delta_beta=delta_beta, delta_decay=delta_decay, delta_gate=delta_gate, norm_gain=norm_gain)


rope_theta = 10000000.0

def apply_rotary(field, shift_amount):
    half = ROTARY_ENTRIES // 2
    index = jnp.arange(half).astype(jnp.float32)
    freq = rope_theta ** (-2.0 * index / ROTARY_ENTRIES)
    angle = shift_amount.astype(jnp.float32)[:, None, None] * freq[None, None, :]
    angular_cos_table = jnp.cos(angle)
    sine = jnp.sin(angle)
    first = field[..., :half]
    second = field[..., half:ROTARY_ENTRIES]
    return jnp.concatenate([first * angular_cos_table - second * sine, second * angular_cos_table + first * sine, field[..., ROTARY_ENTRIES:]], axis=-1)

def normalize(field):
    return field * lax.rsqrt(lax.optimization_barrier(jnp.sum(field * field, axis=-1, keepdims=True)) + 1e-06)

def reference(segment_ids, attn_query, attention_keys, attention_values, attn_gate, delta_query, delta_key, update_rule_payload, delta_beta, delta_decay, delta_gate, norm_gain):
    slot_number = jnp.arange(TOKEN_SPAN_TOTAL, dtype=jnp.int32)
    boundary = jnp.concatenate([jnp.ones((1,), dtype=bool), segment_ids[1:] != segment_ids[:-1]])
    starts = lax.cummax(jnp.where(boundary, slot_number, 0), axis=0)
    shift_amount = slot_number - starts
    query_vector = apply_rotary(attn_query.astype(jnp.float32).reshape(TOKEN_SPAN_TOTAL, QUERY_HEADS, HEAD_WIDTH), shift_amount).astype(jnp.bfloat16)
    key_rows = apply_rotary(attention_keys.astype(jnp.float32).reshape(TOKEN_SPAN_TOTAL, KEY_VALUE_HEADS, HEAD_WIDTH), shift_amount).astype(jnp.bfloat16)
    value_matrix = attention_values.reshape(TOKEN_SPAN_TOTAL, KEY_VALUE_HEADS, HEAD_WIDTH)
    gates = jax.nn.sigmoid(attn_gate.astype(jnp.float32)).reshape(TOKEN_SPAN_TOTAL, QUERY_HEADS, HEAD_WIDTH)
    allowed = (slot_number[None, :] <= slot_number[:, None]) & (slot_number[None, :] >= starts[:, None])
    shared_portion = QUERY_HEADS // KEY_VALUE_HEADS
    heads = []
    for head in range(QUERY_HEADS):
        scores = jnp.dot(query_vector[:, head], key_rows[:, head // shared_portion].T, preferred_element_type=jnp.float32) * HEAD_WIDTH ** (-0.5)
        scores = jnp.where(allowed, scores, -jnp.inf)
        highest_score = lax.optimization_barrier(jnp.max(scores, axis=1, keepdims=True))
        weights = jnp.where(allowed, jnp.exp(scores - highest_score), 0.0)
        total = lax.optimization_barrier(jnp.sum(weights, axis=1, keepdims=True))
        mixed = jnp.dot(weights.astype(jnp.bfloat16), value_matrix[:, head // shared_portion], preferred_element_type=jnp.float32)
        heads.append(mixed / total * gates[:, head])
    attn_mixed = jnp.stack(heads, axis=1).reshape(TOKEN_SPAN_TOTAL, QUERY_HEADS * HEAD_WIDTH).astype(jnp.bfloat16)
    unit_query = normalize(delta_query.astype(jnp.float32).reshape(TOKEN_SPAN_TOTAL, HK, DK)) * DK ** (-0.5)
    unit_key = normalize(delta_key.astype(jnp.float32).reshape(TOKEN_SPAN_TOTAL, HK, DK))
    unit_query = jnp.repeat(unit_query, GROUP, axis=1)
    unit_key = jnp.repeat(unit_key, GROUP, axis=1)
    value_rows = update_rule_payload.astype(jnp.float32).reshape(TOKEN_SPAN_TOTAL, HV, DV)
    retain = jnp.exp(delta_decay) * (shift_amount != 0).astype(jnp.float32)[:, None]

    def advance(recurrent_state, inputs):
        query_entry, key_vector, value_row, beta_row, retain_row = inputs
        recurrent_state = retain_row[:, None, None] * recurrent_state
        estimate = jnp.einsum('cmp,cm->cp', recurrent_state, key_vector, precision=lax.Precision.HIGHEST)
        recurrent_state = recurrent_state + key_vector[:, :, None] * (beta_row[:, None] * (value_row - estimate))[:, None, :]
        return (recurrent_state, jnp.einsum('cmp,cm->cp', recurrent_state, query_entry, precision=lax.Precision.HIGHEST))
    final_state, outputs = lax.scan(advance, jnp.zeros((HV, DK, DV), jnp.float32), (unit_query, unit_key, value_rows, delta_beta, retain))
    spread = lax.rsqrt(lax.optimization_barrier(jnp.mean(outputs * outputs, axis=-1, keepdims=True)) + 1e-06)
    gate_rows = jax.nn.silu(delta_gate.astype(jnp.float32).reshape(TOKEN_SPAN_TOTAL, HV, DV))
    delta_mixed = (outputs * spread * norm_gain * gate_rows).reshape(TOKEN_SPAN_TOTAL, HV * DV).astype(jnp.bfloat16)
    return (attn_mixed, delta_mixed)
```

```python
from functools import partial

import jax
import jax.numpy as jnp
from jax import lax
from jax.experimental import pallas as pl
from jax.experimental.pallas import tpu as pltpu
from jax.sharding import PartitionSpec as P

HEAD_WIDTH = 256
ROTARY_ENTRIES = 64
DK = 128
DV = 128
DOCS = 8
ROPE_THETA = 10000000.0
LOG2E = 1.4426950408889634
MASKED = -1e30
EPS = 1e-6
LEVELS = 7
TILE = 128
KEYS_PER_STEP = 2
VMEM_LIMIT = 48 * 1024 * 1024

f32 = jnp.float32
bf16 = jnp.bfloat16


def dot(a, b, precision=None):
    return jnp.dot(a, b, preferred_element_type=f32, precision=precision)


def params():
    return pltpu.CompilerParams(vmem_limit_bytes=VMEM_LIMIT)


def cost(flops, nbytes, exps=0):
    return pl.CostEstimate(flops=flops, bytes_accessed=nbytes, transcendentals=exps)


def delta_local_kernel(
    half_ref,
    seg_ref,
    q_ref,
    k_ref,
    v_ref,
    beta_ref,
    decay_ref,
    map_add_ref,
    reach_ref,
    inner_ref,
    mask_ref,
    level_ref,
    crow_ref,
    ccol_ref,
    bcol_ref,
    first_ref,
):
    rows = q_ref.shape[0]
    step = pl.program_id(0)
    heads = 2 * KEYS_PER_STEP

    @pl.when(step == 0)
    def _():
        seg_row = seg_ref[...]
        seg_col = jnp.transpose(jnp.broadcast_to(seg_row, (TILE, rows)))
        seg_cols = jnp.concatenate([seg_col] * (rows // TILE), axis=1)
        r = lax.broadcasted_iota(jnp.int32, (rows, rows), 0)
        c = lax.broadcasted_iota(jnp.int32, (rows, rows), 1)
        mask_ref[...] = jnp.where((seg_cols == seg_row) & (r >= c), 0.0, MASKED)
        first_ref[...] = jnp.where(seg_col == seg_row[:, :1], 1.0, 0.0)
        r = lax.broadcasted_iota(jnp.int32, (TILE, TILE), 0)
        c = lax.broadcasted_iota(jnp.int32, (TILE, TILE), 1)
        top = jnp.bitwise_xor(r, c)
        for level in range(LEVELS):
            inside = (r > c) & (lax.shift_right_logical(top, level) == 1)
            level_ref[level] = jnp.where(inside, 1.0, 0.0).astype(bf16)
        all_heads = decay_ref.shape[1]
        base = half_ref[0] * (all_heads // 2)
        er = lax.broadcasted_iota(jnp.int32, (all_heads, TILE), 0)
        ec = lax.broadcasted_iota(jnp.int32, (all_heads, TILE), 1)
        pick = jnp.where(er - ec == base, 1.0, 0.0)
        tr = lax.broadcasted_iota(jnp.int32, (rows, rows), 0)
        tc = lax.broadcasted_iota(jnp.int32, (rows, rows), 1)
        tril = jnp.where(tr >= tc, 1.0, 0.0)
        decay = dot(decay_ref[...], pick, lax.Precision.HIGHEST) * LOG2E
        cumulative = dot(tril, decay, lax.Precision.HIGHEST)
        ccol_ref[...] = cumulative
        crow_ref[...] = jnp.transpose(cumulative)
        bcol_ref[...] = dot(beta_ref[...], pick, lax.Precision.HIGHEST)

    shift = lax.rem(TILE - step * heads, TILE)
    ccol = pltpu.roll(ccol_ref[...], shift, 1)
    bcol = pltpu.roll(bcol_ref[...], shift, 1)
    first = first_ref[...]
    eye = jnp.where(
        lax.broadcasted_iota(jnp.int32, (TILE, TILE), 0)
        == lax.broadcasted_iota(jnp.int32, (TILE, TILE), 1),
        1.0,
        0.0,
    )
    work = []
    for kk in range(KEYS_PER_STEP):
        cols = slice(kk * DK, (kk + 1) * DK)
        k_raw = k_ref[:, cols]
        q_raw = q_ref[:, cols]
        kf = k_raw.astype(f32)
        qf = q_raw.astype(f32)
        rk_col = lax.rsqrt(jnp.sum(kf * kf, axis=1, keepdims=True) + EPS)
        rq_col = lax.rsqrt(jnp.sum(qf * qf, axis=1, keepdims=True) + EPS) * DK**-0.5
        kt = jnp.transpose(kf)
        rk_row = lax.rsqrt(jnp.sum(kt * kt, axis=0, keepdims=True) + EPS)
        ktb = kt.astype(bf16)
        upper = dot(jnp.concatenate([k_raw[:TILE], q_raw[:TILE]], axis=0), ktb[:, :TILE])
        lower = dot(jnp.concatenate([k_raw[TILE:], q_raw[TILE:]], axis=0), ktb)
        gram1 = upper[:TILE] * rk_row[:, :TILE]
        probe1 = upper[TILE:] * rk_row[:, :TILE] * rq_col[:TILE]
        gram2 = lower[:TILE] * rk_row
        probe2 = lower[TILE:] * rk_row * rq_col[TILE:]
        kn = kf * rk_col
        qn = qf * rq_col
        for j in range(2):
            h = 2 * kk + j
            cc = ccol[:, h : h + 1]
            bt = bcol[:, h : h + 1]
            cr = crow_ref[pl.ds(step * heads + h, 1), :]
            span1 = jnp.exp2(cc[:TILE] - cr[:, :TILE] + mask_ref[:TILE, :TILE])
            span2 = jnp.exp2(cc[TILE:] - cr + mask_ref[TILE:, :])
            scale = -bt * rk_col
            d11 = (span1 * scale[:TILE] * gram1).astype(bf16)
            d2 = (span2 * scale[TILE:] * gram2).astype(bf16)
            p11 = (span1 * probe1).astype(bf16)
            p2 = (span2 * probe2).astype(bf16)
            entry = jnp.exp2(cc) * first
            right = jnp.concatenate(
                [bt * entry * kn, bt * v_ref[:, h * DV : (h + 1) * DV].astype(f32)], axis=1
            )
            kd = (kt * (rk_row * span2[TILE - 1 : TILE, :])).astype(bf16)
            work.append(
                dict(h=h, d=[d11, d2[:, TILE:]], d21=d2[:, :TILE], p11=p11, p2=p2, kd=kd,
                     right=right, reach=entry * qn, last=entry[rows - 1 : rows, :])
            )
    mats = [m for w in work for m in w["d"]]
    inverses = [m * level_ref[0] for m in mats]
    for level in range(1, LEVELS):
        keep = level_ref[level]
        picked = [m * keep for m in mats]
        ys = [
            (p.astype(f32) + dot(p, x)).astype(bf16) for p, x in zip(picked, inverses)
        ]
        inverses = [
            x + (y.astype(f32) + dot(x, y)).astype(bf16) for x, y in zip(inverses, ys)
        ]
    for i, w in enumerate(work):
        x1, x2 = inverses[2 * i], inverses[2 * i + 1]
        h = w["h"]
        r1 = w["right"][:TILE]
        u1 = (r1 + dot(x1, r1.astype(bf16))).astype(bf16)
        r2 = w["right"][TILE:] + dot(w["d21"], u1)
        u2 = (r2 + dot(x2, r2.astype(bf16))).astype(bf16)
        u = jnp.concatenate([u1, u2], axis=0)
        pu = jnp.concatenate([dot(w["p11"], u1), dot(w["p2"], u)], axis=0)
        ma = dot(w["kd"], u)
        map_add_ref[h] = jnp.concatenate(
            [w["last"] * eye - ma[:, :DK], ma[:, DK:]], axis=1
        ).astype(bf16)
        reach_ref[:, h * DK : (h + 1) * DK] = (w["reach"] - pu[:, :DK]).astype(bf16)
        inner_ref[:, h * DV : (h + 1) * DV] = pu[:, DK:].astype(inner_ref.dtype)


def delta_local(half, seg_row, query, key, value, beta, decay):
    rows = query.shape[0]
    heads = 2 * KEYS_PER_STEP
    n = value.shape[1] // DV // 2
    steps = n // heads
    kw = KEYS_PER_STEP * DK
    vw = heads * DV

    def at_half(i, s):
        return (0, s[0] * steps + i)

    def whole(i, s):
        return (0, 0)

    return pl.pallas_call(
        delta_local_kernel,
        grid_spec=pltpu.PrefetchScalarGridSpec(
            num_scalar_prefetch=1,
            grid=(steps,),
            in_specs=[
                pl.BlockSpec((1, rows), whole),
                pl.BlockSpec((rows, kw), at_half),
                pl.BlockSpec((rows, kw), at_half),
                pl.BlockSpec((rows, vw), at_half),
                pl.BlockSpec(beta.shape, whole),
                pl.BlockSpec(decay.shape, whole),
            ],
            out_specs=[
                pl.BlockSpec((heads, DK, DK + DV), lambda i, s: (i, 0, 0)),
                pl.BlockSpec((rows, heads * DK), lambda i, s: (0, i)),
                pl.BlockSpec((rows, vw), lambda i, s: (0, i)),
            ],
            scratch_shapes=[
                pltpu.VMEM((rows, rows), f32),
                pltpu.VMEM((LEVELS, TILE, TILE), bf16),
                pltpu.VMEM((TILE, rows), f32),
                pltpu.VMEM((rows, TILE), f32),
                pltpu.VMEM((rows, TILE), f32),
                pltpu.VMEM((rows, TILE), f32),
            ],
        ),
        out_shape=[
            jax.ShapeDtypeStruct((n, DK, DK + DV), bf16),
            jax.ShapeDtypeStruct((rows, n * DK), bf16),
            jax.ShapeDtypeStruct((rows, n * DV), f32),
        ],
        compiler_params=params(),
        cost_estimate=cost(6 * 10**9, 3 * 2**20),
        name="delta_local",
    )(half, seg_row, query, key, value, beta, decay)


def flag(flags_ref, i):
    return flags_ref[i].astype(f32)


def ordered(flags_ref, mine, other):
    odd = flags_ref[0] == 1
    return jnp.where(odd, other, mine), jnp.where(odd, mine, other)


def compose_kernel(flags_ref, mine_ref, other_ref, map_ref, add_ref):
    into, across = flag(flags_ref, 1), flag(flags_ref, 2)
    for h in range(mine_ref.shape[0]):
        early, late = ordered(flags_ref, mine_ref[h], other_ref[h])
        both = dot(late[:, :DK], early) * across
        map_ref[h] = (both[:, :DK] * into).astype(bf16)
        add_ref[h] = (both[:, DK:] + late[:, DK:].astype(f32)).astype(bf16)


def relay_kernel(map_ref, add_ref, state_ref, out_ref):
    for h in range(map_ref.shape[0]):
        out_ref[h] = (dot(map_ref[h], state_ref[h]) + add_ref[h].astype(f32)).astype(bf16)


def arrive_kernel(flags_ref, mine_ref, other_ref, state_ref, keep_ref, give_ref):
    into, across = flag(flags_ref, 1), flag(flags_ref, 2)
    odd = flags_ref[0] == 1
    for h in range(mine_ref.shape[0]):
        early, _ = ordered(flags_ref, mine_ref[h], other_ref[h])
        first = state_ref[h] * into.astype(bf16)
        second = (
            (dot(early[:, :DK], first) + early[:, DK:].astype(f32)) * across
        ).astype(bf16)
        keep_ref[h] = jnp.where(odd, second, first)
        give_ref[h] = jnp.where(odd, first, second)


SMEM = pl.BlockSpec(memory_space=pltpu.SMEM)
VMEM = pl.BlockSpec(memory_space=pltpu.VMEM)


def small_call(kernel, name, outs, *args, scalars=0):
    return pl.pallas_call(
        kernel,
        in_specs=[SMEM] * scalars + [VMEM] * (len(args) - scalars),
        out_specs=[VMEM] * len(outs),
        out_shape=outs,
        compiler_params=params(),
        cost_estimate=cost(10**8, 2**20),
        name=name,
    )(*args)


def delta_out_kernel(half_ref, reach_ref, inner_ref, state_ref, gate_ref, gain_ref, *rest):
    out_ref = rest[-1]
    gain = gain_ref[...]
    for h in range(state_ref.shape[0]):
        cols = slice(h * DV, (h + 1) * DV)
        out = inner_ref[:, cols] + dot(reach_ref[:, cols], state_ref[h])
        spread = lax.rsqrt(jnp.mean(out * out, axis=1, keepdims=True) + EPS)
        gate = gate_ref[:, cols].astype(f32)
        gate = gate * jax.nn.sigmoid(gate)
        out_ref[:, cols] = (out * spread * gain * gate).astype(bf16)


def delta_out(half, reach, inner, state, gate, gain, partial_out=None):
    rows = reach.shape[0]
    n = state.shape[0]
    heads = 4
    steps = n // heads

    def at_half(i, s):
        return (0, s[0] * steps + i)

    in_specs = [
        pl.BlockSpec((rows, heads * DK), lambda i, s: (0, i)),
        pl.BlockSpec((rows, heads * DV), lambda i, s: (0, i)),
        pl.BlockSpec((heads, DK, DV), lambda i, s: (i, 0, 0)),
        pl.BlockSpec((rows, heads * DV), at_half),
        pl.BlockSpec((1, DV), lambda i, s: (0, 0)),
    ]
    args = [half, reach, inner, state, gate, gain]
    aliases = {}
    if partial_out is not None:
        in_specs.append(pl.BlockSpec(memory_space=pl.ANY))
        args.append(partial_out)
        aliases = {6: 0}
    return pl.pallas_call(
        delta_out_kernel,
        grid_spec=pltpu.PrefetchScalarGridSpec(
            num_scalar_prefetch=1,
            grid=(steps,),
            in_specs=in_specs,
            out_specs=pl.BlockSpec((rows, heads * DV), at_half),
        ),
        out_shape=jax.ShapeDtypeStruct(gate.shape, bf16),
        input_output_aliases=aliases,
        compiler_params=params(),
        cost_estimate=cost(10**8, 3 * 2**20),
        name="delta_out",
    )(*args)


def attention_kernel(ids_ref, freq_ref, q_ref, gate_ref, *rest):
    *pieces, out_ref, kt_ref, v_ref, mask_ref, cos_ref, sin_ref = rest
    rows = q_ref.shape[0]
    window = ids_ref.shape[1]
    half = ROTARY_ENTRIES // 2

    @pl.when(pl.program_id(0) == 0)
    def _():
        ids = jnp.broadcast_to(ids_ref[...], (DOCS, window))
        docs = lax.broadcasted_iota(jnp.int32, (DOCS, window), 0).astype(f32)
        before = jnp.sum(jnp.where(ids < docs, 1.0, 0.0), axis=1, keepdims=True)
        start = jnp.sum(jnp.where(ids == docs, before, 0.0), axis=0, keepdims=True)
        place = lax.broadcasted_iota(jnp.int32, (1, window), 1).astype(f32)
        angle = freq_ref[:, :1] * (place - start)
        cosine = jnp.cos(angle)
        sine = jnp.sin(angle)
        for b, (ref, index) in enumerate(blocks_of(pieces)):
            cols = slice(b * rows, (b + 1) * rows)
            piece = ref[...] if index is None else ref[index]
            kt = jnp.transpose(piece[:, :HEAD_WIDTH].astype(f32))
            one, two = kt[:half], kt[half:ROTARY_ENTRIES]
            cb, sb = cosine[:, cols], sine[:, cols]
            kt_ref[:half, cols] = (one * cb - two * sb).astype(bf16)
            kt_ref[half:ROTARY_ENTRIES, cols] = (two * cb + one * sb).astype(bf16)
            kt_ref[ROTARY_ENTRIES:, cols] = kt[ROTARY_ENTRIES:].astype(bf16)
            v_ref[cols, :] = piece[:, HEAD_WIDTH:]
        cq, sq = cosine[:, window - rows :], sine[:, window - rows :]
        rest_rows = TILE - ROTARY_ENTRIES
        cos_ref[...] = jnp.transpose(
            jnp.concatenate([cq, cq, jnp.ones((rest_rows, rows), f32)], axis=0)
        )
        sin_ref[...] = jnp.transpose(
            jnp.concatenate([-sq, sq, jnp.zeros((rest_rows, rows), f32)], axis=0)
        )
        own = ids_ref[:, window - rows :]
        own_col = jnp.transpose(jnp.broadcast_to(own, (TILE, rows)))
        own_cols = jnp.concatenate([own_col] * (window // TILE), axis=1)
        r = lax.broadcasted_iota(jnp.int32, (rows, window), 0) + (window - rows)
        c = lax.broadcasted_iota(jnp.int32, (rows, window), 1)
        mask_ref[...] = jnp.where((own_cols == ids_ref[...]) & (c <= r), 0.0, MASKED)

    scaling = HEAD_WIDTH**-0.5
    lane = lax.broadcasted_iota(jnp.int32, (rows, TILE), 1)
    for h in range(q_ref.shape[1] // HEAD_WIDTH):
        base = h * HEAD_WIDTH
        x = q_ref[:, base : base + TILE].astype(f32)
        swapped = jnp.where(lane < half, pltpu.roll(x, TILE - half, 1), pltpu.roll(x, half, 1))
        rotated = ((x * cos_ref[...] + swapped * sin_ref[...]) * scaling).astype(bf16)
        tail = q_ref[:, base + TILE : base + HEAD_WIDTH] * jnp.asarray(scaling, bf16)
        scores = dot(jnp.concatenate([rotated, tail], axis=1), kt_ref[...]) + mask_ref[...]
        best = jnp.max(scores, axis=1, keepdims=True)
        weights = jnp.exp(scores - best)
        total = jnp.sum(weights, axis=1, keepdims=True)
        mixed = dot(weights.astype(bf16), v_ref[...])
        gate = jax.nn.sigmoid(gate_ref[:, base : base + HEAD_WIDTH].astype(f32))
        out_ref[:, base : base + HEAD_WIDTH] = (mixed / total * gate).astype(bf16)


def blocks_of(pieces):
    own, *same, other = pieces
    order = [(own, None)]
    for i, ref in enumerate(same):
        order += [(other, i), (ref, None)]
    return order[::-1]


def attention(ids, freq, query, gate, own, same, other):
    rows = query.shape[0]
    window = ids.shape[1]
    heads = 2
    width = heads * HEAD_WIDTH
    pieces = [own, *same, other]
    whole = [pl.BlockSpec(p.shape, lambda i, n=p.ndim: (0,) * n) for p in pieces]
    return pl.pallas_call(
        attention_kernel,
        grid=(query.shape[1] // width,),
        in_specs=[
            pl.BlockSpec(ids.shape, lambda i: (0, 0)),
            pl.BlockSpec(freq.shape, lambda i: (0, 0)),
            pl.BlockSpec((rows, width), lambda i: (0, i)),
            pl.BlockSpec((rows, width), lambda i: (0, i)),
            *whole,
        ],
        out_specs=pl.BlockSpec((rows, width), lambda i: (0, i)),
        out_shape=jax.ShapeDtypeStruct(query.shape, bf16),
        scratch_shapes=[
            pltpu.VMEM((HEAD_WIDTH, window), bf16),
            pltpu.VMEM((window, HEAD_WIDTH), bf16),
            pltpu.VMEM((rows, window), f32),
            pltpu.VMEM((rows, TILE), f32),
            pltpu.VMEM((rows, TILE), f32),
        ],
        compiler_params=params(),
        cost_estimate=cost(6 * 10**9, 5 * 2**20, 3 * 10**6),
        name="attention",
    )(ids, freq, query, gate, *pieces)


def up_chip(value, ranks):
    return lax.ppermute(value, "ctx", [(i, i + 2) for i in range(ranks - 2)])


def swap_cores(value, ranks):
    return lax.ppermute(value, "ctx", [(i, i ^ 1) for i in range(ranks)])


def per_device(
    segment_ids,
    attn_query,
    attention_keys,
    attention_values,
    attn_gate,
    delta_query,
    delta_key,
    update_rule_payload,
    delta_beta,
    delta_decay,
    delta_gate,
    norm_gain,
):
    ranks = lax.axis_size("ctx")
    rank = lax.axis_index("ctx")
    rows = segment_ids.shape[0]
    hops = ranks // 4
    core = rank % 2
    odd = core == 1

    ids = lax.all_gather(segment_ids, "ctx", axis=0, tiled=True)

    own = jnp.concatenate([attention_keys, attention_values], axis=1)
    same = []
    for _ in range(hops):
        same.append(up_chip(same[-1] if same else own, ranks))
    chain = [own, *same]
    other = swap_cores(
        jnp.stack([jnp.where(odd, chain[i + 1], chain[i]) for i in range(hops)]), ranks
    )

    seg_row = segment_ids.astype(f32).reshape(1, rows)
    keep_half = core.reshape(1).astype(jnp.int32)
    give_half = 1 - keep_half
    local = partial(
        delta_local,
        seg_row=seg_row,
        query=delta_query,
        key=delta_key,
        value=update_rule_payload,
        beta=delta_beta,
        decay=delta_decay,
    )
    give_ma, give_reach, give_inner = local(give_half)
    other_ma = swap_cores(give_ma, ranks)
    keep_ma, keep_reach, keep_inner = local(keep_half)

    chip_first = (rank - core) * rows
    into = (rank > 1) & (ids[jnp.maximum(chip_first - 1, 0)] == ids[chip_first])
    across = ids[chip_first + rows - 1] == ids[chip_first + rows]
    flags = jnp.stack([core, into, across]).astype(jnp.int32)

    n = keep_ma.shape[0]
    state_like = jax.ShapeDtypeStruct((n, DK, DV), bf16)
    chip_map, chip_add = small_call(
        compose_kernel, "compose", [state_like] * 2, flags, keep_ma, other_ma, scalars=1
    )
    state = up_chip(chip_add, ranks)
    for _ in range(hops - 1):
        (leaving,) = small_call(relay_kernel, "relay", [state_like], chip_map, chip_add, state)
        state = up_chip(leaving, ranks)
    keep_state, pass_state = small_call(
        arrive_kernel, "arrive", [state_like] * 2, flags, keep_ma, other_ma, state, scalars=1
    )
    give_state = swap_cores(pass_state, ranks)

    window = (2 * hops + 1) * rows
    padded = jnp.concatenate([jnp.full((window - rows,), -1, jnp.int32), ids]).astype(f32)
    window_ids = lax.dynamic_slice(padded, (rank * rows,), (window,)).reshape(1, window)
    index = jnp.arange(ROTARY_ENTRIES // 2).astype(f32)
    freq = ROPE_THETA ** (-2.0 * index / ROTARY_ENTRIES)
    freq = jnp.broadcast_to(freq[:, None], (ROTARY_ENTRIES // 2, TILE))
    attn_mixed = attention(window_ids, freq, attn_query, attn_gate, own, same, other)

    gain = norm_gain.reshape(1, DV)
    delta_mixed = delta_out(keep_half, keep_reach, keep_inner, keep_state, delta_gate, gain)
    delta_mixed = delta_out(
        give_half, give_reach, give_inner, give_state, delta_gate, gain, delta_mixed
    )
    return (attn_mixed, delta_mixed)


def solution(mesh):
    rows = P(("dp", "ctx"))
    wide = P(("dp", "ctx"), None)
    return jax.shard_map(
        per_device,
        mesh=mesh,
        in_specs=(rows,) + (wide,) * 10 + (P(),),
        out_specs=(wide, wide),
        check_vma=False,
    )
```

```python
from functools import partial

import jax
import jax.numpy as jnp
from jax import lax
from jax.experimental import pallas as pl
from jax.experimental.pallas import tpu as pltpu
from jax.sharding import PartitionSpec as P

HEAD_WIDTH = 256
ROTARY_ENTRIES = 64
DK = 128
DV = 128
DOCS = 8
ROPE_THETA = 10000000.0
LOG2E = 1.4426950408889634
MASKED = -1e30
EPS = 1e-6
TILE = 128
KEYS_PER_STEP = 2
VMEM_LIMIT = 60 * 1024 * 1024

f32 = jnp.float32
bf16 = jnp.bfloat16


def dot(a, b, precision=None):
    return jnp.dot(a, b, preferred_element_type=f32, precision=precision)


def params():
    return pltpu.CompilerParams(vmem_limit_bytes=VMEM_LIMIT)


def cost(flops, nbytes, exps=0):
    return pl.CostEstimate(flops=flops, bytes_accessed=nbytes, transcendentals=exps)


BLOCK = 16
MERGES = 3


def odd_rows(m, b):
    return jnp.concatenate([m[i + b : i + 2 * b] for i in range(0, TILE, 2 * b)], axis=0)


def interleave(even, odd, b):
    parts = []
    for i in range(0, TILE // 2, b):
        parts += [even[i : i + b], odd[i : i + b]]
    return jnp.concatenate(parts, axis=0)


def even_rows(m, b):
    return jnp.concatenate([m[i : i + b] for i in range(0, TILE, 2 * b)], axis=0)


def block_inverses(mats):
    row = lax.broadcasted_iota(jnp.int32, (BLOCK, TILE), 0)
    lane = lax.broadcasted_iota(jnp.int32, (BLOCK, TILE), 1)
    within = lax.rem(lane, BLOCK)
    group = lane // BLOCK
    folded = []
    for m in mats:
        z = jnp.where(group == 0, m[:BLOCK], 0.0)
        for r in range(1, TILE // BLOCK):
            z = jnp.where(group == r, m[r * BLOCK : (r + 1) * BLOCK], z)
        folded.append(jnp.where(row > within, z, 0.0))
    xs = [jnp.where(row == within, 1.0, 0.0)] * len(mats)
    small = 8
    for k in range(BLOCK - 1):
        low = 0 if k < small - 1 else small
        at = (group * BLOCK + k)[low:]
        for i, z in enumerate(folded):
            spread = jnp.take_along_axis(z[low:], at, axis=1)
            x = xs[i]
            new = x[low:] + spread * x[k : k + 1]
            xs[i] = new if low == 0 else jnp.concatenate([x[:low], new], axis=0)
    out = []
    for x in xs:
        x = jnp.where(row > within, x, 0.0)
        out.append(
            jnp.concatenate(
                [jnp.where(group == r, x, 0.0) for r in range(TILE // BLOCK)], axis=0
            ).astype(bf16)
        )
    return out


def delta_local_kernel(
    half_ref,
    seg_ref,
    q_ref,
    k_ref,
    v_ref,
    beta_ref,
    decay_ref,
    map_add_ref,
    reach_ref,
    inner_ref,
    mask_ref,
    level_ref,
    crow_ref,
    ccol_ref,
    bcol_ref,
    first_ref,
):
    rows = q_ref.shape[0]
    step = pl.program_id(0)
    heads = 2 * KEYS_PER_STEP

    @pl.when(step == 0)
    def _():
        seg_row = seg_ref[...]
        seg_col = jnp.transpose(jnp.broadcast_to(seg_row, (TILE, rows)))
        seg_cols = jnp.concatenate([seg_col] * (rows // TILE), axis=1)
        r = lax.broadcasted_iota(jnp.int32, (rows, rows), 0)
        c = lax.broadcasted_iota(jnp.int32, (rows, rows), 1)
        mask_ref[...] = jnp.where((seg_cols == seg_row) & (r >= c), 0.0, MASKED)
        first_ref[...] = jnp.where(seg_col == seg_row[:, :1], 1.0, 0.0)
        r = lax.broadcasted_iota(jnp.int32, (TILE, TILE), 0)
        c = lax.broadcasted_iota(jnp.int32, (TILE, TILE), 1)
        for level in range(MERGES):
            b = BLOCK << level
            sibling = jnp.where(r // b == c // b + 1, 1.0, 0.0)
            level_ref[level] = odd_rows(sibling, b).astype(bf16)
        all_heads = decay_ref.shape[1]
        base = half_ref[0] * (all_heads // 2)
        er = lax.broadcasted_iota(jnp.int32, (all_heads, TILE), 0)
        ec = lax.broadcasted_iota(jnp.int32, (all_heads, TILE), 1)
        pick = jnp.where(er - ec == base, 1.0, 0.0)
        tr = lax.broadcasted_iota(jnp.int32, (rows, rows), 0)
        tc = lax.broadcasted_iota(jnp.int32, (rows, rows), 1)
        tril = jnp.where(tr >= tc, 1.0, 0.0)
        decay = dot(decay_ref[...], pick, lax.Precision.HIGHEST) * LOG2E
        cumulative = dot(tril, decay, lax.Precision.HIGHEST)
        ccol_ref[...] = cumulative
        crow_ref[...] = jnp.transpose(cumulative)
        bcol_ref[...] = dot(beta_ref[...], pick, lax.Precision.HIGHEST)
        end = map_add_ref.shape[0] - BLOCK
        map_add_ref[end:, :] = jnp.broadcast_to(seg_row, (BLOCK, rows)).astype(bf16)

    shift = lax.rem(TILE - step * heads, TILE)
    ccol = pltpu.roll(ccol_ref[...], shift, 1)
    bcol = pltpu.roll(bcol_ref[...], shift, 1)
    first = first_ref[...]
    eye = jnp.where(
        lax.broadcasted_iota(jnp.int32, (TILE, TILE), 0)
        == lax.broadcasted_iota(jnp.int32, (TILE, TILE), 1),
        1.0,
        0.0,
    )
    work = []
    for kk in range(KEYS_PER_STEP):
        cols = slice(kk * DK, (kk + 1) * DK)
        k_raw = k_ref[:, cols]
        q_raw = q_ref[:, cols]
        kf = k_raw.astype(f32)
        qf = q_raw.astype(f32)
        rk_col = lax.rsqrt(jnp.sum(kf * kf, axis=1, keepdims=True) + EPS)
        rq_col = lax.rsqrt(jnp.sum(qf * qf, axis=1, keepdims=True) + EPS) * DK**-0.5
        kt = jnp.transpose(kf)
        rk_row = lax.rsqrt(jnp.sum(kt * kt, axis=0, keepdims=True) + EPS)
        ktb = kt.astype(bf16)
        upper = dot(jnp.concatenate([k_raw[:TILE], q_raw[:TILE]], axis=0), ktb[:, :TILE])
        lower = dot(jnp.concatenate([k_raw[TILE:], q_raw[TILE:]], axis=0), ktb)
        gram1 = upper[:TILE] * rk_row[:, :TILE]
        probe1 = upper[TILE:] * rk_row[:, :TILE] * rq_col[:TILE]
        gram2 = lower[:TILE] * rk_row
        probe2 = lower[TILE:] * rk_row * rq_col[TILE:]
        kn = kf * rk_col
        qn = qf * rq_col
        for j in range(2):
            h = 2 * kk + j
            cc = ccol[:, h : h + 1]
            bt = bcol[:, h : h + 1]
            cr = crow_ref[pl.ds(step * heads + h, 1), :]
            span1 = jnp.exp2(cc[:TILE] - cr[:, :TILE] + mask_ref[:TILE, :TILE])
            span2 = jnp.exp2(cc[TILE:] - cr + mask_ref[TILE:, :])
            scale = -bt * rk_col
            d11 = span1 * scale[:TILE] * gram1
            d2 = span2 * scale[TILE:] * gram2
            p11 = (span1 * probe1).astype(bf16)
            p2 = (span2 * probe2).astype(bf16)
            entry = jnp.exp2(cc) * first
            right = jnp.concatenate(
                [bt * entry * kn, bt * v_ref[:, h * DV : (h + 1) * DV].astype(f32)], axis=1
            )
            kd = (kt * (rk_row * span2[TILE - 1 : TILE, :])).astype(bf16)
            work.append(
                dict(h=h, d=[d11, d2[:, TILE:]], d21=d2[:, :TILE].astype(bf16), p11=p11, p2=p2,
                     kd=kd, right=right, reach=entry * qn, last=entry[rows - 1 : rows, :])
            )
    mats = [m for w in work for m in w["d"]]
    inverses = block_inverses(mats)
    mats = [m.astype(bf16) for m in mats]
    zeros = jnp.zeros((TILE // 2, TILE), bf16)
    for level in range(MERGES):
        b = BLOCK << level
        keep = level_ref[level]
        picked = [odd_rows(m, b) * keep for m in mats]
        ys = [(p.astype(f32) + dot(p, x)).astype(bf16) for p, x in zip(picked, inverses)]
        odds = [odd_rows(x, b) for x in inverses]
        odds = [
            x + (y.astype(f32) + dot(x, interleave(zeros, y, b))).astype(bf16)
            for x, y in zip(odds, ys)
        ]
        inverses = [interleave(even_rows(x, b), o, b) for x, o in zip(inverses, odds)]
    for i, w in enumerate(work):
        x1, x2 = inverses[2 * i], inverses[2 * i + 1]
        h = w["h"]
        r1 = w["right"][:TILE]
        u1 = (r1 + dot(x1, r1.astype(bf16))).astype(bf16)
        r2 = w["right"][TILE:] + dot(w["d21"], u1)
        u2 = (r2 + dot(x2, r2.astype(bf16))).astype(bf16)
        u = jnp.concatenate([u1, u2], axis=0)
        pu = jnp.concatenate([dot(w["p11"], u1), dot(w["p2"], u)], axis=0)
        ma = dot(w["kd"], u)
        at = pl.multiple_of((step * heads + h) * DK, DK)
        map_add_ref[pl.ds(at, DK), :] = jnp.concatenate(
            [w["last"] * eye - ma[:, :DK], ma[:, DK:]], axis=1
        ).astype(bf16)
        reach_ref[:, h * DK : (h + 1) * DK] = (w["reach"] - pu[:, :DK]).astype(bf16)
        inner_ref[:, h * DV : (h + 1) * DV] = pu[:, DK:].astype(inner_ref.dtype)


def delta_local(half, seg_row, query, key, value, beta, decay):
    rows = query.shape[0]
    heads = 2 * KEYS_PER_STEP
    n = value.shape[1] // DV // 2
    steps = n // heads
    kw = KEYS_PER_STEP * DK
    vw = heads * DV
    tall = n * DK + BLOCK

    def at_half(i, s):
        return (0, s[0] * steps + i)

    def whole(i, s):
        return (0, 0)

    return pl.pallas_call(
        delta_local_kernel,
        grid_spec=pltpu.PrefetchScalarGridSpec(
            num_scalar_prefetch=1,
            grid=(steps,),
            in_specs=[
                pl.BlockSpec((1, rows), whole),
                pl.BlockSpec((rows, kw), at_half),
                pl.BlockSpec((rows, kw), at_half),
                pl.BlockSpec((rows, vw), at_half),
                pl.BlockSpec(beta.shape, whole),
                pl.BlockSpec(decay.shape, whole),
            ],
            out_specs=[
                pl.BlockSpec((tall, DK + DV), whole),
                pl.BlockSpec((rows, heads * DK), lambda i, s: (0, i)),
                pl.BlockSpec((rows, vw), lambda i, s: (0, i)),
            ],
            scratch_shapes=[
                pltpu.VMEM((rows, rows), f32),
                pltpu.VMEM((MERGES, TILE // 2, TILE), bf16),
                pltpu.VMEM((TILE, rows), f32),
                pltpu.VMEM((rows, TILE), f32),
                pltpu.VMEM((rows, TILE), f32),
                pltpu.VMEM((rows, TILE), f32),
            ],
        ),
        out_shape=[
            jax.ShapeDtypeStruct((tall, DK + DV), bf16),
            jax.ShapeDtypeStruct((rows, n * DK), bf16),
            jax.ShapeDtypeStruct((rows, n * DV), f32),
        ],
        compiler_params=params(),
        cost_estimate=cost(6 * 10**9, 3 * 2**20),
        name="delta_local",
    )(half, seg_row, query, key, value, beta, decay)


def ids_of(ref):
    end = ref.shape[0] - BLOCK
    return ref[end : end + BLOCK, :].astype(f32)[:1]


def put_id(ref, value):
    end = ref.shape[0] - BLOCK
    ref[end:, :] = jnp.broadcast_to(value, (BLOCK, ref.shape[1])).astype(bf16)


def matching(a, b):
    return jnp.where(a == b, 1.0, 0.0)


def compose_kernel(core_ref, mine_ref, other_ref, map_ref, add_ref):
    odd = core_ref[0] == 1
    mine_ids, other_ids = ids_of(mine_ref), ids_of(other_ref)
    early_ids = jnp.where(odd, other_ids, mine_ids)
    late_ids = jnp.where(odd, mine_ids, other_ids)
    across = matching(early_ids[:, -1:], late_ids[:, :1])
    put_id(map_ref, early_ids[:, :1])
    put_id(add_ref, late_ids[:, -1:])
    for h in range(mine_ref.shape[0] // DK):
        at = slice(h * DK, (h + 1) * DK)
        mine, other = mine_ref[at], other_ref[at]
        early, late = jnp.where(odd, other, mine), jnp.where(odd, mine, other)
        both = dot(late[:, :DK], early) * across
        map_ref[at] = both[:, :DK].astype(bf16)
        add_ref[at] = (both[:, DK:] + late[:, DK:].astype(f32)).astype(bf16)


def relay_kernel(map_ref, add_ref, state_ref, out_ref):
    into = matching(ids_of(state_ref), ids_of(map_ref))
    put_id(out_ref, ids_of(add_ref))
    for h in range(map_ref.shape[0] // DK):
        at = slice(h * DK, (h + 1) * DK)
        out_ref[at] = (dot(map_ref[at], state_ref[at]) * into + add_ref[at].astype(f32)).astype(bf16)


def arrive_kernel(core_ref, mine_ref, other_ref, state_ref, keep_ref, give_ref):
    odd = core_ref[0] == 1
    mine_ids, other_ids = ids_of(mine_ref), ids_of(other_ref)
    early_ids = jnp.where(odd, other_ids, mine_ids)
    late_ids = jnp.where(odd, mine_ids, other_ids)
    across = matching(early_ids[:, -1:], late_ids[:, :1])
    into = matching(ids_of(state_ref), early_ids[:, :1])
    for h in range(keep_ref.shape[0] // DK):
        at = slice(h * DK, (h + 1) * DK)
        early = jnp.where(odd, other_ref[at], mine_ref[at])
        first = (state_ref[at].astype(f32) * into).astype(bf16)
        second = (
            (dot(early[:, :DK], first) + early[:, DK:].astype(f32)) * across
        ).astype(bf16)
        keep_ref[at] = jnp.where(odd, second, first)
        give_ref[at] = jnp.where(odd, first, second)


SMEM = pl.BlockSpec(memory_space=pltpu.SMEM)
VMEM = pl.BlockSpec(memory_space=pltpu.VMEM)


def small_call(kernel, name, outs, *args, scalars=0):
    return pl.pallas_call(
        kernel,
        in_specs=[SMEM] * scalars + [VMEM] * (len(args) - scalars),
        out_specs=[VMEM] * len(outs),
        out_shape=outs,
        compiler_params=params(),
        cost_estimate=cost(10**8, 2**20),
        name=name,
    )(*args)


def delta_out_kernel(half_ref, reach_ref, inner_ref, state_ref, gate_ref, gain_ref, *rest):
    out_ref = rest[-1]
    gain = gain_ref[...]
    for h in range(state_ref.shape[0] // DK):
        cols = slice(h * DV, (h + 1) * DV)
        state = state_ref[h * DK : (h + 1) * DK]
        out = inner_ref[:, cols].astype(f32) + dot(reach_ref[:, cols], state)
        spread = lax.rsqrt(jnp.mean(out * out, axis=1, keepdims=True) + EPS)
        gate = gate_ref[:, cols].astype(f32)
        gate = gate * jax.nn.sigmoid(gate)
        out_ref[:, cols] = (out * spread * gain * gate).astype(bf16)


def delta_out(half, reach, inner, state, gate, gain, partial_out=None):
    rows = reach.shape[0]
    n = state.shape[0] // DK
    heads = 4
    steps = n // heads

    def at_half(i, s):
        return (0, s[0] * steps + i)

    in_specs = [
        pl.BlockSpec((rows, heads * DK), lambda i, s: (0, i)),
        pl.BlockSpec((rows, heads * DV), lambda i, s: (0, i)),
        pl.BlockSpec((heads * DK, DV), lambda i, s: (i, 0)),
        pl.BlockSpec((rows, heads * DV), at_half),
        pl.BlockSpec((1, DV), lambda i, s: (0, 0)),
    ]
    args = [half, reach, inner, state, gate, gain]
    aliases = {}
    if partial_out is not None:
        in_specs.append(pl.BlockSpec(memory_space=pl.ANY))
        args.append(partial_out)
        aliases = {6: 0}
    return pl.pallas_call(
        delta_out_kernel,
        grid_spec=pltpu.PrefetchScalarGridSpec(
            num_scalar_prefetch=1,
            grid=(steps,),
            in_specs=in_specs,
            out_specs=pl.BlockSpec((rows, heads * DV), at_half),
        ),
        out_shape=jax.ShapeDtypeStruct(gate.shape, bf16),
        input_output_aliases=aliases,
        compiler_params=params(),
        cost_estimate=cost(10**8, 3 * 2**20),
        name="delta_out",
    )(*args)


def blocks_of(pieces):
    own, *same, other = pieces
    order = [(own, None)]
    for i, ref in enumerate(same):
        order += [(other, i), (ref, None)]
    return order[::-1]


def window_kernel(freq_ref, *rest):
    *pieces, kt_ref, v_ref, ids_ref, cos_ref, sin_ref = rest
    rows = cos_ref.shape[0]
    window = ids_ref.shape[1]
    half = ROTARY_ENTRIES // 2
    blocks = [ref if index is None else ref.at[index] for ref, index in blocks_of(pieces)]
    row_ids = jnp.concatenate(
        [ref[rows : rows + BLOCK, :rows].astype(f32)[:1] for ref in blocks], axis=1
    )
    ids_ref[...] = row_ids
    ids = jnp.broadcast_to(row_ids, (DOCS, window))
    docs = lax.broadcasted_iota(jnp.int32, (DOCS, window), 0).astype(f32) + 1.0
    before = jnp.sum(jnp.where(ids < docs, 1.0, 0.0), axis=1, keepdims=True)
    start = jnp.sum(jnp.where(ids == docs, before, 0.0), axis=0, keepdims=True)
    place = lax.broadcasted_iota(jnp.int32, (1, window), 1).astype(f32)
    angle = freq_ref[:, :1] * (place - start)
    cosine = jnp.cos(angle)
    sine = jnp.sin(angle)
    for b, ref in enumerate(blocks):
        cols = slice(b * rows, (b + 1) * rows)
        kt = jnp.transpose(ref[:rows, :HEAD_WIDTH].astype(f32))
        one, two = kt[:half], kt[half:ROTARY_ENTRIES]
        cb, sb = cosine[:, cols], sine[:, cols]
        kt_ref[:half, cols] = (one * cb - two * sb).astype(bf16)
        kt_ref[half:ROTARY_ENTRIES, cols] = (two * cb + one * sb).astype(bf16)
        kt_ref[ROTARY_ENTRIES:, cols] = kt[ROTARY_ENTRIES:].astype(bf16)
        v_ref[cols, :] = ref[:rows, HEAD_WIDTH:]
    cq, sq = cosine[:, window - rows :], sine[:, window - rows :]
    rest_rows = TILE - ROTARY_ENTRIES
    cos_ref[...] = jnp.transpose(
        jnp.concatenate([cq, cq, jnp.ones((rest_rows, rows), f32)], axis=0)
    )
    sin_ref[...] = jnp.transpose(
        jnp.concatenate([-sq, sq, jnp.zeros((rest_rows, rows), f32)], axis=0)
    )


def attention_kernel(ids_ref, cos_ref, sin_ref, kt_ref, v_ref, q_ref, gate_ref, *rest):
    out_ref, mask_ref = rest[-2:]
    rows = q_ref.shape[0]
    window = ids_ref.shape[1]
    half = ROTARY_ENTRIES // 2

    @pl.when(pl.program_id(0) == 0)
    def _():
        own = ids_ref[:, window - rows :]
        own_col = jnp.transpose(jnp.broadcast_to(own, (TILE, rows)))
        own_cols = jnp.concatenate([own_col] * (window // TILE), axis=1)
        r = lax.broadcasted_iota(jnp.int32, (rows, window), 0) + (window - rows)
        c = lax.broadcasted_iota(jnp.int32, (rows, window), 1)
        mask_ref[...] = jnp.where((own_cols == ids_ref[...]) & (c <= r), 0.0, MASKED)

    scaling = HEAD_WIDTH**-0.5
    lane = lax.broadcasted_iota(jnp.int32, (rows, TILE), 1)
    for h in range(q_ref.shape[1] // HEAD_WIDTH):
        base = h * HEAD_WIDTH
        x = q_ref[:, base : base + TILE].astype(f32)
        swapped = jnp.where(lane < half, pltpu.roll(x, TILE - half, 1), pltpu.roll(x, half, 1))
        rotated = ((x * cos_ref[...] + swapped * sin_ref[...]) * scaling).astype(bf16)
        tail = q_ref[:, base + TILE : base + HEAD_WIDTH] * jnp.asarray(scaling, bf16)
        scores = dot(jnp.concatenate([rotated, tail], axis=1), kt_ref[...]) + mask_ref[...]
        best = jnp.max(scores, axis=1, keepdims=True)
        weights = jnp.exp(scores - best)
        total = jnp.sum(weights, axis=1, keepdims=True)
        mixed = dot(weights.astype(bf16), v_ref[...])
        gate = jax.nn.sigmoid(gate_ref[:, base : base + HEAD_WIDTH].astype(f32))
        out_ref[:, base : base + HEAD_WIDTH] = (mixed / total * gate).astype(bf16)


def attention_half(part, window_arrays, query, gate, partial_out=None):
    rows = query.shape[0]
    window = window_arrays[0].shape[1]
    heads = 2
    width = heads * HEAD_WIDTH
    steps = query.shape[1] // width // 2

    def at_part(i):
        return (0, part * steps + i)

    in_specs = [pl.BlockSpec(a.shape, lambda i: (0, 0)) for a in window_arrays]
    in_specs += [pl.BlockSpec((rows, width), at_part)] * 2
    args = [*window_arrays, query, gate]
    aliases = {}
    if partial_out is not None:
        aliases = {len(args): 0}
        in_specs.append(pl.BlockSpec(memory_space=pl.ANY))
        args.append(partial_out)
    return pl.pallas_call(
        attention_kernel,
        grid=(steps,),
        in_specs=in_specs,
        out_specs=pl.BlockSpec((rows, width), at_part),
        out_shape=jax.ShapeDtypeStruct(query.shape, bf16),
        scratch_shapes=[pltpu.VMEM((rows, window), f32)],
        input_output_aliases=aliases,
        compiler_params=params(),
        cost_estimate=cost(5 * 10**9, 3 * 2**20, 10**6),
        name="attention",
    )(*args)


def up_chip(value, ranks):
    return lax.ppermute(value, "ctx", [(i, i + 2) for i in range(ranks - 2)])


def swap_cores(value, ranks):
    return lax.ppermute(value, "ctx", [(i, i ^ 1) for i in range(ranks)])


def per_device(
    segment_ids,
    attn_query,
    attention_keys,
    attention_values,
    attn_gate,
    delta_query,
    delta_key,
    update_rule_payload,
    delta_beta,
    delta_decay,
    delta_gate,
    norm_gain,
):
    ranks = lax.axis_size("ctx")
    rank = lax.axis_index("ctx")
    rows = segment_ids.shape[0]
    hops = ranks // 4
    core = rank % 2
    odd = core == 1

    ids = segment_ids.astype(f32).reshape(1, rows) + 1.0

    id_rows = jnp.broadcast_to(jnp.concatenate([ids, ids], axis=1), (BLOCK, 2 * rows))
    own = jnp.concatenate(
        [jnp.concatenate([attention_keys, attention_values], axis=1), id_rows.astype(bf16)], axis=0
    )
    same = []
    for _ in range(hops):
        same.append(up_chip(same[-1] if same else own, ranks))
    chain = [own, *same]
    other = swap_cores(
        jnp.stack([jnp.where(odd, chain[i + 1], chain[i]) for i in range(hops)]), ranks
    )

    keep_half = core.reshape(1).astype(jnp.int32)
    give_half = 1 - keep_half
    local = partial(
        delta_local,
        seg_row=ids,
        query=delta_query,
        key=delta_key,
        value=update_rule_payload,
        beta=delta_beta,
        decay=delta_decay,
    )
    give_ma, give_reach, give_inner = local(give_half)
    other_ma = swap_cores(give_ma, ranks)
    keep_ma, keep_reach, keep_inner = local(keep_half)

    tall = keep_ma.shape[0]
    state_like = jax.ShapeDtypeStruct((tall, DV), bf16)
    chip_map, chip_add = small_call(
        compose_kernel, "compose", [state_like] * 2, keep_half, keep_ma, other_ma, scalars=1
    )
    state = up_chip(chip_add, ranks)
    for _ in range(hops - 1):
        (leaving,) = small_call(relay_kernel, "relay", [state_like], chip_map, chip_add, state)
        state = up_chip(leaving, ranks)
    final_like = jax.ShapeDtypeStruct((tall - BLOCK, DV), bf16)
    keep_state, pass_state = small_call(
        arrive_kernel, "arrive", [final_like] * 2, keep_half, keep_ma, other_ma, state, scalars=1
    )
    give_state = swap_cores(pass_state, ranks)

    window = (2 * hops + 1) * rows
    index = jnp.arange(ROTARY_ENTRIES // 2).astype(f32)
    freq = ROPE_THETA ** (-2.0 * index / ROTARY_ENTRIES)
    freq = jnp.broadcast_to(freq[:, None], (ROTARY_ENTRIES // 2, TILE))
    kt, v_all, window_ids, cosine, sine = small_call(
        window_kernel,
        "window",
        [
            jax.ShapeDtypeStruct((HEAD_WIDTH, window), bf16),
            jax.ShapeDtypeStruct((window, HEAD_WIDTH), bf16),
            jax.ShapeDtypeStruct((1, window), f32),
            jax.ShapeDtypeStruct((rows, TILE), f32),
            jax.ShapeDtypeStruct((rows, TILE), f32),
        ],
        freq,
        own,
        *same,
        other,
    )
    window_arrays = (window_ids, cosine, sine, kt, v_all)
    attn_mixed = attention_half(0, window_arrays, attn_query, attn_gate)
    attn_mixed = attention_half(1, window_arrays, attn_query, attn_gate, attn_mixed)

    gain = norm_gain.reshape(1, DV)
    delta_mixed = delta_out(keep_half, keep_reach, keep_inner, keep_state, delta_gate, gain)
    delta_mixed = delta_out(
        give_half, give_reach, give_inner, give_state, delta_gate, gain, delta_mixed
    )
    return (attn_mixed, delta_mixed)


def solution(mesh):
    rows = P(("dp", "ctx"))
    wide = P(("dp", "ctx"), None)
    return jax.shard_map(
        per_device,
        mesh=mesh,
        in_specs=(rows,) + (wide,) * 10 + (P(),),
        out_specs=(wide, wide),
        check_vma=False,
    )
```

```python
from functools import partial

import jax
import jax.numpy as jnp
from jax import lax
from jax.experimental import pallas as pl
from jax.experimental.pallas import tpu as pltpu
from jax.sharding import PartitionSpec as P

HEAD_WIDTH = 256
ROTARY_ENTRIES = 64
DK = 128
DV = 128
DOCS = 8
ROPE_THETA = 10000000.0
LOG2E = 1.4426950408889634
MASKED = -1e30
EPS = 1e-6
TILE = 128
KEYS_PER_STEP = 1
MIB = 1024 * 1024

f32 = jnp.float32
bf16 = jnp.bfloat16


def dot(a, b, precision=None):
    return jnp.dot(a, b, preferred_element_type=f32, precision=precision)


def params(mib=16):
    return pltpu.CompilerParams(vmem_limit_bytes=mib * MIB)


def sigmoid(x):
    return 0.5 * jnp.tanh(0.5 * x) + 0.5


def cost(flops, nbytes, exps=0):
    return pl.CostEstimate(flops=flops, bytes_accessed=nbytes, transcendentals=exps)


BLOCK = 16
MERGES = 3


def odd_rows(m, b):
    return jnp.concatenate([m[i + b : i + 2 * b] for i in range(0, TILE, 2 * b)], axis=0)


def interleave(even, odd, b):
    parts = []
    for i in range(0, TILE // 2, b):
        parts += [even[i : i + b], odd[i : i + b]]
    return jnp.concatenate(parts, axis=0)


def even_rows(m, b):
    return jnp.concatenate([m[i : i + b] for i in range(0, TILE, 2 * b)], axis=0)


def block_inverses(mats):
    row = lax.broadcasted_iota(jnp.int32, (BLOCK, TILE), 0)
    lane = lax.broadcasted_iota(jnp.int32, (BLOCK, TILE), 1)
    within = lax.rem(lane, BLOCK)
    group = lane // BLOCK
    folded = []
    for m in mats:
        z = jnp.where(group == 0, m[:BLOCK], 0.0)
        for r in range(1, TILE // BLOCK):
            z = jnp.where(group == r, m[r * BLOCK : (r + 1) * BLOCK], z)
        folded.append(jnp.where(row > within, z, 0.0))
    xs = [jnp.where(row == within, 1.0, 0.0)] * len(mats)
    small = 8
    for k in range(BLOCK - 1):
        low = 0 if k < small - 1 else small
        at = (group * BLOCK + k)[low:]
        for i, z in enumerate(folded):
            spread = jnp.take_along_axis(z[low:], at, axis=1)
            x = xs[i]
            new = x[low:] + spread * x[k : k + 1]
            xs[i] = new if low == 0 else jnp.concatenate([x[:low], new], axis=0)
    out = []
    for x in xs:
        x = jnp.where(row > within, x, 0.0)
        out.append(
            jnp.concatenate(
                [jnp.where(group == r, x, 0.0) for r in range(TILE // BLOCK)], axis=0
            ).astype(bf16)
        )
    return out


def delta_local_kernel(
    half_ref,
    seg_ref,
    q_ref,
    k_ref,
    v_ref,
    beta_ref,
    decay_ref,
    map_add_ref,
    reach_ref,
    inner_ref,
    mask_ref,
    level_ref,
    crow_ref,
    ccol_ref,
    first_ref,
):
    rows = q_ref.shape[0]
    step = pl.program_id(0)
    heads = 2 * KEYS_PER_STEP

    @pl.when(step == 0)
    def _():
        seg_row = seg_ref[...].astype(f32) + 1.0
        seg_col = jnp.transpose(jnp.broadcast_to(seg_row, (TILE, rows)))
        seg_cols = jnp.concatenate([seg_col] * (rows // TILE), axis=1)
        r = lax.broadcasted_iota(jnp.int32, (rows, rows), 0)
        c = lax.broadcasted_iota(jnp.int32, (rows, rows), 1)
        mask_ref[...] = jnp.where((seg_cols == seg_row) & (r >= c), 0.0, MASKED)
        first_ref[...] = jnp.where(seg_col == seg_row[:, :1], 1.0, 0.0)
        r = lax.broadcasted_iota(jnp.int32, (TILE, TILE), 0)
        c = lax.broadcasted_iota(jnp.int32, (TILE, TILE), 1)
        for level in range(MERGES):
            b = BLOCK << level
            sibling = jnp.where(r // b == c // b + 1, 1.0, 0.0)
            level_ref[level] = odd_rows(sibling, b).astype(bf16)
        n = map_add_ref.shape[0] // DK
        base = pl.multiple_of(half_ref[0] * n, n)
        decay = decay_ref[pl.ds(base, n), :] * LOG2E
        high = decay.astype(bf16)
        rest = decay - high.astype(f32)
        middle = rest.astype(bf16)
        parts = [high, middle, (rest - middle.astype(f32)).astype(bf16)]
        parts = jnp.concatenate([p.astype(f32) for p in parts], axis=0).astype(bf16)
        r = lax.broadcasted_iota(jnp.int32, (rows, rows), 0)
        c = lax.broadcasted_iota(jnp.int32, (rows, rows), 1)
        sums = dot(parts, jnp.where(r <= c, 1.0, 0.0).astype(bf16))
        cumulative = sums[:n] + sums[n : 2 * n] + sums[2 * n :]
        crow_ref[...] = cumulative
        fill = jnp.zeros((TILE - 2 * n, rows), f32)
        both = jnp.concatenate([cumulative, beta_ref[pl.ds(base, n), :], fill], axis=0)
        ccol_ref[...] = jnp.transpose(both)
        end = map_add_ref.shape[0] - BLOCK
        map_add_ref[end:, :] = jnp.broadcast_to(seg_row, (BLOCK, rows)).astype(bf16)

    shift = lax.rem(TILE - step * heads, TILE)
    columns = pltpu.roll(ccol_ref[...], shift, 1)
    n = map_add_ref.shape[0] // DK
    first = first_ref[...]
    eye = jnp.where(
        lax.broadcasted_iota(jnp.int32, (TILE, TILE), 0)
        == lax.broadcasted_iota(jnp.int32, (TILE, TILE), 1),
        1.0,
        0.0,
    )
    work = []
    for kk in range(KEYS_PER_STEP):
        cols = slice(kk * DK, (kk + 1) * DK)
        k_raw = k_ref[:, cols]
        q_raw = q_ref[:, cols]
        kf = k_raw.astype(f32)
        qf = q_raw.astype(f32)
        rk_col = lax.rsqrt(jnp.sum(kf * kf, axis=1, keepdims=True) + EPS)
        rq_col = lax.rsqrt(jnp.sum(qf * qf, axis=1, keepdims=True) + EPS) * DK**-0.5
        kt = jnp.transpose(kf)
        rk_row = lax.rsqrt(jnp.sum(kt * kt, axis=0, keepdims=True) + EPS)
        ktb = kt.astype(bf16)
        upper = dot(jnp.concatenate([k_raw[:TILE], q_raw[:TILE]], axis=0), ktb[:, :TILE])
        lower = dot(jnp.concatenate([k_raw[TILE:], q_raw[TILE:]], axis=0), ktb)
        gram1 = upper[:TILE] * rk_row[:, :TILE] * -rk_col[:TILE]
        probe1 = upper[TILE:] * rk_row[:, :TILE] * rq_col[:TILE]
        gram2 = lower[:TILE] * rk_row * -rk_col[TILE:]
        probe2 = lower[TILE:] * rk_row * rq_col[TILE:]
        kn = kf * rk_col
        qn = qf * rq_col
        for j in range(2):
            h = 2 * kk + j
            cc = columns[:, h : h + 1]
            bt = columns[:, n + h : n + h + 1]
            cr = crow_ref[pl.ds(step * heads + h, 1), :]
            span1 = jnp.exp2(cc[:TILE] - cr[:, :TILE] + mask_ref[:TILE, :TILE])
            span2 = jnp.exp2(cc[TILE:] - cr + mask_ref[TILE:, :])
            d11 = span1 * bt[:TILE] * gram1
            d2 = span2 * bt[TILE:] * gram2
            p11 = (span1 * probe1).astype(bf16)
            p2 = (span2 * probe2).astype(bf16)
            entry = jnp.exp2(cc) * first
            right = jnp.concatenate(
                [bt * entry * kn, bt * v_ref[:, h * DV : (h + 1) * DV].astype(f32)], axis=1
            )
            kd = (kt * (rk_row * span2[TILE - 1 : TILE, :])).astype(bf16)
            work.append(
                dict(h=h, d=[d11, d2[:, TILE:]], d21=d2[:, :TILE].astype(bf16), p11=p11, p2=p2,
                     kd=kd, right=right, reach=entry * qn, last=entry[rows - 1 : rows, :])
            )
    mats = [m for w in work for m in w["d"]]
    inverses = block_inverses(mats)
    mats = [m.astype(bf16) for m in mats]
    zeros = jnp.zeros((TILE // 2, TILE), bf16)
    for level in range(MERGES):
        b = BLOCK << level
        keep = level_ref[level]
        picked = [odd_rows(m, b) * keep for m in mats]
        ys = [(p.astype(f32) + dot(p, x)).astype(bf16) for p, x in zip(picked, inverses)]
        odds = [odd_rows(x, b) for x in inverses]
        odds = [
            x + (y.astype(f32) + dot(x, interleave(zeros, y, b))).astype(bf16)
            for x, y in zip(odds, ys)
        ]
        inverses = [interleave(even_rows(x, b), o, b) for x, o in zip(inverses, odds)]
    for i, w in enumerate(work):
        x1, x2 = inverses[2 * i], inverses[2 * i + 1]
        h = w["h"]
        r1 = w["right"][:TILE]
        u1 = (r1 + dot(x1, r1.astype(bf16))).astype(bf16)
        after = dot(jnp.concatenate([w["d21"], w["p11"]], axis=0), u1)
        r2 = w["right"][TILE:] + after[:TILE]
        u2 = (r2 + dot(x2, r2.astype(bf16))).astype(bf16)
        u = jnp.concatenate([u1, u2], axis=0)
        last = dot(jnp.concatenate([w["p2"], w["kd"]], axis=0), u)
        pu = jnp.concatenate([after[TILE:], last[:TILE]], axis=0)
        ma = last[TILE:]
        at = pl.multiple_of((step * heads + h) * DK, DK)
        map_add_ref[pl.ds(at, DK), :] = jnp.concatenate(
            [w["last"] * eye - ma[:, :DK], ma[:, DK:]], axis=1
        ).astype(bf16)
        reach_ref[:, h * DK : (h + 1) * DK] = (w["reach"] - pu[:, :DK]).astype(bf16)
        inner_ref[:, h * DV : (h + 1) * DV] = pu[:, DK:].astype(inner_ref.dtype)


def delta_local(half, mib, seg_row, query, key, value, beta, decay):
    rows = query.shape[0]
    heads = 2 * KEYS_PER_STEP
    n = value.shape[1] // DV // 2
    steps = n // heads
    kw = KEYS_PER_STEP * DK
    vw = heads * DV
    tall = n * DK + BLOCK

    def at_half(i, s):
        return (0, s[0] * steps + i)

    def whole(i, s):
        return (0, 0)

    return pl.pallas_call(
        delta_local_kernel,
        grid_spec=pltpu.PrefetchScalarGridSpec(
            num_scalar_prefetch=1,
            grid=(steps,),
            in_specs=[
                pl.BlockSpec((1, rows), whole),
                pl.BlockSpec((rows, kw), at_half),
                pl.BlockSpec((rows, kw), at_half),
                pl.BlockSpec((rows, vw), at_half),
                pl.BlockSpec(beta.shape, whole),
                pl.BlockSpec(decay.shape, whole),
            ],
            out_specs=[
                pl.BlockSpec((tall, DK + DV), whole),
                pl.BlockSpec((rows, heads * DK), lambda i, s: (0, i)),
                pl.BlockSpec((rows, vw), lambda i, s: (0, i)),
            ],
            scratch_shapes=[
                pltpu.VMEM((rows, rows), f32),
                pltpu.VMEM((MERGES, TILE // 2, TILE), bf16),
                pltpu.VMEM((n, rows), f32),
                pltpu.VMEM((rows, TILE), f32),
                pltpu.VMEM((rows, TILE), f32),
            ],
        ),
        out_shape=[
            jax.ShapeDtypeStruct((tall, DK + DV), bf16),
            jax.ShapeDtypeStruct((rows, n * DK), bf16),
            jax.ShapeDtypeStruct((rows, n * DV), f32),
        ],
        compiler_params=params(mib),
        cost_estimate=cost(6 * 10**9, 3 * 2**20),
        name="delta_local",
    )(half, seg_row, query, key, value, beta, decay)


def ids_of(ref):
    end = ref.shape[0] - BLOCK
    return ref[end : end + BLOCK, :].astype(f32)[:1]


def put_id(ref, value):
    end = ref.shape[0] - BLOCK
    ref[end:, :] = jnp.broadcast_to(value, (BLOCK, ref.shape[1])).astype(bf16)


def matching(a, b):
    return jnp.where(a == b, 1.0, 0.0)


def compose_kernel(core_ref, mine_ref, other_ref, map_ref, add_ref):
    odd = core_ref[0] == 1
    mine_ids, other_ids = ids_of(mine_ref), ids_of(other_ref)
    early_ids = jnp.where(odd, other_ids, mine_ids)
    late_ids = jnp.where(odd, mine_ids, other_ids)
    across = matching(early_ids[:, -1:], late_ids[:, :1])
    put_id(map_ref, early_ids[:, :1])
    put_id(add_ref, late_ids[:, -1:])
    for h in range(mine_ref.shape[0] // DK):
        at = slice(h * DK, (h + 1) * DK)
        mine, other = mine_ref[at], other_ref[at]
        early, late = jnp.where(odd, other, mine), jnp.where(odd, mine, other)
        both = dot(late[:, :DK], early) * across
        map_ref[at] = both[:, :DK].astype(bf16)
        add_ref[at] = (both[:, DK:] + late[:, DK:].astype(f32)).astype(bf16)


def relay_kernel(map_ref, add_ref, state_ref, out_ref):
    into = matching(ids_of(state_ref), ids_of(map_ref))
    put_id(out_ref, ids_of(add_ref))
    for h in range(map_ref.shape[0] // DK):
        at = slice(h * DK, (h + 1) * DK)
        out_ref[at] = (dot(map_ref[at], state_ref[at]) * into + add_ref[at].astype(f32)).astype(bf16)


def arrive_kernel(core_ref, mine_ref, other_ref, state_ref, keep_ref, give_ref):
    odd = core_ref[0] == 1
    mine_ids, other_ids = ids_of(mine_ref), ids_of(other_ref)
    early_ids = jnp.where(odd, other_ids, mine_ids)
    late_ids = jnp.where(odd, mine_ids, other_ids)
    across = matching(early_ids[:, -1:], late_ids[:, :1])
    into = matching(ids_of(state_ref), early_ids[:, :1])
    for h in range(keep_ref.shape[0] // DK):
        at = slice(h * DK, (h + 1) * DK)
        early = jnp.where(odd, other_ref[at], mine_ref[at])
        first = (state_ref[at].astype(f32) * into).astype(bf16)
        second = (
            (dot(early[:, :DK], first) + early[:, DK:].astype(f32)) * across
        ).astype(bf16)
        keep_ref[at] = jnp.where(odd, second, first)
        give_ref[at] = jnp.where(odd, first, second)


SMEM = pl.BlockSpec(memory_space=pltpu.SMEM)
VMEM = pl.BlockSpec(memory_space=pltpu.VMEM)


def small_call(kernel, name, outs, *args, scalars=0, mib=16):
    return pl.pallas_call(
        kernel,
        in_specs=[SMEM] * scalars + [VMEM] * (len(args) - scalars),
        out_specs=[VMEM] * len(outs),
        out_shape=outs,
        compiler_params=params(mib),
        cost_estimate=cost(10**8, 2**20),
        name=name,
    )(*args)


def delta_out_kernel(half_ref, reach_ref, inner_ref, state_ref, gate_ref, gain_ref, *rest):
    out_ref = rest[-1]
    gain = gain_ref[...]
    for h in range(state_ref.shape[0] // DK):
        cols = slice(h * DV, (h + 1) * DV)
        state = state_ref[h * DK : (h + 1) * DK]
        out = inner_ref[:, cols].astype(f32) + dot(reach_ref[:, cols], state)
        spread = lax.rsqrt(jnp.mean(out * out, axis=1, keepdims=True) + EPS)
        gate = gate_ref[:, cols].astype(f32)
        gate = gate * sigmoid(gate)
        out_ref[:, cols] = (out * spread * gain * gate).astype(bf16)


def delta_out(half, reach, inner, state, gate, gain, partial_out=None):
    rows = reach.shape[0]
    n = state.shape[0] // DK
    heads = 4
    steps = n // heads

    def at_half(i, s):
        return (0, s[0] * steps + i)

    in_specs = [
        pl.BlockSpec((rows, heads * DK), lambda i, s: (0, i)),
        pl.BlockSpec((rows, heads * DV), lambda i, s: (0, i)),
        pl.BlockSpec((heads * DK, DV), lambda i, s: (i, 0)),
        pl.BlockSpec((rows, heads * DV), at_half),
        pl.BlockSpec((1, DV), lambda i, s: (0, 0)),
    ]
    args = [half, reach, inner, state, gate, gain]
    aliases = {}
    if partial_out is not None:
        in_specs.append(pl.BlockSpec(memory_space=pl.ANY))
        args.append(partial_out)
        aliases = {6: 0}
    return pl.pallas_call(
        delta_out_kernel,
        grid_spec=pltpu.PrefetchScalarGridSpec(
            num_scalar_prefetch=1,
            grid=(steps,),
            in_specs=in_specs,
            out_specs=pl.BlockSpec((rows, heads * DV), at_half),
        ),
        out_shape=jax.ShapeDtypeStruct(gate.shape, bf16),
        input_output_aliases=aliases,
        compiler_params=params(),
        cost_estimate=cost(10**8, 3 * 2**20),
        name="delta_out",
    )(*args)


def blocks_of(pieces):
    own, *same, other = pieces
    order = [(own, None)]
    for i, ref in enumerate(same):
        order += [(other, i), (ref, None)]
    return order[::-1]


def pack_kernel(seg_ref, key_ref, value_ref, out_ref):
    rows = key_ref.shape[0]
    ids = seg_ref[...].astype(f32) + 1.0
    out_ref[:rows, :HEAD_WIDTH] = key_ref[...]
    out_ref[:rows, HEAD_WIDTH:] = value_ref[...]
    out_ref[rows:, :rows] = jnp.broadcast_to(ids, (BLOCK, rows)).astype(bf16)
    out_ref[rows:, rows:] = jnp.zeros((BLOCK, 2 * HEAD_WIDTH - rows), bf16)


def window_kernel(freq_ref, *rest):
    *pieces, kt_ref, v_ref, ids_ref, cos_ref, sin_ref = rest
    rows = cos_ref.shape[0]
    window = ids_ref.shape[1]
    half = ROTARY_ENTRIES // 2
    blocks = [ref if index is None else ref.at[index] for ref, index in blocks_of(pieces)]
    row_ids = jnp.concatenate(
        [ref[rows : rows + BLOCK, :rows].astype(f32)[:1] for ref in blocks], axis=1
    )
    ids_ref[...] = row_ids
    ids = jnp.broadcast_to(row_ids, (DOCS, window))
    docs = lax.broadcasted_iota(jnp.int32, (DOCS, window), 0).astype(f32) + 1.0
    before = jnp.sum(jnp.where(ids < docs, 1.0, 0.0), axis=1, keepdims=True)
    start = jnp.sum(jnp.where(ids == docs, before, 0.0), axis=0, keepdims=True)
    place = lax.broadcasted_iota(jnp.int32, (1, window), 1).astype(f32)
    angle = freq_ref[:, :1] * (place - start)
    cosine = jnp.cos(angle)
    sine = jnp.sin(angle)
    for b, ref in enumerate(blocks):
        cols = slice(b * rows, (b + 1) * rows)
        kt = jnp.transpose(ref[:rows, :HEAD_WIDTH].astype(f32))
        one, two = kt[:half], kt[half:ROTARY_ENTRIES]
        cb, sb = cosine[:, cols], sine[:, cols]
        kt_ref[:half, cols] = (one * cb - two * sb).astype(bf16)
        kt_ref[half:ROTARY_ENTRIES, cols] = (two * cb + one * sb).astype(bf16)
        kt_ref[ROTARY_ENTRIES:, cols] = kt[ROTARY_ENTRIES:].astype(bf16)
        v_ref[cols, :] = ref[:rows, HEAD_WIDTH:]
    cq, sq = cosine[:, window - rows :], sine[:, window - rows :]
    rest_rows = TILE - ROTARY_ENTRIES
    cos_ref[...] = jnp.transpose(
        jnp.concatenate([cq, cq, jnp.ones((rest_rows, rows), f32)], axis=0)
    )
    sin_ref[...] = jnp.transpose(
        jnp.concatenate([-sq, sq, jnp.zeros((rest_rows, rows), f32)], axis=0)
    )


def attention_kernel(ids_ref, cos_ref, sin_ref, kt_ref, v_ref, q_ref, gate_ref, *rest):
    out_ref, mask_ref = rest[-2:]
    rows = q_ref.shape[0]
    window = ids_ref.shape[1]
    half = ROTARY_ENTRIES // 2

    @pl.when(pl.program_id(0) == 0)
    def _():
        own = ids_ref[:, window - rows :]
        own_col = jnp.transpose(jnp.broadcast_to(own, (TILE, rows)))
        own_cols = jnp.concatenate([own_col] * (window // TILE), axis=1)
        r = lax.broadcasted_iota(jnp.int32, (rows, window), 0) + (window - rows)
        c = lax.broadcasted_iota(jnp.int32, (rows, window), 1)
        mask_ref[...] = jnp.where((own_cols == ids_ref[...]) & (c <= r), 0.0, MASKED)

    scaling = HEAD_WIDTH**-0.5
    lane = lax.broadcasted_iota(jnp.int32, (TILE, TILE), 1)
    reach = window - rows + TILE
    for h in range(q_ref.shape[1] // HEAD_WIDTH):
        base = h * HEAD_WIDTH
        for first in range(0, rows, TILE):
            at = slice(first, first + TILE)
            keys = slice(first, first + reach)
            x = q_ref[at, base : base + TILE].astype(f32)
            swapped = jnp.where(
                lane < half, pltpu.roll(x, TILE - half, 1), pltpu.roll(x, half, 1)
            )
            rotated = ((x * cos_ref[at] + swapped * sin_ref[at]) * scaling).astype(bf16)
            tail = q_ref[at, base + TILE : base + HEAD_WIDTH] * jnp.asarray(scaling, bf16)
            scores = dot(jnp.concatenate([rotated, tail], axis=1), kt_ref[:, keys])
            scores = scores + mask_ref[at, keys]
            best = jnp.max(scores, axis=1, keepdims=True)
            weights = jnp.exp(scores - best)
            total = jnp.sum(weights, axis=1, keepdims=True)
            mixed = dot(weights.astype(bf16), v_ref[keys, :])
            gate = sigmoid(gate_ref[at, base : base + HEAD_WIDTH].astype(f32))
            out_ref[at, base : base + HEAD_WIDTH] = (mixed * (1.0 / total) * gate).astype(bf16)


def attention_half(part, window_arrays, query, gate, partial_out=None):
    rows = query.shape[0]
    window = window_arrays[0].shape[1]
    heads = 2
    width = heads * HEAD_WIDTH
    steps = query.shape[1] // width // 2

    def at_part(i):
        return (0, part * steps + i)

    in_specs = [pl.BlockSpec(a.shape, lambda i: (0, 0)) for a in window_arrays]
    in_specs += [pl.BlockSpec((rows, width), at_part)] * 2
    args = [*window_arrays, query, gate]
    aliases = {}
    if partial_out is not None:
        aliases = {len(args): 0}
        in_specs.append(pl.BlockSpec(memory_space=pl.ANY))
        args.append(partial_out)
    return pl.pallas_call(
        attention_kernel,
        grid=(steps,),
        in_specs=in_specs,
        out_specs=pl.BlockSpec((rows, width), at_part),
        out_shape=jax.ShapeDtypeStruct(query.shape, bf16),
        scratch_shapes=[pltpu.VMEM((rows, window), f32)],
        input_output_aliases=aliases,
        compiler_params=params(),
        cost_estimate=cost(5 * 10**9, 3 * 2**20, 10**6),
        name="attention",
    )(*args)


def up_chip(value, ranks):
    return lax.ppermute(value, "ctx", [(i, i + 2) for i in range(ranks - 2)])


def swap_cores(value, ranks):
    return lax.ppermute(value, "ctx", [(i, i ^ 1) for i in range(ranks)])


def per_device(
    segment_ids,
    attn_query,
    attention_keys,
    attention_values,
    attn_gate,
    delta_query,
    delta_key,
    update_rule_payload,
    delta_beta,
    delta_decay,
    delta_gate,
    norm_gain,
):
    ranks = lax.axis_size("ctx")
    rank = lax.axis_index("ctx")
    rows = segment_ids.shape[0]
    hops = ranks // 4
    core = rank % 2
    odd = core == 1

    ids = segment_ids.reshape(1, rows)

    (own,) = small_call(
        pack_kernel,
        "pack",
        [jax.ShapeDtypeStruct((rows + BLOCK, 2 * HEAD_WIDTH), bf16)],
        ids,
        attention_keys,
        attention_values,
        mib=60,
    )
    nearest = up_chip(own, ranks)

    keep_half = core.reshape(1).astype(jnp.int32)
    give_half = 1 - keep_half
    local = partial(
        delta_local,
        seg_row=ids,
        query=delta_query,
        key=delta_key,
        value=update_rule_payload,
        beta=delta_beta.T,
        decay=delta_decay.T,
    )
    give_ma, give_reach, give_inner = local(give_half, 60)
    other_ma = swap_cores(give_ma, ranks)
    nearest, give_ma = lax.optimization_barrier((nearest, give_ma))
    same = [nearest]
    for _ in range(hops - 1):
        same.append(up_chip(same[-1], ranks))
    keep_ma, keep_reach, keep_inner = local(keep_half, 20)
    same, keep_ma = lax.optimization_barrier((same, keep_ma))
    chain = [own, *same]
    other = swap_cores(
        jnp.stack([jnp.where(odd, chain[i + 1], chain[i]) for i in range(hops)]), ranks
    )

    tall = keep_ma.shape[0]
    state_like = jax.ShapeDtypeStruct((tall, DV), bf16)
    chip_map, chip_add = small_call(
        compose_kernel, "compose", [state_like] * 2, keep_half, keep_ma, other_ma, scalars=1
    )
    state = up_chip(chip_add, ranks)

    window = (2 * hops + 1) * rows
    index = jnp.arange(ROTARY_ENTRIES // 2).astype(f32)
    freq = ROPE_THETA ** (-2.0 * index / ROTARY_ENTRIES)
    freq = jnp.broadcast_to(freq[:, None], (ROTARY_ENTRIES // 2, TILE))
    window_arrays = small_call(
        window_kernel,
        "window",
        [
            jax.ShapeDtypeStruct((HEAD_WIDTH, window), bf16),
            jax.ShapeDtypeStruct((window, HEAD_WIDTH), bf16),
            jax.ShapeDtypeStruct((1, window), f32),
            jax.ShapeDtypeStruct((rows, TILE), f32),
            jax.ShapeDtypeStruct((rows, TILE), f32),
        ],
        freq,
        own,
        *same,
        other,
    )
    state, window_arrays = lax.optimization_barrier((state, window_arrays))
    for _ in range(hops - 1):
        (leaving,) = small_call(relay_kernel, "relay", [state_like], chip_map, chip_add, state)
        state = up_chip(leaving, ranks)
    kt, v_all, window_ids, cosine, sine = window_arrays
    window_arrays = (window_ids, cosine, sine, kt, v_all)
    attn_mixed = attention_half(0, window_arrays, attn_query, attn_gate)
    state, attn_mixed = lax.optimization_barrier((state, attn_mixed))

    final_like = jax.ShapeDtypeStruct((tall - BLOCK, DV), bf16)
    keep_state, pass_state = small_call(
        arrive_kernel, "arrive", [final_like] * 2, keep_half, keep_ma, other_ma, state, scalars=1
    )
    give_state = swap_cores(pass_state, ranks)
    attn_mixed = attention_half(1, window_arrays, attn_query, attn_gate, attn_mixed)

    gain = norm_gain.reshape(1, DV)
    delta_mixed = delta_out(keep_half, keep_reach, keep_inner, keep_state, delta_gate, gain)
    delta_mixed = delta_out(
        give_half, give_reach, give_inner, give_state, delta_gate, gain, delta_mixed
    )
    return (attn_mixed, delta_mixed)


def solution(mesh):
    rows = P(("dp", "ctx"))
    wide = P(("dp", "ctx"), None)
    return jax.shard_map(
        per_device,
        mesh=mesh,
        in_specs=(rows,) + (wide,) * 10 + (P(),),
        out_specs=(wide, wide),
        check_vma=False,
    )
```

```python
from functools import partial

import jax
import jax.numpy as jnp
from jax import lax
from jax.experimental import pallas as pl
from jax.experimental.pallas import tpu as pltpu
from jax.sharding import PartitionSpec as P

HEAD_WIDTH = 256
ROTARY_ENTRIES = 64
DK = 128
DV = 128
DOCS = 8
ROPE_THETA = 10000000.0
LOG2E = 1.4426950408889634
MASKED = -1e30
EPS = 1e-6
TILE = 128
KEYS_PER_STEP = 1
MIB = 1024 * 1024

f32 = jnp.float32
bf16 = jnp.bfloat16


def dot(a, b, precision=None):
    return jnp.dot(a, b, preferred_element_type=f32, precision=precision)


def params(mib=16):
    return pltpu.CompilerParams(vmem_limit_bytes=mib * MIB)


def sigmoid(x):
    return 0.5 * jnp.tanh(0.5 * x) + 0.5


def cost(flops, nbytes, exps=0):
    return pl.CostEstimate(flops=flops, bytes_accessed=nbytes, transcendentals=exps)


BLOCK = 16
MERGES = 3
STRIP = 32
FINE = 16


def odd_rows(m, b):
    return jnp.concatenate([m[i + b : i + 2 * b] for i in range(0, TILE, 2 * b)], axis=0)


def interleave(even, odd, b):
    parts = []
    for i in range(0, TILE // 2, b):
        parts += [even[i : i + b], odd[i : i + b]]
    return jnp.concatenate(parts, axis=0)


def even_rows(m, b):
    return jnp.concatenate([m[i : i + b] for i in range(0, TILE, 2 * b)], axis=0)


def block_inverses(mats):
    row = lax.broadcasted_iota(jnp.int32, (BLOCK, TILE), 0)
    lane = lax.broadcasted_iota(jnp.int32, (BLOCK, TILE), 1)
    within = lax.rem(lane, BLOCK)
    group = lane // BLOCK
    folded = []
    for m in mats:
        z = jnp.where(group == 0, m[:BLOCK], 0.0)
        for r in range(1, TILE // BLOCK):
            z = jnp.where(group == r, m[r * BLOCK : (r + 1) * BLOCK], z)
        folded.append(jnp.where(row > within, z, 0.0))
    xs = [jnp.where(row == within, 1.0, 0.0)] * len(mats)
    small = 8
    for k in range(BLOCK - 1):
        low = 0 if k < small - 1 else small
        at = (group * BLOCK + k)[low:]
        for i, z in enumerate(folded):
            spread = jnp.take_along_axis(z[low:], at, axis=1, mode="promise_in_bounds")
            x = xs[i]
            new = x[low:] + spread * x[k : k + 1]
            xs[i] = new if low == 0 else jnp.concatenate([x[:low], new], axis=0)
    out = []
    for x in xs:
        x = jnp.where(row > within, x, 0.0)
        out.append(
            jnp.concatenate(
                [jnp.where(group == r, x, 0.0) for r in range(TILE // BLOCK)], axis=0
            ).astype(bf16)
        )
    return out


def delta_local_kernel(
    half_ref,
    seg_ref,
    q_ref,
    k_ref,
    v_ref,
    beta_ref,
    decay_ref,
    map_add_ref,
    reach_ref,
    inner_ref,
    mask_ref,
    level_ref,
    crow_ref,
    ccol_ref,
    first_ref,
):
    rows = q_ref.shape[0]
    step = pl.program_id(0)
    heads = 2 * KEYS_PER_STEP

    @pl.when(step == 0)
    def _():
        seg_row = seg_ref[...].astype(f32) + 1.0
        seg_col = jnp.transpose(jnp.broadcast_to(seg_row, (TILE, rows)))
        seg_cols = jnp.concatenate([seg_col] * (rows // TILE), axis=1)
        r = lax.broadcasted_iota(jnp.int32, (rows, rows), 0)
        c = lax.broadcasted_iota(jnp.int32, (rows, rows), 1)
        mask_ref[...] = jnp.where((seg_cols == seg_row) & (r >= c), 0.0, MASKED)
        first_ref[...] = jnp.where(seg_col == seg_row[:, :1], 1.0, 0.0)
        r = lax.broadcasted_iota(jnp.int32, (TILE, TILE), 0)
        c = lax.broadcasted_iota(jnp.int32, (TILE, TILE), 1)
        for level in range(MERGES):
            b = BLOCK << level
            sibling = jnp.where(r // b == c // b + 1, 1.0, 0.0)
            level_ref[level] = odd_rows(sibling, b).astype(bf16)
        n = map_add_ref.shape[0] // DK
        base = pl.multiple_of(half_ref[0] * n, n)
        decay = decay_ref[pl.ds(base, n), :] * LOG2E
        high = decay.astype(bf16)
        rest = decay - high.astype(f32)
        middle = rest.astype(bf16)
        parts = [high, middle, (rest - middle.astype(f32)).astype(bf16)]
        parts = jnp.concatenate([p.astype(f32) for p in parts], axis=0).astype(bf16)
        r = lax.broadcasted_iota(jnp.int32, (rows, rows), 0)
        c = lax.broadcasted_iota(jnp.int32, (rows, rows), 1)
        sums = dot(parts, jnp.where(r <= c, 1.0, 0.0).astype(bf16))
        cumulative = sums[:n] + sums[n : 2 * n] + sums[2 * n :]
        crow_ref[...] = cumulative
        fill = jnp.zeros((TILE - 2 * n, rows), f32)
        both = jnp.concatenate([cumulative, beta_ref[pl.ds(base, n), :], fill], axis=0)
        ccol_ref[...] = jnp.transpose(both)
        end = map_add_ref.shape[0] - BLOCK
        map_add_ref[end:, :] = jnp.broadcast_to(seg_row, (BLOCK, rows)).astype(bf16)

    shift = lax.rem(TILE - step * heads, TILE)
    columns = pltpu.roll(ccol_ref[...], shift, 1)
    n = map_add_ref.shape[0] // DK
    first = first_ref[...]
    eye = jnp.where(
        lax.broadcasted_iota(jnp.int32, (TILE, TILE), 0)
        == lax.broadcasted_iota(jnp.int32, (TILE, TILE), 1),
        1.0,
        0.0,
    )
    work = []
    strips = [slice(i, i + STRIP) for i in range(0, rows, STRIP)]
    for kk in range(KEYS_PER_STEP):
        cols = slice(kk * DK, (kk + 1) * DK)
        k_raw = k_ref[:, cols]
        q_raw = q_ref[:, cols]
        kt = jnp.transpose(k_raw.astype(f32))
        rk_row = lax.rsqrt(jnp.sum(kt * kt, axis=0, keepdims=True) + EPS)
        ktb = kt.astype(bf16)
        upper = dot(jnp.concatenate([k_raw[:TILE], q_raw[:TILE]], axis=0), ktb[:, :TILE])
        lower = dot(jnp.concatenate([k_raw[TILE:], q_raw[TILE:]], axis=0), ktb)
        pair = [
            dict(h=2 * kk + j, d=[], p=[], right=[], scaled=[],
                 cr=crow_ref[pl.ds(step * heads + 2 * kk + j, 1), :])
            for j in range(2)
        ]
        work += pair
        for at in strips:
            raw, start = (upper, at.start) if at.start < TILE else (lower, at.start - TILE)
            wide = slice(0, raw.shape[1])
            kf = k_raw[at].astype(f32)
            qf = q_raw[at].astype(f32)
            rk = lax.rsqrt(jnp.sum(kf * kf, axis=1, keepdims=True) + EPS)
            rq = lax.rsqrt(jnp.sum(qf * qf, axis=1, keepdims=True) + EPS) * DK**-0.5
            kn = kf * rk
            qn = qf * rq
            gram = raw[start : start + STRIP] * rk_row[:, wide] * -rk
            probe = raw[TILE + start : TILE + start + STRIP] * rk_row[:, wide] * rq
            for w in pair:
                h = w["h"]
                cc = jnp.broadcast_to(columns[at, h : h + 1], (STRIP, TILE))
                bt = jnp.broadcast_to(columns[at, n + h : n + h + 1], (STRIP, TILE))
                ccw, btw = cc, bt
                if raw.shape[1] > TILE:
                    ccw = jnp.concatenate([cc, cc], axis=1)
                    btw = jnp.concatenate([bt, bt], axis=1)
                span = jnp.exp2(ccw - w["cr"][:, wide] + mask_ref[at, wide])
                w["d"].append(span * btw * gram)
                w["p"].append((span * probe).astype(bf16))
                entry = jnp.exp2(cc) * first[at]
                value = v_ref[at, h * DV : (h + 1) * DV].astype(f32)
                w["right"].append(
                    jnp.concatenate([bt * entry * kn, bt * value], axis=1).astype(bf16)
                )
                w["scaled"].append((entry * qn).astype(bf16))
                if at.stop == rows:
                    w["last"] = entry[STRIP - 1 :]
                    w["kd"] = (kt * (rk_row * span[STRIP - 1 :])).astype(bf16)
        top = TILE // STRIP
        for w in pair:
            d11 = jnp.concatenate(w["d"][:top], axis=0)
            d2 = jnp.concatenate(w["d"][top:], axis=0)
            w["d"] = [d11, d2[:, TILE:]]
            w["d21"] = d2[:, :TILE].astype(bf16)
            w["p11"] = jnp.concatenate(w["p"][:top], axis=0)
            w["p2"] = jnp.concatenate(w["p"][top:], axis=0)
            w["right"] = jnp.concatenate(w["right"], axis=0)
    mats = [m for w in work for m in w["d"]]
    inverses = block_inverses(mats)
    mats = [m.astype(bf16) for m in mats]
    zeros = jnp.zeros((TILE // 2, TILE), bf16)
    for level in range(MERGES):
        b = BLOCK << level
        keep = level_ref[level]
        picked = [odd_rows(m, b) * keep for m in mats]
        ys = [(p.astype(f32) + dot(p, x)).astype(bf16) for p, x in zip(picked, inverses)]
        odds = [odd_rows(x, b) for x in inverses]
        odds = [
            x + (y.astype(f32) + dot(x, interleave(zeros, y, b))).astype(bf16)
            for x, y in zip(odds, ys)
        ]
        inverses = [interleave(even_rows(x, b), o, b) for x, o in zip(inverses, odds)]
    for i, w in enumerate(work):
        x1, x2 = inverses[2 * i], inverses[2 * i + 1]
        h = w["h"]
        r1 = w["right"][:TILE]
        u1 = add_strips(r1, dot(x1, r1))
        after = dot(jnp.concatenate([w["d21"], w["p11"]], axis=0), u1)
        r2 = add_strips(w["right"][TILE:], after[:TILE])
        u2 = add_strips(r2, dot(x2, r2))
        u = jnp.concatenate([u1, u2], axis=0)
        last = dot(jnp.concatenate([w["p2"], w["kd"]], axis=0), u)
        for at, scaled in zip(strips, w["scaled"]):
            pu = after[TILE + at.start :] if at.start < TILE else last[at.start - TILE :]
            pu = pu[:STRIP]
            reach_ref[at, h * DK : (h + 1) * DK] = (scaled.astype(f32) - pu[:, :DK]).astype(bf16)
            inner_ref[at, h * DV : (h + 1) * DV] = pu[:, DK:].astype(inner_ref.dtype)
        base = pl.multiple_of((step * heads + h) * DK, DK)
        for start in range(0, DK, STRIP):
            ma = last[TILE + start : TILE + start + STRIP]
            kept = w["last"] * eye[start : start + STRIP]
            map_add_ref[pl.ds(base + start, STRIP), :] = jnp.concatenate(
                [kept - ma[:, :DK], ma[:, DK:]], axis=1
            ).astype(bf16)


def add_strips(a, b):
    return jnp.concatenate(
        [
            (a[i : i + STRIP].astype(f32) + b[i : i + STRIP]).astype(bf16)
            for i in range(0, a.shape[0], STRIP)
        ],
        axis=0,
    )


def delta_local(half, mib, seg_row, query, key, value, beta, decay):
    rows = query.shape[0]
    heads = 2 * KEYS_PER_STEP
    n = value.shape[1] // DV // 2
    steps = n // heads
    kw = KEYS_PER_STEP * DK
    vw = heads * DV
    tall = n * DK + BLOCK

    def at_half(i, s):
        return (0, s[0] * steps + i)

    def whole(i, s):
        return (0, 0)

    return pl.pallas_call(
        delta_local_kernel,
        grid_spec=pltpu.PrefetchScalarGridSpec(
            num_scalar_prefetch=1,
            grid=(steps,),
            in_specs=[
                pl.BlockSpec((1, rows), whole),
                pl.BlockSpec((rows, kw), at_half),
                pl.BlockSpec((rows, kw), at_half),
                pl.BlockSpec((rows, vw), at_half),
                pl.BlockSpec(beta.shape, whole),
                pl.BlockSpec(decay.shape, whole),
            ],
            out_specs=[
                pl.BlockSpec((tall, DK + DV), whole),
                pl.BlockSpec((rows, heads * DK), lambda i, s: (0, i)),
                pl.BlockSpec((rows, vw), lambda i, s: (0, i)),
            ],
            scratch_shapes=[
                pltpu.VMEM((rows, rows), f32),
                pltpu.VMEM((MERGES, TILE // 2, TILE), bf16),
                pltpu.VMEM((n, rows), f32),
                pltpu.VMEM((rows, TILE), f32),
                pltpu.VMEM((rows, TILE), f32),
            ],
        ),
        out_shape=[
            jax.ShapeDtypeStruct((tall, DK + DV), bf16),
            jax.ShapeDtypeStruct((rows, n * DK), bf16),
            jax.ShapeDtypeStruct((rows, n * DV), f32),
        ],
        compiler_params=params(mib),
        cost_estimate=cost(6 * 10**9, 3 * 2**20),
        name="delta_local",
    )(half, seg_row, query, key, value, beta, decay)


def ids_of(ref):
    end = ref.shape[0] - BLOCK
    return ref[end : end + BLOCK, :].astype(f32)[:1]


def put_id(ref, value):
    end = ref.shape[0] - BLOCK
    ref[end:, :] = jnp.broadcast_to(value, (BLOCK, ref.shape[1])).astype(bf16)


def matching(a, b):
    return jnp.where(a == b, 1.0, 0.0)


def compose_kernel(core_ref, mine_ref, other_ref, map_ref, add_ref):
    odd = core_ref[0] == 1
    mine_ids, other_ids = ids_of(mine_ref), ids_of(other_ref)
    early_ids = jnp.where(odd, other_ids, mine_ids)
    late_ids = jnp.where(odd, mine_ids, other_ids)
    across = matching(early_ids[:, -1:], late_ids[:, :1])
    put_id(map_ref, early_ids[:, :1])
    put_id(add_ref, late_ids[:, -1:])
    for h in range(mine_ref.shape[0] // DK):
        at = slice(h * DK, (h + 1) * DK)
        mine, other = mine_ref[at], other_ref[at]
        early, late = jnp.where(odd, other, mine), jnp.where(odd, mine, other)
        both = dot(late[:, :DK], early) * across
        map_ref[at] = both[:, :DK].astype(bf16)
        add_ref[at] = (both[:, DK:] + late[:, DK:].astype(f32)).astype(bf16)


def relay_kernel(map_ref, add_ref, state_ref, out_ref):
    into = matching(ids_of(state_ref), ids_of(map_ref))
    put_id(out_ref, ids_of(add_ref))
    for h in range(map_ref.shape[0] // DK):
        at = slice(h * DK, (h + 1) * DK)
        out_ref[at] = (dot(map_ref[at], state_ref[at]) * into + add_ref[at].astype(f32)).astype(bf16)


def arrive_kernel(core_ref, mine_ref, other_ref, state_ref, keep_ref, give_ref):
    odd = core_ref[0] == 1
    mine_ids, other_ids = ids_of(mine_ref), ids_of(other_ref)
    early_ids = jnp.where(odd, other_ids, mine_ids)
    late_ids = jnp.where(odd, mine_ids, other_ids)
    across = matching(early_ids[:, -1:], late_ids[:, :1])
    into = matching(ids_of(state_ref), early_ids[:, :1])
    for h in range(keep_ref.shape[0] // DK):
        at = slice(h * DK, (h + 1) * DK)
        early = jnp.where(odd, other_ref[at], mine_ref[at])
        first = (state_ref[at].astype(f32) * into).astype(bf16)
        second = (
            (dot(early[:, :DK], first) + early[:, DK:].astype(f32)) * across
        ).astype(bf16)
        keep_ref[at] = jnp.where(odd, second, first)
        give_ref[at] = jnp.where(odd, first, second)


SMEM = pl.BlockSpec(memory_space=pltpu.SMEM)
VMEM = pl.BlockSpec(memory_space=pltpu.VMEM)


def small_call(kernel, name, outs, *args, scalars=0, mib=16):
    return pl.pallas_call(
        kernel,
        in_specs=[SMEM] * scalars + [VMEM] * (len(args) - scalars),
        out_specs=[VMEM] * len(outs),
        out_shape=outs,
        compiler_params=params(mib),
        cost_estimate=cost(10**8, 2**20),
        name=name,
    )(*args)


def delta_out_kernel(half_ref, reach_ref, inner_ref, state_ref, gate_ref, gain_ref, *rest):
    out_ref = rest[-1]
    gain = gain_ref[...]
    for h in range(state_ref.shape[0] // DK):
        cols = slice(h * DV, (h + 1) * DV)
        state = state_ref[h * DK : (h + 1) * DK]
        carried = dot(reach_ref[:, cols], state)
        for i in range(0, carried.shape[0], STRIP):
            at = slice(i, i + STRIP)
            out = inner_ref[at, cols].astype(f32) + carried[at]
            spread = lax.rsqrt(jnp.mean(out * out, axis=1, keepdims=True) + EPS)
            gate = gate_ref[at, cols].astype(f32)
            gate = gate * sigmoid(gate)
            out_ref[at, cols] = (out * spread * gain * gate).astype(bf16)


def delta_out(half, reach, inner, state, gate, gain, partial_out=None):
    rows = reach.shape[0]
    n = state.shape[0] // DK
    heads = 4
    steps = n // heads

    def at_half(i, s):
        return (0, s[0] * steps + i)

    in_specs = [
        pl.BlockSpec((rows, heads * DK), lambda i, s: (0, i)),
        pl.BlockSpec((rows, heads * DV), lambda i, s: (0, i)),
        pl.BlockSpec((heads * DK, DV), lambda i, s: (i, 0)),
        pl.BlockSpec((rows, heads * DV), at_half),
        pl.BlockSpec((1, DV), lambda i, s: (0, 0)),
    ]
    args = [half, reach, inner, state, gate, gain]
    aliases = {}
    if partial_out is not None:
        in_specs.append(pl.BlockSpec(memory_space=pl.ANY))
        args.append(partial_out)
        aliases = {6: 0}
    return pl.pallas_call(
        delta_out_kernel,
        grid_spec=pltpu.PrefetchScalarGridSpec(
            num_scalar_prefetch=1,
            grid=(steps,),
            in_specs=in_specs,
            out_specs=pl.BlockSpec((rows, heads * DV), at_half),
        ),
        out_shape=jax.ShapeDtypeStruct(gate.shape, bf16),
        input_output_aliases=aliases,
        compiler_params=params(),
        cost_estimate=cost(10**8, 3 * 2**20),
        name="delta_out",
    )(*args)


def blocks_of(pieces):
    own, *same, other = pieces
    order = [(own, None)]
    for i, ref in enumerate(same):
        order += [(other, i), (ref, None)]
    return order[::-1]


def pack_kernel(seg_ref, key_ref, value_ref, out_ref):
    rows = key_ref.shape[0]
    ids = seg_ref[...].astype(f32) + 1.0
    out_ref[:rows, :HEAD_WIDTH] = key_ref[...]
    out_ref[:rows, HEAD_WIDTH:] = value_ref[...]
    out_ref[rows:, :rows] = jnp.broadcast_to(ids, (BLOCK, rows)).astype(bf16)
    out_ref[rows:, rows:] = jnp.zeros((BLOCK, 2 * HEAD_WIDTH - rows), bf16)


def window_kernel(freq_ref, *rest):
    *pieces, kt_ref, v_ref, ids_ref, cos_ref, sin_ref = rest
    rows = cos_ref.shape[0]
    window = ids_ref.shape[1]
    half = ROTARY_ENTRIES // 2
    blocks = [ref if index is None else ref.at[index] for ref, index in blocks_of(pieces)]
    row_ids = jnp.concatenate(
        [ref[rows : rows + BLOCK, :rows].astype(f32)[:1] for ref in blocks], axis=1
    )
    ids_ref[...] = row_ids
    ids = jnp.broadcast_to(row_ids, (DOCS, window))
    docs = lax.broadcasted_iota(jnp.int32, (DOCS, window), 0).astype(f32) + 1.0
    before = jnp.sum(jnp.where(ids < docs, 1.0, 0.0), axis=1, keepdims=True)
    start = jnp.sum(jnp.where(ids == docs, before, 0.0), axis=0, keepdims=True)
    place = lax.broadcasted_iota(jnp.int32, (1, window), 1).astype(f32)
    angle = freq_ref[:, :1] * (place - start)
    cosine = jnp.cos(angle)
    sine = jnp.sin(angle)
    for b, ref in enumerate(blocks):
        cols = slice(b * rows, (b + 1) * rows)
        kt = jnp.transpose(ref[:rows, :HEAD_WIDTH].astype(f32))
        one, two = kt[:half], kt[half:ROTARY_ENTRIES]
        cb, sb = cosine[:, cols], sine[:, cols]
        kt_ref[:half, cols] = (one * cb - two * sb).astype(bf16)
        kt_ref[half:ROTARY_ENTRIES, cols] = (two * cb + one * sb).astype(bf16)
        kt_ref[ROTARY_ENTRIES:, cols] = kt[ROTARY_ENTRIES:].astype(bf16)
        v_ref[cols, :] = ref[:rows, HEAD_WIDTH:]
    cq, sq = cosine[:, window - rows :], sine[:, window - rows :]
    rest_rows = TILE - ROTARY_ENTRIES
    cos_ref[...] = jnp.transpose(
        jnp.concatenate([cq, cq, jnp.ones((rest_rows, rows), f32)], axis=0)
    )
    sin_ref[...] = jnp.transpose(
        jnp.concatenate([-sq, sq, jnp.zeros((rest_rows, rows), f32)], axis=0)
    )


def attention_kernel(ids_ref, cos_ref, sin_ref, kt_ref, v_ref, q_ref, gate_ref, *rest):
    out_ref, mask_ref = rest[-2:]
    rows = q_ref.shape[0]
    window = ids_ref.shape[1]
    half = ROTARY_ENTRIES // 2

    @pl.when(pl.program_id(0) == 0)
    def _():
        own = ids_ref[:, window - rows :]
        own_col = jnp.transpose(jnp.broadcast_to(own, (TILE, rows)))
        own_cols = jnp.concatenate([own_col] * (window // TILE), axis=1)
        r = lax.broadcasted_iota(jnp.int32, (rows, window), 0) + (window - rows)
        c = lax.broadcasted_iota(jnp.int32, (rows, window), 1)
        mask_ref[...] = jnp.where((own_cols == ids_ref[...]) & (c <= r), 0.0, MASKED)

    scaling = HEAD_WIDTH**-0.5
    lane = lax.broadcasted_iota(jnp.int32, (TILE, TILE), 1)
    reach = window - rows + TILE
    for h in range(q_ref.shape[1] // HEAD_WIDTH):
        base = h * HEAD_WIDTH
        for first in range(0, rows, TILE):
            at = slice(first, first + TILE)
            keys = slice(first, first + reach)
            x = q_ref[at, base : base + TILE].astype(f32)
            swapped = jnp.where(
                lane < half, pltpu.roll(x, TILE - half, 1), pltpu.roll(x, half, 1)
            )
            rotated = ((x * cos_ref[at] + swapped * sin_ref[at]) * scaling).astype(bf16)
            tail = q_ref[at, base + TILE : base + HEAD_WIDTH] * jnp.asarray(scaling, bf16)
            scores = dot(jnp.concatenate([rotated, tail], axis=1), kt_ref[:, keys])
            weights = []
            totals = []
            for i in range(0, TILE, FINE):
                strip = scores[i : i + FINE] + mask_ref[first + i : first + i + FINE, keys]
                strip = jnp.exp(strip - jnp.max(strip, axis=1, keepdims=True))
                totals.append(1.0 / jnp.sum(strip, axis=1, keepdims=True))
                weights.append(strip.astype(bf16))
            mixed = dot(jnp.concatenate(weights, axis=0), v_ref[keys, :])
            for i, inverse in zip(range(0, TILE, FINE), totals):
                rows_at = slice(first + i, first + i + FINE)
                gate = sigmoid(gate_ref[rows_at, base : base + HEAD_WIDTH].astype(f32))
                out_ref[rows_at, base : base + HEAD_WIDTH] = (
                    mixed[i : i + FINE] * inverse * gate
                ).astype(bf16)


def attention_half(part, window_arrays, query, gate, partial_out=None):
    rows = query.shape[0]
    window = window_arrays[0].shape[1]
    heads = 2
    width = heads * HEAD_WIDTH
    steps = query.shape[1] // width // 2

    def at_part(i):
        return (0, part * steps + i)

    in_specs = [pl.BlockSpec(a.shape, lambda i: (0, 0)) for a in window_arrays]
    in_specs += [pl.BlockSpec((rows, width), at_part)] * 2
    args = [*window_arrays, query, gate]
    aliases = {}
    if partial_out is not None:
        aliases = {len(args): 0}
        in_specs.append(pl.BlockSpec(memory_space=pl.ANY))
        args.append(partial_out)
    return pl.pallas_call(
        attention_kernel,
        grid=(steps,),
        in_specs=in_specs,
        out_specs=pl.BlockSpec((rows, width), at_part),
        out_shape=jax.ShapeDtypeStruct(query.shape, bf16),
        scratch_shapes=[pltpu.VMEM((rows, window), f32)],
        input_output_aliases=aliases,
        compiler_params=params(),
        cost_estimate=cost(5 * 10**9, 3 * 2**20, 10**6),
        name="attention",
    )(*args)


def up_chip(value, ranks):
    return lax.ppermute(value, "ctx", [(i, i + 2) for i in range(ranks - 2)])


def swap_cores(value, ranks):
    return lax.ppermute(value, "ctx", [(i, i ^ 1) for i in range(ranks)])


def per_device(
    segment_ids,
    attn_query,
    attention_keys,
    attention_values,
    attn_gate,
    delta_query,
    delta_key,
    update_rule_payload,
    delta_beta,
    delta_decay,
    delta_gate,
    norm_gain,
):
    ranks = lax.axis_size("ctx")
    rank = lax.axis_index("ctx")
    rows = segment_ids.shape[0]
    hops = ranks // 4
    core = rank % 2
    odd = core == 1

    ids = segment_ids.reshape(1, rows)

    (own,) = small_call(
        pack_kernel,
        "pack",
        [jax.ShapeDtypeStruct((rows + BLOCK, 2 * HEAD_WIDTH), bf16)],
        ids,
        attention_keys,
        attention_values,
        mib=60,
    )
    nearest = up_chip(own, ranks)

    keep_half = core.reshape(1).astype(jnp.int32)
    give_half = 1 - keep_half
    local = partial(
        delta_local,
        seg_row=ids,
        query=delta_query,
        key=delta_key,
        value=update_rule_payload,
        beta=delta_beta.T,
        decay=delta_decay.T,
    )
    give_ma, give_reach, give_inner = local(give_half, 60)
    other_ma = swap_cores(give_ma, ranks)
    nearest, give_ma = lax.optimization_barrier((nearest, give_ma))
    same = [nearest]
    for _ in range(hops - 1):
        same.append(up_chip(same[-1], ranks))
    keep_ma, keep_reach, keep_inner = local(keep_half, 20)
    same, keep_ma = lax.optimization_barrier((same, keep_ma))
    chain = [own, *same]
    other = swap_cores(
        jnp.stack([jnp.where(odd, chain[i + 1], chain[i]) for i in range(hops)]), ranks
    )

    tall = keep_ma.shape[0]
    state_like = jax.ShapeDtypeStruct((tall, DV), bf16)
    chip_map, chip_add = small_call(
        compose_kernel, "compose", [state_like] * 2, keep_half, keep_ma, other_ma, scalars=1
    )
    state = up_chip(chip_add, ranks)

    window = (2 * hops + 1) * rows
    index = jnp.arange(ROTARY_ENTRIES // 2).astype(f32)
    freq = ROPE_THETA ** (-2.0 * index / ROTARY_ENTRIES)
    freq = jnp.broadcast_to(freq[:, None], (ROTARY_ENTRIES // 2, TILE))
    window_arrays = small_call(
        window_kernel,
        "window",
        [
            jax.ShapeDtypeStruct((HEAD_WIDTH, window), bf16),
            jax.ShapeDtypeStruct((window, HEAD_WIDTH), bf16),
            jax.ShapeDtypeStruct((1, window), f32),
            jax.ShapeDtypeStruct((rows, TILE), f32),
            jax.ShapeDtypeStruct((rows, TILE), f32),
        ],
        freq,
        own,
        *same,
        other,
    )
    state, window_arrays = lax.optimization_barrier((state, window_arrays))
    for _ in range(hops - 1):
        (leaving,) = small_call(relay_kernel, "relay", [state_like], chip_map, chip_add, state)
        state = up_chip(leaving, ranks)
    kt, v_all, window_ids, cosine, sine = window_arrays
    window_arrays = (window_ids, cosine, sine, kt, v_all)
    attn_mixed = attention_half(0, window_arrays, attn_query, attn_gate)
    state, attn_mixed = lax.optimization_barrier((state, attn_mixed))

    final_like = jax.ShapeDtypeStruct((tall - BLOCK, DV), bf16)
    keep_state, pass_state = small_call(
        arrive_kernel, "arrive", [final_like] * 2, keep_half, keep_ma, other_ma, state, scalars=1
    )
    give_state = swap_cores(pass_state, ranks)
    attn_mixed = attention_half(1, window_arrays, attn_query, attn_gate, attn_mixed)

    gain = norm_gain.reshape(1, DV)
    delta_mixed = delta_out(keep_half, keep_reach, keep_inner, keep_state, delta_gate, gain)
    delta_mixed = delta_out(
        give_half, give_reach, give_inner, give_state, delta_gate, gain, delta_mixed
    )
    return (attn_mixed, delta_mixed)


def solution(mesh):
    rows = P(("dp", "ctx"))
    wide = P(("dp", "ctx"), None)
    return jax.shard_map(
        per_device,
        mesh=mesh,
        in_specs=(rows,) + (wide,) * 10 + (P(),),
        out_specs=(wide, wide),
        check_vma=False,
    )
```

```python
from functools import partial

import jax
import jax.numpy as jnp
from jax import lax
from jax.experimental import pallas as pl
from jax.experimental.pallas import tpu as pltpu
from jax.sharding import PartitionSpec as P

HEAD_WIDTH = 256
ROTARY_ENTRIES = 64
DK = 128
DV = 128
DOCS = 8
ROPE_THETA = 10000000.0
LOG2E = 1.4426950408889634
MASKED = -1e30
EPS = 1e-6
TILE = 128
KEYS_PER_STEP = 4
MIB = 1024 * 1024

f32 = jnp.float32
bf16 = jnp.bfloat16


def dot(a, b, precision=None):
    return jnp.dot(a, b, preferred_element_type=f32, precision=precision)


def params(mib=16):
    return pltpu.CompilerParams(vmem_limit_bytes=mib * MIB)


def sigmoid(x):
    return 0.5 * jnp.tanh(0.5 * x) + 0.5


def cost(flops, nbytes, exps=0):
    return pl.CostEstimate(flops=flops, bytes_accessed=nbytes, transcendentals=exps)


BLOCK = 16
MERGES = 3
STRIP = 32
FINE = 16


def odd_rows(m, b):
    return jnp.concatenate([m[i + b : i + 2 * b] for i in range(0, TILE, 2 * b)], axis=0)


def interleave(even, odd, b):
    parts = []
    for i in range(0, TILE // 2, b):
        parts += [even[i : i + b], odd[i : i + b]]
    return jnp.concatenate(parts, axis=0)


def even_rows(m, b):
    return jnp.concatenate([m[i : i + b] for i in range(0, TILE, 2 * b)], axis=0)


def block_inverses(mats):
    row = lax.broadcasted_iota(jnp.int32, (BLOCK, TILE), 0)
    lane = lax.broadcasted_iota(jnp.int32, (BLOCK, TILE), 1)
    within = lax.rem(lane, BLOCK)
    group = lane // BLOCK
    folded = []
    for m in mats:
        z = jnp.where(group == 0, m[:BLOCK], 0.0)
        for r in range(1, TILE // BLOCK):
            z = jnp.where(group == r, m[r * BLOCK : (r + 1) * BLOCK], z)
        folded.append(jnp.where(row > within, z, 0.0))
    xs = [jnp.where(row == within, 1.0, 0.0)] * len(mats)
    small = 8
    for k in range(BLOCK - 1):
        low = 0 if k < small - 1 else small
        at = (group * BLOCK + k)[low:]
        for i, z in enumerate(folded):
            spread = jnp.take_along_axis(z[low:], at, axis=1, mode="promise_in_bounds")
            x = xs[i]
            new = x[low:] + spread * x[k : k + 1]
            xs[i] = new if low == 0 else jnp.concatenate([x[:low], new], axis=0)
    out = []
    for x in xs:
        x = jnp.where(row > within, x, 0.0)
        out.append(
            jnp.concatenate(
                [jnp.where(group == r, x, 0.0) for r in range(TILE // BLOCK)], axis=0
            ).astype(bf16)
        )
    return out


def delta_local_kernel(
    half_ref,
    seg_ref,
    q_ref,
    k_ref,
    v_ref,
    beta_ref,
    decay_ref,
    map_add_ref,
    reach_ref,
    inner_ref,
    mask_ref,
    level_ref,
    crow_ref,
    ccol_ref,
    first_ref,
):
    rows = q_ref.shape[0]
    step = pl.program_id(0)
    heads = 2 * KEYS_PER_STEP

    @pl.when(step == 0)
    def _():
        seg_row = seg_ref[...].astype(f32) + 1.0
        seg_col = jnp.transpose(jnp.broadcast_to(seg_row, (TILE, rows)))
        seg_cols = jnp.concatenate([seg_col] * (rows // TILE), axis=1)
        r = lax.broadcasted_iota(jnp.int32, (rows, rows), 0)
        c = lax.broadcasted_iota(jnp.int32, (rows, rows), 1)
        mask_ref[...] = jnp.where((seg_cols == seg_row) & (r >= c), 0.0, MASKED)
        first_ref[...] = jnp.where(seg_col == seg_row[:, :1], 1.0, 0.0)
        r = lax.broadcasted_iota(jnp.int32, (TILE, TILE), 0)
        c = lax.broadcasted_iota(jnp.int32, (TILE, TILE), 1)
        for level in range(MERGES):
            b = BLOCK << level
            sibling = jnp.where(r // b == c // b + 1, 1.0, 0.0)
            level_ref[level] = odd_rows(sibling, b).astype(bf16)
        n = map_add_ref.shape[0] // DK
        base = pl.multiple_of(half_ref[0] * n, n)
        decay = decay_ref[pl.ds(base, n), :] * LOG2E
        high = decay.astype(bf16)
        rest = decay - high.astype(f32)
        middle = rest.astype(bf16)
        parts = [high, middle, (rest - middle.astype(f32)).astype(bf16)]
        parts = jnp.concatenate([p.astype(f32) for p in parts], axis=0).astype(bf16)
        r = lax.broadcasted_iota(jnp.int32, (rows, rows), 0)
        c = lax.broadcasted_iota(jnp.int32, (rows, rows), 1)
        sums = dot(parts, jnp.where(r <= c, 1.0, 0.0).astype(bf16))
        cumulative = sums[:n] + sums[n : 2 * n] + sums[2 * n :]
        crow_ref[...] = cumulative
        fill = jnp.zeros((TILE - 2 * n, rows), f32)
        both = jnp.concatenate([cumulative, beta_ref[pl.ds(base, n), :], fill], axis=0)
        ccol_ref[...] = jnp.transpose(both)
        end = map_add_ref.shape[0] - BLOCK
        map_add_ref[end:, :] = jnp.broadcast_to(seg_row, (BLOCK, rows)).astype(bf16)

    shift = lax.rem(TILE - step * heads, TILE)
    columns = pltpu.roll(ccol_ref[...], shift, 1)
    n = map_add_ref.shape[0] // DK
    first = first_ref[...]
    eye = jnp.where(
        lax.broadcasted_iota(jnp.int32, (TILE, TILE), 0)
        == lax.broadcasted_iota(jnp.int32, (TILE, TILE), 1),
        1.0,
        0.0,
    )
    work = []
    strips = [slice(i, i + STRIP) for i in range(0, rows, STRIP)]
    for kk in range(KEYS_PER_STEP):
        cols = slice(kk * DK, (kk + 1) * DK)
        k_raw = k_ref[:, cols]
        q_raw = q_ref[:, cols]
        kt = jnp.transpose(k_raw.astype(f32))
        rk_row = lax.rsqrt(jnp.sum(kt * kt, axis=0, keepdims=True) + EPS)
        ktb = kt.astype(bf16)
        upper = dot(jnp.concatenate([k_raw[:TILE], q_raw[:TILE]], axis=0), ktb[:, :TILE])
        lower = dot(jnp.concatenate([k_raw[TILE:], q_raw[TILE:]], axis=0), ktb)
        pair = [
            dict(h=2 * kk + j, d=[], p=[], right=[], scaled=[],
                 cr=crow_ref[pl.ds(step * heads + 2 * kk + j, 1), :])
            for j in range(2)
        ]
        work += pair
        for at in strips:
            raw, start = (upper, at.start) if at.start < TILE else (lower, at.start - TILE)
            wide = slice(0, raw.shape[1])
            kf = k_raw[at].astype(f32)
            qf = q_raw[at].astype(f32)
            rk = lax.rsqrt(jnp.sum(kf * kf, axis=1, keepdims=True) + EPS)
            rq = lax.rsqrt(jnp.sum(qf * qf, axis=1, keepdims=True) + EPS) * DK**-0.5
            kn = kf * rk
            qn = qf * rq
            gram = raw[start : start + STRIP] * rk_row[:, wide] * -rk
            probe = raw[TILE + start : TILE + start + STRIP] * rk_row[:, wide] * rq
            for w in pair:
                h = w["h"]
                cc = jnp.broadcast_to(columns[at, h : h + 1], (STRIP, TILE))
                bt = jnp.broadcast_to(columns[at, n + h : n + h + 1], (STRIP, TILE))
                ccw, btw = cc, bt
                if raw.shape[1] > TILE:
                    ccw = jnp.concatenate([cc, cc], axis=1)
                    btw = jnp.concatenate([bt, bt], axis=1)
                span = jnp.exp2(ccw - w["cr"][:, wide] + mask_ref[at, wide])
                w["d"].append(span * btw * gram)
                w["p"].append((span * probe).astype(bf16))
                entry = jnp.exp2(cc) * first[at]
                value = v_ref[at, h * DV : (h + 1) * DV].astype(f32)
                w["right"].append(
                    jnp.concatenate([bt * entry * kn, bt * value], axis=1).astype(bf16)
                )
                w["scaled"].append((entry * qn).astype(bf16))
                if at.stop == rows:
                    w["last"] = entry[STRIP - 1 :]
                    w["kd"] = (kt * (rk_row * span[STRIP - 1 :])).astype(bf16)
        top = TILE // STRIP
        for w in pair:
            d11 = jnp.concatenate(w["d"][:top], axis=0)
            d2 = jnp.concatenate(w["d"][top:], axis=0)
            w["d"] = [d11, d2[:, TILE:]]
            w["d21"] = d2[:, :TILE].astype(bf16)
            w["p11"] = jnp.concatenate(w["p"][:top], axis=0)
            w["p2"] = jnp.concatenate(w["p"][top:], axis=0)
            w["right"] = jnp.concatenate(w["right"], axis=0)
    mats = [m for w in work for m in w["d"]]
    inverses = block_inverses(mats)
    mats = [m.astype(bf16) for m in mats]
    zeros = jnp.zeros((TILE // 2, TILE), bf16)
    for level in range(MERGES):
        b = BLOCK << level
        keep = level_ref[level]
        picked = [odd_rows(m, b) * keep for m in mats]
        ys = [(p.astype(f32) + dot(p, x)).astype(bf16) for p, x in zip(picked, inverses)]
        odds = [odd_rows(x, b) for x in inverses]
        odds = [
            x + (y.astype(f32) + dot(x, interleave(zeros, y, b))).astype(bf16)
            for x, y in zip(odds, ys)
        ]
        inverses = [interleave(even_rows(x, b), o, b) for x, o in zip(inverses, odds)]
    for i, w in enumerate(work):
        x1, x2 = inverses[2 * i], inverses[2 * i + 1]
        h = w["h"]
        r1 = w["right"][:TILE]
        u1 = add_strips(r1, dot(x1, r1))
        after = dot(jnp.concatenate([w["d21"], w["p11"]], axis=0), u1)
        r2 = add_strips(w["right"][TILE:], after[:TILE])
        u2 = add_strips(r2, dot(x2, r2))
        u = jnp.concatenate([u1, u2], axis=0)
        last = dot(jnp.concatenate([w["p2"], w["kd"]], axis=0), u)
        for at, scaled in zip(strips, w["scaled"]):
            pu = after[TILE + at.start :] if at.start < TILE else last[at.start - TILE :]
            pu = pu[:STRIP]
            reach_ref[at, h * DK : (h + 1) * DK] = (scaled.astype(f32) - pu[:, :DK]).astype(bf16)
            inner_ref[at, h * DV : (h + 1) * DV] = pu[:, DK:].astype(inner_ref.dtype)
        base = pl.multiple_of((step * heads + h) * DK, DK)
        for start in range(0, DK, STRIP):
            ma = last[TILE + start : TILE + start + STRIP]
            kept = w["last"] * eye[start : start + STRIP]
            map_add_ref[pl.ds(base + start, STRIP), :] = jnp.concatenate(
                [kept - ma[:, :DK], ma[:, DK:]], axis=1
            ).astype(bf16)


def add_strips(a, b):
    return jnp.concatenate(
        [
            (a[i : i + STRIP].astype(f32) + b[i : i + STRIP]).astype(bf16)
            for i in range(0, a.shape[0], STRIP)
        ],
        axis=0,
    )


def delta_local(half, mib, seg_row, query, key, value, beta, decay):
    rows = query.shape[0]
    heads = 2 * KEYS_PER_STEP
    n = value.shape[1] // DV // 2
    steps = n // heads
    kw = KEYS_PER_STEP * DK
    vw = heads * DV
    tall = n * DK + BLOCK

    def at_half(i, s):
        return (0, s[0] * steps + i)

    def whole(i, s):
        return (0, 0)

    return pl.pallas_call(
        delta_local_kernel,
        grid_spec=pltpu.PrefetchScalarGridSpec(
            num_scalar_prefetch=1,
            grid=(steps,),
            in_specs=[
                pl.BlockSpec((1, rows), whole),
                pl.BlockSpec((rows, kw), at_half),
                pl.BlockSpec((rows, kw), at_half),
                pl.BlockSpec((rows, vw), at_half),
                pl.BlockSpec(beta.shape, whole),
                pl.BlockSpec(decay.shape, whole),
            ],
            out_specs=[
                pl.BlockSpec((tall, DK + DV), whole),
                pl.BlockSpec((rows, heads * DK), lambda i, s: (0, i)),
                pl.BlockSpec((rows, vw), lambda i, s: (0, i)),
            ],
            scratch_shapes=[
                pltpu.VMEM((rows, rows), f32),
                pltpu.VMEM((MERGES, TILE // 2, TILE), bf16),
                pltpu.VMEM((n, rows), f32),
                pltpu.VMEM((rows, TILE), f32),
                pltpu.VMEM((rows, TILE), f32),
            ],
        ),
        out_shape=[
            jax.ShapeDtypeStruct((tall, DK + DV), bf16),
            jax.ShapeDtypeStruct((rows, n * DK), bf16),
            jax.ShapeDtypeStruct((rows, n * DV), f32),
        ],
        compiler_params=params(mib),
        cost_estimate=cost(6 * 10**9, 3 * 2**20),
        name="delta_local",
    )(half, seg_row, query, key, value, beta, decay)


def ids_of(ref):
    end = ref.shape[0] - BLOCK
    return ref[end : end + BLOCK, :].astype(f32)[:1]


def put_id(ref, value):
    end = ref.shape[0] - BLOCK
    ref[end:, :] = jnp.broadcast_to(value, (BLOCK, ref.shape[1])).astype(bf16)


def matching(a, b):
    return jnp.where(a == b, 1.0, 0.0)


def compose_kernel(core_ref, mine_ref, other_ref, map_ref, add_ref):
    odd = core_ref[0] == 1
    mine_ids, other_ids = ids_of(mine_ref), ids_of(other_ref)
    early_ids = jnp.where(odd, other_ids, mine_ids)
    late_ids = jnp.where(odd, mine_ids, other_ids)
    across = matching(early_ids[:, -1:], late_ids[:, :1])
    put_id(map_ref, early_ids[:, :1])
    put_id(add_ref, late_ids[:, -1:])
    for h in range(mine_ref.shape[0] // DK):
        at = slice(h * DK, (h + 1) * DK)
        mine, other = mine_ref[at], other_ref[at]
        early, late = jnp.where(odd, other, mine), jnp.where(odd, mine, other)
        both = dot(late[:, :DK], early) * across
        map_ref[at] = both[:, :DK].astype(bf16)
        add_ref[at] = (both[:, DK:] + late[:, DK:].astype(f32)).astype(bf16)


def relay_kernel(map_ref, add_ref, state_ref, out_ref):
    into = matching(ids_of(state_ref), ids_of(map_ref))
    put_id(out_ref, ids_of(add_ref))
    for h in range(map_ref.shape[0] // DK):
        at = slice(h * DK, (h + 1) * DK)
        out_ref[at] = (dot(map_ref[at], state_ref[at]) * into + add_ref[at].astype(f32)).astype(bf16)


def arrive_kernel(core_ref, mine_ref, other_ref, state_ref, keep_ref, give_ref):
    odd = core_ref[0] == 1
    mine_ids, other_ids = ids_of(mine_ref), ids_of(other_ref)
    early_ids = jnp.where(odd, other_ids, mine_ids)
    late_ids = jnp.where(odd, mine_ids, other_ids)
    across = matching(early_ids[:, -1:], late_ids[:, :1])
    into = matching(ids_of(state_ref), early_ids[:, :1])
    for h in range(keep_ref.shape[0] // DK):
        at = slice(h * DK, (h + 1) * DK)
        early = jnp.where(odd, other_ref[at], mine_ref[at])
        first = (state_ref[at].astype(f32) * into).astype(bf16)
        second = (
            (dot(early[:, :DK], first) + early[:, DK:].astype(f32)) * across
        ).astype(bf16)
        keep_ref[at] = jnp.where(odd, second, first)
        give_ref[at] = jnp.where(odd, first, second)


SMEM = pl.BlockSpec(memory_space=pltpu.SMEM)
VMEM = pl.BlockSpec(memory_space=pltpu.VMEM)


def small_call(kernel, name, outs, *args, scalars=0, mib=16):
    return pl.pallas_call(
        kernel,
        in_specs=[SMEM] * scalars + [VMEM] * (len(args) - scalars),
        out_specs=[VMEM] * len(outs),
        out_shape=outs,
        compiler_params=params(mib),
        cost_estimate=cost(10**8, 2**20),
        name=name,
    )(*args)


def delta_out_kernel(half_ref, reach_ref, inner_ref, state_ref, gate_ref, gain_ref, *rest):
    out_ref = rest[-1]
    gain = gain_ref[...]
    for h in range(state_ref.shape[0] // DK):
        cols = slice(h * DV, (h + 1) * DV)
        state = state_ref[h * DK : (h + 1) * DK]
        carried = dot(reach_ref[:, cols], state)
        for i in range(0, carried.shape[0], STRIP):
            at = slice(i, i + STRIP)
            out = inner_ref[at, cols].astype(f32) + carried[at]
            spread = lax.rsqrt(jnp.mean(out * out, axis=1, keepdims=True) + EPS)
            gate = gate_ref[at, cols].astype(f32)
            gate = gate * sigmoid(gate)
            out_ref[at, cols] = (out * spread * gain * gate).astype(bf16)


def delta_out(half, reach, inner, state, gate, gain, partial_out=None):
    rows = reach.shape[0]
    n = state.shape[0] // DK
    heads = 4
    steps = n // heads

    def at_half(i, s):
        return (0, s[0] * steps + i)

    in_specs = [
        pl.BlockSpec((rows, heads * DK), lambda i, s: (0, i)),
        pl.BlockSpec((rows, heads * DV), lambda i, s: (0, i)),
        pl.BlockSpec((heads * DK, DV), lambda i, s: (i, 0)),
        pl.BlockSpec((rows, heads * DV), at_half),
        pl.BlockSpec((1, DV), lambda i, s: (0, 0)),
    ]
    args = [half, reach, inner, state, gate, gain]
    aliases = {}
    if partial_out is not None:
        in_specs.append(pl.BlockSpec(memory_space=pl.ANY))
        args.append(partial_out)
        aliases = {6: 0}
    return pl.pallas_call(
        delta_out_kernel,
        grid_spec=pltpu.PrefetchScalarGridSpec(
            num_scalar_prefetch=1,
            grid=(steps,),
            in_specs=in_specs,
            out_specs=pl.BlockSpec((rows, heads * DV), at_half),
        ),
        out_shape=jax.ShapeDtypeStruct(gate.shape, bf16),
        input_output_aliases=aliases,
        compiler_params=params(),
        cost_estimate=cost(10**8, 3 * 2**20),
        name="delta_out",
    )(*args)


def blocks_of(pieces):
    own, *same, other = pieces
    order = [(own, None)]
    for i, ref in enumerate(same):
        order += [(other, i), (ref, None)]
    return order[::-1]


def pack_kernel(seg_ref, key_ref, value_ref, out_ref):
    rows = key_ref.shape[0]
    ids = seg_ref[...].astype(f32) + 1.0
    out_ref[:rows, :HEAD_WIDTH] = key_ref[...]
    out_ref[:rows, HEAD_WIDTH:] = value_ref[...]
    out_ref[rows:, :rows] = jnp.broadcast_to(ids, (BLOCK, rows)).astype(bf16)
    out_ref[rows:, rows:] = jnp.zeros((BLOCK, 2 * HEAD_WIDTH - rows), bf16)


def window_kernel(freq_ref, *rest):
    *pieces, kt_ref, v_ref, ids_ref, cos_ref, sin_ref = rest
    rows = cos_ref.shape[0]
    window = ids_ref.shape[1]
    half = ROTARY_ENTRIES // 2
    blocks = [ref if index is None else ref.at[index] for ref, index in blocks_of(pieces)]
    row_ids = jnp.concatenate(
        [ref[rows : rows + BLOCK, :rows].astype(f32)[:1] for ref in blocks], axis=1
    )
    ids_ref[...] = row_ids
    ids = jnp.broadcast_to(row_ids, (DOCS, window))
    docs = lax.broadcasted_iota(jnp.int32, (DOCS, window), 0).astype(f32) + 1.0
    before = jnp.sum(jnp.where(ids < docs, 1.0, 0.0), axis=1, keepdims=True)
    start = jnp.sum(jnp.where(ids == docs, before, 0.0), axis=0, keepdims=True)
    place = lax.broadcasted_iota(jnp.int32, (1, window), 1).astype(f32)
    angle = freq_ref[:, :1] * (place - start)
    cosine = jnp.cos(angle)
    sine = jnp.sin(angle)
    for b, ref in enumerate(blocks):
        cols = slice(b * rows, (b + 1) * rows)
        kt = jnp.transpose(ref[:rows, :HEAD_WIDTH].astype(f32))
        one, two = kt[:half], kt[half:ROTARY_ENTRIES]
        cb, sb = cosine[:, cols], sine[:, cols]
        kt_ref[:half, cols] = (one * cb - two * sb).astype(bf16)
        kt_ref[half:ROTARY_ENTRIES, cols] = (two * cb + one * sb).astype(bf16)
        kt_ref[ROTARY_ENTRIES:, cols] = kt[ROTARY_ENTRIES:].astype(bf16)
        v_ref[cols, :] = ref[:rows, HEAD_WIDTH:]
    cq, sq = cosine[:, window - rows :], sine[:, window - rows :]
    rest_rows = TILE - ROTARY_ENTRIES
    cos_ref[...] = jnp.transpose(
        jnp.concatenate([cq, cq, jnp.ones((rest_rows, rows), f32)], axis=0)
    )
    sin_ref[...] = jnp.transpose(
        jnp.concatenate([-sq, sq, jnp.zeros((rest_rows, rows), f32)], axis=0)
    )


def attention_kernel(ids_ref, cos_ref, sin_ref, kt_ref, v_ref, q_ref, gate_ref, *rest):
    out_ref, mask_ref = rest[-2:]
    rows = q_ref.shape[0]
    window = ids_ref.shape[1]
    half = ROTARY_ENTRIES // 2

    @pl.when(pl.program_id(0) == 0)
    def _():
        own = ids_ref[:, window - rows :]
        own_col = jnp.transpose(jnp.broadcast_to(own, (TILE, rows)))
        own_cols = jnp.concatenate([own_col] * (window // TILE), axis=1)
        r = lax.broadcasted_iota(jnp.int32, (rows, window), 0) + (window - rows)
        c = lax.broadcasted_iota(jnp.int32, (rows, window), 1)
        mask_ref[...] = jnp.where((own_cols == ids_ref[...]) & (c <= r), 0.0, MASKED)

    scaling = HEAD_WIDTH**-0.5
    lane = lax.broadcasted_iota(jnp.int32, (TILE, TILE), 1)
    reach = window - rows + TILE
    heads = q_ref.shape[1] // HEAD_WIDTH
    for first in range(0, rows, TILE):
        at = slice(first, first + TILE)
        keys = slice(first, first + reach)
        queries = []
        for h in range(heads):
            base = h * HEAD_WIDTH
            x = q_ref[at, base : base + TILE].astype(f32)
            swapped = jnp.where(
                lane < half, pltpu.roll(x, TILE - half, 1), pltpu.roll(x, half, 1)
            )
            rotated = ((x * cos_ref[at] + swapped * sin_ref[at]) * scaling).astype(bf16)
            tail = q_ref[at, base + TILE : base + HEAD_WIDTH] * jnp.asarray(scaling, bf16)
            queries.append(jnp.concatenate([rotated, tail], axis=1))
        scores = dot(jnp.concatenate(queries, axis=0), kt_ref[:, keys])
        weights = []
        totals = []
        for i in range(0, heads * TILE, FINE):
            row = first + i % TILE
            strip = scores[i : i + FINE] + mask_ref[row : row + FINE, keys]
            strip = jnp.exp(strip - jnp.max(strip, axis=1, keepdims=True))
            totals.append(1.0 / jnp.sum(strip, axis=1, keepdims=True))
            weights.append(strip.astype(bf16))
        mixed = dot(jnp.concatenate(weights, axis=0), v_ref[keys, :])
        for i, inverse in zip(range(0, heads * TILE, FINE), totals):
            rows_at = slice(first + i % TILE, first + i % TILE + FINE)
            cols = slice(i // TILE * HEAD_WIDTH, (i // TILE + 1) * HEAD_WIDTH)
            gate = sigmoid(gate_ref[rows_at, cols].astype(f32))
            out_ref[rows_at, cols] = (mixed[i : i + FINE] * inverse * gate).astype(bf16)


def attention_half(part, window_arrays, query, gate, partial_out=None):
    rows = query.shape[0]
    window = window_arrays[0].shape[1]
    heads = 4
    width = heads * HEAD_WIDTH
    steps = query.shape[1] // width // 2

    def at_part(i):
        return (0, part * steps + i)

    in_specs = [pl.BlockSpec(a.shape, lambda i: (0, 0)) for a in window_arrays]
    in_specs += [pl.BlockSpec((rows, width), at_part)] * 2
    args = [*window_arrays, query, gate]
    aliases = {}
    if partial_out is not None:
        aliases = {len(args): 0}
        in_specs.append(pl.BlockSpec(memory_space=pl.ANY))
        args.append(partial_out)
    return pl.pallas_call(
        attention_kernel,
        grid=(steps,),
        in_specs=in_specs,
        out_specs=pl.BlockSpec((rows, width), at_part),
        out_shape=jax.ShapeDtypeStruct(query.shape, bf16),
        scratch_shapes=[pltpu.VMEM((rows, window), f32)],
        input_output_aliases=aliases,
        compiler_params=params(28),
        cost_estimate=cost(5 * 10**9, 3 * 2**20, 10**6),
        name="attention",
    )(*args)


def up_chip(value, ranks):
    return lax.ppermute(value, "ctx", [(i, i + 2) for i in range(ranks - 2)])


def swap_cores(value, ranks):
    return lax.ppermute(value, "ctx", [(i, i ^ 1) for i in range(ranks)])


def per_device(
    segment_ids,
    attn_query,
    attention_keys,
    attention_values,
    attn_gate,
    delta_query,
    delta_key,
    update_rule_payload,
    delta_beta,
    delta_decay,
    delta_gate,
    norm_gain,
):
    ranks = lax.axis_size("ctx")
    rank = lax.axis_index("ctx")
    rows = segment_ids.shape[0]
    hops = ranks // 4
    core = rank % 2
    odd = core == 1

    ids = segment_ids.reshape(1, rows)

    (own,) = small_call(
        pack_kernel,
        "pack",
        [jax.ShapeDtypeStruct((rows + BLOCK, 2 * HEAD_WIDTH), bf16)],
        ids,
        attention_keys,
        attention_values,
        mib=60,
    )
    nearest = up_chip(own, ranks)

    keep_half = core.reshape(1).astype(jnp.int32)
    give_half = 1 - keep_half
    local = partial(
        delta_local,
        seg_row=ids,
        query=delta_query,
        key=delta_key,
        value=update_rule_payload,
        beta=delta_beta.T,
        decay=delta_decay.T,
    )
    give_ma, give_reach, give_inner = local(give_half, 60)
    other_ma = swap_cores(give_ma, ranks)
    nearest, give_ma = lax.optimization_barrier((nearest, give_ma))
    same = [nearest]
    for _ in range(hops - 1):
        same.append(up_chip(same[-1], ranks))
    keep_ma, keep_reach, keep_inner = local(keep_half, 60)
    same, keep_ma = lax.optimization_barrier((same, keep_ma))
    chain = [own, *same]
    other = swap_cores(
        jnp.stack([jnp.where(odd, chain[i + 1], chain[i]) for i in range(hops)]), ranks
    )

    tall = keep_ma.shape[0]
    state_like = jax.ShapeDtypeStruct((tall, DV), bf16)
    chip_map, chip_add = small_call(
        compose_kernel, "compose", [state_like] * 2, keep_half, keep_ma, other_ma, scalars=1
    )
    state = up_chip(chip_add, ranks)

    window = (2 * hops + 1) * rows
    index = jnp.arange(ROTARY_ENTRIES // 2).astype(f32)
    freq = ROPE_THETA ** (-2.0 * index / ROTARY_ENTRIES)
    freq = jnp.broadcast_to(freq[:, None], (ROTARY_ENTRIES // 2, TILE))
    window_arrays = small_call(
        window_kernel,
        "window",
        [
            jax.ShapeDtypeStruct((HEAD_WIDTH, window), bf16),
            jax.ShapeDtypeStruct((window, HEAD_WIDTH), bf16),
            jax.ShapeDtypeStruct((1, window), f32),
            jax.ShapeDtypeStruct((rows, TILE), f32),
            jax.ShapeDtypeStruct((rows, TILE), f32),
        ],
        freq,
        own,
        *same,
        other,
    )
    state, window_arrays = lax.optimization_barrier((state, window_arrays))
    for _ in range(hops - 1):
        (leaving,) = small_call(relay_kernel, "relay", [state_like], chip_map, chip_add, state)
        state = up_chip(leaving, ranks)
    kt, v_all, window_ids, cosine, sine = window_arrays
    window_arrays = (window_ids, cosine, sine, kt, v_all)
    attn_mixed = attention_half(0, window_arrays, attn_query, attn_gate)
    state, attn_mixed = lax.optimization_barrier((state, attn_mixed))

    final_like = jax.ShapeDtypeStruct((tall - BLOCK, DV), bf16)
    keep_state, pass_state = small_call(
        arrive_kernel, "arrive", [final_like] * 2, keep_half, keep_ma, other_ma, state, scalars=1
    )
    give_state = swap_cores(pass_state, ranks)
    attn_mixed = attention_half(1, window_arrays, attn_query, attn_gate, attn_mixed)

    gain = norm_gain.reshape(1, DV)
    delta_mixed = delta_out(keep_half, keep_reach, keep_inner, keep_state, delta_gate, gain)
    delta_mixed = delta_out(
        give_half, give_reach, give_inner, give_state, delta_gate, gain, delta_mixed
    )
    return (attn_mixed, delta_mixed)


def solution(mesh):
    rows = P(("dp", "ctx"))
    wide = P(("dp", "ctx"), None)
    return jax.shard_map(
        per_device,
        mesh=mesh,
        in_specs=(rows,) + (wide,) * 10 + (P(),),
        out_specs=(wide, wide),
        check_vma=False,
    )
```

```python
from functools import partial

import jax
import jax.numpy as jnp
from jax import lax
from jax.experimental import pallas as pl
from jax.experimental.pallas import tpu as pltpu
from jax.sharding import PartitionSpec as P

HEAD_WIDTH = 256
ROTARY_ENTRIES = 64
DK = 128
DV = 128
DOCS = 8
ROPE_THETA = 10000000.0
LOG2E = 1.4426950408889634
MASKED = -1e30
EPS = 1e-6
TILE = 128
KEYS_PER_STEP = 4
MIB = 1024 * 1024

f32 = jnp.float32
bf16 = jnp.bfloat16


def dot(a, b, precision=None):
    return jnp.dot(a, b, preferred_element_type=f32, precision=precision)


def params(mib=16):
    return pltpu.CompilerParams(vmem_limit_bytes=mib * MIB)


def sigmoid(x):
    return 0.5 * jnp.tanh(0.5 * x) + 0.5


def cost(flops, nbytes, exps=0):
    return pl.CostEstimate(flops=flops, bytes_accessed=nbytes, transcendentals=exps)


BLOCK = 16
MERGES = 3
STRIP = 32
FINE = 16
DONE = object()


def odd_rows(m, b):
    return jnp.concatenate([m[i + b : i + 2 * b] for i in range(0, TILE, 2 * b)], axis=0)


def interleave(even, odd, b):
    parts = []
    for i in range(0, TILE // 2, b):
        parts += [even[i : i + b], odd[i : i + b]]
    return jnp.concatenate(parts, axis=0)


def even_rows(m, b):
    return jnp.concatenate([m[i : i + b] for i in range(0, TILE, 2 * b)], axis=0)


def block_inverses(mats):
    row = lax.broadcasted_iota(jnp.int32, (BLOCK, TILE), 0)
    lane = lax.broadcasted_iota(jnp.int32, (BLOCK, TILE), 1)
    within = lax.rem(lane, BLOCK)
    group = lane // BLOCK
    folded = []
    for m in mats:
        z = jnp.where(group == 0, m[:BLOCK], 0.0)
        for r in range(1, TILE // BLOCK):
            z = jnp.where(group == r, m[r * BLOCK : (r + 1) * BLOCK], z)
        folded.append(jnp.where(row > within, z, 0.0))
    xs = [jnp.where(row == within, 1.0, 0.0)] * len(mats)
    small = 8
    for k in range(BLOCK - 1):
        low = 0 if k < small - 1 else small
        at = (group * BLOCK + k)[low:]
        for i, z in enumerate(folded):
            spread = jnp.take_along_axis(z[low:], at, axis=1, mode="promise_in_bounds")
            x = xs[i]
            new = x[low:] + spread * x[k : k + 1]
            xs[i] = new if low == 0 else jnp.concatenate([x[:low], new], axis=0)
    out = []
    for x in xs:
        x = jnp.where(row > within, x, 0.0)
        out.append(
            jnp.concatenate(
                [jnp.where(group == r, x, 0.0) for r in range(TILE // BLOCK)], axis=0
            ).astype(bf16)
        )
    return out


def delta_local_kernel(
    half_ref,
    seg_ref,
    q_ref,
    k_ref,
    v_ref,
    beta_ref,
    decay_ref,
    map_add_ref,
    reach_ref,
    inner_ref,
    mask_ref,
    level_ref,
    crow_ref,
    ccol_ref,
    first_ref,
):
    rows = q_ref.shape[0]
    step = pl.program_id(0)
    heads = 2 * KEYS_PER_STEP

    @pl.when(step == 0)
    def _():
        seg_row = seg_ref[...].astype(f32) + 1.0
        seg_col = jnp.transpose(jnp.broadcast_to(seg_row, (TILE, rows)))
        seg_cols = jnp.concatenate([seg_col] * (rows // TILE), axis=1)
        r = lax.broadcasted_iota(jnp.int32, (rows, rows), 0)
        c = lax.broadcasted_iota(jnp.int32, (rows, rows), 1)
        mask_ref[...] = jnp.where((seg_cols == seg_row) & (r >= c), 0.0, MASKED)
        first_ref[...] = jnp.where(seg_col == seg_row[:, :1], 1.0, 0.0)
        r = lax.broadcasted_iota(jnp.int32, (TILE, TILE), 0)
        c = lax.broadcasted_iota(jnp.int32, (TILE, TILE), 1)
        for level in range(MERGES):
            b = BLOCK << level
            sibling = jnp.where(r // b == c // b + 1, 1.0, 0.0)
            level_ref[level] = odd_rows(sibling, b).astype(bf16)
        n = map_add_ref.shape[0] // DK
        base = pl.multiple_of(half_ref[0] * n, n)
        decay = decay_ref[pl.ds(base, n), :] * LOG2E
        high = decay.astype(bf16)
        rest = decay - high.astype(f32)
        middle = rest.astype(bf16)
        parts = [high, middle, (rest - middle.astype(f32)).astype(bf16)]
        parts = jnp.concatenate([p.astype(f32) for p in parts], axis=0).astype(bf16)
        r = lax.broadcasted_iota(jnp.int32, (rows, rows), 0)
        c = lax.broadcasted_iota(jnp.int32, (rows, rows), 1)
        sums = dot(parts, jnp.where(r <= c, 1.0, 0.0).astype(bf16))
        cumulative = sums[:n] + sums[n : 2 * n] + sums[2 * n :]
        crow_ref[...] = cumulative
        fill = jnp.zeros((TILE - 2 * n, rows), f32)
        both = jnp.concatenate([cumulative, beta_ref[pl.ds(base, n), :], fill], axis=0)
        ccol_ref[...] = jnp.transpose(both)
        end = map_add_ref.shape[0] - BLOCK
        map_add_ref[end:, :] = jnp.broadcast_to(seg_row, (BLOCK, rows)).astype(bf16)

    shift = lax.rem(TILE - step * heads, TILE)
    columns = pltpu.roll(ccol_ref[...], shift, 1)
    n = map_add_ref.shape[0] // DK
    first = first_ref[...]
    eye = jnp.where(
        lax.broadcasted_iota(jnp.int32, (TILE, TILE), 0)
        == lax.broadcasted_iota(jnp.int32, (TILE, TILE), 1),
        1.0,
        0.0,
    )
    strips = [slice(i, i + STRIP) for i in range(0, rows, STRIP)]

    def elementwise(kk, pair):
        cols = slice(kk * DK, (kk + 1) * DK)
        k_raw = k_ref[:, cols]
        q_raw = q_ref[:, cols]
        kt = jnp.transpose(k_raw.astype(f32))
        rk_row = lax.rsqrt(jnp.sum(kt * kt, axis=0, keepdims=True) + EPS)
        ktb = kt.astype(bf16)
        upper = dot(jnp.concatenate([k_raw[:TILE], q_raw[:TILE]], axis=0), ktb[:, :TILE])
        lower = dot(jnp.concatenate([k_raw[TILE:], q_raw[TILE:]], axis=0), ktb)
        pair += [
            dict(h=2 * kk + j, d=[], p=[], right=[], scaled=[],
                 cr=crow_ref[pl.ds(step * heads + 2 * kk + j, 1), :])
            for j in range(2)
        ]
        yield
        for at in strips:
            raw, start = (upper, at.start) if at.start < TILE else (lower, at.start - TILE)
            wide = slice(0, raw.shape[1])
            kf = k_raw[at].astype(f32)
            qf = q_raw[at].astype(f32)
            rk = lax.rsqrt(jnp.sum(kf * kf, axis=1, keepdims=True) + EPS)
            rq = lax.rsqrt(jnp.sum(qf * qf, axis=1, keepdims=True) + EPS) * DK**-0.5
            kn = kf * rk
            qn = qf * rq
            gram = raw[start : start + STRIP] * rk_row[:, wide] * -rk
            probe = raw[TILE + start : TILE + start + STRIP] * rk_row[:, wide] * rq
            for w in pair:
                h = w["h"]
                cc = jnp.broadcast_to(columns[at, h : h + 1], (STRIP, TILE))
                bt = jnp.broadcast_to(columns[at, n + h : n + h + 1], (STRIP, TILE))
                ccw, btw = cc, bt
                if raw.shape[1] > TILE:
                    ccw = jnp.concatenate([cc, cc], axis=1)
                    btw = jnp.concatenate([bt, bt], axis=1)
                span = jnp.exp2(ccw - w["cr"][:, wide] + mask_ref[at, wide])
                w["d"].append(span * btw * gram)
                w["p"].append((span * probe).astype(bf16))
                entry = jnp.exp2(cc) * first[at]
                value = v_ref[at, h * DV : (h + 1) * DV].astype(f32)
                w["right"].append(
                    jnp.concatenate([bt * entry * kn, bt * value], axis=1).astype(bf16)
                )
                w["scaled"].append((entry * qn).astype(bf16))
                if at.stop == rows:
                    w["last"] = entry[STRIP - 1 :]
                    w["kd"] = (kt * (rk_row * span[STRIP - 1 :])).astype(bf16)
            yield
        top = TILE // STRIP
        for w in pair:
            d11 = jnp.concatenate(w["d"][:top], axis=0)
            d2 = jnp.concatenate(w["d"][top:], axis=0)
            w["d"] = [d11, d2[:, TILE:]]
            w["d21"] = d2[:, :TILE].astype(bf16)
            w["p11"] = jnp.concatenate(w["p"][:top], axis=0)
            w["p2"] = jnp.concatenate(w["p"][top:], axis=0)
            w["right"] = jnp.concatenate(w["right"], axis=0)
        yield

    def invert(pair):
        mats = [m for w in pair for m in w["d"]]
        inverses = block_inverses(mats)
        yield
        mats = [m.astype(bf16) for m in mats]
        zeros = jnp.zeros((TILE // 2, TILE), bf16)
        for level in range(MERGES):
            b = BLOCK << level
            keep = level_ref[level]
            picked = [odd_rows(m, b) * keep for m in mats]
            ys = [(p.astype(f32) + dot(p, x)).astype(bf16) for p, x in zip(picked, inverses)]
            yield
            odds = [odd_rows(x, b) for x in inverses]
            odds = [
                x + (y.astype(f32) + dot(x, interleave(zeros, y, b))).astype(bf16)
                for x, y in zip(odds, ys)
            ]
            inverses = [interleave(even_rows(x, b), o, b) for x, o in zip(inverses, odds)]
            yield
        for i, w in enumerate(pair):
            w["x"] = inverses[2 * i : 2 * i + 2]

    def finish(pair):
        for w in pair:
            w["u1"] = add_strips(w["right"][:TILE], dot(w["x"][0], w["right"][:TILE]))
        yield
        for w in pair:
            w["after"] = dot(jnp.concatenate([w["d21"], w["p11"]], axis=0), w["u1"])
        yield
        for w in pair:
            r2 = add_strips(w["right"][TILE:], w["after"][:TILE])
            w["u"] = jnp.concatenate([w["u1"], add_strips(r2, dot(w["x"][1], r2))], axis=0)
        yield
        for w in pair:
            w["end"] = dot(jnp.concatenate([w["p2"], w["kd"]], axis=0), w["u"])
        yield
        for w in pair:
            h, after, last = w["h"], w["after"], w["end"]
            for at, scaled in zip(strips, w["scaled"]):
                pu = after[TILE + at.start :] if at.start < TILE else last[at.start - TILE :]
                pu = pu[:STRIP]
                reach_ref[at, h * DK : (h + 1) * DK] = (
                    scaled.astype(f32) - pu[:, :DK]
                ).astype(bf16)
                inner_ref[at, h * DV : (h + 1) * DV] = pu[:, DK:].astype(inner_ref.dtype)
            base = pl.multiple_of((step * heads + h) * DK, DK)
            for start in range(0, DK, STRIP):
                ma = last[TILE + start : TILE + start + STRIP]
                kept = w["last"] * eye[start : start + STRIP]
                map_add_ref[pl.ds(base + start, STRIP), :] = jnp.concatenate(
                    [kept - ma[:, :DK], ma[:, DK:]], axis=1
                ).astype(bf16)
            yield

    pairs = [[] for _ in range(KEYS_PER_STEP)]
    for slot in range(KEYS_PER_STEP + 2):
        phases = []
        if slot < KEYS_PER_STEP:
            phases.append(elementwise(slot, pairs[slot]))
        if 0 <= slot - 1 < KEYS_PER_STEP:
            phases.append(invert(pairs[slot - 1]))
        if 0 <= slot - 2:
            phases.append(finish(pairs[slot - 2]))
        while phases:
            phases = [p for p in phases if next(p, DONE) is not DONE]


def add_strips(a, b):
    return jnp.concatenate(
        [
            (a[i : i + STRIP].astype(f32) + b[i : i + STRIP]).astype(bf16)
            for i in range(0, a.shape[0], STRIP)
        ],
        axis=0,
    )


def delta_local(half, mib, seg_row, query, key, value, beta, decay):
    rows = query.shape[0]
    heads = 2 * KEYS_PER_STEP
    n = value.shape[1] // DV // 2
    steps = n // heads
    kw = KEYS_PER_STEP * DK
    vw = heads * DV
    tall = n * DK + BLOCK

    def at_half(i, s):
        return (0, s[0] * steps + i)

    def whole(i, s):
        return (0, 0)

    return pl.pallas_call(
        delta_local_kernel,
        grid_spec=pltpu.PrefetchScalarGridSpec(
            num_scalar_prefetch=1,
            grid=(steps,),
            in_specs=[
                pl.BlockSpec((1, rows), whole),
                pl.BlockSpec((rows, kw), at_half),
                pl.BlockSpec((rows, kw), at_half),
                pl.BlockSpec((rows, vw), at_half),
                pl.BlockSpec(beta.shape, whole),
                pl.BlockSpec(decay.shape, whole),
            ],
            out_specs=[
                pl.BlockSpec((tall, DK + DV), whole),
                pl.BlockSpec((rows, heads * DK), lambda i, s: (0, i)),
                pl.BlockSpec((rows, vw), lambda i, s: (0, i)),
            ],
            scratch_shapes=[
                pltpu.VMEM((rows, rows), f32),
                pltpu.VMEM((MERGES, TILE // 2, TILE), bf16),
                pltpu.VMEM((n, rows), f32),
                pltpu.VMEM((rows, TILE), f32),
                pltpu.VMEM((rows, TILE), f32),
            ],
        ),
        out_shape=[
            jax.ShapeDtypeStruct((tall, DK + DV), bf16),
            jax.ShapeDtypeStruct((rows, n * DK), bf16),
            jax.ShapeDtypeStruct((rows, n * DV), f32),
        ],
        compiler_params=params(mib),
        cost_estimate=cost(6 * 10**9, 3 * 2**20),
        name="delta_local",
    )(half, seg_row, query, key, value, beta, decay)


def ids_of(ref):
    end = ref.shape[0] - BLOCK
    return ref[end : end + BLOCK, :].astype(f32)[:1]


def put_id(ref, value):
    end = ref.shape[0] - BLOCK
    ref[end:, :] = jnp.broadcast_to(value, (BLOCK, ref.shape[1])).astype(bf16)


def matching(a, b):
    return jnp.where(a == b, 1.0, 0.0)


def compose_kernel(core_ref, mine_ref, other_ref, map_ref, add_ref):
    odd = core_ref[0] == 1
    mine_ids, other_ids = ids_of(mine_ref), ids_of(other_ref)
    early_ids = jnp.where(odd, other_ids, mine_ids)
    late_ids = jnp.where(odd, mine_ids, other_ids)
    across = matching(early_ids[:, -1:], late_ids[:, :1])
    put_id(map_ref, early_ids[:, :1])
    put_id(add_ref, late_ids[:, -1:])
    for h in range(mine_ref.shape[0] // DK):
        at = slice(h * DK, (h + 1) * DK)
        mine, other = mine_ref[at], other_ref[at]
        early, late = jnp.where(odd, other, mine), jnp.where(odd, mine, other)
        both = dot(late[:, :DK], early) * across
        map_ref[at] = both[:, :DK].astype(bf16)
        add_ref[at] = (both[:, DK:] + late[:, DK:].astype(f32)).astype(bf16)


def relay_kernel(map_ref, add_ref, state_ref, out_ref):
    into = matching(ids_of(state_ref), ids_of(map_ref))
    put_id(out_ref, ids_of(add_ref))
    for h in range(map_ref.shape[0] // DK):
        at = slice(h * DK, (h + 1) * DK)
        out_ref[at] = (dot(map_ref[at], state_ref[at]) * into + add_ref[at].astype(f32)).astype(bf16)


def arrive_kernel(core_ref, mine_ref, other_ref, state_ref, keep_ref, give_ref):
    odd = core_ref[0] == 1
    mine_ids, other_ids = ids_of(mine_ref), ids_of(other_ref)
    early_ids = jnp.where(odd, other_ids, mine_ids)
    late_ids = jnp.where(odd, mine_ids, other_ids)
    across = matching(early_ids[:, -1:], late_ids[:, :1])
    into = matching(ids_of(state_ref), early_ids[:, :1])
    for h in range(keep_ref.shape[0] // DK):
        at = slice(h * DK, (h + 1) * DK)
        early = jnp.where(odd, other_ref[at], mine_ref[at])
        first = (state_ref[at].astype(f32) * into).astype(bf16)
        second = (
            (dot(early[:, :DK], first) + early[:, DK:].astype(f32)) * across
        ).astype(bf16)
        keep_ref[at] = jnp.where(odd, second, first)
        give_ref[at] = jnp.where(odd, first, second)


SMEM = pl.BlockSpec(memory_space=pltpu.SMEM)
VMEM = pl.BlockSpec(memory_space=pltpu.VMEM)


def small_call(kernel, name, outs, *args, scalars=0, mib=16):
    return pl.pallas_call(
        kernel,
        in_specs=[SMEM] * scalars + [VMEM] * (len(args) - scalars),
        out_specs=[VMEM] * len(outs),
        out_shape=outs,
        compiler_params=params(mib),
        cost_estimate=cost(10**8, 2**20),
        name=name,
    )(*args)


def delta_out_kernel(half_ref, reach_ref, inner_ref, state_ref, gate_ref, gain_ref, *rest):
    out_ref = rest[-1]
    gain = gain_ref[...]
    for h in range(state_ref.shape[0] // DK):
        cols = slice(h * DV, (h + 1) * DV)
        state = state_ref[h * DK : (h + 1) * DK]
        carried = dot(reach_ref[:, cols], state)
        for i in range(0, carried.shape[0], STRIP):
            at = slice(i, i + STRIP)
            out = inner_ref[at, cols].astype(f32) + carried[at]
            spread = lax.rsqrt(jnp.mean(out * out, axis=1, keepdims=True) + EPS)
            gate = gate_ref[at, cols].astype(f32)
            gate = gate * sigmoid(gate)
            out_ref[at, cols] = (out * spread * gain * gate).astype(bf16)


def delta_out(half, reach, inner, state, gate, gain, partial_out=None):
    rows = reach.shape[0]
    n = state.shape[0] // DK
    heads = 4
    steps = n // heads

    def at_half(i, s):
        return (0, s[0] * steps + i)

    in_specs = [
        pl.BlockSpec((rows, heads * DK), lambda i, s: (0, i)),
        pl.BlockSpec((rows, heads * DV), lambda i, s: (0, i)),
        pl.BlockSpec((heads * DK, DV), lambda i, s: (i, 0)),
        pl.BlockSpec((rows, heads * DV), at_half),
        pl.BlockSpec((1, DV), lambda i, s: (0, 0)),
    ]
    args = [half, reach, inner, state, gate, gain]
    aliases = {}
    if partial_out is not None:
        in_specs.append(pl.BlockSpec(memory_space=pl.ANY))
        args.append(partial_out)
        aliases = {6: 0}
    return pl.pallas_call(
        delta_out_kernel,
        grid_spec=pltpu.PrefetchScalarGridSpec(
            num_scalar_prefetch=1,
            grid=(steps,),
            in_specs=in_specs,
            out_specs=pl.BlockSpec((rows, heads * DV), at_half),
        ),
        out_shape=jax.ShapeDtypeStruct(gate.shape, bf16),
        input_output_aliases=aliases,
        compiler_params=params(),
        cost_estimate=cost(10**8, 3 * 2**20),
        name="delta_out",
    )(*args)


def blocks_of(pieces):
    own, *same, other = pieces
    order = [(own, None)]
    for i, ref in enumerate(same):
        order += [(other, i), (ref, None)]
    return order[::-1]


def pack_kernel(seg_ref, key_ref, value_ref, out_ref):
    rows = key_ref.shape[0]
    ids = seg_ref[...].astype(f32) + 1.0
    out_ref[:rows, :HEAD_WIDTH] = key_ref[...]
    out_ref[:rows, HEAD_WIDTH:] = value_ref[...]
    out_ref[rows:, :rows] = jnp.broadcast_to(ids, (BLOCK, rows)).astype(bf16)
    out_ref[rows:, rows:] = jnp.zeros((BLOCK, 2 * HEAD_WIDTH - rows), bf16)


def window_kernel(freq_ref, *rest):
    *pieces, kt_ref, v_ref, ids_ref, cos_ref, sin_ref = rest
    rows = cos_ref.shape[0]
    window = ids_ref.shape[1]
    half = ROTARY_ENTRIES // 2
    blocks = [ref if index is None else ref.at[index] for ref, index in blocks_of(pieces)]
    row_ids = jnp.concatenate(
        [ref[rows : rows + BLOCK, :rows].astype(f32)[:1] for ref in blocks], axis=1
    )
    ids_ref[...] = row_ids
    ids = jnp.broadcast_to(row_ids, (DOCS, window))
    docs = lax.broadcasted_iota(jnp.int32, (DOCS, window), 0).astype(f32) + 1.0
    before = jnp.sum(jnp.where(ids < docs, 1.0, 0.0), axis=1, keepdims=True)
    start = jnp.sum(jnp.where(ids == docs, before, 0.0), axis=0, keepdims=True)
    place = lax.broadcasted_iota(jnp.int32, (1, window), 1).astype(f32)
    angle = freq_ref[:, :1] * (place - start)
    cosine = jnp.cos(angle)
    sine = jnp.sin(angle)
    for b, ref in enumerate(blocks):
        cols = slice(b * rows, (b + 1) * rows)
        kt = jnp.transpose(ref[:rows, :HEAD_WIDTH].astype(f32))
        one, two = kt[:half], kt[half:ROTARY_ENTRIES]
        cb, sb = cosine[:, cols], sine[:, cols]
        kt_ref[:half, cols] = (one * cb - two * sb).astype(bf16)
        kt_ref[half:ROTARY_ENTRIES, cols] = (two * cb + one * sb).astype(bf16)
        kt_ref[ROTARY_ENTRIES:, cols] = kt[ROTARY_ENTRIES:].astype(bf16)
        v_ref[cols, :] = ref[:rows, HEAD_WIDTH:]
    cq, sq = cosine[:, window - rows :], sine[:, window - rows :]
    rest_rows = TILE - ROTARY_ENTRIES
    cos_ref[...] = jnp.transpose(
        jnp.concatenate([cq, cq, jnp.ones((rest_rows, rows), f32)], axis=0)
    )
    sin_ref[...] = jnp.transpose(
        jnp.concatenate([-sq, sq, jnp.zeros((rest_rows, rows), f32)], axis=0)
    )


def attention_kernel(ids_ref, cos_ref, sin_ref, kt_ref, v_ref, q_ref, gate_ref, *rest):
    out_ref, mask_ref = rest[-2:]
    rows = q_ref.shape[0]
    window = ids_ref.shape[1]
    half = ROTARY_ENTRIES // 2

    @pl.when(pl.program_id(0) == 0)
    def _():
        own = ids_ref[:, window - rows :]
        own_col = jnp.transpose(jnp.broadcast_to(own, (TILE, rows)))
        own_cols = jnp.concatenate([own_col] * (window // TILE), axis=1)
        r = lax.broadcasted_iota(jnp.int32, (rows, window), 0) + (window - rows)
        c = lax.broadcasted_iota(jnp.int32, (rows, window), 1)
        mask_ref[...] = jnp.where((own_cols == ids_ref[...]) & (c <= r), 0.0, MASKED)

    scaling = HEAD_WIDTH**-0.5
    lane = lax.broadcasted_iota(jnp.int32, (TILE, TILE), 1)
    reach = window - rows + TILE
    heads = q_ref.shape[1] // HEAD_WIDTH
    for first in range(0, rows, TILE):
        at = slice(first, first + TILE)
        keys = slice(first, first + reach)
        queries = []
        for h in range(heads):
            base = h * HEAD_WIDTH
            x = q_ref[at, base : base + TILE].astype(f32)
            swapped = jnp.where(
                lane < half, pltpu.roll(x, TILE - half, 1), pltpu.roll(x, half, 1)
            )
            rotated = ((x * cos_ref[at] + swapped * sin_ref[at]) * scaling).astype(bf16)
            tail = q_ref[at, base + TILE : base + HEAD_WIDTH] * jnp.asarray(scaling, bf16)
            queries.append(jnp.concatenate([rotated, tail], axis=1))
        scores = dot(jnp.concatenate(queries, axis=0), kt_ref[:, keys])
        weights = []
        totals = []
        for i in range(0, heads * TILE, FINE):
            row = first + i % TILE
            strip = scores[i : i + FINE] + mask_ref[row : row + FINE, keys]
            strip = jnp.exp(strip - jnp.max(strip, axis=1, keepdims=True))
            totals.append(1.0 / jnp.sum(strip, axis=1, keepdims=True))
            weights.append(strip.astype(bf16))
        mixed = dot(jnp.concatenate(weights, axis=0), v_ref[keys, :])
        for i, inverse in zip(range(0, heads * TILE, FINE), totals):
            rows_at = slice(first + i % TILE, first + i % TILE + FINE)
            cols = slice(i // TILE * HEAD_WIDTH, (i // TILE + 1) * HEAD_WIDTH)
            gate = sigmoid(gate_ref[rows_at, cols].astype(f32))
            out_ref[rows_at, cols] = (mixed[i : i + FINE] * inverse * gate).astype(bf16)


def attention_half(part, window_arrays, query, gate, partial_out=None):
    rows = query.shape[0]
    window = window_arrays[0].shape[1]
    heads = 4
    width = heads * HEAD_WIDTH
    steps = query.shape[1] // width // 2

    def at_part(i):
        return (0, part * steps + i)

    in_specs = [pl.BlockSpec(a.shape, lambda i: (0, 0)) for a in window_arrays]
    in_specs += [pl.BlockSpec((rows, width), at_part)] * 2
    args = [*window_arrays, query, gate]
    aliases = {}
    if partial_out is not None:
        aliases = {len(args): 0}
        in_specs.append(pl.BlockSpec(memory_space=pl.ANY))
        args.append(partial_out)
    return pl.pallas_call(
        attention_kernel,
        grid=(steps,),
        in_specs=in_specs,
        out_specs=pl.BlockSpec((rows, width), at_part),
        out_shape=jax.ShapeDtypeStruct(query.shape, bf16),
        scratch_shapes=[pltpu.VMEM((rows, window), f32)],
        input_output_aliases=aliases,
        compiler_params=params(28),
        cost_estimate=cost(5 * 10**9, 3 * 2**20, 10**6),
        name="attention",
    )(*args)


def up_chip(value, ranks):
    return lax.ppermute(value, "ctx", [(i, i + 2) for i in range(ranks - 2)])


def swap_cores(value, ranks):
    return lax.ppermute(value, "ctx", [(i, i ^ 1) for i in range(ranks)])


def per_device(
    segment_ids,
    attn_query,
    attention_keys,
    attention_values,
    attn_gate,
    delta_query,
    delta_key,
    update_rule_payload,
    delta_beta,
    delta_decay,
    delta_gate,
    norm_gain,
):
    ranks = lax.axis_size("ctx")
    rank = lax.axis_index("ctx")
    rows = segment_ids.shape[0]
    hops = ranks // 4
    core = rank % 2
    odd = core == 1

    ids = segment_ids.reshape(1, rows)

    (own,) = small_call(
        pack_kernel,
        "pack",
        [jax.ShapeDtypeStruct((rows + BLOCK, 2 * HEAD_WIDTH), bf16)],
        ids,
        attention_keys,
        attention_values,
        mib=60,
    )
    nearest = up_chip(own, ranks)

    keep_half = core.reshape(1).astype(jnp.int32)
    give_half = 1 - keep_half
    local = partial(
        delta_local,
        seg_row=ids,
        query=delta_query,
        key=delta_key,
        value=update_rule_payload,
        beta=delta_beta.T,
        decay=delta_decay.T,
    )
    give_ma, give_reach, give_inner = local(give_half, 60)
    other_ma = swap_cores(give_ma, ranks)
    nearest, give_ma = lax.optimization_barrier((nearest, give_ma))
    same = [nearest]
    for _ in range(hops - 1):
        same.append(up_chip(same[-1], ranks))
    keep_ma, keep_reach, keep_inner = local(keep_half, 60)
    same, keep_ma, other_ma = lax.optimization_barrier((same, keep_ma, other_ma))
    chain = [own, *same]
    other = swap_cores(
        jnp.stack([jnp.where(odd, chain[i + 1], chain[i]) for i in range(hops)]), ranks
    )

    tall = keep_ma.shape[0]
    state_like = jax.ShapeDtypeStruct((tall, DV), bf16)
    chip_map, chip_add = small_call(
        compose_kernel, "compose", [state_like] * 2, keep_half, keep_ma, other_ma, scalars=1
    )
    state = up_chip(chip_add, ranks)

    window = (2 * hops + 1) * rows
    index = jnp.arange(ROTARY_ENTRIES // 2).astype(f32)
    freq = ROPE_THETA ** (-2.0 * index / ROTARY_ENTRIES)
    freq = jnp.broadcast_to(freq[:, None], (ROTARY_ENTRIES // 2, TILE))
    window_arrays = small_call(
        window_kernel,
        "window",
        [
            jax.ShapeDtypeStruct((HEAD_WIDTH, window), bf16),
            jax.ShapeDtypeStruct((window, HEAD_WIDTH), bf16),
            jax.ShapeDtypeStruct((1, window), f32),
            jax.ShapeDtypeStruct((rows, TILE), f32),
            jax.ShapeDtypeStruct((rows, TILE), f32),
        ],
        freq,
        own,
        *same,
        other,
    )
    kt, v_all, window_ids, cosine, sine = window_arrays
    window_arrays = (window_ids, cosine, sine, kt, v_all)
    attn_mixed = attention_half(0, window_arrays, attn_query, attn_gate)
    state, attn_mixed = lax.optimization_barrier((state, attn_mixed))
    for _ in range(hops - 1):
        (leaving,) = small_call(relay_kernel, "relay", [state_like], chip_map, chip_add, state)
        state = up_chip(leaving, ranks)
    attn_mixed = attention_half(1, window_arrays, attn_query, attn_gate, attn_mixed)
    state, attn_mixed = lax.optimization_barrier((state, attn_mixed))

    final_like = jax.ShapeDtypeStruct((tall - BLOCK, DV), bf16)
    keep_state, pass_state = small_call(
        arrive_kernel, "arrive", [final_like] * 2, keep_half, keep_ma, other_ma, state, scalars=1
    )
    give_state = swap_cores(pass_state, ranks)

    gain = norm_gain.reshape(1, DV)
    delta_mixed = delta_out(keep_half, keep_reach, keep_inner, keep_state, delta_gate, gain)
    delta_mixed = delta_out(
        give_half, give_reach, give_inner, give_state, delta_gate, gain, delta_mixed
    )
    return (attn_mixed, delta_mixed)


def solution(mesh):
    rows = P(("dp", "ctx"))
    wide = P(("dp", "ctx"), None)
    return jax.shard_map(
        per_device,
        mesh=mesh,
        in_specs=(rows,) + (wide,) * 10 + (P(),),
        out_specs=(wide, wide),
        check_vma=False,
    )
```

```python
from functools import partial

import jax
import jax.numpy as jnp
from jax import lax
from jax.experimental import pallas as pl
from jax.experimental.pallas import tpu as pltpu
from jax.sharding import PartitionSpec as P

HEAD_WIDTH = 256
ROTARY_ENTRIES = 64
DK = 128
DV = 128
DOCS = 8
ROPE_THETA = 10000000.0
LOG2E = 1.4426950408889634
MASKED = -1e30
EPS = 1e-6
TILE = 128
MIB = 1024 * 1024

f32 = jnp.float32
bf16 = jnp.bfloat16


def dot(a, b, precision=None):
    return jnp.dot(a, b, preferred_element_type=f32, precision=precision)


def params(mib=16):
    return pltpu.CompilerParams(vmem_limit_bytes=mib * MIB)


def sigmoid(x):
    return 0.5 * jnp.tanh(0.5 * x) + 0.5


def cost(flops, nbytes, exps=0):
    return pl.CostEstimate(flops=flops, bytes_accessed=nbytes, transcendentals=exps)


BLOCK = 16
MERGES = 3
STRIP = 32
FINE = 16
DONE = object()


def odd_rows(m, b):
    return jnp.concatenate([m[i + b : i + 2 * b] for i in range(0, TILE, 2 * b)], axis=0)


def interleave(even, odd, b):
    parts = []
    for i in range(0, TILE // 2, b):
        parts += [even[i : i + b], odd[i : i + b]]
    return jnp.concatenate(parts, axis=0)


def even_rows(m, b):
    return jnp.concatenate([m[i : i + b] for i in range(0, TILE, 2 * b)], axis=0)


def block_inverses(mats):
    row = lax.broadcasted_iota(jnp.int32, (BLOCK, TILE), 0)
    lane = lax.broadcasted_iota(jnp.int32, (BLOCK, TILE), 1)
    within = lax.rem(lane, BLOCK)
    group = lane // BLOCK
    folded = []
    for m in mats:
        z = jnp.where(group == 0, m[:BLOCK], 0.0)
        for r in range(1, TILE // BLOCK):
            z = jnp.where(group == r, m[r * BLOCK : (r + 1) * BLOCK], z)
        folded.append(jnp.where(row > within, z, 0.0))
    xs = [jnp.where(row == within, 1.0, 0.0)] * len(mats)
    small = 8
    for k in range(BLOCK - 1):
        low = 0 if k < small - 1 else small
        at = (group * BLOCK + k)[low:]
        for i, z in enumerate(folded):
            spread = jnp.take_along_axis(z[low:], at, axis=1, mode="promise_in_bounds")
            x = xs[i]
            new = x[low:] + spread * x[k : k + 1]
            xs[i] = new if low == 0 else jnp.concatenate([x[:low], new], axis=0)
    out = []
    for x in xs:
        x = jnp.where(row > within, x, 0.0)
        out.append(
            jnp.concatenate(
                [jnp.where(group == r, x, 0.0) for r in range(TILE // BLOCK)], axis=0
            ).astype(bf16)
        )
    return out


def setup(half_ref, seg_ref, decay_ref, n, mask_ref, crow_ref, ccol_ref, first_ref, beta_ref=None):
    rows = seg_ref.shape[1]
    seg_row = seg_ref[...].astype(f32) + 1.0
    seg_col = jnp.transpose(jnp.broadcast_to(seg_row, (TILE, rows)))
    seg_cols = jnp.concatenate([seg_col] * (rows // TILE), axis=1)
    r = lax.broadcasted_iota(jnp.int32, (rows, rows), 0)
    c = lax.broadcasted_iota(jnp.int32, (rows, rows), 1)
    mask_ref[...] = jnp.where((seg_cols == seg_row) & (r >= c), 0.0, MASKED)
    first_ref[...] = jnp.where(seg_col == seg_row[:, :1], 1.0, 0.0)
    base = pl.multiple_of(half_ref[0] * n, n)
    decay = decay_ref[pl.ds(base, n), :] * LOG2E
    high = decay.astype(bf16)
    rest = decay - high.astype(f32)
    middle = rest.astype(bf16)
    parts = [high, middle, (rest - middle.astype(f32)).astype(bf16)]
    parts = jnp.concatenate([p.astype(f32) for p in parts], axis=0).astype(bf16)
    sums = dot(parts, jnp.where(r <= c, 1.0, 0.0).astype(bf16))
    cumulative = sums[:n] + sums[n : 2 * n] + sums[2 * n :]
    crow_ref[...] = cumulative
    beta = jnp.zeros((n, rows), f32) if beta_ref is None else beta_ref[pl.ds(base, n), :]
    fill = jnp.zeros((TILE - 2 * n, rows), f32)
    ccol_ref[...] = jnp.transpose(jnp.concatenate([cumulative, beta, fill], axis=0))
    return seg_row


def column(ref, at, lane, width):
    one = jnp.broadcast_to(ref[at, lane : lane + 1], (STRIP, TILE))
    return one if width == TILE else jnp.concatenate([one] * (width // TILE), axis=1)


def pipeline(phases, count):
    for slot in range(count + len(phases) - 1):
        running = [
            phase(slot - i) for i, phase in enumerate(phases) if 0 <= slot - i < count
        ]
        while running:
            running = [p for p in running if next(p, DONE) is not DONE]


def delta_local_kernel(
    half_ref,
    seg_ref,
    k_ref,
    v_ref,
    beta_ref,
    decay_ref,
    map_add_ref,
    solved_ref,
    mask_ref,
    level_ref,
    crow_ref,
    ccol_ref,
    first_ref,
):
    rows = k_ref.shape[0]
    n = v_ref.shape[1] // DV
    seg_row = setup(
        half_ref, seg_ref, decay_ref, n, mask_ref, crow_ref, ccol_ref, first_ref, beta_ref
    )
    map_add_ref[n * DK :, :] = jnp.broadcast_to(seg_row, (BLOCK, rows)).astype(bf16)
    r = lax.broadcasted_iota(jnp.int32, (TILE, TILE), 0)
    c = lax.broadcasted_iota(jnp.int32, (TILE, TILE), 1)
    eye = jnp.where(r == c, 1.0, 0.0)
    for level in range(MERGES):
        b = BLOCK << level
        sibling = jnp.where(r // b == c // b + 1, 1.0, 0.0)
        level_ref[level] = odd_rows(sibling, b).astype(bf16)
    strips = [slice(i, i + STRIP) for i in range(0, rows, STRIP)]
    pairs = [
        [dict(h=2 * kk + j, d=[], right=[]) for j in range(2)] for kk in range(n // 2)
    ]

    def elementwise(kk):
        pair = pairs[kk]
        k_raw = k_ref[:, kk * DK : (kk + 1) * DK]
        kt = jnp.transpose(k_raw.astype(f32))
        rk_row = lax.rsqrt(jnp.sum(kt * kt, axis=0, keepdims=True) + EPS)
        ktb = kt.astype(bf16)
        upper = dot(k_raw[:TILE], ktb[:, :TILE])
        lower = dot(k_raw[TILE:], ktb)
        yield
        for at in strips:
            raw, start = (upper, at.start) if at.start < TILE else (lower, at.start - TILE)
            width = raw.shape[1]
            kf = k_raw[at].astype(f32)
            rk = lax.rsqrt(jnp.sum(kf * kf, axis=1, keepdims=True) + EPS)
            kn = kf * rk
            gram = raw[start : start + STRIP] * rk_row[:, :width] * -rk
            for w in pair:
                h = w["h"]
                cc = column(ccol_ref, at, h, width)
                bt = column(ccol_ref, at, n + h, width)
                span = jnp.exp2(cc - crow_ref[h : h + 1, :width] + mask_ref[at, :width])
                w["d"].append(span * bt * gram)
                cc, bt = cc[:, :TILE], bt[:, :TILE]
                entry = jnp.exp2(cc) * first_ref[at]
                value = v_ref[at, h * DV : (h + 1) * DV].astype(f32)
                w["right"].append(
                    jnp.concatenate([bt * entry * kn, bt * value], axis=1).astype(bf16)
                )
                if at.stop == rows:
                    w["last"] = entry[STRIP - 1 :]
                    w["kd"] = (kt * (rk_row * span[STRIP - 1 :])).astype(bf16)
            yield
        top = TILE // STRIP
        for w in pair:
            d11 = jnp.concatenate(w["d"][:top], axis=0)
            d2 = jnp.concatenate(w["d"][top:], axis=0)
            w["d"] = [d11, d2[:, TILE:]]
            w["d21"] = d2[:, :TILE].astype(bf16)
            w["right"] = jnp.concatenate(w["right"], axis=0)
        yield

    def invert(kk):
        pair = pairs[kk]
        mats = [m for w in pair for m in w["d"]]
        inverses = block_inverses(mats)
        yield
        mats = [m.astype(bf16) for m in mats]
        zeros = jnp.zeros((TILE // 2, TILE), bf16)
        for level in range(MERGES):
            b = BLOCK << level
            keep = level_ref[level]
            picked = [odd_rows(m, b) * keep for m in mats]
            ys = [(p.astype(f32) + dot(p, x)).astype(bf16) for p, x in zip(picked, inverses)]
            yield
            odds = [odd_rows(x, b) for x in inverses]
            odds = [
                x + (y.astype(f32) + dot(x, interleave(zeros, y, b))).astype(bf16)
                for x, y in zip(odds, ys)
            ]
            inverses = [interleave(even_rows(x, b), o, b) for x, o in zip(inverses, odds)]
            yield
        for i, w in enumerate(pair):
            w["x"] = inverses[2 * i : 2 * i + 2]

    def finish(kk):
        pair = pairs[kk]
        for w in pair:
            w["u1"] = add_strips(w["right"][:TILE], dot(w["x"][0], w["right"][:TILE]))
        yield
        for w in pair:
            w["r2"] = add_strips(w["right"][TILE:], dot(w["d21"], w["u1"]))
        yield
        for w in pair:
            u2 = add_strips(w["r2"], dot(w["x"][1], w["r2"]))
            w["u"] = jnp.concatenate([w["u1"], u2], axis=0)
            solved_ref[w["h"] * rows : (w["h"] + 1) * rows, :] = w["u"]
        yield
        for w in pair:
            h = w["h"]
            ma = dot(w["kd"], w["u"])
            for start in range(0, DK, STRIP):
                part = ma[start : start + STRIP]
                kept = w["last"] * eye[start : start + STRIP]
                map_add_ref[h * DK + start : h * DK + start + STRIP, :] = jnp.concatenate(
                    [kept - part[:, :DK], part[:, DK:]], axis=1
                ).astype(bf16)
            yield

    pipeline([elementwise, invert, finish], n // 2)


def add_strips(a, b):
    return jnp.concatenate(
        [
            (a[i : i + STRIP].astype(f32) + b[i : i + STRIP]).astype(bf16)
            for i in range(0, a.shape[0], STRIP)
        ],
        axis=0,
    )


def delta_reach_kernel(
    half_ref,
    seg_ref,
    q_ref,
    k_ref,
    decay_ref,
    solved_ref,
    reach_ref,
    inner_ref,
    mask_ref,
    crow_ref,
    ccol_ref,
    first_ref,
):
    rows = k_ref.shape[0]
    n = reach_ref.shape[1] // DK
    setup(half_ref, seg_ref, decay_ref, n, mask_ref, crow_ref, ccol_ref, first_ref)
    strips = [slice(i, i + STRIP) for i in range(0, rows, STRIP)]
    pairs = [
        [dict(h=2 * kk + j, p=[], scaled=[]) for j in range(2)] for kk in range(n // 2)
    ]

    def elementwise(kk):
        pair = pairs[kk]
        cols = slice(kk * DK, (kk + 1) * DK)
        k_raw = k_ref[:, cols]
        q_raw = q_ref[:, cols]
        kt = jnp.transpose(k_raw.astype(f32))
        rk_row = lax.rsqrt(jnp.sum(kt * kt, axis=0, keepdims=True) + EPS)
        ktb = kt.astype(bf16)
        upper = dot(q_raw[:TILE], ktb[:, :TILE])
        lower = dot(q_raw[TILE:], ktb)
        yield
        for at in strips:
            raw, start = (upper, at.start) if at.start < TILE else (lower, at.start - TILE)
            width = raw.shape[1]
            qf = q_raw[at].astype(f32)
            rq = lax.rsqrt(jnp.sum(qf * qf, axis=1, keepdims=True) + EPS) * DK**-0.5
            qn = qf * rq
            probe = raw[start : start + STRIP] * rk_row[:, :width] * rq
            for w in pair:
                h = w["h"]
                cc = column(ccol_ref, at, h, width)
                span = jnp.exp2(cc - crow_ref[h : h + 1, :width] + mask_ref[at, :width])
                w["p"].append((span * probe).astype(bf16))
                entry = jnp.exp2(cc[:, :TILE]) * first_ref[at]
                w["scaled"].append((entry * qn).astype(bf16))
            yield

    def finish(kk):
        top = TILE // STRIP
        for w in pairs[kk]:
            h = w["h"]
            u = solved_ref[h * rows : (h + 1) * rows, :]
            upper = dot(jnp.concatenate(w["p"][:top], axis=0), u[:TILE])
            lower = dot(jnp.concatenate(w["p"][top:], axis=0), u)
            for at, scaled in zip(strips, w["scaled"]):
                pu = upper[at.start :] if at.start < TILE else lower[at.start - TILE :]
                pu = pu[:STRIP]
                reach_ref[at, h * DK : (h + 1) * DK] = (
                    scaled.astype(f32) - pu[:, :DK]
                ).astype(bf16)
                inner_ref[at, h * DV : (h + 1) * DV] = pu[:, DK:]
            yield

    pipeline([elementwise, finish], n // 2)


def half_call(kernel, name, mib, half, operands, outs, scratch):
    def at_half(i, s):
        return (0, s[0])

    def at_zero(i, s):
        return (0, 0)

    specs = []
    args = []
    for a in operands:
        if isinstance(a, tuple):
            (a,) = a
            specs.append(pl.BlockSpec((a.shape[0], a.shape[1] // 2), at_half))
        else:
            specs.append(pl.BlockSpec(a.shape, at_zero))
        args.append(a)
    return pl.pallas_call(
        kernel,
        grid_spec=pltpu.PrefetchScalarGridSpec(
            num_scalar_prefetch=1,
            grid=(1,),
            in_specs=specs,
            out_specs=[pl.BlockSpec(o.shape, at_zero) for o in outs],
            scratch_shapes=scratch,
        ),
        out_shape=outs,
        compiler_params=params(mib),
        cost_estimate=cost(4 * 10**9, 3 * 2**20),
        name=name,
    )(half, *args)


def setup_scratch(rows, n):
    return [
        pltpu.VMEM((rows, rows), f32),
        pltpu.VMEM((n, rows), f32),
        pltpu.VMEM((rows, TILE), f32),
        pltpu.VMEM((rows, TILE), f32),
    ]


def delta_local(half, mib, seg_row, key, value, beta, decay):
    rows = key.shape[0]
    n = value.shape[1] // DV // 2
    mask, *others = setup_scratch(rows, n)
    return half_call(
        delta_local_kernel,
        "delta_local",
        mib,
        half,
        [seg_row, (key,), (value,), beta, decay],
        [
            jax.ShapeDtypeStruct((n * DK + BLOCK, DK + DV), bf16),
            jax.ShapeDtypeStruct((n * rows, DK + DV), bf16),
        ],
        [mask, pltpu.VMEM((MERGES, TILE // 2, TILE), bf16), *others],
    )


def delta_reach(half, seg_row, query, key, decay, solved):
    rows = key.shape[0]
    n = solved.shape[0] // rows
    return half_call(
        delta_reach_kernel,
        "delta_reach",
        20,
        half,
        [seg_row, (query,), (key,), decay, solved],
        [
            jax.ShapeDtypeStruct((rows, n * DK), bf16),
            jax.ShapeDtypeStruct((rows, n * DV), f32),
        ],
        setup_scratch(rows, n),
    )


def ids_of(ref):
    end = ref.shape[0] - BLOCK
    return ref[end : end + BLOCK, :].astype(f32)[:1]


def put_id(ref, value):
    end = ref.shape[0] - BLOCK
    ref[end:, :] = jnp.broadcast_to(value, (BLOCK, ref.shape[1])).astype(bf16)


def matching(a, b):
    return jnp.where(a == b, 1.0, 0.0)


def compose_kernel(core_ref, mine_ref, other_ref, map_ref, add_ref):
    odd = core_ref[0] == 1
    mine_ids, other_ids = ids_of(mine_ref), ids_of(other_ref)
    early_ids = jnp.where(odd, other_ids, mine_ids)
    late_ids = jnp.where(odd, mine_ids, other_ids)
    across = matching(early_ids[:, -1:], late_ids[:, :1])
    put_id(map_ref, early_ids[:, :1])
    put_id(add_ref, late_ids[:, -1:])
    for h in range(mine_ref.shape[0] // DK):
        at = slice(h * DK, (h + 1) * DK)
        mine, other = mine_ref[at], other_ref[at]
        early, late = jnp.where(odd, other, mine), jnp.where(odd, mine, other)
        both = dot(late[:, :DK], early) * across
        map_ref[at] = both[:, :DK].astype(bf16)
        add_ref[at] = (both[:, DK:] + late[:, DK:].astype(f32)).astype(bf16)


def relay_kernel(map_ref, add_ref, state_ref, out_ref):
    into = matching(ids_of(state_ref), ids_of(map_ref))
    put_id(out_ref, ids_of(add_ref))
    for h in range(map_ref.shape[0] // DK):
        at = slice(h * DK, (h + 1) * DK)
        out_ref[at] = (dot(map_ref[at], state_ref[at]) * into + add_ref[at].astype(f32)).astype(bf16)


def arrive_kernel(core_ref, mine_ref, other_ref, state_ref, keep_ref, give_ref):
    odd = core_ref[0] == 1
    mine_ids, other_ids = ids_of(mine_ref), ids_of(other_ref)
    early_ids = jnp.where(odd, other_ids, mine_ids)
    late_ids = jnp.where(odd, mine_ids, other_ids)
    across = matching(early_ids[:, -1:], late_ids[:, :1])
    into = matching(ids_of(state_ref), early_ids[:, :1])
    for h in range(keep_ref.shape[0] // DK):
        at = slice(h * DK, (h + 1) * DK)
        early = jnp.where(odd, other_ref[at], mine_ref[at])
        first = (state_ref[at].astype(f32) * into).astype(bf16)
        second = (
            (dot(early[:, :DK], first) + early[:, DK:].astype(f32)) * across
        ).astype(bf16)
        keep_ref[at] = jnp.where(odd, second, first)
        give_ref[at] = jnp.where(odd, first, second)


SMEM = pl.BlockSpec(memory_space=pltpu.SMEM)
VMEM = pl.BlockSpec(memory_space=pltpu.VMEM)


def small_call(kernel, name, outs, *args, scalars=0, mib=16):
    return pl.pallas_call(
        kernel,
        in_specs=[SMEM] * scalars + [VMEM] * (len(args) - scalars),
        out_specs=[VMEM] * len(outs),
        out_shape=outs,
        compiler_params=params(mib),
        cost_estimate=cost(10**8, 2**20),
        name=name,
    )(*args)


def delta_out_kernel(half_ref, reach_ref, inner_ref, state_ref, gate_ref, gain_ref, *rest):
    out_ref = rest[-1]
    gain = gain_ref[...]
    for h in range(state_ref.shape[0] // DK):
        cols = slice(h * DV, (h + 1) * DV)
        state = state_ref[h * DK : (h + 1) * DK]
        carried = dot(reach_ref[:, cols], state)
        for i in range(0, carried.shape[0], STRIP):
            at = slice(i, i + STRIP)
            out = inner_ref[at, cols].astype(f32) + carried[at]
            spread = lax.rsqrt(jnp.mean(out * out, axis=1, keepdims=True) + EPS)
            gate = gate_ref[at, cols].astype(f32)
            gate = gate * sigmoid(gate)
            out_ref[at, cols] = (out * spread * gain * gate).astype(bf16)


def delta_out(half, reach, inner, state, gate, gain, partial_out=None):
    rows = reach.shape[0]
    n = state.shape[0] // DK
    heads = 4
    steps = n // heads

    def at_half(i, s):
        return (0, s[0] * steps + i)

    in_specs = [
        pl.BlockSpec((rows, heads * DK), lambda i, s: (0, i)),
        pl.BlockSpec((rows, heads * DV), lambda i, s: (0, i)),
        pl.BlockSpec((heads * DK, DV), lambda i, s: (i, 0)),
        pl.BlockSpec((rows, heads * DV), at_half),
        pl.BlockSpec((1, DV), lambda i, s: (0, 0)),
    ]
    args = [half, reach, inner, state, gate, gain]
    aliases = {}
    if partial_out is not None:
        in_specs.append(pl.BlockSpec(memory_space=pl.ANY))
        args.append(partial_out)
        aliases = {6: 0}
    return pl.pallas_call(
        delta_out_kernel,
        grid_spec=pltpu.PrefetchScalarGridSpec(
            num_scalar_prefetch=1,
            grid=(steps,),
            in_specs=in_specs,
            out_specs=pl.BlockSpec((rows, heads * DV), at_half),
        ),
        out_shape=jax.ShapeDtypeStruct(gate.shape, bf16),
        input_output_aliases=aliases,
        compiler_params=params(),
        cost_estimate=cost(10**8, 3 * 2**20),
        name="delta_out",
    )(*args)


def blocks_of(pieces):
    own, *same, other = pieces
    order = [(own, None)]
    for i, ref in enumerate(same):
        order += [(other, i), (ref, None)]
    return order[::-1]


def pack_kernel(seg_ref, key_ref, value_ref, out_ref):
    rows = key_ref.shape[0]
    ids = seg_ref[...].astype(f32) + 1.0
    out_ref[:rows, :HEAD_WIDTH] = key_ref[...]
    out_ref[:rows, HEAD_WIDTH:] = value_ref[...]
    out_ref[rows:, :rows] = jnp.broadcast_to(ids, (BLOCK, rows)).astype(bf16)
    out_ref[rows:, rows:] = jnp.zeros((BLOCK, 2 * HEAD_WIDTH - rows), bf16)


def window_kernel(freq_ref, *rest):
    *pieces, kt_ref, v_ref, ids_ref, cos_ref, sin_ref = rest
    rows = cos_ref.shape[0]
    window = ids_ref.shape[1]
    half = ROTARY_ENTRIES // 2
    blocks = [ref if index is None else ref.at[index] for ref, index in blocks_of(pieces)]
    row_ids = jnp.concatenate(
        [ref[rows : rows + BLOCK, :rows].astype(f32)[:1] for ref in blocks], axis=1
    )
    ids_ref[...] = row_ids
    ids = jnp.broadcast_to(row_ids, (DOCS, window))
    docs = lax.broadcasted_iota(jnp.int32, (DOCS, window), 0).astype(f32) + 1.0
    before = jnp.sum(jnp.where(ids < docs, 1.0, 0.0), axis=1, keepdims=True)
    start = jnp.sum(jnp.where(ids == docs, before, 0.0), axis=0, keepdims=True)
    place = lax.broadcasted_iota(jnp.int32, (1, window), 1).astype(f32)
    angle = freq_ref[:, :1] * (place - start)
    cosine = jnp.cos(angle)
    sine = jnp.sin(angle)
    for b, ref in enumerate(blocks):
        cols = slice(b * rows, (b + 1) * rows)
        kt = jnp.transpose(ref[:rows, :HEAD_WIDTH].astype(f32))
        one, two = kt[:half], kt[half:ROTARY_ENTRIES]
        cb, sb = cosine[:, cols], sine[:, cols]
        kt_ref[:half, cols] = (one * cb - two * sb).astype(bf16)
        kt_ref[half:ROTARY_ENTRIES, cols] = (two * cb + one * sb).astype(bf16)
        kt_ref[ROTARY_ENTRIES:, cols] = kt[ROTARY_ENTRIES:].astype(bf16)
        v_ref[cols, :] = ref[:rows, HEAD_WIDTH:]
    cq, sq = cosine[:, window - rows :], sine[:, window - rows :]
    rest_rows = TILE - ROTARY_ENTRIES
    cos_ref[...] = jnp.transpose(
        jnp.concatenate([cq, cq, jnp.ones((rest_rows, rows), f32)], axis=0)
    )
    sin_ref[...] = jnp.transpose(
        jnp.concatenate([-sq, sq, jnp.zeros((rest_rows, rows), f32)], axis=0)
    )


def attention_kernel(ids_ref, cos_ref, sin_ref, kt_ref, v_ref, q_ref, gate_ref, *rest):
    out_ref, mask_ref = rest[-2:]
    rows = q_ref.shape[0]
    window = ids_ref.shape[1]
    half = ROTARY_ENTRIES // 2

    @pl.when(pl.program_id(0) == 0)
    def _():
        own = ids_ref[:, window - rows :]
        own_col = jnp.transpose(jnp.broadcast_to(own, (TILE, rows)))
        own_cols = jnp.concatenate([own_col] * (window // TILE), axis=1)
        r = lax.broadcasted_iota(jnp.int32, (rows, window), 0) + (window - rows)
        c = lax.broadcasted_iota(jnp.int32, (rows, window), 1)
        mask_ref[...] = jnp.where((own_cols == ids_ref[...]) & (c <= r), 0.0, MASKED)

    scaling = HEAD_WIDTH**-0.5
    lane = lax.broadcasted_iota(jnp.int32, (TILE, TILE), 1)
    reach = window - rows + TILE
    heads = q_ref.shape[1] // HEAD_WIDTH
    for first in range(0, rows, TILE):
        at = slice(first, first + TILE)
        keys = slice(first, first + reach)
        queries = []
        for h in range(heads):
            base = h * HEAD_WIDTH
            x = q_ref[at, base : base + TILE].astype(f32)
            swapped = jnp.where(
                lane < half, pltpu.roll(x, TILE - half, 1), pltpu.roll(x, half, 1)
            )
            rotated = ((x * cos_ref[at] + swapped * sin_ref[at]) * scaling).astype(bf16)
            tail = q_ref[at, base + TILE : base + HEAD_WIDTH] * jnp.asarray(scaling, bf16)
            queries.append(jnp.concatenate([rotated, tail], axis=1))
        scores = dot(jnp.concatenate(queries, axis=0), kt_ref[:, keys])
        weights = []
        totals = []
        for i in range(0, heads * TILE, FINE):
            row = first + i % TILE
            strip = scores[i : i + FINE] + mask_ref[row : row + FINE, keys]
            strip = jnp.exp(strip - jnp.max(strip, axis=1, keepdims=True))
            totals.append(1.0 / jnp.sum(strip, axis=1, keepdims=True))
            weights.append(strip.astype(bf16))
        mixed = dot(jnp.concatenate(weights, axis=0), v_ref[keys, :])
        for i, inverse in zip(range(0, heads * TILE, FINE), totals):
            rows_at = slice(first + i % TILE, first + i % TILE + FINE)
            cols = slice(i // TILE * HEAD_WIDTH, (i // TILE + 1) * HEAD_WIDTH)
            gate = sigmoid(gate_ref[rows_at, cols].astype(f32))
            out_ref[rows_at, cols] = (mixed[i : i + FINE] * inverse * gate).astype(bf16)


def attention_half(part, window_arrays, query, gate, partial_out=None):
    rows = query.shape[0]
    window = window_arrays[0].shape[1]
    heads = 4
    width = heads * HEAD_WIDTH
    steps = query.shape[1] // width // 2

    def at_part(i):
        return (0, part * steps + i)

    in_specs = [pl.BlockSpec(a.shape, lambda i: (0, 0)) for a in window_arrays]
    in_specs += [pl.BlockSpec((rows, width), at_part)] * 2
    args = [*window_arrays, query, gate]
    aliases = {}
    if partial_out is not None:
        aliases = {len(args): 0}
        in_specs.append(pl.BlockSpec(memory_space=pl.ANY))
        args.append(partial_out)
    return pl.pallas_call(
        attention_kernel,
        grid=(steps,),
        in_specs=in_specs,
        out_specs=pl.BlockSpec((rows, width), at_part),
        out_shape=jax.ShapeDtypeStruct(query.shape, bf16),
        scratch_shapes=[pltpu.VMEM((rows, window), f32)],
        input_output_aliases=aliases,
        compiler_params=params(28),
        cost_estimate=cost(5 * 10**9, 3 * 2**20, 10**6),
        name="attention",
    )(*args)


def up_chip(value, ranks):
    return lax.ppermute(value, "ctx", [(i, i + 2) for i in range(ranks - 2)])


def swap_cores(value, ranks):
    return lax.ppermute(value, "ctx", [(i, i ^ 1) for i in range(ranks)])


def per_device(
    segment_ids,
    attn_query,
    attention_keys,
    attention_values,
    attn_gate,
    delta_query,
    delta_key,
    update_rule_payload,
    delta_beta,
    delta_decay,
    delta_gate,
    norm_gain,
):
    ranks = lax.axis_size("ctx")
    rank = lax.axis_index("ctx")
    rows = segment_ids.shape[0]
    hops = ranks // 4
    core = rank % 2
    odd = core == 1

    ids = segment_ids.reshape(1, rows)

    (own,) = small_call(
        pack_kernel,
        "pack",
        [jax.ShapeDtypeStruct((rows + BLOCK, 2 * HEAD_WIDTH), bf16)],
        ids,
        attention_keys,
        attention_values,
        mib=60,
    )
    nearest = up_chip(own, ranks)

    keep_half = core.reshape(1).astype(jnp.int32)
    give_half = 1 - keep_half
    decay_rows = delta_decay.T
    local = partial(
        delta_local,
        seg_row=ids,
        key=delta_key,
        value=update_rule_payload,
        beta=delta_beta.T,
        decay=decay_rows,
    )
    reach = partial(
        delta_reach, seg_row=ids, query=delta_query, key=delta_key, decay=decay_rows
    )
    give_ma, give_solved = local(give_half, 60)
    other_ma = swap_cores(give_ma, ranks)
    nearest, give_ma = lax.optimization_barrier((nearest, give_ma))
    same = [nearest]
    for _ in range(hops - 1):
        same.append(up_chip(same[-1], ranks))
    keep_ma, keep_solved = local(keep_half, 60)
    same, keep_ma, other_ma = lax.optimization_barrier((same, keep_ma, other_ma))
    chain = [own, *same]
    other = swap_cores(
        jnp.stack([jnp.where(odd, chain[i + 1], chain[i]) for i in range(hops)]), ranks
    )

    tall = keep_ma.shape[0]
    state_like = jax.ShapeDtypeStruct((tall, DV), bf16)
    chip_map, chip_add = small_call(
        compose_kernel, "compose", [state_like] * 2, keep_half, keep_ma, other_ma, scalars=1
    )
    state = up_chip(chip_add, ranks)

    window = (2 * hops + 1) * rows
    index = jnp.arange(ROTARY_ENTRIES // 2).astype(f32)
    freq = ROPE_THETA ** (-2.0 * index / ROTARY_ENTRIES)
    freq = jnp.broadcast_to(freq[:, None], (ROTARY_ENTRIES // 2, TILE))
    window_arrays = small_call(
        window_kernel,
        "window",
        [
            jax.ShapeDtypeStruct((HEAD_WIDTH, window), bf16),
            jax.ShapeDtypeStruct((window, HEAD_WIDTH), bf16),
            jax.ShapeDtypeStruct((1, window), f32),
            jax.ShapeDtypeStruct((rows, TILE), f32),
            jax.ShapeDtypeStruct((rows, TILE), f32),
        ],
        freq,
        own,
        *same,
        other,
    )
    kt, v_all, window_ids, cosine, sine = window_arrays
    window_arrays = (window_ids, cosine, sine, kt, v_all)
    attn_mixed = attention_half(0, window_arrays, attn_query, attn_gate)
    give_solved, chip_add = lax.optimization_barrier((give_solved, chip_add))
    give_rows = reach(give_half, solved=give_solved)
    state, attn_mixed, give_rows = lax.optimization_barrier((state, attn_mixed, give_rows))
    leaving = chip_add
    for _ in range(hops - 1):
        (leaving,) = small_call(relay_kernel, "relay", [state_like], chip_map, chip_add, state)
        state = up_chip(leaving, ranks)
    attn_mixed = attention_half(1, window_arrays, attn_query, attn_gate, attn_mixed)
    keep_solved, leaving = lax.optimization_barrier((keep_solved, leaving))
    keep_rows = reach(keep_half, solved=keep_solved)
    state, attn_mixed, keep_rows = lax.optimization_barrier((state, attn_mixed, keep_rows))

    final_like = jax.ShapeDtypeStruct((tall - BLOCK, DV), bf16)
    keep_state, pass_state = small_call(
        arrive_kernel, "arrive", [final_like] * 2, keep_half, keep_ma, other_ma, state, scalars=1
    )
    give_state = swap_cores(pass_state, ranks)

    gain = norm_gain.reshape(1, DV)
    delta_mixed = delta_out(keep_half, *keep_rows, keep_state, delta_gate, gain)
    delta_mixed = delta_out(
        give_half, *give_rows, give_state, delta_gate, gain, delta_mixed
    )
    return (attn_mixed, delta_mixed)


def solution(mesh):
    rows = P(("dp", "ctx"))
    wide = P(("dp", "ctx"), None)
    return jax.shard_map(
        per_device,
        mesh=mesh,
        in_specs=(rows,) + (wide,) * 10 + (P(),),
        out_specs=(wide, wide),
        check_vma=False,
    )
```

```python
from functools import partial

import jax
import jax.numpy as jnp
from jax import lax
from jax.experimental import pallas as pl
from jax.experimental.pallas import tpu as pltpu
from jax.sharding import PartitionSpec as P

HEAD_WIDTH = 256
ROTARY_ENTRIES = 64
DK = 128
DV = 128
DOCS = 8
ROPE_THETA = 10000000.0
LOG2E = 1.4426950408889634
MASKED = -1e30
EPS = 1e-6
TILE = 128
MIB = 1024 * 1024

f32 = jnp.float32
bf16 = jnp.bfloat16


def dot(a, b, precision=None):
    return jnp.dot(a, b, preferred_element_type=f32, precision=precision)


def params(mib=16):
    return pltpu.CompilerParams(vmem_limit_bytes=mib * MIB)


def sigmoid(x):
    return 0.5 * jnp.tanh(0.5 * x) + 0.5


def cost(flops, nbytes, exps=0):
    return pl.CostEstimate(flops=flops, bytes_accessed=nbytes, transcendentals=exps)


BLOCK = 16
MERGES = 3
STRIP = 32
FINE = 16
DONE = object()


def odd_rows(m, b):
    return jnp.concatenate([m[i + b : i + 2 * b] for i in range(0, TILE, 2 * b)], axis=0)


def interleave(even, odd, b):
    parts = []
    for i in range(0, TILE // 2, b):
        parts += [even[i : i + b], odd[i : i + b]]
    return jnp.concatenate(parts, axis=0)


def even_rows(m, b):
    return jnp.concatenate([m[i : i + b] for i in range(0, TILE, 2 * b)], axis=0)


def fold(m):
    row = lax.broadcasted_iota(jnp.int32, (BLOCK, TILE), 0)
    lane = lax.broadcasted_iota(jnp.int32, (BLOCK, TILE), 1)
    group = lane // BLOCK
    z = jnp.where(group == 0, m[:BLOCK], 0.0)
    for r in range(1, TILE // BLOCK):
        z = jnp.where(group == r, m[r * BLOCK : (r + 1) * BLOCK], z)
    return jnp.where(row > lax.rem(lane, BLOCK), z, 0.0).astype(bf16)


def fill_spread(spread_ref):
    row = lax.broadcasted_iota(jnp.int32, (TILE, TILE), 0)
    lane = lax.broadcasted_iota(jnp.int32, (TILE, TILE), 1)
    base = row - lane // BLOCK * BLOCK
    for k in range(BLOCK - 1):
        spread_ref[:, k * TILE : (k + 1) * TILE] = jnp.where(base == k, 1.0, 0.0).astype(bf16)


def block_inverses(folded, spread_ref):
    row = lax.broadcasted_iota(jnp.int32, (BLOCK, TILE), 0)
    lane = lax.broadcasted_iota(jnp.int32, (BLOCK, TILE), 1)
    group = lane // BLOCK
    within = lax.rem(lane, BLOCK)
    spread = dot(jnp.concatenate(folded, axis=0), spread_ref[...])
    unit = jnp.where(row == within, 1.0, 0.0)
    small = BLOCK // 2
    out = []
    tops = [unit[:small]] * len(folded)
    lows = [unit[small:]] * len(folded)
    for k in range(BLOCK - 1):
        at = slice(k * TILE, (k + 1) * TILE)
        for i in range(len(folded)):
            rows = spread[i * BLOCK : (i + 1) * BLOCK, at]
            source = tops[i][k : k + 1] if k < small else lows[i][k - small : k - small + 1]
            if k < small - 1:
                tops[i] = tops[i] + rows[:small] * source
            lows[i] = lows[i] + rows[small:] * source
    for top, low in zip(tops, lows):
        x = jnp.where(row > within, jnp.concatenate([top, low], axis=0), 0.0)
        out.append(
            jnp.concatenate(
                [jnp.where(group == r, x, 0.0) for r in range(TILE // BLOCK)], axis=0
            ).astype(bf16)
        )
    return out


def setup(half_ref, seg_ref, decay_ref, n, mask_ref, crow_ref, ccol_ref, first_ref, beta_ref=None):
    rows = seg_ref.shape[1]
    seg_row = seg_ref[...].astype(f32) + 1.0
    seg_col = jnp.transpose(jnp.broadcast_to(seg_row, (TILE, rows)))
    seg_cols = jnp.concatenate([seg_col] * (rows // TILE), axis=1)
    r = lax.broadcasted_iota(jnp.int32, (rows, rows), 0)
    c = lax.broadcasted_iota(jnp.int32, (rows, rows), 1)
    mask_ref[...] = jnp.where((seg_cols == seg_row) & (r >= c), 0.0, MASKED)
    first_ref[...] = jnp.where(seg_col == seg_row[:, :1], 1.0, 0.0)
    base = pl.multiple_of(half_ref[0] * n, n)
    decay = decay_ref[pl.ds(base, n), :] * LOG2E
    high = decay.astype(bf16)
    rest = decay - high.astype(f32)
    middle = rest.astype(bf16)
    parts = [high, middle, (rest - middle.astype(f32)).astype(bf16)]
    parts = jnp.concatenate([p.astype(f32) for p in parts], axis=0).astype(bf16)
    sums = dot(parts, jnp.where(r <= c, 1.0, 0.0).astype(bf16))
    cumulative = sums[:n] + sums[n : 2 * n] + sums[2 * n :]
    crow_ref[...] = cumulative
    beta = jnp.zeros((n, rows), f32) if beta_ref is None else beta_ref[pl.ds(base, n), :]
    fill = jnp.zeros((TILE - 2 * n, rows), f32)
    ccol_ref[...] = jnp.transpose(jnp.concatenate([cumulative, beta, fill], axis=0))
    return seg_row


def column(ref, at, lane, width):
    one = jnp.broadcast_to(ref[at, lane : lane + 1], (STRIP, TILE))
    return one if width == TILE else jnp.concatenate([one] * (width // TILE), axis=1)


def pipeline(phases, count):
    for slot in range(count + len(phases) - 1):
        running = [
            phase(slot - i) for i, phase in enumerate(phases) if 0 <= slot - i < count
        ]
        while running:
            running = [p for p in running if next(p, DONE) is not DONE]


def delta_local_kernel(
    half_ref,
    seg_ref,
    k_ref,
    v_ref,
    beta_ref,
    decay_ref,
    map_add_ref,
    solved_ref,
    mask_ref,
    level_ref,
    spread_ref,
    crow_ref,
    ccol_ref,
    first_ref,
):
    rows = k_ref.shape[0]
    n = v_ref.shape[1] // DV
    fill_spread(spread_ref)
    seg_row = setup(
        half_ref, seg_ref, decay_ref, n, mask_ref, crow_ref, ccol_ref, first_ref, beta_ref
    )
    map_add_ref[n * DK :, :] = jnp.broadcast_to(seg_row, (BLOCK, rows)).astype(bf16)
    r = lax.broadcasted_iota(jnp.int32, (TILE, TILE), 0)
    c = lax.broadcasted_iota(jnp.int32, (TILE, TILE), 1)
    eye = jnp.where(r == c, 1.0, 0.0)
    for level in range(MERGES):
        b = BLOCK << level
        sibling = jnp.where(r // b == c // b + 1, 1.0, 0.0)
        level_ref[level] = odd_rows(sibling, b).astype(bf16)
    strips = [slice(i, i + STRIP) for i in range(0, rows, STRIP)]
    pairs = [
        [dict(h=2 * kk + j, d=[], right=[]) for j in range(2)] for kk in range(n // 2)
    ]

    def elementwise(kk):
        pair = pairs[kk]
        k_raw = k_ref[:, kk * DK : (kk + 1) * DK]
        kt = jnp.transpose(k_raw.astype(f32))
        rk_row = lax.rsqrt(jnp.sum(kt * kt, axis=0, keepdims=True) + EPS)
        ktb = kt.astype(bf16)
        upper = dot(k_raw[:TILE], ktb[:, :TILE])
        lower = dot(k_raw[TILE:], ktb)
        yield
        for at in strips:
            raw, start = (upper, at.start) if at.start < TILE else (lower, at.start - TILE)
            width = raw.shape[1]
            kf = k_raw[at].astype(f32)
            rk = lax.rsqrt(jnp.sum(kf * kf, axis=1, keepdims=True) + EPS)
            kn = kf * rk
            gram = raw[start : start + STRIP] * rk_row[:, :width] * -rk
            for w in pair:
                h = w["h"]
                cc = column(ccol_ref, at, h, width)
                bt = column(ccol_ref, at, n + h, width)
                span = jnp.exp2(cc - crow_ref[h : h + 1, :width] + mask_ref[at, :width])
                w["d"].append(span * bt * gram)
                cc, bt = cc[:, :TILE], bt[:, :TILE]
                entry = jnp.exp2(cc) * first_ref[at]
                value = v_ref[at, h * DV : (h + 1) * DV].astype(f32)
                w["right"].append(
                    jnp.concatenate([bt * entry * kn, bt * value], axis=1).astype(bf16)
                )
                if at.stop == rows:
                    w["last"] = entry[STRIP - 1 :]
                    w["kd"] = (kt * (rk_row * span[STRIP - 1 :])).astype(bf16)
            yield
        top = TILE // STRIP
        for w in pair:
            d11 = jnp.concatenate(w["d"][:top], axis=0)
            d2 = jnp.concatenate(w["d"][top:], axis=0)
            blocks = [d11, d2[:, TILE:]]
            w["folded"] = [fold(m) for m in blocks]
            w["d"] = [m.astype(bf16) for m in blocks]
            w["d21"] = d2[:, :TILE].astype(bf16)
            w["right"] = jnp.concatenate(w["right"], axis=0)
        yield

    def invert():
        work = [w for pair in pairs for w in pair]
        mats = [m for w in work for m in w["d"]]
        inverses = block_inverses([z for w in work for z in w["folded"]], spread_ref)
        zeros = jnp.zeros((TILE // 2, TILE), bf16)
        for level in range(MERGES):
            b = BLOCK << level
            keep = level_ref[level]
            picked = [odd_rows(m, b) * keep for m in mats]
            ys = [(p.astype(f32) + dot(p, x)).astype(bf16) for p, x in zip(picked, inverses)]
            odds = [odd_rows(x, b) for x in inverses]
            odds = [
                x + (y.astype(f32) + dot(x, interleave(zeros, y, b))).astype(bf16)
                for x, y in zip(odds, ys)
            ]
            inverses = [interleave(even_rows(x, b), o, b) for x, o in zip(inverses, odds)]
        for i, w in enumerate(work):
            w["x"] = inverses[2 * i : 2 * i + 2]

    def finish(kk):
        pair = pairs[kk]
        for w in pair:
            w["u1"] = add_strips(w["right"][:TILE], dot(w["x"][0], w["right"][:TILE]))
        yield
        for w in pair:
            w["r2"] = add_strips(w["right"][TILE:], dot(w["d21"], w["u1"]))
        yield
        for w in pair:
            u2 = add_strips(w["r2"], dot(w["x"][1], w["r2"]))
            w["u"] = jnp.concatenate([w["u1"], u2], axis=0)
            solved_ref[w["h"] * rows : (w["h"] + 1) * rows, :] = w["u"]
        yield
        for w in pair:
            h = w["h"]
            ma = dot(w["kd"], w["u"])
            for start in range(0, DK, STRIP):
                part = ma[start : start + STRIP]
                kept = w["last"] * eye[start : start + STRIP]
                map_add_ref[h * DK + start : h * DK + start + STRIP, :] = jnp.concatenate(
                    [kept - part[:, :DK], part[:, DK:]], axis=1
                ).astype(bf16)
            yield

    pipeline([elementwise], n // 2)
    invert()
    pipeline([finish], n // 2)


def add_strips(a, b):
    return jnp.concatenate(
        [
            (a[i : i + STRIP].astype(f32) + b[i : i + STRIP]).astype(bf16)
            for i in range(0, a.shape[0], STRIP)
        ],
        axis=0,
    )


def delta_reach_kernel(
    half_ref,
    seg_ref,
    q_ref,
    k_ref,
    decay_ref,
    solved_ref,
    reach_ref,
    inner_ref,
    mask_ref,
    crow_ref,
    ccol_ref,
    first_ref,
):
    rows = k_ref.shape[0]
    n = reach_ref.shape[1] // DK
    setup(half_ref, seg_ref, decay_ref, n, mask_ref, crow_ref, ccol_ref, first_ref)
    strips = [slice(i, i + STRIP) for i in range(0, rows, STRIP)]
    pairs = [
        [dict(h=2 * kk + j, p=[], scaled=[]) for j in range(2)] for kk in range(n // 2)
    ]

    def elementwise(kk):
        pair = pairs[kk]
        cols = slice(kk * DK, (kk + 1) * DK)
        k_raw = k_ref[:, cols]
        q_raw = q_ref[:, cols]
        kt = jnp.transpose(k_raw.astype(f32))
        rk_row = lax.rsqrt(jnp.sum(kt * kt, axis=0, keepdims=True) + EPS)
        ktb = kt.astype(bf16)
        upper = dot(q_raw[:TILE], ktb[:, :TILE])
        lower = dot(q_raw[TILE:], ktb)
        yield
        for at in strips:
            raw, start = (upper, at.start) if at.start < TILE else (lower, at.start - TILE)
            width = raw.shape[1]
            qf = q_raw[at].astype(f32)
            rq = lax.rsqrt(jnp.sum(qf * qf, axis=1, keepdims=True) + EPS) * DK**-0.5
            qn = qf * rq
            probe = raw[start : start + STRIP] * rk_row[:, :width] * rq
            for w in pair:
                h = w["h"]
                cc = column(ccol_ref, at, h, width)
                span = jnp.exp2(cc - crow_ref[h : h + 1, :width] + mask_ref[at, :width])
                w["p"].append((span * probe).astype(bf16))
                entry = jnp.exp2(cc[:, :TILE]) * first_ref[at]
                w["scaled"].append((entry * qn).astype(bf16))
            yield

    def finish(kk):
        top = TILE // STRIP
        for w in pairs[kk]:
            h = w["h"]
            u = solved_ref[h * rows : (h + 1) * rows, :]
            upper = dot(jnp.concatenate(w["p"][:top], axis=0), u[:TILE])
            lower = dot(jnp.concatenate(w["p"][top:], axis=0), u)
            for at, scaled in zip(strips, w["scaled"]):
                pu = upper[at.start :] if at.start < TILE else lower[at.start - TILE :]
                pu = pu[:STRIP]
                reach_ref[at, h * DK : (h + 1) * DK] = (
                    scaled.astype(f32) - pu[:, :DK]
                ).astype(bf16)
                inner_ref[at, h * DV : (h + 1) * DV] = pu[:, DK:]
            yield

    pipeline([elementwise, finish], n // 2)


def half_call(kernel, name, mib, half, operands, outs, scratch):
    def at_half(i, s):
        return (0, s[0])

    def at_zero(i, s):
        return (0, 0)

    specs = []
    args = []
    for a in operands:
        if isinstance(a, tuple):
            (a,) = a
            specs.append(pl.BlockSpec((a.shape[0], a.shape[1] // 2), at_half))
        else:
            specs.append(pl.BlockSpec(a.shape, at_zero))
        args.append(a)
    return pl.pallas_call(
        kernel,
        grid_spec=pltpu.PrefetchScalarGridSpec(
            num_scalar_prefetch=1,
            grid=(1,),
            in_specs=specs,
            out_specs=[pl.BlockSpec(o.shape, at_zero) for o in outs],
            scratch_shapes=scratch,
        ),
        out_shape=outs,
        compiler_params=params(mib),
        cost_estimate=cost(4 * 10**9, 3 * 2**20),
        name=name,
    )(half, *args)


def setup_scratch(rows, n):
    return [
        pltpu.VMEM((rows, rows), f32),
        pltpu.VMEM((n, rows), f32),
        pltpu.VMEM((rows, TILE), f32),
        pltpu.VMEM((rows, TILE), f32),
    ]


def delta_local(half, mib, seg_row, key, value, beta, decay):
    rows = key.shape[0]
    n = value.shape[1] // DV // 2
    mask, *others = setup_scratch(rows, n)
    return half_call(
        delta_local_kernel,
        "delta_local",
        mib,
        half,
        [seg_row, (key,), (value,), beta, decay],
        [
            jax.ShapeDtypeStruct((n * DK + BLOCK, DK + DV), bf16),
            jax.ShapeDtypeStruct((n * rows, DK + DV), bf16),
        ],
        [
            mask,
            pltpu.VMEM((MERGES, TILE // 2, TILE), bf16),
            pltpu.VMEM((TILE, (BLOCK - 1) * TILE), bf16),
            *others,
        ],
    )


def delta_reach(half, seg_row, query, key, decay, solved):
    rows = key.shape[0]
    n = solved.shape[0] // rows
    return half_call(
        delta_reach_kernel,
        "delta_reach",
        20,
        half,
        [seg_row, (query,), (key,), decay, solved],
        [
            jax.ShapeDtypeStruct((rows, n * DK), bf16),
            jax.ShapeDtypeStruct((rows, n * DV), f32),
        ],
        setup_scratch(rows, n),
    )


def ids_of(ref):
    end = ref.shape[0] - BLOCK
    return ref[end : end + BLOCK, :].astype(f32)[:1]


def put_id(ref, value):
    end = ref.shape[0] - BLOCK
    ref[end:, :] = jnp.broadcast_to(value, (BLOCK, ref.shape[1])).astype(bf16)


def matching(a, b):
    return jnp.where(a == b, 1.0, 0.0)


def compose_kernel(core_ref, mine_ref, other_ref, map_ref, add_ref):
    odd = core_ref[0] == 1
    mine_ids, other_ids = ids_of(mine_ref), ids_of(other_ref)
    early_ids = jnp.where(odd, other_ids, mine_ids)
    late_ids = jnp.where(odd, mine_ids, other_ids)
    across = matching(early_ids[:, -1:], late_ids[:, :1])
    put_id(map_ref, early_ids[:, :1])
    put_id(add_ref, late_ids[:, -1:])
    for h in range(mine_ref.shape[0] // DK):
        at = slice(h * DK, (h + 1) * DK)
        mine, other = mine_ref[at], other_ref[at]
        early, late = jnp.where(odd, other, mine), jnp.where(odd, mine, other)
        both = dot(late[:, :DK], early) * across
        map_ref[at] = both[:, :DK].astype(bf16)
        add_ref[at] = (both[:, DK:] + late[:, DK:].astype(f32)).astype(bf16)


def relay_kernel(map_ref, add_ref, state_ref, out_ref):
    into = matching(ids_of(state_ref), ids_of(map_ref))
    put_id(out_ref, ids_of(add_ref))
    for h in range(map_ref.shape[0] // DK):
        at = slice(h * DK, (h + 1) * DK)
        out_ref[at] = (dot(map_ref[at], state_ref[at]) * into + add_ref[at].astype(f32)).astype(bf16)


def arrive_kernel(core_ref, mine_ref, other_ref, state_ref, keep_ref, give_ref):
    odd = core_ref[0] == 1
    mine_ids, other_ids = ids_of(mine_ref), ids_of(other_ref)
    early_ids = jnp.where(odd, other_ids, mine_ids)
    late_ids = jnp.where(odd, mine_ids, other_ids)
    across = matching(early_ids[:, -1:], late_ids[:, :1])
    into = matching(ids_of(state_ref), early_ids[:, :1])
    for h in range(keep_ref.shape[0] // DK):
        at = slice(h * DK, (h + 1) * DK)
        early = jnp.where(odd, other_ref[at], mine_ref[at])
        first = (state_ref[at].astype(f32) * into).astype(bf16)
        second = (
            (dot(early[:, :DK], first) + early[:, DK:].astype(f32)) * across
        ).astype(bf16)
        keep_ref[at] = jnp.where(odd, second, first)
        give_ref[at] = jnp.where(odd, first, second)


SMEM = pl.BlockSpec(memory_space=pltpu.SMEM)
VMEM = pl.BlockSpec(memory_space=pltpu.VMEM)


def small_call(kernel, name, outs, *args, scalars=0, mib=16):
    return pl.pallas_call(
        kernel,
        in_specs=[SMEM] * scalars + [VMEM] * (len(args) - scalars),
        out_specs=[VMEM] * len(outs),
        out_shape=outs,
        compiler_params=params(mib),
        cost_estimate=cost(10**8, 2**20),
        name=name,
    )(*args)


def delta_out_kernel(half_ref, reach_ref, inner_ref, state_ref, gate_ref, gain_ref, *rest):
    out_ref = rest[-1]
    gain = gain_ref[...]
    for h in range(state_ref.shape[0] // DK):
        cols = slice(h * DV, (h + 1) * DV)
        state = state_ref[h * DK : (h + 1) * DK]
        carried = dot(reach_ref[:, cols], state)
        for i in range(0, carried.shape[0], STRIP):
            at = slice(i, i + STRIP)
            out = inner_ref[at, cols].astype(f32) + carried[at]
            spread = lax.rsqrt(jnp.mean(out * out, axis=1, keepdims=True) + EPS)
            gate = gate_ref[at, cols].astype(f32)
            gate = gate * sigmoid(gate)
            out_ref[at, cols] = (out * spread * gain * gate).astype(bf16)


def delta_out(half, reach, inner, state, gate, gain, partial_out=None):
    rows = reach.shape[0]
    n = state.shape[0] // DK
    heads = 4
    steps = n // heads

    def at_half(i, s):
        return (0, s[0] * steps + i)

    in_specs = [
        pl.BlockSpec((rows, heads * DK), lambda i, s: (0, i)),
        pl.BlockSpec((rows, heads * DV), lambda i, s: (0, i)),
        pl.BlockSpec((heads * DK, DV), lambda i, s: (i, 0)),
        pl.BlockSpec((rows, heads * DV), at_half),
        pl.BlockSpec((1, DV), lambda i, s: (0, 0)),
    ]
    args = [half, reach, inner, state, gate, gain]
    aliases = {}
    if partial_out is not None:
        in_specs.append(pl.BlockSpec(memory_space=pl.ANY))
        args.append(partial_out)
        aliases = {6: 0}
    return pl.pallas_call(
        delta_out_kernel,
        grid_spec=pltpu.PrefetchScalarGridSpec(
            num_scalar_prefetch=1,
            grid=(steps,),
            in_specs=in_specs,
            out_specs=pl.BlockSpec((rows, heads * DV), at_half),
        ),
        out_shape=jax.ShapeDtypeStruct(gate.shape, bf16),
        input_output_aliases=aliases,
        compiler_params=params(),
        cost_estimate=cost(10**8, 3 * 2**20),
        name="delta_out",
    )(*args)


def blocks_of(pieces):
    own, *same, other = pieces
    order = [(own, None)]
    for i, ref in enumerate(same):
        order += [(other, i), (ref, None)]
    return order[::-1]


def pack_kernel(seg_ref, key_ref, value_ref, out_ref):
    rows = key_ref.shape[0]
    ids = seg_ref[...].astype(f32) + 1.0
    out_ref[:rows, :HEAD_WIDTH] = key_ref[...]
    out_ref[:rows, HEAD_WIDTH:] = value_ref[...]
    out_ref[rows:, :rows] = jnp.broadcast_to(ids, (BLOCK, rows)).astype(bf16)
    out_ref[rows:, rows:] = jnp.zeros((BLOCK, 2 * HEAD_WIDTH - rows), bf16)


def window_kernel(freq_ref, *rest):
    *pieces, kt_ref, v_ref, ids_ref, cos_ref, sin_ref = rest
    rows = cos_ref.shape[0]
    window = ids_ref.shape[1]
    half = ROTARY_ENTRIES // 2
    blocks = [ref if index is None else ref.at[index] for ref, index in blocks_of(pieces)]
    row_ids = jnp.concatenate(
        [ref[rows : rows + BLOCK, :rows].astype(f32)[:1] for ref in blocks], axis=1
    )
    ids_ref[...] = row_ids
    ids = jnp.broadcast_to(row_ids, (DOCS, window))
    docs = lax.broadcasted_iota(jnp.int32, (DOCS, window), 0).astype(f32) + 1.0
    before = jnp.sum(jnp.where(ids < docs, 1.0, 0.0), axis=1, keepdims=True)
    start = jnp.sum(jnp.where(ids == docs, before, 0.0), axis=0, keepdims=True)
    place = lax.broadcasted_iota(jnp.int32, (1, window), 1).astype(f32)
    angle = freq_ref[:, :1] * (place - start)
    cosine = jnp.cos(angle)
    sine = jnp.sin(angle)
    for b, ref in enumerate(blocks):
        cols = slice(b * rows, (b + 1) * rows)
        kt = jnp.transpose(ref[:rows, :HEAD_WIDTH].astype(f32))
        one, two = kt[:half], kt[half:ROTARY_ENTRIES]
        cb, sb = cosine[:, cols], sine[:, cols]
        kt_ref[:half, cols] = (one * cb - two * sb).astype(bf16)
        kt_ref[half:ROTARY_ENTRIES, cols] = (two * cb + one * sb).astype(bf16)
        kt_ref[ROTARY_ENTRIES:, cols] = kt[ROTARY_ENTRIES:].astype(bf16)
        v_ref[cols, :] = ref[:rows, HEAD_WIDTH:]
    cq, sq = cosine[:, window - rows :], sine[:, window - rows :]
    rest_rows = TILE - ROTARY_ENTRIES
    cos_ref[...] = jnp.transpose(
        jnp.concatenate([cq, cq, jnp.ones((rest_rows, rows), f32)], axis=0)
    )
    sin_ref[...] = jnp.transpose(
        jnp.concatenate([-sq, sq, jnp.zeros((rest_rows, rows), f32)], axis=0)
    )


def attention_kernel(ids_ref, cos_ref, sin_ref, kt_ref, v_ref, q_ref, gate_ref, *rest):
    out_ref, mask_ref = rest[-2:]
    rows = q_ref.shape[0]
    window = ids_ref.shape[1]
    half = ROTARY_ENTRIES // 2

    @pl.when(pl.program_id(0) == 0)
    def _():
        own = ids_ref[:, window - rows :]
        own_col = jnp.transpose(jnp.broadcast_to(own, (TILE, rows)))
        own_cols = jnp.concatenate([own_col] * (window // TILE), axis=1)
        r = lax.broadcasted_iota(jnp.int32, (rows, window), 0) + (window - rows)
        c = lax.broadcasted_iota(jnp.int32, (rows, window), 1)
        mask_ref[...] = jnp.where((own_cols == ids_ref[...]) & (c <= r), 0.0, MASKED)

    scaling = HEAD_WIDTH**-0.5
    lane = lax.broadcasted_iota(jnp.int32, (TILE, TILE), 1)
    reach = window - rows + TILE
    heads = q_ref.shape[1] // HEAD_WIDTH
    for first in range(0, rows, TILE):
        at = slice(first, first + TILE)
        keys = slice(first, first + reach)
        queries = []
        for h in range(heads):
            base = h * HEAD_WIDTH
            x = q_ref[at, base : base + TILE].astype(f32)
            swapped = jnp.where(
                lane < half, pltpu.roll(x, TILE - half, 1), pltpu.roll(x, half, 1)
            )
            rotated = ((x * cos_ref[at] + swapped * sin_ref[at]) * scaling).astype(bf16)
            tail = q_ref[at, base + TILE : base + HEAD_WIDTH] * jnp.asarray(scaling, bf16)
            queries.append(jnp.concatenate([rotated, tail], axis=1))
        scores = dot(jnp.concatenate(queries, axis=0), kt_ref[:, keys])
        weights = []
        totals = []
        for i in range(0, heads * TILE, FINE):
            row = first + i % TILE
            strip = scores[i : i + FINE] + mask_ref[row : row + FINE, keys]
            strip = jnp.exp(strip - jnp.max(strip, axis=1, keepdims=True))
            totals.append(1.0 / jnp.sum(strip, axis=1, keepdims=True))
            weights.append(strip.astype(bf16))
        mixed = dot(jnp.concatenate(weights, axis=0), v_ref[keys, :])
        for i, inverse in zip(range(0, heads * TILE, FINE), totals):
            rows_at = slice(first + i % TILE, first + i % TILE + FINE)
            cols = slice(i // TILE * HEAD_WIDTH, (i // TILE + 1) * HEAD_WIDTH)
            gate = sigmoid(gate_ref[rows_at, cols].astype(f32))
            out_ref[rows_at, cols] = (mixed[i : i + FINE] * inverse * gate).astype(bf16)


def attention_half(part, window_arrays, query, gate, partial_out=None):
    rows = query.shape[0]
    window = window_arrays[0].shape[1]
    heads = 4
    width = heads * HEAD_WIDTH
    steps = query.shape[1] // width // 2

    def at_part(i):
        return (0, part * steps + i)

    in_specs = [pl.BlockSpec(a.shape, lambda i: (0, 0)) for a in window_arrays]
    in_specs += [pl.BlockSpec((rows, width), at_part)] * 2
    args = [*window_arrays, query, gate]
    aliases = {}
    if partial_out is not None:
        aliases = {len(args): 0}
        in_specs.append(pl.BlockSpec(memory_space=pl.ANY))
        args.append(partial_out)
    return pl.pallas_call(
        attention_kernel,
        grid=(steps,),
        in_specs=in_specs,
        out_specs=pl.BlockSpec((rows, width), at_part),
        out_shape=jax.ShapeDtypeStruct(query.shape, bf16),
        scratch_shapes=[pltpu.VMEM((rows, window), f32)],
        input_output_aliases=aliases,
        compiler_params=params(28),
        cost_estimate=cost(5 * 10**9, 3 * 2**20, 10**6),
        name="attention",
    )(*args)


def up_chip(value, ranks):
    return lax.ppermute(value, "ctx", [(i, i + 2) for i in range(ranks - 2)])


def swap_cores(value, ranks):
    return lax.ppermute(value, "ctx", [(i, i ^ 1) for i in range(ranks)])


def per_device(
    segment_ids,
    attn_query,
    attention_keys,
    attention_values,
    attn_gate,
    delta_query,
    delta_key,
    update_rule_payload,
    delta_beta,
    delta_decay,
    delta_gate,
    norm_gain,
):
    ranks = lax.axis_size("ctx")
    rank = lax.axis_index("ctx")
    rows = segment_ids.shape[0]
    hops = ranks // 4
    core = rank % 2
    odd = core == 1

    ids = segment_ids.reshape(1, rows)

    (own,) = small_call(
        pack_kernel,
        "pack",
        [jax.ShapeDtypeStruct((rows + BLOCK, 2 * HEAD_WIDTH), bf16)],
        ids,
        attention_keys,
        attention_values,
        mib=60,
    )
    nearest = up_chip(own, ranks)

    keep_half = core.reshape(1).astype(jnp.int32)
    give_half = 1 - keep_half
    decay_rows = delta_decay.T
    local = partial(
        delta_local,
        seg_row=ids,
        key=delta_key,
        value=update_rule_payload,
        beta=delta_beta.T,
        decay=decay_rows,
    )
    reach = partial(
        delta_reach, seg_row=ids, query=delta_query, key=delta_key, decay=decay_rows
    )
    give_ma, give_solved = local(give_half, 60)
    other_ma = swap_cores(give_ma, ranks)
    nearest, give_ma = lax.optimization_barrier((nearest, give_ma))
    same = [nearest]
    for _ in range(hops - 1):
        same.append(up_chip(same[-1], ranks))
    keep_ma, keep_solved = local(keep_half, 60)
    same, keep_ma, other_ma = lax.optimization_barrier((same, keep_ma, other_ma))
    chain = [own, *same]
    other = swap_cores(
        jnp.stack([jnp.where(odd, chain[i + 1], chain[i]) for i in range(hops)]), ranks
    )

    tall = keep_ma.shape[0]
    state_like = jax.ShapeDtypeStruct((tall, DV), bf16)
    chip_map, chip_add = small_call(
        compose_kernel, "compose", [state_like] * 2, keep_half, keep_ma, other_ma, scalars=1
    )
    state = up_chip(chip_add, ranks)

    window = (2 * hops + 1) * rows
    index = jnp.arange(ROTARY_ENTRIES // 2).astype(f32)
    freq = ROPE_THETA ** (-2.0 * index / ROTARY_ENTRIES)
    freq = jnp.broadcast_to(freq[:, None], (ROTARY_ENTRIES // 2, TILE))
    window_arrays = small_call(
        window_kernel,
        "window",
        [
            jax.ShapeDtypeStruct((HEAD_WIDTH, window), bf16),
            jax.ShapeDtypeStruct((window, HEAD_WIDTH), bf16),
            jax.ShapeDtypeStruct((1, window), f32),
            jax.ShapeDtypeStruct((rows, TILE), f32),
            jax.ShapeDtypeStruct((rows, TILE), f32),
        ],
        freq,
        own,
        *same,
        other,
    )
    kt, v_all, window_ids, cosine, sine = window_arrays
    window_arrays = (window_ids, cosine, sine, kt, v_all)
    attn_mixed = attention_half(0, window_arrays, attn_query, attn_gate)
    give_solved, chip_add = lax.optimization_barrier((give_solved, chip_add))
    give_rows = reach(give_half, solved=give_solved)
    state, attn_mixed, give_rows = lax.optimization_barrier((state, attn_mixed, give_rows))
    leaving = chip_add
    for _ in range(hops - 1):
        (leaving,) = small_call(relay_kernel, "relay", [state_like], chip_map, chip_add, state)
        state = up_chip(leaving, ranks)
    attn_mixed = attention_half(1, window_arrays, attn_query, attn_gate, attn_mixed)
    keep_solved, leaving = lax.optimization_barrier((keep_solved, leaving))
    keep_rows = reach(keep_half, solved=keep_solved)
    state, attn_mixed, keep_rows = lax.optimization_barrier((state, attn_mixed, keep_rows))

    final_like = jax.ShapeDtypeStruct((tall - BLOCK, DV), bf16)
    keep_state, pass_state = small_call(
        arrive_kernel, "arrive", [final_like] * 2, keep_half, keep_ma, other_ma, state, scalars=1
    )
    give_state = swap_cores(pass_state, ranks)

    gain = norm_gain.reshape(1, DV)
    delta_mixed = delta_out(keep_half, *keep_rows, keep_state, delta_gate, gain)
    delta_mixed = delta_out(
        give_half, *give_rows, give_state, delta_gate, gain, delta_mixed
    )
    return (attn_mixed, delta_mixed)


def solution(mesh):
    rows = P(("dp", "ctx"))
    wide = P(("dp", "ctx"), None)
    return jax.shard_map(
        per_device,
        mesh=mesh,
        in_specs=(rows,) + (wide,) * 10 + (P(),),
        out_specs=(wide, wide),
        check_vma=False,
    )
```

```python
from functools import partial

import jax
import jax.numpy as jnp
from jax import lax
from jax.experimental import pallas as pl
from jax.experimental.pallas import tpu as pltpu
from jax.sharding import PartitionSpec as P

HEAD_WIDTH = 256
ROTARY_ENTRIES = 64
DK = 128
DV = 128
DOCS = 8
ROPE_THETA = 10000000.0
LOG2E = 1.4426950408889634
MASKED = -1e30
EPS = 1e-6
TILE = 128
MIB = 1024 * 1024

f32 = jnp.float32
bf16 = jnp.bfloat16


def dot(a, b, precision=None):
    return jnp.dot(a, b, preferred_element_type=f32, precision=precision)


def params(mib=16):
    return pltpu.CompilerParams(vmem_limit_bytes=mib * MIB)


def sigmoid(x):
    return 0.5 * jnp.tanh(0.5 * x) + 0.5


def cost(flops, nbytes, exps=0):
    return pl.CostEstimate(flops=flops, bytes_accessed=nbytes, transcendentals=exps)


BLOCK = 16
MERGES = 3
STRIP = 32
FINE = 16
DONE = object()


def odd_rows(m, b):
    return jnp.concatenate([m[i + b : i + 2 * b] for i in range(0, TILE, 2 * b)], axis=0)


def interleave(even, odd, b):
    parts = []
    for i in range(0, TILE // 2, b):
        parts += [even[i : i + b], odd[i : i + b]]
    return jnp.concatenate(parts, axis=0)


def even_rows(m, b):
    return jnp.concatenate([m[i : i + b] for i in range(0, TILE, 2 * b)], axis=0)


def fold(m):
    row = lax.broadcasted_iota(jnp.int32, (BLOCK, TILE), 0)
    lane = lax.broadcasted_iota(jnp.int32, (BLOCK, TILE), 1)
    group = lane // BLOCK
    z = jnp.where(group == 0, m[:BLOCK], 0.0)
    for r in range(1, TILE // BLOCK):
        z = jnp.where(group == r, m[r * BLOCK : (r + 1) * BLOCK], z)
    return jnp.where(row > lax.rem(lane, BLOCK), z, 0.0).astype(bf16)


def fill_spread(spread_ref):
    row = lax.broadcasted_iota(jnp.int32, (TILE, TILE), 0)
    lane = lax.broadcasted_iota(jnp.int32, (TILE, TILE), 1)
    base = row - lane // BLOCK * BLOCK
    for k in range(BLOCK - 1):
        spread_ref[:, k * TILE : (k + 1) * TILE] = jnp.where(base == k, 1.0, 0.0).astype(bf16)


def block_inverses(folded, spread_ref):
    row = lax.broadcasted_iota(jnp.int32, (BLOCK, TILE), 0)
    lane = lax.broadcasted_iota(jnp.int32, (BLOCK, TILE), 1)
    group = lane // BLOCK
    within = lax.rem(lane, BLOCK)
    spread = dot(jnp.concatenate(folded, axis=0), spread_ref[...])
    unit = jnp.where(row == within, 1.0, 0.0)
    small = BLOCK // 2
    out = []
    tops = [unit[:small]] * len(folded)
    lows = [unit[small:]] * len(folded)
    for k in range(BLOCK - 1):
        at = slice(k * TILE, (k + 1) * TILE)
        for i in range(len(folded)):
            rows = spread[i * BLOCK : (i + 1) * BLOCK, at]
            source = tops[i][k : k + 1] if k < small else lows[i][k - small : k - small + 1]
            if k < small - 1:
                tops[i] = tops[i] + rows[:small] * source
            lows[i] = lows[i] + rows[small:] * source
    for top, low in zip(tops, lows):
        x = jnp.where(row > within, jnp.concatenate([top, low], axis=0), 0.0)
        out.append(
            jnp.concatenate(
                [jnp.where(group == r, x, 0.0) for r in range(TILE // BLOCK)], axis=0
            ).astype(bf16)
        )
    return out


def setup(half_ref, seg_ref, decay_ref, n, mask_ref, crow_ref, ccol_ref, first_ref, beta_ref=None):
    rows = seg_ref.shape[1]
    seg_row = seg_ref[...].astype(f32) + 1.0
    seg_col = jnp.transpose(jnp.broadcast_to(seg_row, (TILE, rows)))
    seg_cols = jnp.concatenate([seg_col] * (rows // TILE), axis=1)
    r = lax.broadcasted_iota(jnp.int32, (rows, rows), 0)
    c = lax.broadcasted_iota(jnp.int32, (rows, rows), 1)
    mask_ref[...] = jnp.where((seg_cols == seg_row) & (r >= c), 0.0, MASKED)
    first_ref[...] = jnp.where(seg_col == seg_row[:, :1], 1.0, 0.0)
    base = pl.multiple_of(half_ref[0] * n, n)
    decay = decay_ref[pl.ds(base, n), :] * LOG2E
    high = decay.astype(bf16)
    rest = decay - high.astype(f32)
    middle = rest.astype(bf16)
    parts = [high, middle, (rest - middle.astype(f32)).astype(bf16)]
    parts = jnp.concatenate([p.astype(f32) for p in parts], axis=0).astype(bf16)
    sums = dot(parts, jnp.where(r <= c, 1.0, 0.0).astype(bf16))
    cumulative = sums[:n] + sums[n : 2 * n] + sums[2 * n :]
    crow_ref[...] = cumulative
    beta = jnp.zeros((n, rows), f32) if beta_ref is None else beta_ref[pl.ds(base, n), :]
    fill = jnp.zeros((TILE - 2 * n, rows), f32)
    ccol_ref[...] = jnp.transpose(jnp.concatenate([cumulative, beta, fill], axis=0))
    return seg_row


def column(ref, at, lane, width):
    one = jnp.broadcast_to(ref[at, lane : lane + 1], (STRIP, TILE))
    return one if width == TILE else jnp.concatenate([one] * (width // TILE), axis=1)


def pipeline(phases, count):
    for slot in range(count + len(phases) - 1):
        running = [
            phase(slot - i) for i, phase in enumerate(phases) if 0 <= slot - i < count
        ]
        while running:
            running = [p for p in running if next(p, DONE) is not DONE]


def delta_local_kernel(
    half_ref,
    seg_ref,
    k_hbm,
    v_hbm,
    beta_ref,
    decay_ref,
    map_add_hbm,
    solved_hbm,
    mask_ref,
    level_ref,
    spread_ref,
    k_ref,
    v_ref,
    map_add_ref,
    solved_ref,
    in_sem,
    out_sem,
    crow_ref,
    ccol_ref,
    first_ref,
):
    rows = k_ref.shape[0]
    n = v_ref.shape[1] // DV
    arriving = []
    for kk in range(n // 2):
        for i, (source, target, width) in enumerate(
            [(k_hbm, k_ref, DK), (v_hbm, v_ref, 2 * DV)]
        ):
            at = pl.multiple_of(half_ref[0] * (width * n // 2) + kk * width, width)
            arriving.append(
                pltpu.make_async_copy(
                    source.at[:, pl.ds(at, width)],
                    target.at[:, pl.ds(kk * width, width)],
                    in_sem.at[2 * kk + i],
                )
            )
            arriving[-1].start()
    leaving = []

    def send(source, target, at, size):
        part = pl.ds(at, size)
        leaving.append(
            pltpu.make_async_copy(source.at[part], target.at[part], out_sem.at[len(leaving)])
        )
        leaving[-1].start()

    fill_spread(spread_ref)
    seg_row = setup(
        half_ref, seg_ref, decay_ref, n, mask_ref, crow_ref, ccol_ref, first_ref, beta_ref
    )
    map_add_ref[n * DK :, :] = jnp.broadcast_to(seg_row, (BLOCK, rows)).astype(bf16)
    send(map_add_ref, map_add_hbm, n * DK, BLOCK)
    r = lax.broadcasted_iota(jnp.int32, (TILE, TILE), 0)
    c = lax.broadcasted_iota(jnp.int32, (TILE, TILE), 1)
    eye = jnp.where(r == c, 1.0, 0.0)
    for level in range(MERGES):
        b = BLOCK << level
        sibling = jnp.where(r // b == c // b + 1, 1.0, 0.0)
        level_ref[level] = odd_rows(sibling, b).astype(bf16)
    strips = [slice(i, i + STRIP) for i in range(0, rows, STRIP)]
    pairs = [
        [dict(h=2 * kk + j, d=[], right=[]) for j in range(2)] for kk in range(n // 2)
    ]

    def elementwise(kk):
        pair = pairs[kk]
        arriving[2 * kk].wait()
        arriving[2 * kk + 1].wait()
        k_raw = k_ref[:, kk * DK : (kk + 1) * DK]
        kt = jnp.transpose(k_raw.astype(f32))
        rk_row = lax.rsqrt(jnp.sum(kt * kt, axis=0, keepdims=True) + EPS)
        ktb = kt.astype(bf16)
        upper = dot(k_raw[:TILE], ktb[:, :TILE])
        lower = dot(k_raw[TILE:], ktb)
        yield
        for at in strips:
            raw, start = (upper, at.start) if at.start < TILE else (lower, at.start - TILE)
            width = raw.shape[1]
            kf = k_raw[at].astype(f32)
            rk = lax.rsqrt(jnp.sum(kf * kf, axis=1, keepdims=True) + EPS)
            kn = kf * rk
            gram = raw[start : start + STRIP] * rk_row[:, :width] * -rk
            for w in pair:
                h = w["h"]
                cc = column(ccol_ref, at, h, width)
                bt = column(ccol_ref, at, n + h, width)
                span = jnp.exp2(cc - crow_ref[h : h + 1, :width] + mask_ref[at, :width])
                w["d"].append(span * bt * gram)
                cc, bt = cc[:, :TILE], bt[:, :TILE]
                entry = jnp.exp2(cc) * first_ref[at]
                value = v_ref[at, h * DV : (h + 1) * DV].astype(f32)
                w["right"].append(
                    jnp.concatenate([bt * entry * kn, bt * value], axis=1).astype(bf16)
                )
                if at.stop == rows:
                    w["last"] = entry[STRIP - 1 :]
                    w["kd"] = (kt * (rk_row * span[STRIP - 1 :])).astype(bf16)
            yield
        top = TILE // STRIP
        for w in pair:
            d11 = jnp.concatenate(w["d"][:top], axis=0)
            d2 = jnp.concatenate(w["d"][top:], axis=0)
            blocks = [d11, d2[:, TILE:]]
            w["folded"] = [fold(m) for m in blocks]
            w["d"] = [m.astype(bf16) for m in blocks]
            w["d21"] = d2[:, :TILE].astype(bf16)
            w["right"] = jnp.concatenate(w["right"], axis=0)
        yield

    def invert():
        work = [w for pair in pairs for w in pair]
        mats = [m for w in work for m in w["d"]]
        inverses = block_inverses([z for w in work for z in w["folded"]], spread_ref)
        zeros = jnp.zeros((TILE // 2, TILE), bf16)
        for level in range(MERGES):
            b = BLOCK << level
            keep = level_ref[level]
            picked = [odd_rows(m, b) * keep for m in mats]
            ys = [(p.astype(f32) + dot(p, x)).astype(bf16) for p, x in zip(picked, inverses)]
            odds = [odd_rows(x, b) for x in inverses]
            odds = [
                x + (y.astype(f32) + dot(x, interleave(zeros, y, b))).astype(bf16)
                for x, y in zip(odds, ys)
            ]
            inverses = [interleave(even_rows(x, b), o, b) for x, o in zip(inverses, odds)]
        for i, w in enumerate(work):
            w["x"] = inverses[2 * i : 2 * i + 2]

    def finish(kk):
        pair = pairs[kk]
        for w in pair:
            w["u1"] = add_strips(w["right"][:TILE], dot(w["x"][0], w["right"][:TILE]))
        yield
        for w in pair:
            w["r2"] = add_strips(w["right"][TILE:], dot(w["d21"], w["u1"]))
        yield
        for w in pair:
            u2 = add_strips(w["r2"], dot(w["x"][1], w["r2"]))
            w["u"] = jnp.concatenate([w["u1"], u2], axis=0)
            solved_ref[w["h"] * rows : (w["h"] + 1) * rows, :] = w["u"]
            send(solved_ref, solved_hbm, w["h"] * rows, rows)
        yield
        for w in pair:
            h = w["h"]
            ma = dot(w["kd"], w["u"])
            for start in range(0, DK, STRIP):
                part = ma[start : start + STRIP]
                kept = w["last"] * eye[start : start + STRIP]
                map_add_ref[h * DK + start : h * DK + start + STRIP, :] = jnp.concatenate(
                    [kept - part[:, :DK], part[:, DK:]], axis=1
                ).astype(bf16)
            send(map_add_ref, map_add_hbm, h * DK, DK)
            yield

    pipeline([elementwise], n // 2)
    invert()
    pipeline([finish], n // 2)
    for copy in leaving:
        copy.wait()


def add_strips(a, b):
    return jnp.concatenate(
        [
            (a[i : i + STRIP].astype(f32) + b[i : i + STRIP]).astype(bf16)
            for i in range(0, a.shape[0], STRIP)
        ],
        axis=0,
    )


def delta_reach_kernel(
    half_ref,
    seg_ref,
    q_ref,
    k_ref,
    decay_ref,
    solved_ref,
    gate_ref,
    gain_ref,
    reach_ref,
    inner_ref,
    factor_ref,
    mask_ref,
    crow_ref,
    ccol_ref,
    first_ref,
):
    rows = k_ref.shape[0]
    n = reach_ref.shape[1] // DK
    setup(half_ref, seg_ref, decay_ref, n, mask_ref, crow_ref, ccol_ref, first_ref)
    strips = [slice(i, i + STRIP) for i in range(0, rows, STRIP)]
    pairs = [
        [dict(h=2 * kk + j, p=[], scaled=[]) for j in range(2)] for kk in range(n // 2)
    ]

    def elementwise(kk):
        pair = pairs[kk]
        cols = slice(kk * DK, (kk + 1) * DK)
        k_raw = k_ref[:, cols]
        q_raw = q_ref[:, cols]
        kt = jnp.transpose(k_raw.astype(f32))
        rk_row = lax.rsqrt(jnp.sum(kt * kt, axis=0, keepdims=True) + EPS)
        ktb = kt.astype(bf16)
        upper = dot(q_raw[:TILE], ktb[:, :TILE])
        lower = dot(q_raw[TILE:], ktb)
        yield
        for at in strips:
            raw, start = (upper, at.start) if at.start < TILE else (lower, at.start - TILE)
            width = raw.shape[1]
            qf = q_raw[at].astype(f32)
            rq = lax.rsqrt(jnp.sum(qf * qf, axis=1, keepdims=True) + EPS) * DK**-0.5
            qn = qf * rq
            probe = raw[start : start + STRIP] * rk_row[:, :width] * rq
            for w in pair:
                h = w["h"]
                cc = column(ccol_ref, at, h, width)
                span = jnp.exp2(cc - crow_ref[h : h + 1, :width] + mask_ref[at, :width])
                w["p"].append((span * probe).astype(bf16))
                entry = jnp.exp2(cc[:, :TILE]) * first_ref[at]
                w["scaled"].append((entry * qn).astype(bf16))
                cols = slice(h * DV, (h + 1) * DV)
                gate = gate_ref[at, cols].astype(f32)
                factor_ref[at, cols] = gate * sigmoid(gate) * gain_ref[...]
            yield

    def finish(kk):
        top = TILE // STRIP
        for w in pairs[kk]:
            h = w["h"]
            u = solved_ref[h * rows : (h + 1) * rows, :]
            upper = dot(jnp.concatenate(w["p"][:top], axis=0), u[:TILE])
            lower = dot(jnp.concatenate(w["p"][top:], axis=0), u)
            for at, scaled in zip(strips, w["scaled"]):
                pu = upper[at.start :] if at.start < TILE else lower[at.start - TILE :]
                pu = pu[:STRIP]
                reach_ref[at, h * DK : (h + 1) * DK] = (
                    scaled.astype(f32) - pu[:, :DK]
                ).astype(bf16)
                inner_ref[at, h * DV : (h + 1) * DV] = pu[:, DK:]
            yield

    pipeline([elementwise, finish], n // 2)


def half_call(kernel, name, mib, half, operands, outs, scratch, hbm=False):
    def at_half(i, s):
        return (0, s[0])

    def at_zero(i, s):
        return (0, 0)

    specs = []
    args = []
    for a in operands:
        if isinstance(a, tuple):
            (a,) = a
            if hbm:
                specs.append(pl.BlockSpec(memory_space=pl.ANY))
            else:
                specs.append(pl.BlockSpec((a.shape[0], a.shape[1] // 2), at_half))
        else:
            specs.append(pl.BlockSpec(a.shape, at_zero))
        args.append(a)
    return pl.pallas_call(
        kernel,
        grid_spec=pltpu.PrefetchScalarGridSpec(
            num_scalar_prefetch=1,
            grid=(1,),
            in_specs=specs,
            out_specs=[
                pl.BlockSpec(memory_space=pl.ANY) if hbm else pl.BlockSpec(o.shape, at_zero)
                for o in outs
            ],
            scratch_shapes=scratch,
        ),
        out_shape=outs,
        compiler_params=params(mib),
        cost_estimate=cost(4 * 10**9, 3 * 2**20),
        name=name,
    )(half, *args)


def setup_scratch(rows, n):
    return [
        pltpu.VMEM((rows, rows), f32),
        pltpu.VMEM((n, rows), f32),
        pltpu.VMEM((rows, TILE), f32),
        pltpu.VMEM((rows, TILE), f32),
    ]


def delta_local(half, mib, seg_row, key, value, beta, decay):
    rows = key.shape[0]
    n = value.shape[1] // DV // 2
    mask, *others = setup_scratch(rows, n)
    return half_call(
        delta_local_kernel,
        "delta_local",
        mib,
        half,
        [seg_row, (key,), (value,), beta, decay],
        [
            jax.ShapeDtypeStruct((n * DK + BLOCK, DK + DV), bf16),
            jax.ShapeDtypeStruct((n * rows, DK + DV), bf16),
        ],
        [
            mask,
            pltpu.VMEM((MERGES, TILE // 2, TILE), bf16),
            pltpu.VMEM((TILE, (BLOCK - 1) * TILE), bf16),
            pltpu.VMEM((rows, n // 2 * DK), bf16),
            pltpu.VMEM((rows, n * DV), bf16),
            pltpu.VMEM((n * DK + BLOCK, DK + DV), bf16),
            pltpu.VMEM((n * rows, DK + DV), bf16),
            pltpu.SemaphoreType.DMA((n,)),
            pltpu.SemaphoreType.DMA((2 * n + 1,)),
            *others,
        ],
        hbm=True,
    )


def delta_reach(half, seg_row, query, key, decay, gate, gain, solved):
    rows = key.shape[0]
    n = solved.shape[0] // rows
    return half_call(
        delta_reach_kernel,
        "delta_reach",
        20,
        half,
        [seg_row, (query,), (key,), decay, solved, (gate,), gain],
        [
            jax.ShapeDtypeStruct((rows, n * DK), bf16),
            jax.ShapeDtypeStruct((rows, n * DV), f32),
            jax.ShapeDtypeStruct((rows, n * DV), f32),
        ],
        setup_scratch(rows, n),
    )


def ids_of(ref):
    end = ref.shape[0] - BLOCK
    return ref[end : end + BLOCK, :].astype(f32)[:1]


def put_id(ref, value):
    end = ref.shape[0] - BLOCK
    ref[end:, :] = jnp.broadcast_to(value, (BLOCK, ref.shape[1])).astype(bf16)


def matching(a, b):
    return jnp.where(a == b, 1.0, 0.0)


def compose_kernel(core_ref, mine_ref, other_ref, map_ref, add_ref):
    odd = core_ref[0] == 1
    mine_ids, other_ids = ids_of(mine_ref), ids_of(other_ref)
    early_ids = jnp.where(odd, other_ids, mine_ids)
    late_ids = jnp.where(odd, mine_ids, other_ids)
    across = matching(early_ids[:, -1:], late_ids[:, :1])
    put_id(map_ref, early_ids[:, :1])
    put_id(add_ref, late_ids[:, -1:])
    for h in range(mine_ref.shape[0] // DK):
        at = slice(h * DK, (h + 1) * DK)
        mine, other = mine_ref[at], other_ref[at]
        early, late = jnp.where(odd, other, mine), jnp.where(odd, mine, other)
        both = dot(late[:, :DK], early) * across
        map_ref[at] = both[:, :DK].astype(bf16)
        add_ref[at] = (both[:, DK:] + late[:, DK:].astype(f32)).astype(bf16)


def relay_kernel(map_ref, add_ref, state_ref, out_ref):
    into = matching(ids_of(state_ref), ids_of(map_ref))
    put_id(out_ref, ids_of(add_ref))
    for h in range(map_ref.shape[0] // DK):
        at = slice(h * DK, (h + 1) * DK)
        out_ref[at] = (dot(map_ref[at], state_ref[at]) * into + add_ref[at].astype(f32)).astype(bf16)


def arrive_kernel(core_ref, mine_ref, other_ref, state_ref, keep_ref, give_ref):
    odd = core_ref[0] == 1
    mine_ids, other_ids = ids_of(mine_ref), ids_of(other_ref)
    early_ids = jnp.where(odd, other_ids, mine_ids)
    late_ids = jnp.where(odd, mine_ids, other_ids)
    across = matching(early_ids[:, -1:], late_ids[:, :1])
    into = matching(ids_of(state_ref), early_ids[:, :1])
    for h in range(keep_ref.shape[0] // DK):
        at = slice(h * DK, (h + 1) * DK)
        early = jnp.where(odd, other_ref[at], mine_ref[at])
        first = (state_ref[at].astype(f32) * into).astype(bf16)
        second = (
            (dot(early[:, :DK], first) + early[:, DK:].astype(f32)) * across
        ).astype(bf16)
        keep_ref[at] = jnp.where(odd, second, first)
        give_ref[at] = jnp.where(odd, first, second)


SMEM = pl.BlockSpec(memory_space=pltpu.SMEM)
VMEM = pl.BlockSpec(memory_space=pltpu.VMEM)


def small_call(kernel, name, outs, *args, scalars=0, mib=16):
    return pl.pallas_call(
        kernel,
        in_specs=[SMEM] * scalars + [VMEM] * (len(args) - scalars),
        out_specs=[VMEM] * len(outs),
        out_shape=outs,
        compiler_params=params(mib),
        cost_estimate=cost(10**8, 2**20),
        name=name,
    )(*args)


def delta_out_kernel(half_ref, reach_ref, inner_ref, factor_ref, state_ref, *rest):
    out_hbm, out_ref, sem = rest[-3:]
    n = state_ref.shape[0] // DK
    width = 2 * DV
    copies = []
    for h in range(n):
        cols = slice(h * DV, (h + 1) * DV)
        carried = dot(reach_ref[:, cols], state_ref[h * DK : (h + 1) * DK])
        for i in range(0, carried.shape[0], STRIP):
            at = slice(i, i + STRIP)
            out = inner_ref[at, cols] + carried[at]
            spread = lax.rsqrt(jnp.mean(out * out, axis=1, keepdims=True) + EPS)
            out_ref[at, cols] = (out * spread * factor_ref[at, cols]).astype(bf16)
        if h % 2 == 1:
            start = (h - 1) * DV
            target = pl.multiple_of(half_ref[0] * (n * DV) + start, width)
            copies.append(
                pltpu.make_async_copy(
                    out_ref.at[:, pl.ds(start, width)],
                    out_hbm.at[:, pl.ds(target, width)],
                    sem.at[h // 2],
                )
            )
            copies[-1].start()
    for copy in copies:
        copy.wait()


def delta_out(half, reach, inner, factor, state, partial_out=None):
    rows = reach.shape[0]
    n = state.shape[0] // DK
    in_specs = [SMEM] + [VMEM] * 4
    args = [half, reach, inner, factor, state]
    aliases = {}
    if partial_out is not None:
        aliases = {len(args): 0}
        in_specs.append(pl.BlockSpec(memory_space=pl.ANY))
        args.append(partial_out)
    return pl.pallas_call(
        delta_out_kernel,
        in_specs=in_specs,
        out_specs=pl.BlockSpec(memory_space=pl.ANY),
        out_shape=jax.ShapeDtypeStruct((rows, 2 * n * DV), bf16),
        scratch_shapes=[pltpu.VMEM((rows, n * DV), bf16), pltpu.SemaphoreType.DMA((n // 2,))],
        input_output_aliases=aliases,
        compiler_params=params(),
        cost_estimate=cost(10**8, 3 * 2**20),
        name="delta_out",
    )(*args)


def blocks_of(pieces):
    own, *same, other = pieces
    order = [(own, None)]
    for i, ref in enumerate(same):
        order += [(other, i), (ref, None)]
    return order[::-1]


def pack_kernel(seg_ref, key_hbm, value_hbm, out_hbm, ids_ref, sem):
    rows = seg_ref.shape[1]
    body = out_hbm.at[pl.ds(0, rows)]
    copies = [
        pltpu.make_async_copy(key_hbm, body.at[:, pl.ds(0, HEAD_WIDTH)], sem.at[0]),
        pltpu.make_async_copy(value_hbm, body.at[:, pl.ds(HEAD_WIDTH, HEAD_WIDTH)], sem.at[1]),
        pltpu.make_async_copy(ids_ref, out_hbm.at[pl.ds(rows, BLOCK)], sem.at[2]),
    ]
    copies[0].start()
    copies[1].start()
    ids = jnp.broadcast_to(seg_ref[...].astype(f32) + 1.0, (BLOCK, rows))
    unused = jnp.zeros((BLOCK, 2 * HEAD_WIDTH - rows), f32)
    ids_ref[...] = jnp.concatenate([ids, unused], axis=1).astype(bf16)
    copies[2].start()
    for copy in copies:
        copy.wait()


def pack(ids, keys, values):
    rows = keys.shape[0]
    free = pl.BlockSpec(memory_space=pl.ANY)
    return pl.pallas_call(
        pack_kernel,
        in_specs=[VMEM, free, free],
        out_specs=free,
        out_shape=jax.ShapeDtypeStruct((rows + BLOCK, 2 * HEAD_WIDTH), bf16),
        scratch_shapes=[
            pltpu.VMEM((BLOCK, 2 * HEAD_WIDTH), bf16),
            pltpu.SemaphoreType.DMA((3,)),
        ],
        compiler_params=params(60),
        cost_estimate=cost(10**6, 2**19),
        name="pack",
    )(ids, keys, values)


def window_kernel(freq_ref, *rest):
    *pieces, kt_ref, v_ref, ids_ref, cos_ref, sin_ref = rest
    rows = cos_ref.shape[0]
    window = ids_ref.shape[1]
    half = ROTARY_ENTRIES // 2
    blocks = [ref if index is None else ref.at[index] for ref, index in blocks_of(pieces)]
    row_ids = jnp.concatenate(
        [ref[rows : rows + BLOCK, :rows].astype(f32)[:1] for ref in blocks], axis=1
    )
    ids_ref[...] = row_ids
    ids = jnp.broadcast_to(row_ids, (DOCS, window))
    docs = lax.broadcasted_iota(jnp.int32, (DOCS, window), 0).astype(f32) + 1.0
    before = jnp.sum(jnp.where(ids < docs, 1.0, 0.0), axis=1, keepdims=True)
    start = jnp.sum(jnp.where(ids == docs, before, 0.0), axis=0, keepdims=True)
    place = lax.broadcasted_iota(jnp.int32, (1, window), 1).astype(f32)
    angle = freq_ref[:, :1] * (place - start)
    cosine = jnp.cos(angle)
    sine = jnp.sin(angle)
    for b, ref in enumerate(blocks):
        cols = slice(b * rows, (b + 1) * rows)
        kt = jnp.transpose(ref[:rows, :HEAD_WIDTH].astype(f32))
        one, two = kt[:half], kt[half:ROTARY_ENTRIES]
        cb, sb = cosine[:, cols], sine[:, cols]
        kt_ref[:half, cols] = (one * cb - two * sb).astype(bf16)
        kt_ref[half:ROTARY_ENTRIES, cols] = (two * cb + one * sb).astype(bf16)
        kt_ref[ROTARY_ENTRIES:, cols] = kt[ROTARY_ENTRIES:].astype(bf16)
        v_ref[cols, :] = ref[:rows, HEAD_WIDTH:]
    cq, sq = cosine[:, window - rows :], sine[:, window - rows :]
    rest_rows = TILE - ROTARY_ENTRIES
    cos_ref[...] = jnp.transpose(
        jnp.concatenate([cq, cq, jnp.ones((rest_rows, rows), f32)], axis=0)
    )
    sin_ref[...] = jnp.transpose(
        jnp.concatenate([-sq, sq, jnp.zeros((rest_rows, rows), f32)], axis=0)
    )


def attention_kernel(ids_ref, cos_ref, sin_ref, kt_ref, v_ref, q_ref, gate_ref, *rest):
    out_ref, mask_ref = rest[-2:]
    rows = q_ref.shape[0]
    window = ids_ref.shape[1]
    half = ROTARY_ENTRIES // 2

    @pl.when(pl.program_id(0) == 0)
    def _():
        own = ids_ref[:, window - rows :]
        own_col = jnp.transpose(jnp.broadcast_to(own, (TILE, rows)))
        own_cols = jnp.concatenate([own_col] * (window // TILE), axis=1)
        r = lax.broadcasted_iota(jnp.int32, (rows, window), 0) + (window - rows)
        c = lax.broadcasted_iota(jnp.int32, (rows, window), 1)
        mask_ref[...] = jnp.where((own_cols == ids_ref[...]) & (c <= r), 0.0, MASKED)

    scaling = HEAD_WIDTH**-0.5
    lane = lax.broadcasted_iota(jnp.int32, (TILE, TILE), 1)
    reach = window - rows + TILE
    heads = q_ref.shape[1] // HEAD_WIDTH
    for first in range(0, rows, TILE):
        at = slice(first, first + TILE)
        keys = slice(first, first + reach)
        queries = []
        for h in range(heads):
            base = h * HEAD_WIDTH
            x = q_ref[at, base : base + TILE].astype(f32)
            swapped = jnp.where(
                lane < half, pltpu.roll(x, TILE - half, 1), pltpu.roll(x, half, 1)
            )
            rotated = ((x * cos_ref[at] + swapped * sin_ref[at]) * scaling).astype(bf16)
            tail = q_ref[at, base + TILE : base + HEAD_WIDTH] * jnp.asarray(scaling, bf16)
            queries.append(jnp.concatenate([rotated, tail], axis=1))
        scores = dot(jnp.concatenate(queries, axis=0), kt_ref[:, keys])
        weights = []
        totals = []
        for i in range(0, heads * TILE, FINE):
            row = first + i % TILE
            strip = scores[i : i + FINE] + mask_ref[row : row + FINE, keys]
            strip = jnp.exp(strip - jnp.max(strip, axis=1, keepdims=True))
            totals.append(1.0 / jnp.sum(strip, axis=1, keepdims=True))
            weights.append(strip.astype(bf16))
        mixed = dot(jnp.concatenate(weights, axis=0), v_ref[keys, :])
        for i, inverse in zip(range(0, heads * TILE, FINE), totals):
            rows_at = slice(first + i % TILE, first + i % TILE + FINE)
            cols = slice(i // TILE * HEAD_WIDTH, (i // TILE + 1) * HEAD_WIDTH)
            gate = sigmoid(gate_ref[rows_at, cols].astype(f32))
            out_ref[rows_at, cols] = (mixed[i : i + FINE] * inverse * gate).astype(bf16)


def attention_half(part, window_arrays, query, gate, partial_out=None):
    rows = query.shape[0]
    window = window_arrays[0].shape[1]
    heads = 4
    width = heads * HEAD_WIDTH
    steps = query.shape[1] // width // 2

    def at_part(i):
        return (0, part * steps + i)

    in_specs = [pl.BlockSpec(a.shape, lambda i: (0, 0)) for a in window_arrays]
    in_specs += [pl.BlockSpec((rows, width), at_part)] * 2
    args = [*window_arrays, query, gate]
    aliases = {}
    if partial_out is not None:
        aliases = {len(args): 0}
        in_specs.append(pl.BlockSpec(memory_space=pl.ANY))
        args.append(partial_out)
    return pl.pallas_call(
        attention_kernel,
        grid=(steps,),
        in_specs=in_specs,
        out_specs=pl.BlockSpec((rows, width), at_part),
        out_shape=jax.ShapeDtypeStruct(query.shape, bf16),
        scratch_shapes=[pltpu.VMEM((rows, window), f32)],
        input_output_aliases=aliases,
        compiler_params=params(28),
        cost_estimate=cost(5 * 10**9, 3 * 2**20, 10**6),
        name="attention",
    )(*args)


def up_chip(value, ranks):
    return lax.ppermute(value, "ctx", [(i, i + 2) for i in range(ranks - 2)])


def swap_cores(value, ranks):
    return lax.ppermute(value, "ctx", [(i, i ^ 1) for i in range(ranks)])


def per_device(
    segment_ids,
    attn_query,
    attention_keys,
    attention_values,
    attn_gate,
    delta_query,
    delta_key,
    update_rule_payload,
    delta_beta,
    delta_decay,
    delta_gate,
    norm_gain,
):
    ranks = lax.axis_size("ctx")
    rank = lax.axis_index("ctx")
    rows = segment_ids.shape[0]
    hops = ranks // 4
    core = rank % 2
    odd = core == 1

    ids = segment_ids.reshape(1, rows)

    own = pack(ids, attention_keys, attention_values)
    nearest = up_chip(own, ranks)

    keep_half = core.reshape(1).astype(jnp.int32)
    give_half = 1 - keep_half
    decay_rows = delta_decay.T
    local = partial(
        delta_local,
        seg_row=ids,
        key=delta_key,
        value=update_rule_payload,
        beta=delta_beta.T,
        decay=decay_rows,
    )
    reach = partial(
        delta_reach,
        seg_row=ids,
        query=delta_query,
        key=delta_key,
        decay=decay_rows,
        gate=delta_gate,
        gain=norm_gain.reshape(1, DV),
    )
    give_ma, give_solved = local(give_half, 60)
    other_ma = swap_cores(give_ma, ranks)
    nearest, give_ma = lax.optimization_barrier((nearest, give_ma))
    same = [nearest]
    for _ in range(hops - 1):
        same.append(up_chip(same[-1], ranks))
    keep_ma, keep_solved = local(keep_half, 60)
    same, keep_ma, other_ma = lax.optimization_barrier((same, keep_ma, other_ma))
    chain = [own, *same]
    other = swap_cores(
        jnp.stack([jnp.where(odd, chain[i + 1], chain[i]) for i in range(hops)]), ranks
    )

    tall = keep_ma.shape[0]
    state_like = jax.ShapeDtypeStruct((tall, DV), bf16)
    chip_map, chip_add = small_call(
        compose_kernel, "compose", [state_like] * 2, keep_half, keep_ma, other_ma, scalars=1
    )
    state = up_chip(chip_add, ranks)

    window = (2 * hops + 1) * rows
    index = jnp.arange(ROTARY_ENTRIES // 2).astype(f32)
    freq = ROPE_THETA ** (-2.0 * index / ROTARY_ENTRIES)
    freq = jnp.broadcast_to(freq[:, None], (ROTARY_ENTRIES // 2, TILE))
    window_arrays = small_call(
        window_kernel,
        "window",
        [
            jax.ShapeDtypeStruct((HEAD_WIDTH, window), bf16),
            jax.ShapeDtypeStruct((window, HEAD_WIDTH), bf16),
            jax.ShapeDtypeStruct((1, window), f32),
            jax.ShapeDtypeStruct((rows, TILE), f32),
            jax.ShapeDtypeStruct((rows, TILE), f32),
        ],
        freq,
        own,
        *same,
        other,
    )
    kt, v_all, window_ids, cosine, sine = window_arrays
    window_arrays = (window_ids, cosine, sine, kt, v_all)
    attn_mixed = attention_half(0, window_arrays, attn_query, attn_gate)
    give_solved, chip_add = lax.optimization_barrier((give_solved, chip_add))
    give_rows = reach(give_half, solved=give_solved)
    state, attn_mixed, give_rows = lax.optimization_barrier((state, attn_mixed, give_rows))
    leaving = chip_add
    for _ in range(hops - 1):
        (leaving,) = small_call(relay_kernel, "relay", [state_like], chip_map, chip_add, state)
        state = up_chip(leaving, ranks)
    attn_mixed, keep_solved, leaving = lax.optimization_barrier((attn_mixed, keep_solved, leaving))
    attn_mixed = attention_half(1, window_arrays, attn_query, attn_gate, attn_mixed)
    keep_rows = reach(keep_half, solved=keep_solved)
    state, attn_mixed, keep_rows = lax.optimization_barrier((state, attn_mixed, keep_rows))

    final_like = jax.ShapeDtypeStruct((tall - BLOCK, DV), bf16)
    keep_state, pass_state = small_call(
        arrive_kernel, "arrive", [final_like] * 2, keep_half, keep_ma, other_ma, state, scalars=1
    )
    give_state = swap_cores(pass_state, ranks)

    delta_mixed = delta_out(keep_half, *keep_rows, keep_state)
    delta_mixed = delta_out(give_half, *give_rows, give_state, delta_mixed)
    return (attn_mixed, delta_mixed)


def solution(mesh):
    rows = P(("dp", "ctx"))
    wide = P(("dp", "ctx"), None)
    return jax.shard_map(
        per_device,
        mesh=mesh,
        in_specs=(rows,) + (wide,) * 10 + (P(),),
        out_specs=(wide, wide),
        check_vma=False,
    )
```

```python
from functools import partial

import jax
import jax.numpy as jnp
from jax import lax
from jax.experimental import pallas as pl
from jax.experimental.pallas import tpu as pltpu
from jax.sharding import PartitionSpec as P

HEAD_WIDTH = 256
ROTARY_ENTRIES = 64
DK = 128
DV = 128
DOCS = 8
ROPE_THETA = 10000000.0
LOG2E = 1.4426950408889634
MASKED = -1e30
EPS = 1e-6
TILE = 128
MIB = 1024 * 1024

f32 = jnp.float32
bf16 = jnp.bfloat16


def dot(a, b, precision=None):
    return jnp.dot(a, b, preferred_element_type=f32, precision=precision)


def params(mib=16):
    return pltpu.CompilerParams(vmem_limit_bytes=mib * MIB)


def sigmoid(x):
    return 0.5 * jnp.tanh(0.5 * x) + 0.5


def cost(flops, nbytes, exps=0):
    return pl.CostEstimate(flops=flops, bytes_accessed=nbytes, transcendentals=exps)


BLOCK = 16
MERGES = 3
STRIP = 32
FINE = 16
DONE = object()


def odd_rows(m, b):
    return jnp.concatenate([m[i + b : i + 2 * b] for i in range(0, TILE, 2 * b)], axis=0)


def interleave(even, odd, b):
    parts = []
    for i in range(0, TILE // 2, b):
        parts += [even[i : i + b], odd[i : i + b]]
    return jnp.concatenate(parts, axis=0)


def even_rows(m, b):
    return jnp.concatenate([m[i : i + b] for i in range(0, TILE, 2 * b)], axis=0)


def fold(m):
    row = lax.broadcasted_iota(jnp.int32, (BLOCK, TILE), 0)
    lane = lax.broadcasted_iota(jnp.int32, (BLOCK, TILE), 1)
    group = lane // BLOCK
    z = jnp.where(group == 0, m[:BLOCK], 0.0)
    for r in range(1, TILE // BLOCK):
        z = jnp.where(group == r, m[r * BLOCK : (r + 1) * BLOCK], z)
    return jnp.where(row > lax.rem(lane, BLOCK), z, 0.0).astype(bf16)


def fill_spread(spread_ref):
    row = lax.broadcasted_iota(jnp.int32, (TILE, TILE), 0)
    lane = lax.broadcasted_iota(jnp.int32, (TILE, TILE), 1)
    base = row - lane // BLOCK * BLOCK
    for k in range(BLOCK - 1):
        spread_ref[:, k * TILE : (k + 1) * TILE] = jnp.where(base == k, 1.0, 0.0).astype(bf16)


def block_inverses(folded, spread_ref):
    row = lax.broadcasted_iota(jnp.int32, (BLOCK, TILE), 0)
    lane = lax.broadcasted_iota(jnp.int32, (BLOCK, TILE), 1)
    group = lane // BLOCK
    within = lax.rem(lane, BLOCK)
    spread = dot(jnp.concatenate(folded, axis=0), spread_ref[...])
    unit = jnp.where(row == within, 1.0, 0.0)
    small = BLOCK // 2
    out = []
    tops = [unit[:small]] * len(folded)
    lows = [unit[small:]] * len(folded)
    for k in range(BLOCK - 1):
        at = slice(k * TILE, (k + 1) * TILE)
        for i in range(len(folded)):
            rows = spread[i * BLOCK : (i + 1) * BLOCK, at]
            source = tops[i][k : k + 1] if k < small else lows[i][k - small : k - small + 1]
            if k < small - 1:
                tops[i] = tops[i] + rows[:small] * source
            lows[i] = lows[i] + rows[small:] * source
    for top, low in zip(tops, lows):
        x = jnp.where(row > within, jnp.concatenate([top, low], axis=0), 0.0)
        out.append(
            jnp.concatenate(
                [jnp.where(group == r, x, 0.0) for r in range(TILE // BLOCK)], axis=0
            ).astype(bf16)
        )
    return out


def setup(half_ref, seg_ref, decay_ref, n, mask_ref, crow_ref, ccol_ref, first_ref, beta_ref=None):
    rows = seg_ref.shape[1]
    seg_row = seg_ref[...].astype(f32) + 1.0
    seg_col = jnp.transpose(jnp.broadcast_to(seg_row, (TILE, rows)))
    seg_cols = jnp.concatenate([seg_col] * (rows // TILE), axis=1)
    r = lax.broadcasted_iota(jnp.int32, (rows, rows), 0)
    c = lax.broadcasted_iota(jnp.int32, (rows, rows), 1)
    mask_ref[...] = jnp.where((seg_cols == seg_row) & (r >= c), 0.0, MASKED)
    first_ref[...] = jnp.where(seg_col == seg_row[:, :1], 1.0, 0.0)
    base = pl.multiple_of(half_ref[0] * n, n)
    decay = decay_ref[pl.ds(base, n), :] * LOG2E
    high = decay.astype(bf16)
    rest = decay - high.astype(f32)
    middle = rest.astype(bf16)
    parts = [high, middle, (rest - middle.astype(f32)).astype(bf16)]
    parts = jnp.concatenate([p.astype(f32) for p in parts], axis=0).astype(bf16)
    sums = dot(parts, jnp.where(r <= c, 1.0, 0.0).astype(bf16))
    cumulative = sums[:n] + sums[n : 2 * n] + sums[2 * n :]
    crow_ref[...] = cumulative
    beta = jnp.zeros((n, rows), f32) if beta_ref is None else beta_ref[pl.ds(base, n), :]
    fill = jnp.zeros((TILE - 2 * n, rows), f32)
    ccol_ref[...] = jnp.transpose(jnp.concatenate([cumulative, beta, fill], axis=0))
    return seg_row


def column(ref, at, lane, width):
    one = jnp.broadcast_to(ref[at, lane : lane + 1], (STRIP, TILE))
    return one if width == TILE else jnp.concatenate([one] * (width // TILE), axis=1)


def pipeline(phases, count):
    for slot in range(count + len(phases) - 1):
        running = [
            phase(slot - i) for i, phase in enumerate(phases) if 0 <= slot - i < count
        ]
        while running:
            running = [p for p in running if next(p, DONE) is not DONE]


def delta_local_kernel(
    half_ref,
    seg_ref,
    k_ref,
    v_ref,
    beta_ref,
    decay_ref,
    map_add_ref,
    solved_ref,
    mask_ref,
    level_ref,
    spread_ref,
    crow_ref,
    ccol_ref,
    first_ref,
):
    rows = k_ref.shape[0]
    n = v_ref.shape[1] // DV
    fill_spread(spread_ref)
    seg_row = setup(
        half_ref, seg_ref, decay_ref, n, mask_ref, crow_ref, ccol_ref, first_ref, beta_ref
    )
    map_add_ref[n * DK :, :] = jnp.broadcast_to(seg_row, (BLOCK, rows)).astype(bf16)
    r = lax.broadcasted_iota(jnp.int32, (TILE, TILE), 0)
    c = lax.broadcasted_iota(jnp.int32, (TILE, TILE), 1)
    eye = jnp.where(r == c, 1.0, 0.0)
    for level in range(MERGES):
        b = BLOCK << level
        sibling = jnp.where(r // b == c // b + 1, 1.0, 0.0)
        level_ref[level] = odd_rows(sibling, b).astype(bf16)
    strips = [slice(i, i + STRIP) for i in range(0, rows, STRIP)]
    pairs = [
        [dict(h=2 * kk + j, d=[], right=[]) for j in range(2)] for kk in range(n // 2)
    ]

    def elementwise(kk):
        pair = pairs[kk]
        k_raw = k_ref[:, kk * DK : (kk + 1) * DK]
        kt = jnp.transpose(k_raw.astype(f32))
        rk_row = lax.rsqrt(jnp.sum(kt * kt, axis=0, keepdims=True) + EPS)
        ktb = kt.astype(bf16)
        upper = dot(k_raw[:TILE], ktb[:, :TILE])
        lower = dot(k_raw[TILE:], ktb)
        yield
        for at in strips:
            raw, start = (upper, at.start) if at.start < TILE else (lower, at.start - TILE)
            width = raw.shape[1]
            kf = k_raw[at].astype(f32)
            rk = lax.rsqrt(jnp.sum(kf * kf, axis=1, keepdims=True) + EPS)
            kn = kf * rk
            gram = raw[start : start + STRIP] * rk_row[:, :width] * -rk
            for w in pair:
                h = w["h"]
                cc = column(ccol_ref, at, h, width)
                bt = column(ccol_ref, at, n + h, width)
                span = jnp.exp2(cc - crow_ref[h : h + 1, :width] + mask_ref[at, :width])
                w["d"].append(span * bt * gram)
                cc, bt = cc[:, :TILE], bt[:, :TILE]
                entry = jnp.exp2(cc) * first_ref[at]
                value = v_ref[at, h * DV : (h + 1) * DV].astype(f32)
                w["right"].append(
                    jnp.concatenate([bt * entry * kn, bt * value], axis=1).astype(bf16)
                )
                if at.stop == rows:
                    w["last"] = entry[STRIP - 1 :]
                    w["kd"] = (kt * (rk_row * span[STRIP - 1 :])).astype(bf16)
            yield
        top = TILE // STRIP
        for w in pair:
            d11 = jnp.concatenate(w["d"][:top], axis=0)
            d2 = jnp.concatenate(w["d"][top:], axis=0)
            blocks = [d11, d2[:, TILE:]]
            w["folded"] = [fold(m) for m in blocks]
            w["d"] = [m.astype(bf16) for m in blocks]
            w["d21"] = d2[:, :TILE].astype(bf16)
            w["right"] = jnp.concatenate(w["right"], axis=0)
        yield

    def invert():
        work = [w for pair in pairs for w in pair]
        mats = [m for w in work for m in w["d"]]
        inverses = block_inverses([z for w in work for z in w["folded"]], spread_ref)
        zeros = jnp.zeros((TILE // 2, TILE), bf16)
        for level in range(MERGES):
            b = BLOCK << level
            keep = level_ref[level]
            picked = [odd_rows(m, b) * keep for m in mats]
            ys = [(p.astype(f32) + dot(p, x)).astype(bf16) for p, x in zip(picked, inverses)]
            odds = [odd_rows(x, b) for x in inverses]
            odds = [
                x + (y.astype(f32) + dot(x, interleave(zeros, y, b))).astype(bf16)
                for x, y in zip(odds, ys)
            ]
            inverses = [interleave(even_rows(x, b), o, b) for x, o in zip(inverses, odds)]
        for i, w in enumerate(work):
            w["x"] = inverses[2 * i : 2 * i + 2]

    def finish(kk):
        pair = pairs[kk]
        for w in pair:
            w["u1"] = add_strips(w["right"][:TILE], dot(w["x"][0], w["right"][:TILE]))
        yield
        for w in pair:
            w["r2"] = add_strips(w["right"][TILE:], dot(w["d21"], w["u1"]))
        yield
        for w in pair:
            u2 = add_strips(w["r2"], dot(w["x"][1], w["r2"]))
            w["u"] = jnp.concatenate([w["u1"], u2], axis=0)
            solved_ref[w["h"] * rows : (w["h"] + 1) * rows, :] = w["u"]
        yield
        for w in pair:
            h = w["h"]
            ma = dot(w["kd"], w["u"])
            for start in range(0, DK, STRIP):
                part = ma[start : start + STRIP]
                kept = w["last"] * eye[start : start + STRIP]
                map_add_ref[h * DK + start : h * DK + start + STRIP, :] = jnp.concatenate(
                    [kept - part[:, :DK], part[:, DK:]], axis=1
                ).astype(bf16)
            yield

    pipeline([elementwise], n // 2)
    invert()
    pipeline([finish], n // 2)


def add_strips(a, b):
    return jnp.concatenate(
        [
            (a[i : i + STRIP].astype(f32) + b[i : i + STRIP]).astype(bf16)
            for i in range(0, a.shape[0], STRIP)
        ],
        axis=0,
    )


def delta_reach_kernel(
    half_ref,
    seg_ref,
    q_ref,
    k_ref,
    decay_ref,
    solved_ref,
    gate_ref,
    gain_ref,
    reach_ref,
    inner_ref,
    factor_ref,
    mask_ref,
    crow_ref,
    ccol_ref,
    first_ref,
):
    rows = k_ref.shape[0]
    n = reach_ref.shape[1] // DK
    setup(half_ref, seg_ref, decay_ref, n, mask_ref, crow_ref, ccol_ref, first_ref)
    strips = [slice(i, i + STRIP) for i in range(0, rows, STRIP)]
    pairs = [
        [dict(h=2 * kk + j, p=[], scaled=[]) for j in range(2)] for kk in range(n // 2)
    ]

    def elementwise(kk):
        pair = pairs[kk]
        cols = slice(kk * DK, (kk + 1) * DK)
        k_raw = k_ref[:, cols]
        q_raw = q_ref[:, cols]
        kt = jnp.transpose(k_raw.astype(f32))
        rk_row = lax.rsqrt(jnp.sum(kt * kt, axis=0, keepdims=True) + EPS)
        ktb = kt.astype(bf16)
        upper = dot(q_raw[:TILE], ktb[:, :TILE])
        lower = dot(q_raw[TILE:], ktb)
        yield
        for at in strips:
            raw, start = (upper, at.start) if at.start < TILE else (lower, at.start - TILE)
            width = raw.shape[1]
            qf = q_raw[at].astype(f32)
            rq = lax.rsqrt(jnp.sum(qf * qf, axis=1, keepdims=True) + EPS) * DK**-0.5
            qn = qf * rq
            probe = raw[start : start + STRIP] * rk_row[:, :width] * rq
            for w in pair:
                h = w["h"]
                cc = column(ccol_ref, at, h, width)
                span = jnp.exp2(cc - crow_ref[h : h + 1, :width] + mask_ref[at, :width])
                w["p"].append((span * probe).astype(bf16))
                entry = jnp.exp2(cc[:, :TILE]) * first_ref[at]
                w["scaled"].append((entry * qn).astype(bf16))
                cols = slice(h * DV, (h + 1) * DV)
                gate = gate_ref[at, cols].astype(f32)
                factor_ref[at, cols] = gate * sigmoid(gate) * gain_ref[...]
            yield

    def finish(kk):
        top = TILE // STRIP
        for w in pairs[kk]:
            h = w["h"]
            u = solved_ref[h * rows : (h + 1) * rows, :]
            upper = dot(jnp.concatenate(w["p"][:top], axis=0), u[:TILE])
            lower = dot(jnp.concatenate(w["p"][top:], axis=0), u)
            for at, scaled in zip(strips, w["scaled"]):
                pu = upper[at.start :] if at.start < TILE else lower[at.start - TILE :]
                pu = pu[:STRIP]
                reach_ref[at, h * DK : (h + 1) * DK] = (
                    scaled.astype(f32) - pu[:, :DK]
                ).astype(bf16)
                inner_ref[at, h * DV : (h + 1) * DV] = pu[:, DK:]
            yield

    pipeline([elementwise, finish], n // 2)


def half_call(kernel, name, mib, half, operands, outs, scratch):
    def at_half(i, s):
        return (0, s[0])

    def at_zero(i, s):
        return (0, 0)

    specs = []
    args = []
    for a in operands:
        if isinstance(a, tuple):
            (a,) = a
            specs.append(pl.BlockSpec((a.shape[0], a.shape[1] // 2), at_half))
        else:
            specs.append(pl.BlockSpec(a.shape, at_zero))
        args.append(a)
    return pl.pallas_call(
        kernel,
        grid_spec=pltpu.PrefetchScalarGridSpec(
            num_scalar_prefetch=1,
            grid=(1,),
            in_specs=specs,
            out_specs=[pl.BlockSpec(o.shape, at_zero) for o in outs],
            scratch_shapes=scratch,
        ),
        out_shape=outs,
        compiler_params=params(mib),
        cost_estimate=cost(4 * 10**9, 3 * 2**20),
        name=name,
    )(half, *args)


def setup_scratch(rows, n):
    return [
        pltpu.VMEM((rows, rows), f32),
        pltpu.VMEM((n, rows), f32),
        pltpu.VMEM((rows, TILE), f32),
        pltpu.VMEM((rows, TILE), f32),
    ]


def delta_local(half, mib, seg_row, key, value, beta, decay):
    rows = key.shape[0]
    n = value.shape[1] // DV // 2
    mask, *others = setup_scratch(rows, n)
    return half_call(
        delta_local_kernel,
        "delta_local",
        mib,
        half,
        [seg_row, (key,), (value,), beta, decay],
        [
            jax.ShapeDtypeStruct((n * DK + BLOCK, DK + DV), bf16),
            jax.ShapeDtypeStruct((n * rows, DK + DV), bf16),
        ],
        [
            mask,
            pltpu.VMEM((MERGES, TILE // 2, TILE), bf16),
            pltpu.VMEM((TILE, (BLOCK - 1) * TILE), bf16),
            *others,
        ],
    )


def delta_reach(half, seg_row, query, key, decay, gate, gain, solved):
    rows = key.shape[0]
    n = solved.shape[0] // rows
    return half_call(
        delta_reach_kernel,
        "delta_reach",
        20,
        half,
        [seg_row, (query,), (key,), decay, solved, (gate,), gain],
        [
            jax.ShapeDtypeStruct((rows, n * DK), bf16),
            jax.ShapeDtypeStruct((rows, n * DV), f32),
            jax.ShapeDtypeStruct((rows, n * DV), f32),
        ],
        setup_scratch(rows, n),
    )


def ids_of(ref):
    end = ref.shape[0] - BLOCK
    return ref[end : end + BLOCK, :].astype(f32)[:1]


def put_id(ref, value):
    end = ref.shape[0] - BLOCK
    ref[end:, :] = jnp.broadcast_to(value, (BLOCK, ref.shape[1])).astype(bf16)


def matching(a, b):
    return jnp.where(a == b, 1.0, 0.0)


def compose_kernel(core_ref, mine_ref, other_ref, map_ref, add_ref):
    odd = core_ref[0] == 1
    mine_ids, other_ids = ids_of(mine_ref), ids_of(other_ref)
    early_ids = jnp.where(odd, other_ids, mine_ids)
    late_ids = jnp.where(odd, mine_ids, other_ids)
    across = matching(early_ids[:, -1:], late_ids[:, :1])
    put_id(map_ref, early_ids[:, :1])
    put_id(add_ref, late_ids[:, -1:])
    for h in range(mine_ref.shape[0] // DK):
        at = slice(h * DK, (h + 1) * DK)
        mine, other = mine_ref[at], other_ref[at]
        early, late = jnp.where(odd, other, mine), jnp.where(odd, mine, other)
        both = dot(late[:, :DK], early) * across
        map_ref[at] = both[:, :DK].astype(bf16)
        add_ref[at] = (both[:, DK:] + late[:, DK:].astype(f32)).astype(bf16)


def relay_kernel(map_ref, add_ref, state_ref, out_ref):
    into = matching(ids_of(state_ref), ids_of(map_ref))
    put_id(out_ref, ids_of(add_ref))
    for h in range(map_ref.shape[0] // DK):
        at = slice(h * DK, (h + 1) * DK)
        out_ref[at] = (dot(map_ref[at], state_ref[at]) * into + add_ref[at].astype(f32)).astype(bf16)


def arrive_kernel(core_ref, mine_ref, other_ref, state_ref, keep_ref, give_ref):
    odd = core_ref[0] == 1
    mine_ids, other_ids = ids_of(mine_ref), ids_of(other_ref)
    early_ids = jnp.where(odd, other_ids, mine_ids)
    late_ids = jnp.where(odd, mine_ids, other_ids)
    across = matching(early_ids[:, -1:], late_ids[:, :1])
    into = matching(ids_of(state_ref), early_ids[:, :1])
    for h in range(keep_ref.shape[0] // DK):
        at = slice(h * DK, (h + 1) * DK)
        early = jnp.where(odd, other_ref[at], mine_ref[at])
        first = (state_ref[at].astype(f32) * into).astype(bf16)
        second = (
            (dot(early[:, :DK], first) + early[:, DK:].astype(f32)) * across
        ).astype(bf16)
        keep_ref[at] = jnp.where(odd, second, first)
        give_ref[at] = jnp.where(odd, first, second)


SMEM = pl.BlockSpec(memory_space=pltpu.SMEM)
VMEM = pl.BlockSpec(memory_space=pltpu.VMEM)


def small_call(kernel, name, outs, *args, scalars=0, mib=16):
    return pl.pallas_call(
        kernel,
        in_specs=[SMEM] * scalars + [VMEM] * (len(args) - scalars),
        out_specs=[VMEM] * len(outs),
        out_shape=outs,
        compiler_params=params(mib),
        cost_estimate=cost(10**8, 2**20),
        name=name,
    )(*args)


def delta_out_kernel(half_ref, reach_ref, inner_ref, factor_ref, state_ref, *rest):
    out_hbm, out_ref, sem = rest[-3:]
    n = state_ref.shape[0] // DK
    width = 2 * DV
    copies = []
    for h in range(n):
        cols = slice(h * DV, (h + 1) * DV)
        carried = dot(reach_ref[:, cols], state_ref[h * DK : (h + 1) * DK])
        for i in range(0, carried.shape[0], STRIP):
            at = slice(i, i + STRIP)
            out = inner_ref[at, cols] + carried[at]
            spread = lax.rsqrt(jnp.mean(out * out, axis=1, keepdims=True) + EPS)
            out_ref[at, cols] = (out * spread * factor_ref[at, cols]).astype(bf16)
        if h % 2 == 1:
            start = (h - 1) * DV
            target = pl.multiple_of(half_ref[0] * (n * DV) + start, width)
            copies.append(
                pltpu.make_async_copy(
                    out_ref.at[:, pl.ds(start, width)],
                    out_hbm.at[:, pl.ds(target, width)],
                    sem.at[h // 2],
                )
            )
            copies[-1].start()
    for copy in copies:
        copy.wait()


def delta_out(half, reach, inner, factor, state, partial_out=None):
    rows = reach.shape[0]
    n = state.shape[0] // DK
    in_specs = [SMEM] + [VMEM] * 4
    args = [half, reach, inner, factor, state]
    aliases = {}
    if partial_out is not None:
        aliases = {len(args): 0}
        in_specs.append(pl.BlockSpec(memory_space=pl.ANY))
        args.append(partial_out)
    return pl.pallas_call(
        delta_out_kernel,
        in_specs=in_specs,
        out_specs=pl.BlockSpec(memory_space=pl.ANY),
        out_shape=jax.ShapeDtypeStruct((rows, 2 * n * DV), bf16),
        scratch_shapes=[pltpu.VMEM((rows, n * DV), bf16), pltpu.SemaphoreType.DMA((n // 2,))],
        input_output_aliases=aliases,
        compiler_params=params(),
        cost_estimate=cost(10**8, 3 * 2**20),
        name="delta_out",
    )(*args)


def blocks_of(pieces):
    own, *same, other = pieces
    order = [(own, None)]
    for i, ref in enumerate(same):
        order += [(other, i), (ref, None)]
    return order[::-1]


def pack_kernel(seg_ref, key_ref, value_ref, out_ref):
    rows = key_ref.shape[0]
    ids = seg_ref[...].astype(f32) + 1.0
    out_ref[:rows, :HEAD_WIDTH] = key_ref[...]
    out_ref[:rows, HEAD_WIDTH:] = value_ref[...]
    out_ref[rows:, :rows] = jnp.broadcast_to(ids, (BLOCK, rows)).astype(bf16)
    out_ref[rows:, rows:] = jnp.zeros((BLOCK, 2 * HEAD_WIDTH - rows), bf16)


def window_kernel(freq_ref, *rest):
    *pieces, kt_ref, v_ref, ids_ref, cos_ref, sin_ref = rest
    rows = cos_ref.shape[0]
    window = ids_ref.shape[1]
    half = ROTARY_ENTRIES // 2
    blocks = [ref if index is None else ref.at[index] for ref, index in blocks_of(pieces)]
    row_ids = jnp.concatenate(
        [ref[rows : rows + BLOCK, :rows].astype(f32)[:1] for ref in blocks], axis=1
    )
    ids_ref[...] = row_ids
    ids = jnp.broadcast_to(row_ids, (DOCS, window))
    docs = lax.broadcasted_iota(jnp.int32, (DOCS, window), 0).astype(f32) + 1.0
    before = jnp.sum(jnp.where(ids < docs, 1.0, 0.0), axis=1, keepdims=True)
    start = jnp.sum(jnp.where(ids == docs, before, 0.0), axis=0, keepdims=True)
    place = lax.broadcasted_iota(jnp.int32, (1, window), 1).astype(f32)
    angle = freq_ref[:, :1] * (place - start)
    cosine = jnp.cos(angle)
    sine = jnp.sin(angle)
    for b, ref in enumerate(blocks):
        cols = slice(b * rows, (b + 1) * rows)
        kt = jnp.transpose(ref[:rows, :HEAD_WIDTH].astype(f32))
        one, two = kt[:half], kt[half:ROTARY_ENTRIES]
        cb, sb = cosine[:, cols], sine[:, cols]
        kt_ref[:half, cols] = (one * cb - two * sb).astype(bf16)
        kt_ref[half:ROTARY_ENTRIES, cols] = (two * cb + one * sb).astype(bf16)
        kt_ref[ROTARY_ENTRIES:, cols] = kt[ROTARY_ENTRIES:].astype(bf16)
        v_ref[cols, :] = ref[:rows, HEAD_WIDTH:]
    cq, sq = cosine[:, window - rows :], sine[:, window - rows :]
    rest_rows = TILE - ROTARY_ENTRIES
    cos_ref[...] = jnp.transpose(
        jnp.concatenate([cq, cq, jnp.ones((rest_rows, rows), f32)], axis=0)
    )
    sin_ref[...] = jnp.transpose(
        jnp.concatenate([-sq, sq, jnp.zeros((rest_rows, rows), f32)], axis=0)
    )


def attention_kernel(ids_ref, cos_ref, sin_ref, kt_ref, v_ref, q_ref, gate_ref, *rest):
    out_ref, mask_ref = rest[-2:]
    rows = q_ref.shape[0]
    window = ids_ref.shape[1]
    half = ROTARY_ENTRIES // 2

    @pl.when(pl.program_id(0) == 0)
    def _():
        own = ids_ref[:, window - rows :]
        own_col = jnp.transpose(jnp.broadcast_to(own, (TILE, rows)))
        own_cols = jnp.concatenate([own_col] * (window // TILE), axis=1)
        r = lax.broadcasted_iota(jnp.int32, (rows, window), 0) + (window - rows)
        c = lax.broadcasted_iota(jnp.int32, (rows, window), 1)
        mask_ref[...] = jnp.where((own_cols == ids_ref[...]) & (c <= r), 0.0, MASKED)

    scaling = HEAD_WIDTH**-0.5
    lane = lax.broadcasted_iota(jnp.int32, (TILE, TILE), 1)
    reach = window - rows + TILE
    heads = q_ref.shape[1] // HEAD_WIDTH
    for first in range(0, rows, TILE):
        at = slice(first, first + TILE)
        keys = slice(first, first + reach)
        queries = []
        for h in range(heads):
            base = h * HEAD_WIDTH
            x = q_ref[at, base : base + TILE].astype(f32)
            swapped = jnp.where(
                lane < half, pltpu.roll(x, TILE - half, 1), pltpu.roll(x, half, 1)
            )
            rotated = ((x * cos_ref[at] + swapped * sin_ref[at]) * scaling).astype(bf16)
            tail = q_ref[at, base + TILE : base + HEAD_WIDTH] * jnp.asarray(scaling, bf16)
            queries.append(jnp.concatenate([rotated, tail], axis=1))
        scores = dot(jnp.concatenate(queries, axis=0), kt_ref[:, keys])
        weights = []
        totals = []
        for i in range(0, heads * TILE, FINE):
            row = first + i % TILE
            strip = scores[i : i + FINE] + mask_ref[row : row + FINE, keys]
            strip = jnp.exp(strip - jnp.max(strip, axis=1, keepdims=True))
            totals.append(1.0 / jnp.sum(strip, axis=1, keepdims=True))
            weights.append(strip.astype(bf16))
        mixed = dot(jnp.concatenate(weights, axis=0), v_ref[keys, :])
        for i, inverse in zip(range(0, heads * TILE, FINE), totals):
            rows_at = slice(first + i % TILE, first + i % TILE + FINE)
            cols = slice(i // TILE * HEAD_WIDTH, (i // TILE + 1) * HEAD_WIDTH)
            gate = sigmoid(gate_ref[rows_at, cols].astype(f32))
            out_ref[rows_at, cols] = (mixed[i : i + FINE] * inverse * gate).astype(bf16)


def attention_half(part, window_arrays, query, gate, partial_out=None):
    rows = query.shape[0]
    window = window_arrays[0].shape[1]
    heads = 4
    width = heads * HEAD_WIDTH
    steps = query.shape[1] // width // 2

    def at_part(i):
        return (0, part * steps + i)

    in_specs = [pl.BlockSpec(a.shape, lambda i: (0, 0)) for a in window_arrays]
    in_specs += [pl.BlockSpec((rows, width), at_part)] * 2
    args = [*window_arrays, query, gate]
    aliases = {}
    if partial_out is not None:
        aliases = {len(args): 0}
        in_specs.append(pl.BlockSpec(memory_space=pl.ANY))
        args.append(partial_out)
    return pl.pallas_call(
        attention_kernel,
        grid=(steps,),
        in_specs=in_specs,
        out_specs=pl.BlockSpec((rows, width), at_part),
        out_shape=jax.ShapeDtypeStruct(query.shape, bf16),
        scratch_shapes=[pltpu.VMEM((rows, window), f32)],
        input_output_aliases=aliases,
        compiler_params=params(28),
        cost_estimate=cost(5 * 10**9, 3 * 2**20, 10**6),
        name="attention",
    )(*args)


def up_chip(value, ranks):
    return lax.ppermute(value, "ctx", [(i, i + 2) for i in range(ranks - 2)])


def swap_cores(value, ranks):
    return lax.ppermute(value, "ctx", [(i, i ^ 1) for i in range(ranks)])


def per_device(
    segment_ids,
    attn_query,
    attention_keys,
    attention_values,
    attn_gate,
    delta_query,
    delta_key,
    update_rule_payload,
    delta_beta,
    delta_decay,
    delta_gate,
    norm_gain,
):
    ranks = lax.axis_size("ctx")
    rank = lax.axis_index("ctx")
    rows = segment_ids.shape[0]
    hops = ranks // 4
    core = rank % 2
    odd = core == 1

    ids = segment_ids.reshape(1, rows)

    (own,) = small_call(
        pack_kernel,
        "pack",
        [jax.ShapeDtypeStruct((rows + BLOCK, 2 * HEAD_WIDTH), bf16)],
        ids,
        attention_keys,
        attention_values,
        mib=60,
    )
    nearest = up_chip(own, ranks)

    keep_half = core.reshape(1).astype(jnp.int32)
    give_half = 1 - keep_half
    decay_rows = delta_decay.T
    local = partial(
        delta_local,
        seg_row=ids,
        key=delta_key,
        value=update_rule_payload,
        beta=delta_beta.T,
        decay=decay_rows,
    )
    reach = partial(
        delta_reach,
        seg_row=ids,
        query=delta_query,
        key=delta_key,
        decay=decay_rows,
        gate=delta_gate,
        gain=norm_gain.reshape(1, DV),
    )
    give_ma, give_solved = local(give_half, 20)
    other_ma = swap_cores(give_ma, ranks)
    nearest, give_ma = lax.optimization_barrier((nearest, give_ma))
    same = [nearest]
    for _ in range(hops - 1):
        same.append(up_chip(same[-1], ranks))
    keep_ma, keep_solved = local(keep_half, 20)
    same, keep_ma, other_ma = lax.optimization_barrier((same, keep_ma, other_ma))
    chain = [own, *same]
    other = swap_cores(
        jnp.stack([jnp.where(odd, chain[i + 1], chain[i]) for i in range(hops)]), ranks
    )

    tall = keep_ma.shape[0]
    state_like = jax.ShapeDtypeStruct((tall, DV), bf16)
    chip_map, chip_add = small_call(
        compose_kernel, "compose", [state_like] * 2, keep_half, keep_ma, other_ma, scalars=1
    )
    state = up_chip(chip_add, ranks)

    window = (2 * hops + 1) * rows
    index = jnp.arange(ROTARY_ENTRIES // 2).astype(f32)
    freq = ROPE_THETA ** (-2.0 * index / ROTARY_ENTRIES)
    freq = jnp.broadcast_to(freq[:, None], (ROTARY_ENTRIES // 2, TILE))
    window_arrays = small_call(
        window_kernel,
        "window",
        [
            jax.ShapeDtypeStruct((HEAD_WIDTH, window), bf16),
            jax.ShapeDtypeStruct((window, HEAD_WIDTH), bf16),
            jax.ShapeDtypeStruct((1, window), f32),
            jax.ShapeDtypeStruct((rows, TILE), f32),
            jax.ShapeDtypeStruct((rows, TILE), f32),
        ],
        freq,
        own,
        *same,
        other,
    )
    kt, v_all, window_ids, cosine, sine = window_arrays
    window_arrays = (window_ids, cosine, sine, kt, v_all)
    attn_mixed = attention_half(0, window_arrays, attn_query, attn_gate)
    give_solved, chip_add = lax.optimization_barrier((give_solved, chip_add))
    give_rows = reach(give_half, solved=give_solved)
    state, attn_mixed, give_rows = lax.optimization_barrier((state, attn_mixed, give_rows))
    leaving = chip_add
    for _ in range(hops - 1):
        (leaving,) = small_call(relay_kernel, "relay", [state_like], chip_map, chip_add, state)
        state = up_chip(leaving, ranks)
    attn_mixed, keep_solved, leaving = lax.optimization_barrier((attn_mixed, keep_solved, leaving))
    attn_mixed = attention_half(1, window_arrays, attn_query, attn_gate, attn_mixed)
    keep_rows = reach(keep_half, solved=keep_solved)
    state, attn_mixed, keep_rows = lax.optimization_barrier((state, attn_mixed, keep_rows))

    final_like = jax.ShapeDtypeStruct((tall - BLOCK, DV), bf16)
    keep_state, pass_state = small_call(
        arrive_kernel, "arrive", [final_like] * 2, keep_half, keep_ma, other_ma, state, scalars=1
    )
    give_state = swap_cores(pass_state, ranks)

    delta_mixed = delta_out(keep_half, *keep_rows, keep_state)
    delta_mixed = delta_out(give_half, *give_rows, give_state, delta_mixed)
    return (attn_mixed, delta_mixed)


def solution(mesh):
    rows = P(("dp", "ctx"))
    wide = P(("dp", "ctx"), None)
    return jax.shard_map(
        per_device,
        mesh=mesh,
        in_specs=(rows,) + (wide,) * 10 + (P(),),
        out_specs=(wide, wide),
        check_vma=False,
    )
```

```python
from functools import partial

import jax
import jax.numpy as jnp
from jax import lax
from jax.experimental import pallas as pl
from jax.experimental.pallas import tpu as pltpu
from jax.sharding import PartitionSpec as P

HEAD_WIDTH = 256
ROTARY_ENTRIES = 64
DK = 128
DV = 128
DOCS = 8
ROPE_THETA = 10000000.0
LOG2E = 1.4426950408889634
MASKED = -1e30
EPS = 1e-6
TILE = 128
MIB = 1024 * 1024

f32 = jnp.float32
bf16 = jnp.bfloat16


def dot(a, b, precision=None):
    return jnp.dot(a, b, preferred_element_type=f32, precision=precision)


def params(mib=16):
    return pltpu.CompilerParams(vmem_limit_bytes=mib * MIB)


def sigmoid(x):
    return 0.5 * jnp.tanh(0.5 * x) + 0.5


def cost(flops, nbytes, exps=0):
    return pl.CostEstimate(
        flops=flops // 10**4, bytes_accessed=nbytes // 10**4, transcendentals=exps // 10**4
    )


BLOCK = 16
MERGES = 3
STRIP = 32
FINE = 16
DONE = object()


def odd_rows(m, b):
    return jnp.concatenate([m[i + b : i + 2 * b] for i in range(0, TILE, 2 * b)], axis=0)


def interleave(even, odd, b):
    parts = []
    for i in range(0, TILE // 2, b):
        parts += [even[i : i + b], odd[i : i + b]]
    return jnp.concatenate(parts, axis=0)


def even_rows(m, b):
    return jnp.concatenate([m[i : i + b] for i in range(0, TILE, 2 * b)], axis=0)


def fold(m):
    row = lax.broadcasted_iota(jnp.int32, (BLOCK, TILE), 0)
    lane = lax.broadcasted_iota(jnp.int32, (BLOCK, TILE), 1)
    group = lane // BLOCK
    z = jnp.where(group == 0, m[:BLOCK], 0.0)
    for r in range(1, TILE // BLOCK):
        z = jnp.where(group == r, m[r * BLOCK : (r + 1) * BLOCK], z)
    return jnp.where(row > lax.rem(lane, BLOCK), z, 0.0).astype(bf16)


def fill_spread(spread_ref):
    row = lax.broadcasted_iota(jnp.int32, (TILE, TILE), 0)
    lane = lax.broadcasted_iota(jnp.int32, (TILE, TILE), 1)
    base = row - lane // BLOCK * BLOCK
    for k in range(BLOCK - 1):
        spread_ref[:, k * TILE : (k + 1) * TILE] = jnp.where(base == k, 1.0, 0.0).astype(bf16)


def block_inverses(folded, spread_ref):
    row = lax.broadcasted_iota(jnp.int32, (BLOCK, TILE), 0)
    lane = lax.broadcasted_iota(jnp.int32, (BLOCK, TILE), 1)
    group = lane // BLOCK
    within = lax.rem(lane, BLOCK)
    spread = dot(jnp.concatenate(folded, axis=0), spread_ref[...])
    unit = jnp.where(row == within, 1.0, 0.0)
    small = BLOCK // 2
    out = []
    tops = [unit[:small]] * len(folded)
    lows = [unit[small:]] * len(folded)
    for k in range(BLOCK - 1):
        at = slice(k * TILE, (k + 1) * TILE)
        for i in range(len(folded)):
            rows = spread[i * BLOCK : (i + 1) * BLOCK, at]
            source = tops[i][k : k + 1] if k < small else lows[i][k - small : k - small + 1]
            if k < small - 1:
                tops[i] = tops[i] + rows[:small] * source
            lows[i] = lows[i] + rows[small:] * source
    for top, low in zip(tops, lows):
        x = jnp.where(row > within, jnp.concatenate([top, low], axis=0), 0.0)
        out.append(
            jnp.concatenate(
                [jnp.where(group == r, x, 0.0) for r in range(TILE // BLOCK)], axis=0
            ).astype(bf16)
        )
    return out


def setup(half_ref, seg_ref, decay_ref, n, mask_ref, crow_ref, ccol_ref, first_ref, beta_ref=None):
    rows = seg_ref.shape[1]
    seg_row = seg_ref[...].astype(f32) + 1.0
    seg_col = jnp.transpose(jnp.broadcast_to(seg_row, (TILE, rows)))
    seg_cols = jnp.concatenate([seg_col] * (rows // TILE), axis=1)
    r = lax.broadcasted_iota(jnp.int32, (rows, rows), 0)
    c = lax.broadcasted_iota(jnp.int32, (rows, rows), 1)
    mask_ref[...] = jnp.where((seg_cols == seg_row) & (r >= c), 0.0, MASKED)
    first_ref[...] = jnp.where(seg_col == seg_row[:, :1], 1.0, 0.0)
    base = pl.multiple_of(half_ref[0] * n, n)
    decay = decay_ref[pl.ds(base, n), :] * LOG2E
    high = decay.astype(bf16)
    rest = decay - high.astype(f32)
    middle = rest.astype(bf16)
    parts = [high, middle, (rest - middle.astype(f32)).astype(bf16)]
    parts = jnp.concatenate([p.astype(f32) for p in parts], axis=0).astype(bf16)
    sums = dot(parts, jnp.where(r <= c, 1.0, 0.0).astype(bf16))
    cumulative = sums[:n] + sums[n : 2 * n] + sums[2 * n :]
    crow_ref[...] = cumulative
    beta = jnp.zeros((n, rows), f32) if beta_ref is None else beta_ref[pl.ds(base, n), :]
    fill = jnp.zeros((TILE - 2 * n, rows), f32)
    ccol_ref[...] = jnp.transpose(jnp.concatenate([cumulative, beta, fill], axis=0))
    return seg_row


def column(ref, at, lane, width):
    one = jnp.broadcast_to(ref[at, lane : lane + 1], (STRIP, TILE))
    return one if width == TILE else jnp.concatenate([one] * (width // TILE), axis=1)


def pipeline(phases, count):
    for slot in range(count + len(phases) - 1):
        running = [
            phase(slot - i) for i, phase in enumerate(phases) if 0 <= slot - i < count
        ]
        while running:
            running = [p for p in running if next(p, DONE) is not DONE]


def delta_local_kernel(
    half_ref,
    seg_ref,
    k_ref,
    v_ref,
    beta_ref,
    decay_ref,
    map_add_ref,
    solved_ref,
    mask_ref,
    level_ref,
    spread_ref,
    crow_ref,
    ccol_ref,
    first_ref,
):
    rows = k_ref.shape[0]
    n = v_ref.shape[1] // DV
    fill_spread(spread_ref)
    seg_row = setup(
        half_ref, seg_ref, decay_ref, n, mask_ref, crow_ref, ccol_ref, first_ref, beta_ref
    )
    map_add_ref[n * DK :, :] = jnp.broadcast_to(seg_row, (BLOCK, rows)).astype(bf16)
    r = lax.broadcasted_iota(jnp.int32, (TILE, TILE), 0)
    c = lax.broadcasted_iota(jnp.int32, (TILE, TILE), 1)
    eye = jnp.where(r == c, 1.0, 0.0)
    for level in range(MERGES):
        b = BLOCK << level
        sibling = jnp.where(r // b == c // b + 1, 1.0, 0.0)
        level_ref[level] = odd_rows(sibling, b).astype(bf16)
    strips = [slice(i, i + STRIP) for i in range(0, rows, STRIP)]
    pairs = [
        [dict(h=2 * kk + j, d=[], right=[]) for j in range(2)] for kk in range(n // 2)
    ]

    def elementwise(kk):
        pair = pairs[kk]
        k_raw = k_ref[:, kk * DK : (kk + 1) * DK]
        kt = jnp.transpose(k_raw.astype(f32))
        rk_row = lax.rsqrt(jnp.sum(kt * kt, axis=0, keepdims=True) + EPS)
        ktb = kt.astype(bf16)
        upper = dot(k_raw[:TILE], ktb[:, :TILE])
        lower = dot(k_raw[TILE:], ktb)
        yield
        for at in strips:
            raw, start = (upper, at.start) if at.start < TILE else (lower, at.start - TILE)
            width = raw.shape[1]
            kf = k_raw[at].astype(f32)
            rk = lax.rsqrt(jnp.sum(kf * kf, axis=1, keepdims=True) + EPS)
            kn = kf * rk
            gram = raw[start : start + STRIP] * rk_row[:, :width] * -rk
            for w in pair:
                h = w["h"]
                cc = column(ccol_ref, at, h, width)
                bt = column(ccol_ref, at, n + h, width)
                span = jnp.exp2(cc - crow_ref[h : h + 1, :width] + mask_ref[at, :width])
                w["d"].append(span * bt * gram)
                cc, bt = cc[:, :TILE], bt[:, :TILE]
                entry = jnp.exp2(cc) * first_ref[at]
                value = v_ref[at, h * DV : (h + 1) * DV].astype(f32)
                w["right"].append(
                    jnp.concatenate([bt * entry * kn, bt * value], axis=1).astype(bf16)
                )
                if at.stop == rows:
                    w["last"] = entry[STRIP - 1 :]
                    w["kd"] = (kt * (rk_row * span[STRIP - 1 :])).astype(bf16)
            yield
        top = TILE // STRIP
        for w in pair:
            d11 = jnp.concatenate(w["d"][:top], axis=0)
            d2 = jnp.concatenate(w["d"][top:], axis=0)
            blocks = [d11, d2[:, TILE:]]
            w["folded"] = [fold(m) for m in blocks]
            w["d"] = [m.astype(bf16) for m in blocks]
            w["d21"] = d2[:, :TILE].astype(bf16)
            w["right"] = jnp.concatenate(w["right"], axis=0)
        yield

    def invert():
        work = [w for pair in pairs for w in pair]
        mats = [m for w in work for m in w["d"]]
        inverses = block_inverses([z for w in work for z in w["folded"]], spread_ref)
        zeros = jnp.zeros((TILE // 2, TILE), bf16)
        for level in range(MERGES):
            b = BLOCK << level
            keep = level_ref[level]
            picked = [odd_rows(m, b) * keep for m in mats]
            ys = [(p.astype(f32) + dot(p, x)).astype(bf16) for p, x in zip(picked, inverses)]
            odds = [odd_rows(x, b) for x in inverses]
            odds = [
                x + (y.astype(f32) + dot(x, interleave(zeros, y, b))).astype(bf16)
                for x, y in zip(odds, ys)
            ]
            inverses = [interleave(even_rows(x, b), o, b) for x, o in zip(inverses, odds)]
        for i, w in enumerate(work):
            w["x"] = inverses[2 * i : 2 * i + 2]

    def finish(kk):
        pair = pairs[kk]
        for w in pair:
            w["u1"] = add_strips(w["right"][:TILE], dot(w["x"][0], w["right"][:TILE]))
        yield
        for w in pair:
            w["r2"] = add_strips(w["right"][TILE:], dot(w["d21"], w["u1"]))
        yield
        for w in pair:
            u2 = add_strips(w["r2"], dot(w["x"][1], w["r2"]))
            w["u"] = jnp.concatenate([w["u1"], u2], axis=0)
            solved_ref[w["h"] * rows : (w["h"] + 1) * rows, :] = w["u"]
        yield
        for w in pair:
            h = w["h"]
            ma = dot(w["kd"], w["u"])
            for start in range(0, DK, STRIP):
                part = ma[start : start + STRIP]
                kept = w["last"] * eye[start : start + STRIP]
                map_add_ref[h * DK + start : h * DK + start + STRIP, :] = jnp.concatenate(
                    [kept - part[:, :DK], part[:, DK:]], axis=1
                ).astype(bf16)
            yield

    pipeline([elementwise], n // 2)
    invert()
    pipeline([finish], n // 2)


def add_strips(a, b):
    return jnp.concatenate(
        [
            (a[i : i + STRIP].astype(f32) + b[i : i + STRIP]).astype(bf16)
            for i in range(0, a.shape[0], STRIP)
        ],
        axis=0,
    )


def delta_reach_kernel(
    half_ref,
    seg_ref,
    q_ref,
    k_ref,
    decay_ref,
    solved_ref,
    gate_ref,
    gain_ref,
    reach_ref,
    inner_ref,
    factor_ref,
    mask_ref,
    crow_ref,
    ccol_ref,
    first_ref,
):
    rows = k_ref.shape[0]
    n = reach_ref.shape[1] // DK
    setup(half_ref, seg_ref, decay_ref, n, mask_ref, crow_ref, ccol_ref, first_ref)
    strips = [slice(i, i + STRIP) for i in range(0, rows, STRIP)]
    pairs = [
        [dict(h=2 * kk + j, p=[], scaled=[]) for j in range(2)] for kk in range(n // 2)
    ]

    def elementwise(kk):
        pair = pairs[kk]
        cols = slice(kk * DK, (kk + 1) * DK)
        k_raw = k_ref[:, cols]
        q_raw = q_ref[:, cols]
        kt = jnp.transpose(k_raw.astype(f32))
        rk_row = lax.rsqrt(jnp.sum(kt * kt, axis=0, keepdims=True) + EPS)
        ktb = kt.astype(bf16)
        upper = dot(q_raw[:TILE], ktb[:, :TILE])
        lower = dot(q_raw[TILE:], ktb)
        yield
        for at in strips:
            raw, start = (upper, at.start) if at.start < TILE else (lower, at.start - TILE)
            width = raw.shape[1]
            qf = q_raw[at].astype(f32)
            rq = lax.rsqrt(jnp.sum(qf * qf, axis=1, keepdims=True) + EPS) * DK**-0.5
            qn = qf * rq
            probe = raw[start : start + STRIP] * rk_row[:, :width] * rq
            for w in pair:
                h = w["h"]
                cc = column(ccol_ref, at, h, width)
                span = jnp.exp2(cc - crow_ref[h : h + 1, :width] + mask_ref[at, :width])
                w["p"].append((span * probe).astype(bf16))
                entry = jnp.exp2(cc[:, :TILE]) * first_ref[at]
                w["scaled"].append((entry * qn).astype(bf16))
                cols = slice(h * DV, (h + 1) * DV)
                gate = gate_ref[at, cols].astype(f32)
                factor_ref[at, cols] = gate * sigmoid(gate) * gain_ref[...]
            yield

    def finish(kk):
        top = TILE // STRIP
        for w in pairs[kk]:
            h = w["h"]
            u = solved_ref[h * rows : (h + 1) * rows, :]
            upper = dot(jnp.concatenate(w["p"][:top], axis=0), u[:TILE])
            lower = dot(jnp.concatenate(w["p"][top:], axis=0), u)
            for at, scaled in zip(strips, w["scaled"]):
                pu = upper[at.start :] if at.start < TILE else lower[at.start - TILE :]
                pu = pu[:STRIP]
                reach_ref[at, h * DK : (h + 1) * DK] = (
                    scaled.astype(f32) - pu[:, :DK]
                ).astype(bf16)
                inner_ref[at, h * DV : (h + 1) * DV] = pu[:, DK:]
            yield

    pipeline([elementwise, finish], n // 2)


def half_call(kernel, name, mib, half, operands, outs, scratch):
    def at_half(i, s):
        return (0, s[0])

    def at_zero(i, s):
        return (0, 0)

    specs = []
    args = []
    for a in operands:
        if isinstance(a, tuple):
            (a,) = a
            specs.append(pl.BlockSpec((a.shape[0], a.shape[1] // 2), at_half))
        else:
            specs.append(pl.BlockSpec(a.shape, at_zero))
        args.append(a)
    return pl.pallas_call(
        kernel,
        grid_spec=pltpu.PrefetchScalarGridSpec(
            num_scalar_prefetch=1,
            grid=(1,),
            in_specs=specs,
            out_specs=[pl.BlockSpec(o.shape, at_zero) for o in outs],
            scratch_shapes=scratch,
        ),
        out_shape=outs,
        compiler_params=params(mib),
        cost_estimate=cost(4 * 10**9, 3 * 2**20),
        name=name,
    )(half, *args)


def setup_scratch(rows, n):
    return [
        pltpu.VMEM((rows, rows), f32),
        pltpu.VMEM((n, rows), f32),
        pltpu.VMEM((rows, TILE), f32),
        pltpu.VMEM((rows, TILE), f32),
    ]


def delta_local(half, mib, seg_row, key, value, beta, decay):
    rows = key.shape[0]
    n = value.shape[1] // DV // 2
    mask, *others = setup_scratch(rows, n)
    return half_call(
        delta_local_kernel,
        "delta_local",
        mib,
        half,
        [seg_row, (key,), (value,), beta, decay],
        [
            jax.ShapeDtypeStruct((n * DK + BLOCK, DK + DV), bf16),
            jax.ShapeDtypeStruct((n * rows, DK + DV), bf16),
        ],
        [
            mask,
            pltpu.VMEM((MERGES, TILE // 2, TILE), bf16),
            pltpu.VMEM((TILE, (BLOCK - 1) * TILE), bf16),
            *others,
        ],
    )


def delta_reach(half, seg_row, query, key, decay, gate, gain, solved):
    rows = key.shape[0]
    n = solved.shape[0] // rows
    return half_call(
        delta_reach_kernel,
        "delta_reach",
        20,
        half,
        [seg_row, (query,), (key,), decay, solved, (gate,), gain],
        [
            jax.ShapeDtypeStruct((rows, n * DK), bf16),
            jax.ShapeDtypeStruct((rows, n * DV), f32),
            jax.ShapeDtypeStruct((rows, n * DV), f32),
        ],
        setup_scratch(rows, n),
    )


def ids_of(ref):
    end = ref.shape[0] - BLOCK
    return ref[end : end + BLOCK, :].astype(f32)[:1]


def put_id(ref, value):
    end = ref.shape[0] - BLOCK
    ref[end:, :] = jnp.broadcast_to(value, (BLOCK, ref.shape[1])).astype(bf16)


def matching(a, b):
    return jnp.where(a == b, 1.0, 0.0)


def compose_kernel(core_ref, mine_ref, other_ref, map_ref, add_ref):
    odd = core_ref[0] == 1
    mine_ids, other_ids = ids_of(mine_ref), ids_of(other_ref)
    early_ids = jnp.where(odd, other_ids, mine_ids)
    late_ids = jnp.where(odd, mine_ids, other_ids)
    across = matching(early_ids[:, -1:], late_ids[:, :1])
    put_id(map_ref, early_ids[:, :1])
    put_id(add_ref, late_ids[:, -1:])
    for h in range(mine_ref.shape[0] // DK):
        at = slice(h * DK, (h + 1) * DK)
        mine, other = mine_ref[at], other_ref[at]
        early, late = jnp.where(odd, other, mine), jnp.where(odd, mine, other)
        both = dot(late[:, :DK], early) * across
        map_ref[at] = both[:, :DK].astype(bf16)
        add_ref[at] = (both[:, DK:] + late[:, DK:].astype(f32)).astype(bf16)


def relay_kernel(map_ref, add_ref, state_ref, out_ref):
    into = matching(ids_of(state_ref), ids_of(map_ref))
    put_id(out_ref, ids_of(add_ref))
    for h in range(map_ref.shape[0] // DK):
        at = slice(h * DK, (h + 1) * DK)
        out_ref[at] = (dot(map_ref[at], state_ref[at]) * into + add_ref[at].astype(f32)).astype(bf16)


def arrive_kernel(core_ref, mine_ref, other_ref, state_ref, keep_ref, give_ref):
    odd = core_ref[0] == 1
    mine_ids, other_ids = ids_of(mine_ref), ids_of(other_ref)
    early_ids = jnp.where(odd, other_ids, mine_ids)
    late_ids = jnp.where(odd, mine_ids, other_ids)
    across = matching(early_ids[:, -1:], late_ids[:, :1])
    into = matching(ids_of(state_ref), early_ids[:, :1])
    for h in range(keep_ref.shape[0] // DK):
        at = slice(h * DK, (h + 1) * DK)
        early = jnp.where(odd, other_ref[at], mine_ref[at])
        first = (state_ref[at].astype(f32) * into).astype(bf16)
        second = (
            (dot(early[:, :DK], first) + early[:, DK:].astype(f32)) * across
        ).astype(bf16)
        keep_ref[at] = jnp.where(odd, second, first)
        give_ref[at] = jnp.where(odd, first, second)


SMEM = pl.BlockSpec(memory_space=pltpu.SMEM)
VMEM = pl.BlockSpec(memory_space=pltpu.VMEM)


def small_call(kernel, name, outs, *args, scalars=0, mib=16):
    return pl.pallas_call(
        kernel,
        in_specs=[SMEM] * scalars + [VMEM] * (len(args) - scalars),
        out_specs=[VMEM] * len(outs),
        out_shape=outs,
        compiler_params=params(mib),
        cost_estimate=cost(10**8, 2**20),
        name=name,
    )(*args)


def delta_out_kernel(half_ref, reach_ref, inner_ref, factor_ref, state_ref, *rest):
    out_hbm, out_ref, sem = rest[-3:]
    n = state_ref.shape[0] // DK
    width = 2 * DV
    copies = []
    for h in range(n):
        cols = slice(h * DV, (h + 1) * DV)
        carried = dot(reach_ref[:, cols], state_ref[h * DK : (h + 1) * DK])
        for i in range(0, carried.shape[0], STRIP):
            at = slice(i, i + STRIP)
            out = inner_ref[at, cols] + carried[at]
            spread = lax.rsqrt(jnp.mean(out * out, axis=1, keepdims=True) + EPS)
            out_ref[at, cols] = (out * spread * factor_ref[at, cols]).astype(bf16)
        if h % 2 == 1:
            start = (h - 1) * DV
            target = pl.multiple_of(half_ref[0] * (n * DV) + start, width)
            copies.append(
                pltpu.make_async_copy(
                    out_ref.at[:, pl.ds(start, width)],
                    out_hbm.at[:, pl.ds(target, width)],
                    sem.at[h // 2],
                )
            )
            copies[-1].start()
    for copy in copies:
        copy.wait()


def delta_out(half, reach, inner, factor, state, partial_out=None):
    rows = reach.shape[0]
    n = state.shape[0] // DK
    in_specs = [SMEM] + [VMEM] * 4
    args = [half, reach, inner, factor, state]
    aliases = {}
    if partial_out is not None:
        aliases = {len(args): 0}
        in_specs.append(pl.BlockSpec(memory_space=pl.ANY))
        args.append(partial_out)
    return pl.pallas_call(
        delta_out_kernel,
        in_specs=in_specs,
        out_specs=pl.BlockSpec(memory_space=pl.ANY),
        out_shape=jax.ShapeDtypeStruct((rows, 2 * n * DV), bf16),
        scratch_shapes=[pltpu.VMEM((rows, n * DV), bf16), pltpu.SemaphoreType.DMA((n // 2,))],
        input_output_aliases=aliases,
        compiler_params=params(),
        cost_estimate=cost(10**8, 3 * 2**20),
        name="delta_out",
    )(*args)


def blocks_of(pieces):
    own, *same, other = pieces
    order = [(own, None)]
    for i, ref in enumerate(same):
        order += [(other, i), (ref, None)]
    return order[::-1]


def pack_kernel(seg_ref, key_ref, value_ref, out_ref):
    rows = key_ref.shape[0]
    ids = seg_ref[...].astype(f32) + 1.0
    out_ref[:rows, :HEAD_WIDTH] = key_ref[...]
    out_ref[:rows, HEAD_WIDTH:] = value_ref[...]
    out_ref[rows:, :rows] = jnp.broadcast_to(ids, (BLOCK, rows)).astype(bf16)
    out_ref[rows:, rows:] = jnp.zeros((BLOCK, 2 * HEAD_WIDTH - rows), bf16)


def window_kernel(freq_ref, *rest):
    *pieces, kt_ref, v_ref, ids_ref, cos_ref, sin_ref = rest
    rows = cos_ref.shape[0]
    window = ids_ref.shape[1]
    half = ROTARY_ENTRIES // 2
    blocks = [ref if index is None else ref.at[index] for ref, index in blocks_of(pieces)]
    row_ids = jnp.concatenate(
        [ref[rows : rows + BLOCK, :rows].astype(f32)[:1] for ref in blocks], axis=1
    )
    ids_ref[...] = row_ids
    ids = jnp.broadcast_to(row_ids, (DOCS, window))
    docs = lax.broadcasted_iota(jnp.int32, (DOCS, window), 0).astype(f32) + 1.0
    before = jnp.sum(jnp.where(ids < docs, 1.0, 0.0), axis=1, keepdims=True)
    start = jnp.sum(jnp.where(ids == docs, before, 0.0), axis=0, keepdims=True)
    place = lax.broadcasted_iota(jnp.int32, (1, window), 1).astype(f32)
    angle = freq_ref[:, :1] * (place - start)
    cosine = jnp.cos(angle)
    sine = jnp.sin(angle)
    for b, ref in enumerate(blocks):
        cols = slice(b * rows, (b + 1) * rows)
        kt = jnp.transpose(ref[:rows, :HEAD_WIDTH].astype(f32))
        one, two = kt[:half], kt[half:ROTARY_ENTRIES]
        cb, sb = cosine[:, cols], sine[:, cols]
        kt_ref[:half, cols] = (one * cb - two * sb).astype(bf16)
        kt_ref[half:ROTARY_ENTRIES, cols] = (two * cb + one * sb).astype(bf16)
        kt_ref[ROTARY_ENTRIES:, cols] = kt[ROTARY_ENTRIES:].astype(bf16)
        v_ref[cols, :] = ref[:rows, HEAD_WIDTH:]
    cq, sq = cosine[:, window - rows :], sine[:, window - rows :]
    rest_rows = TILE - ROTARY_ENTRIES
    cos_ref[...] = jnp.transpose(
        jnp.concatenate([cq, cq, jnp.ones((rest_rows, rows), f32)], axis=0)
    )
    sin_ref[...] = jnp.transpose(
        jnp.concatenate([-sq, sq, jnp.zeros((rest_rows, rows), f32)], axis=0)
    )


def attention_kernel(ids_ref, cos_ref, sin_ref, kt_ref, v_ref, q_ref, gate_ref, *rest):
    out_ref, mask_ref = rest[-2:]
    rows = q_ref.shape[0]
    window = ids_ref.shape[1]
    half = ROTARY_ENTRIES // 2

    @pl.when(pl.program_id(0) == 0)
    def _():
        own = ids_ref[:, window - rows :]
        own_col = jnp.transpose(jnp.broadcast_to(own, (TILE, rows)))
        own_cols = jnp.concatenate([own_col] * (window // TILE), axis=1)
        r = lax.broadcasted_iota(jnp.int32, (rows, window), 0) + (window - rows)
        c = lax.broadcasted_iota(jnp.int32, (rows, window), 1)
        mask_ref[...] = jnp.where((own_cols == ids_ref[...]) & (c <= r), 0.0, MASKED)

    scaling = HEAD_WIDTH**-0.5
    lane = lax.broadcasted_iota(jnp.int32, (TILE, TILE), 1)
    reach = window - rows + TILE
    heads = q_ref.shape[1] // HEAD_WIDTH
    for first in range(0, rows, TILE):
        at = slice(first, first + TILE)
        keys = slice(first, first + reach)
        queries = []
        for h in range(heads):
            base = h * HEAD_WIDTH
            x = q_ref[at, base : base + TILE].astype(f32)
            swapped = jnp.where(
                lane < half, pltpu.roll(x, TILE - half, 1), pltpu.roll(x, half, 1)
            )
            rotated = ((x * cos_ref[at] + swapped * sin_ref[at]) * scaling).astype(bf16)
            tail = q_ref[at, base + TILE : base + HEAD_WIDTH] * jnp.asarray(scaling, bf16)
            queries.append(jnp.concatenate([rotated, tail], axis=1))
        scores = dot(jnp.concatenate(queries, axis=0), kt_ref[:, keys])
        weights = []
        totals = []
        for i in range(0, heads * TILE, FINE):
            row = first + i % TILE
            strip = scores[i : i + FINE] + mask_ref[row : row + FINE, keys]
            strip = jnp.exp(strip - jnp.max(strip, axis=1, keepdims=True))
            totals.append(1.0 / jnp.sum(strip, axis=1, keepdims=True))
            weights.append(strip.astype(bf16))
        mixed = dot(jnp.concatenate(weights, axis=0), v_ref[keys, :])
        for i, inverse in zip(range(0, heads * TILE, FINE), totals):
            rows_at = slice(first + i % TILE, first + i % TILE + FINE)
            cols = slice(i // TILE * HEAD_WIDTH, (i // TILE + 1) * HEAD_WIDTH)
            gate = sigmoid(gate_ref[rows_at, cols].astype(f32))
            out_ref[rows_at, cols] = (mixed[i : i + FINE] * inverse * gate).astype(bf16)


def attention_half(part, window_arrays, query, gate, partial_out=None):
    rows = query.shape[0]
    window = window_arrays[0].shape[1]
    heads = 4
    width = heads * HEAD_WIDTH
    steps = query.shape[1] // width // 2

    def at_part(i):
        return (0, part * steps + i)

    in_specs = [pl.BlockSpec(a.shape, lambda i: (0, 0)) for a in window_arrays]
    in_specs += [pl.BlockSpec((rows, width), at_part)] * 2
    args = [*window_arrays, query, gate]
    aliases = {}
    if partial_out is not None:
        aliases = {len(args): 0}
        in_specs.append(pl.BlockSpec(memory_space=pl.ANY))
        args.append(partial_out)
    return pl.pallas_call(
        attention_kernel,
        grid=(steps,),
        in_specs=in_specs,
        out_specs=pl.BlockSpec((rows, width), at_part),
        out_shape=jax.ShapeDtypeStruct(query.shape, bf16),
        scratch_shapes=[pltpu.VMEM((rows, window), f32)],
        input_output_aliases=aliases,
        compiler_params=params(28),
        cost_estimate=cost(5 * 10**9, 3 * 2**20, 10**6),
        name="attention",
    )(*args)


def up_chip(value, ranks):
    return lax.ppermute(value, "ctx", [(i, i + 2) for i in range(ranks - 2)])


def swap_cores(value, ranks):
    return lax.ppermute(value, "ctx", [(i, i ^ 1) for i in range(ranks)])


def per_device(
    segment_ids,
    attn_query,
    attention_keys,
    attention_values,
    attn_gate,
    delta_query,
    delta_key,
    update_rule_payload,
    delta_beta,
    delta_decay,
    delta_gate,
    norm_gain,
):
    ranks = lax.axis_size("ctx")
    rank = lax.axis_index("ctx")
    rows = segment_ids.shape[0]
    hops = ranks // 4
    core = rank % 2
    odd = core == 1

    ids = segment_ids.reshape(1, rows)

    (own,) = small_call(
        pack_kernel,
        "pack",
        [jax.ShapeDtypeStruct((rows + BLOCK, 2 * HEAD_WIDTH), bf16)],
        ids,
        attention_keys,
        attention_values,
        mib=60,
    )
    nearest = up_chip(own, ranks)

    keep_half = core.reshape(1).astype(jnp.int32)
    give_half = 1 - keep_half
    decay_rows = delta_decay.T
    local = partial(
        delta_local,
        seg_row=ids,
        key=delta_key,
        value=update_rule_payload,
        beta=delta_beta.T,
        decay=decay_rows,
    )
    reach = partial(
        delta_reach,
        seg_row=ids,
        query=delta_query,
        key=delta_key,
        decay=decay_rows,
        gate=delta_gate,
        gain=norm_gain.reshape(1, DV),
    )
    give_ma, give_solved = local(give_half, 20)
    other_ma = swap_cores(give_ma, ranks)
    nearest, give_ma = lax.optimization_barrier((nearest, give_ma))
    same = [nearest]
    for _ in range(hops - 1):
        same.append(up_chip(same[-1], ranks))
    keep_ma, keep_solved = local(keep_half, 20)
    keep_ma, other_ma = lax.optimization_barrier((keep_ma, other_ma))

    tall = keep_ma.shape[0]
    state_like = jax.ShapeDtypeStruct((tall, DV), bf16)
    chip_map, chip_add = small_call(
        compose_kernel, "compose", [state_like] * 2, keep_half, keep_ma, other_ma, scalars=1
    )
    state = up_chip(chip_add, ranks)
    give_solved, keep_solved, _ = lax.optimization_barrier((give_solved, keep_solved, chip_add))
    give_rows = reach(give_half, solved=give_solved)
    same, keep_solved, give_rows = lax.optimization_barrier((same, keep_solved, give_rows))
    chain = [own, *same]
    other = swap_cores(
        jnp.stack([jnp.where(odd, chain[i + 1], chain[i]) for i in range(hops)]), ranks
    )

    keep_rows = reach(keep_half, solved=keep_solved)
    other, keep_rows = lax.optimization_barrier((other, keep_rows))

    window = (2 * hops + 1) * rows
    index = jnp.arange(ROTARY_ENTRIES // 2).astype(f32)
    freq = ROPE_THETA ** (-2.0 * index / ROTARY_ENTRIES)
    freq = jnp.broadcast_to(freq[:, None], (ROTARY_ENTRIES // 2, TILE))
    window_arrays = small_call(
        window_kernel,
        "window",
        [
            jax.ShapeDtypeStruct((HEAD_WIDTH, window), bf16),
            jax.ShapeDtypeStruct((window, HEAD_WIDTH), bf16),
            jax.ShapeDtypeStruct((1, window), f32),
            jax.ShapeDtypeStruct((rows, TILE), f32),
            jax.ShapeDtypeStruct((rows, TILE), f32),
        ],
        freq,
        own,
        *same,
        other,
    )
    kt, v_all, window_ids, cosine, sine = window_arrays
    window_arrays = (window_ids, cosine, sine, kt, v_all)
    attn_mixed = attention_half(0, window_arrays, attn_query, attn_gate)
    state, attn_mixed = lax.optimization_barrier((state, attn_mixed))
    leaving = chip_add
    for _ in range(hops - 1):
        (leaving,) = small_call(relay_kernel, "relay", [state_like], chip_map, chip_add, state)
        state = up_chip(leaving, ranks)
    attn_mixed, leaving = lax.optimization_barrier((attn_mixed, leaving))
    attn_mixed = attention_half(1, window_arrays, attn_query, attn_gate, attn_mixed)
    state, attn_mixed = lax.optimization_barrier((state, attn_mixed))

    final_like = jax.ShapeDtypeStruct((tall - BLOCK, DV), bf16)
    keep_state, pass_state = small_call(
        arrive_kernel, "arrive", [final_like] * 2, keep_half, keep_ma, other_ma, state, scalars=1
    )
    give_state = swap_cores(pass_state, ranks)

    delta_mixed = delta_out(keep_half, *keep_rows, keep_state)
    delta_mixed = delta_out(give_half, *give_rows, give_state, delta_mixed)
    return (attn_mixed, delta_mixed)


def solution(mesh):
    rows = P(("dp", "ctx"))
    wide = P(("dp", "ctx"), None)
    return jax.shard_map(
        per_device,
        mesh=mesh,
        in_specs=(rows,) + (wide,) * 10 + (P(),),
        out_specs=(wide, wide),
        check_vma=False,
    )
```

```python
from functools import partial

import jax
import jax.numpy as jnp
from jax import lax
from jax.experimental import pallas as pl
from jax.experimental.pallas import tpu as pltpu
from jax.sharding import PartitionSpec as P

HEAD_WIDTH = 256
ROTARY_ENTRIES = 64
DK = 128
DV = 128
DOCS = 8
ROPE_THETA = 10000000.0
LOG2E = 1.4426950408889634
MASKED = -1e30
EPS = 1e-6
TILE = 128
MIB = 1024 * 1024

f32 = jnp.float32
bf16 = jnp.bfloat16


def dot(a, b, precision=None):
    return jnp.dot(a, b, preferred_element_type=f32, precision=precision)


def params(mib=16):
    return pltpu.CompilerParams(vmem_limit_bytes=mib * MIB)


def sigmoid(x):
    return 0.5 * jnp.tanh(0.5 * x) + 0.5


def cost(flops, nbytes, exps=0):
    return pl.CostEstimate(flops=flops, bytes_accessed=nbytes, transcendentals=exps)


BLOCK = 16
MERGES = 3
STRIP = 32
FINE = 16
DONE = object()


def odd_rows(m, b):
    return jnp.concatenate([m[i + b : i + 2 * b] for i in range(0, TILE, 2 * b)], axis=0)


def interleave(even, odd, b):
    parts = []
    for i in range(0, TILE // 2, b):
        parts += [even[i : i + b], odd[i : i + b]]
    return jnp.concatenate(parts, axis=0)


def even_rows(m, b):
    return jnp.concatenate([m[i : i + b] for i in range(0, TILE, 2 * b)], axis=0)


def fold(m):
    row = lax.broadcasted_iota(jnp.int32, (BLOCK, TILE), 0)
    lane = lax.broadcasted_iota(jnp.int32, (BLOCK, TILE), 1)
    group = lane // BLOCK
    z = jnp.where(group == 0, m[:BLOCK], 0.0)
    for r in range(1, TILE // BLOCK):
        z = jnp.where(group == r, m[r * BLOCK : (r + 1) * BLOCK], z)
    return jnp.where(row > lax.rem(lane, BLOCK), z, 0.0).astype(bf16)


def fill_spread(spread_ref):
    row = lax.broadcasted_iota(jnp.int32, (TILE, TILE), 0)
    lane = lax.broadcasted_iota(jnp.int32, (TILE, TILE), 1)
    base = row - lane // BLOCK * BLOCK
    for k in range(BLOCK - 1):
        spread_ref[:, k * TILE : (k + 1) * TILE] = jnp.where(base == k, 1.0, 0.0).astype(bf16)


def block_inverses(folded, spread_ref):
    row = lax.broadcasted_iota(jnp.int32, (BLOCK, TILE), 0)
    lane = lax.broadcasted_iota(jnp.int32, (BLOCK, TILE), 1)
    group = lane // BLOCK
    within = lax.rem(lane, BLOCK)
    spread = dot(jnp.concatenate(folded, axis=0), spread_ref[...])
    unit = jnp.where(row == within, 1.0, 0.0)
    small = BLOCK // 2
    out = []
    tops = [unit[:small]] * len(folded)
    lows = [unit[small:]] * len(folded)
    for k in range(BLOCK - 1):
        at = slice(k * TILE, (k + 1) * TILE)
        for i in range(len(folded)):
            rows = spread[i * BLOCK : (i + 1) * BLOCK, at]
            source = tops[i][k : k + 1] if k < small else lows[i][k - small : k - small + 1]
            if k < small - 1:
                tops[i] = tops[i] + rows[:small] * source
            lows[i] = lows[i] + rows[small:] * source
    for top, low in zip(tops, lows):
        x = jnp.where(row > within, jnp.concatenate([top, low], axis=0), 0.0)
        out.append(
            jnp.concatenate(
                [jnp.where(group == r, x, 0.0) for r in range(TILE // BLOCK)], axis=0
            ).astype(bf16)
        )
    return out


def setup(half_ref, seg_ref, decay_ref, n, mask_ref, crow_ref, ccol_ref, first_ref, beta_ref=None):
    rows = seg_ref.shape[1]
    seg_row = seg_ref[...].astype(f32) + 1.0
    seg_col = jnp.transpose(jnp.broadcast_to(seg_row, (TILE, rows)))
    seg_cols = jnp.concatenate([seg_col] * (rows // TILE), axis=1)
    r = lax.broadcasted_iota(jnp.int32, (rows, rows), 0)
    c = lax.broadcasted_iota(jnp.int32, (rows, rows), 1)
    mask_ref[...] = jnp.where((seg_cols == seg_row) & (r >= c), 0.0, MASKED)
    first_ref[...] = jnp.where(seg_col == seg_row[:, :1], 1.0, 0.0)
    base = pl.multiple_of(half_ref[0] * n, n)
    decay = decay_ref[pl.ds(base, n), :] * LOG2E
    high = decay.astype(bf16)
    rest = decay - high.astype(f32)
    middle = rest.astype(bf16)
    parts = [high, middle, (rest - middle.astype(f32)).astype(bf16)]
    parts = jnp.concatenate([p.astype(f32) for p in parts], axis=0).astype(bf16)
    sums = dot(parts, jnp.where(r <= c, 1.0, 0.0).astype(bf16))
    cumulative = sums[:n] + sums[n : 2 * n] + sums[2 * n :]
    crow_ref[...] = cumulative
    beta = jnp.zeros((n, rows), f32) if beta_ref is None else beta_ref[pl.ds(base, n), :]
    fill = jnp.zeros((TILE - 2 * n, rows), f32)
    ccol_ref[...] = jnp.transpose(jnp.concatenate([cumulative, beta, fill], axis=0))
    return seg_row


def column(ref, at, lane, width):
    one = jnp.broadcast_to(ref[at, lane : lane + 1], (STRIP, TILE))
    return one if width == TILE else jnp.concatenate([one] * (width // TILE), axis=1)


def pipeline(phases, count):
    for slot in range(count + len(phases) - 1):
        running = [
            phase(slot - i) for i, phase in enumerate(phases) if 0 <= slot - i < count
        ]
        while running:
            running = [p for p in running if next(p, DONE) is not DONE]


def delta_local_kernel(
    half_ref,
    seg_ref,
    k_ref,
    v_ref,
    beta_ref,
    decay_ref,
    map_add_ref,
    solved_ref,
    mask_ref,
    level_ref,
    spread_ref,
    crow_ref,
    ccol_ref,
    first_ref,
):
    rows = k_ref.shape[0]
    n = v_ref.shape[1] // DV
    fill_spread(spread_ref)
    seg_row = setup(
        half_ref, seg_ref, decay_ref, n, mask_ref, crow_ref, ccol_ref, first_ref, beta_ref
    )
    map_add_ref[n * DK :, :] = jnp.broadcast_to(seg_row, (BLOCK, rows)).astype(bf16)
    r = lax.broadcasted_iota(jnp.int32, (TILE, TILE), 0)
    c = lax.broadcasted_iota(jnp.int32, (TILE, TILE), 1)
    eye = jnp.where(r == c, 1.0, 0.0)
    for level in range(MERGES):
        b = BLOCK << level
        sibling = jnp.where(r // b == c // b + 1, 1.0, 0.0)
        level_ref[level] = odd_rows(sibling, b).astype(bf16)
    strips = [slice(i, i + STRIP) for i in range(0, rows, STRIP)]
    pairs = [
        [dict(h=2 * kk + j, d=[], right=[]) for j in range(2)] for kk in range(n // 2)
    ]

    def elementwise(kk):
        pair = pairs[kk]
        k_raw = k_ref[:, kk * DK : (kk + 1) * DK]
        kt = jnp.transpose(k_raw.astype(f32))
        rk_row = lax.rsqrt(jnp.sum(kt * kt, axis=0, keepdims=True) + EPS)
        ktb = kt.astype(bf16)
        upper = dot(k_raw[:TILE], ktb[:, :TILE])
        lower = dot(k_raw[TILE:], ktb)
        yield
        for at in strips:
            raw, start = (upper, at.start) if at.start < TILE else (lower, at.start - TILE)
            width = raw.shape[1]
            kf = k_raw[at].astype(f32)
            rk = lax.rsqrt(jnp.sum(kf * kf, axis=1, keepdims=True) + EPS)
            kn = kf * rk
            gram = raw[start : start + STRIP] * rk_row[:, :width] * -rk
            for w in pair:
                h = w["h"]
                cc = column(ccol_ref, at, h, width)
                bt = column(ccol_ref, at, n + h, width)
                span = jnp.exp2(cc - crow_ref[h : h + 1, :width] + mask_ref[at, :width])
                w["d"].append(span * bt * gram)
                cc, bt = cc[:, :TILE], bt[:, :TILE]
                entry = jnp.exp2(cc) * first_ref[at]
                value = v_ref[at, h * DV : (h + 1) * DV].astype(f32)
                w["right"].append(
                    jnp.concatenate([bt * entry * kn, bt * value], axis=1).astype(bf16)
                )
                if at.stop == rows:
                    w["last"] = entry[STRIP - 1 :]
                    w["kd"] = (kt * (rk_row * span[STRIP - 1 :])).astype(bf16)
            yield
        top = TILE // STRIP
        for w in pair:
            d11 = jnp.concatenate(w["d"][:top], axis=0)
            d2 = jnp.concatenate(w["d"][top:], axis=0)
            blocks = [d11, d2[:, TILE:]]
            w["folded"] = [fold(m) for m in blocks]
            w["d"] = [m.astype(bf16) for m in blocks]
            w["d21"] = d2[:, :TILE].astype(bf16)
            w["right"] = jnp.concatenate(w["right"], axis=0)
        yield

    def invert():
        work = [w for pair in pairs for w in pair]
        mats = [m for w in work for m in w["d"]]
        inverses = block_inverses([z for w in work for z in w["folded"]], spread_ref)
        zeros = jnp.zeros((TILE // 2, TILE), bf16)
        for level in range(MERGES):
            b = BLOCK << level
            keep = level_ref[level]
            picked = [odd_rows(m, b) * keep for m in mats]
            ys = [(p.astype(f32) + dot(p, x)).astype(bf16) for p, x in zip(picked, inverses)]
            odds = [odd_rows(x, b) for x in inverses]
            odds = [
                x + (y.astype(f32) + dot(x, interleave(zeros, y, b))).astype(bf16)
                for x, y in zip(odds, ys)
            ]
            inverses = [interleave(even_rows(x, b), o, b) for x, o in zip(inverses, odds)]
        for i, w in enumerate(work):
            w["x"] = inverses[2 * i : 2 * i + 2]

    def finish(kk):
        pair = pairs[kk]
        for w in pair:
            w["u1"] = add_strips(w["right"][:TILE], dot(w["x"][0], w["right"][:TILE]))
        yield
        for w in pair:
            w["r2"] = add_strips(w["right"][TILE:], dot(w["d21"], w["u1"]))
        yield
        for w in pair:
            u2 = add_strips(w["r2"], dot(w["x"][1], w["r2"]))
            w["u"] = jnp.concatenate([w["u1"], u2], axis=0)
            solved_ref[w["h"] * rows : (w["h"] + 1) * rows, :] = w["u"]
        yield
        for w in pair:
            h = w["h"]
            ma = dot(w["kd"], w["u"])
            for start in range(0, DK, STRIP):
                part = ma[start : start + STRIP]
                kept = w["last"] * eye[start : start + STRIP]
                map_add_ref[h * DK + start : h * DK + start + STRIP, :] = jnp.concatenate(
                    [kept - part[:, :DK], part[:, DK:]], axis=1
                ).astype(bf16)
            yield

    pipeline([elementwise], n // 2)
    invert()
    pipeline([finish], n // 2)


def add_strips(a, b):
    return jnp.concatenate(
        [
            (a[i : i + STRIP].astype(f32) + b[i : i + STRIP]).astype(bf16)
            for i in range(0, a.shape[0], STRIP)
        ],
        axis=0,
    )


def delta_reach_kernel(
    half_ref,
    seg_ref,
    q_ref,
    k_ref,
    decay_ref,
    solved_ref,
    gate_ref,
    gain_ref,
    reach_ref,
    inner_ref,
    factor_ref,
    mask_ref,
    crow_ref,
    ccol_ref,
    first_ref,
):
    rows = k_ref.shape[0]
    n = reach_ref.shape[1] // DK
    setup(half_ref, seg_ref, decay_ref, n, mask_ref, crow_ref, ccol_ref, first_ref)
    strips = [slice(i, i + STRIP) for i in range(0, rows, STRIP)]
    pairs = [
        [dict(h=2 * kk + j, p=[], scaled=[]) for j in range(2)] for kk in range(n // 2)
    ]

    def elementwise(kk):
        pair = pairs[kk]
        cols = slice(kk * DK, (kk + 1) * DK)
        k_raw = k_ref[:, cols]
        q_raw = q_ref[:, cols]
        kt = jnp.transpose(k_raw.astype(f32))
        rk_row = lax.rsqrt(jnp.sum(kt * kt, axis=0, keepdims=True) + EPS)
        ktb = kt.astype(bf16)
        upper = dot(q_raw[:TILE], ktb[:, :TILE])
        lower = dot(q_raw[TILE:], ktb)
        yield
        for at in strips:
            raw, start = (upper, at.start) if at.start < TILE else (lower, at.start - TILE)
            width = raw.shape[1]
            qf = q_raw[at].astype(f32)
            rq = lax.rsqrt(jnp.sum(qf * qf, axis=1, keepdims=True) + EPS) * DK**-0.5
            qn = qf * rq
            probe = raw[start : start + STRIP] * rk_row[:, :width] * rq
            for w in pair:
                h = w["h"]
                cc = column(ccol_ref, at, h, width)
                span = jnp.exp2(cc - crow_ref[h : h + 1, :width] + mask_ref[at, :width])
                w["p"].append((span * probe).astype(bf16))
                entry = jnp.exp2(cc[:, :TILE]) * first_ref[at]
                w["scaled"].append((entry * qn).astype(bf16))
                cols = slice(h * DV, (h + 1) * DV)
                gate = gate_ref[at, cols].astype(f32)
                factor_ref[at, cols] = gate * sigmoid(gate) * gain_ref[...]
            yield

    def finish(kk):
        top = TILE // STRIP
        for w in pairs[kk]:
            h = w["h"]
            u = solved_ref[h * rows : (h + 1) * rows, :]
            upper = dot(jnp.concatenate(w["p"][:top], axis=0), u[:TILE])
            lower = dot(jnp.concatenate(w["p"][top:], axis=0), u)
            for at, scaled in zip(strips, w["scaled"]):
                pu = upper[at.start :] if at.start < TILE else lower[at.start - TILE :]
                pu = pu[:STRIP]
                reach_ref[at, h * DK : (h + 1) * DK] = (
                    scaled.astype(f32) - pu[:, :DK]
                ).astype(bf16)
                inner_ref[at, h * DV : (h + 1) * DV] = pu[:, DK:]
            yield

    pipeline([elementwise, finish], n // 2)


def half_call(kernel, name, mib, flops, half, operands, outs, scratch):
    def at_half(i, s):
        return (0, s[0])

    def at_zero(i, s):
        return (0, 0)

    specs = []
    args = []
    for a in operands:
        if isinstance(a, tuple):
            (a,) = a
            specs.append(pl.BlockSpec((a.shape[0], a.shape[1] // 2), at_half))
        else:
            specs.append(pl.BlockSpec(a.shape, at_zero))
        args.append(a)
    return pl.pallas_call(
        kernel,
        grid_spec=pltpu.PrefetchScalarGridSpec(
            num_scalar_prefetch=1,
            grid=(1,),
            in_specs=specs,
            out_specs=[pl.BlockSpec(o.shape, at_zero) for o in outs],
            scratch_shapes=scratch,
        ),
        out_shape=outs,
        compiler_params=params(mib),
        cost_estimate=cost(flops, 2**14),
        name=name,
    )(half, *args)


def setup_scratch(rows, n):
    return [
        pltpu.VMEM((rows, rows), f32),
        pltpu.VMEM((n, rows), f32),
        pltpu.VMEM((rows, TILE), f32),
        pltpu.VMEM((rows, TILE), f32),
    ]


def delta_local(half, mib, seg_row, key, value, beta, decay):
    rows = key.shape[0]
    n = value.shape[1] // DV // 2
    mask, *others = setup_scratch(rows, n)
    return half_call(
        delta_local_kernel,
        "delta_local",
        mib,
        8 * 10**9,
        half,
        [seg_row, (key,), (value,), beta, decay],
        [
            jax.ShapeDtypeStruct((n * DK + BLOCK, DK + DV), bf16),
            jax.ShapeDtypeStruct((n * rows, DK + DV), bf16),
        ],
        [
            mask,
            pltpu.VMEM((MERGES, TILE // 2, TILE), bf16),
            pltpu.VMEM((TILE, (BLOCK - 1) * TILE), bf16),
            *others,
        ],
    )


def delta_reach(half, seg_row, query, key, decay, gate, gain, solved):
    rows = key.shape[0]
    n = solved.shape[0] // rows
    return half_call(
        delta_reach_kernel,
        "delta_reach",
        20,
        10**6,
        half,
        [seg_row, (query,), (key,), decay, solved, (gate,), gain],
        [
            jax.ShapeDtypeStruct((rows, n * DK), bf16),
            jax.ShapeDtypeStruct((rows, n * DV), f32),
            jax.ShapeDtypeStruct((rows, n * DV), f32),
        ],
        setup_scratch(rows, n),
    )


def ids_of(ref):
    end = ref.shape[0] - BLOCK
    return ref[end : end + BLOCK, :].astype(f32)[:1]


def put_id(ref, value):
    end = ref.shape[0] - BLOCK
    ref[end:, :] = jnp.broadcast_to(value, (BLOCK, ref.shape[1])).astype(bf16)


def matching(a, b):
    return jnp.where(a == b, 1.0, 0.0)


def compose_kernel(core_ref, mine_ref, other_ref, map_ref, add_ref):
    odd = core_ref[0] == 1
    mine_ids, other_ids = ids_of(mine_ref), ids_of(other_ref)
    early_ids = jnp.where(odd, other_ids, mine_ids)
    late_ids = jnp.where(odd, mine_ids, other_ids)
    across = matching(early_ids[:, -1:], late_ids[:, :1])
    put_id(map_ref, early_ids[:, :1])
    put_id(add_ref, late_ids[:, -1:])
    for h in range(mine_ref.shape[0] // DK):
        at = slice(h * DK, (h + 1) * DK)
        mine, other = mine_ref[at], other_ref[at]
        early, late = jnp.where(odd, other, mine), jnp.where(odd, mine, other)
        both = dot(late[:, :DK], early) * across
        map_ref[at] = both[:, :DK].astype(bf16)
        add_ref[at] = (both[:, DK:] + late[:, DK:].astype(f32)).astype(bf16)


def relay_kernel(map_ref, add_ref, state_ref, out_ref):
    into = matching(ids_of(state_ref), ids_of(map_ref))
    put_id(out_ref, ids_of(add_ref))
    for h in range(map_ref.shape[0] // DK):
        at = slice(h * DK, (h + 1) * DK)
        out_ref[at] = (dot(map_ref[at], state_ref[at]) * into + add_ref[at].astype(f32)).astype(bf16)


def arrive_kernel(core_ref, mine_ref, other_ref, state_ref, keep_ref, give_ref):
    odd = core_ref[0] == 1
    mine_ids, other_ids = ids_of(mine_ref), ids_of(other_ref)
    early_ids = jnp.where(odd, other_ids, mine_ids)
    late_ids = jnp.where(odd, mine_ids, other_ids)
    across = matching(early_ids[:, -1:], late_ids[:, :1])
    into = matching(ids_of(state_ref), early_ids[:, :1])
    for h in range(keep_ref.shape[0] // DK):
        at = slice(h * DK, (h + 1) * DK)
        early = jnp.where(odd, other_ref[at], mine_ref[at])
        first = (state_ref[at].astype(f32) * into).astype(bf16)
        second = (
            (dot(early[:, :DK], first) + early[:, DK:].astype(f32)) * across
        ).astype(bf16)
        keep_ref[at] = jnp.where(odd, second, first)
        give_ref[at] = jnp.where(odd, first, second)


SMEM = pl.BlockSpec(memory_space=pltpu.SMEM)
VMEM = pl.BlockSpec(memory_space=pltpu.VMEM)


def small_call(kernel, name, outs, *args, scalars=0, mib=16):
    return pl.pallas_call(
        kernel,
        in_specs=[SMEM] * scalars + [VMEM] * (len(args) - scalars),
        out_specs=[VMEM] * len(outs),
        out_shape=outs,
        compiler_params=params(mib),
        cost_estimate=cost(10**8, 2**20),
        name=name,
    )(*args)


def delta_out_kernel(half_ref, reach_ref, inner_ref, factor_ref, state_ref, *rest):
    out_hbm, out_ref, sem = rest[-3:]
    n = state_ref.shape[0] // DK
    width = 2 * DV
    copies = []
    for h in range(n):
        cols = slice(h * DV, (h + 1) * DV)
        carried = dot(reach_ref[:, cols], state_ref[h * DK : (h + 1) * DK])
        for i in range(0, carried.shape[0], STRIP):
            at = slice(i, i + STRIP)
            out = inner_ref[at, cols] + carried[at]
            spread = lax.rsqrt(jnp.mean(out * out, axis=1, keepdims=True) + EPS)
            out_ref[at, cols] = (out * spread * factor_ref[at, cols]).astype(bf16)
        if h % 2 == 1:
            start = (h - 1) * DV
            target = pl.multiple_of(half_ref[0] * (n * DV) + start, width)
            copies.append(
                pltpu.make_async_copy(
                    out_ref.at[:, pl.ds(start, width)],
                    out_hbm.at[:, pl.ds(target, width)],
                    sem.at[h // 2],
                )
            )
            copies[-1].start()
    for copy in copies:
        copy.wait()


def delta_out(half, reach, inner, factor, state, partial_out=None):
    rows = reach.shape[0]
    n = state.shape[0] // DK
    in_specs = [SMEM] + [VMEM] * 4
    args = [half, reach, inner, factor, state]
    aliases = {}
    if partial_out is not None:
        aliases = {len(args): 0}
        in_specs.append(pl.BlockSpec(memory_space=pl.ANY))
        args.append(partial_out)
    return pl.pallas_call(
        delta_out_kernel,
        in_specs=in_specs,
        out_specs=pl.BlockSpec(memory_space=pl.ANY),
        out_shape=jax.ShapeDtypeStruct((rows, 2 * n * DV), bf16),
        scratch_shapes=[pltpu.VMEM((rows, n * DV), bf16), pltpu.SemaphoreType.DMA((n // 2,))],
        input_output_aliases=aliases,
        compiler_params=params(),
        cost_estimate=cost(10**8, 3 * 2**20),
        name="delta_out",
    )(*args)


def blocks_of(pieces):
    own, *same, other = pieces
    order = [(own, None)]
    for i, ref in enumerate(same):
        order += [(other, i), (ref, None)]
    return order[::-1]


def pack_kernel(seg_ref, key_ref, value_ref, out_ref):
    rows = key_ref.shape[0]
    ids = seg_ref[...].astype(f32) + 1.0
    out_ref[:rows, :HEAD_WIDTH] = key_ref[...]
    out_ref[:rows, HEAD_WIDTH:] = value_ref[...]
    out_ref[rows:, :rows] = jnp.broadcast_to(ids, (BLOCK, rows)).astype(bf16)
    out_ref[rows:, rows:] = jnp.zeros((BLOCK, 2 * HEAD_WIDTH - rows), bf16)


def window_kernel(freq_ref, *rest):
    *pieces, kt_ref, v_ref, ids_ref, cos_ref, sin_ref = rest
    rows = cos_ref.shape[0]
    window = ids_ref.shape[1]
    half = ROTARY_ENTRIES // 2
    blocks = [ref if index is None else ref.at[index] for ref, index in blocks_of(pieces)]
    row_ids = jnp.concatenate(
        [ref[rows : rows + BLOCK, :rows].astype(f32)[:1] for ref in blocks], axis=1
    )
    ids_ref[...] = row_ids
    ids = jnp.broadcast_to(row_ids, (DOCS, window))
    docs = lax.broadcasted_iota(jnp.int32, (DOCS, window), 0).astype(f32) + 1.0
    before = jnp.sum(jnp.where(ids < docs, 1.0, 0.0), axis=1, keepdims=True)
    start = jnp.sum(jnp.where(ids == docs, before, 0.0), axis=0, keepdims=True)
    place = lax.broadcasted_iota(jnp.int32, (1, window), 1).astype(f32)
    angle = freq_ref[:, :1] * (place - start)
    cosine = jnp.cos(angle)
    sine = jnp.sin(angle)
    for b, ref in enumerate(blocks):
        cols = slice(b * rows, (b + 1) * rows)
        kt = jnp.transpose(ref[:rows, :HEAD_WIDTH].astype(f32))
        one, two = kt[:half], kt[half:ROTARY_ENTRIES]
        cb, sb = cosine[:, cols], sine[:, cols]
        kt_ref[:half, cols] = (one * cb - two * sb).astype(bf16)
        kt_ref[half:ROTARY_ENTRIES, cols] = (two * cb + one * sb).astype(bf16)
        kt_ref[ROTARY_ENTRIES:, cols] = kt[ROTARY_ENTRIES:].astype(bf16)
        v_ref[cols, :] = ref[:rows, HEAD_WIDTH:]
    cq, sq = cosine[:, window - rows :], sine[:, window - rows :]
    rest_rows = TILE - ROTARY_ENTRIES
    cos_ref[...] = jnp.transpose(
        jnp.concatenate([cq, cq, jnp.ones((rest_rows, rows), f32)], axis=0)
    )
    sin_ref[...] = jnp.transpose(
        jnp.concatenate([-sq, sq, jnp.zeros((rest_rows, rows), f32)], axis=0)
    )


def attention_kernel(ids_ref, cos_ref, sin_ref, kt_ref, v_ref, q_ref, gate_ref, *rest):
    out_ref, mask_ref = rest[-2:]
    rows = q_ref.shape[0]
    window = ids_ref.shape[1]
    half = ROTARY_ENTRIES // 2

    @pl.when(pl.program_id(0) == 0)
    def _():
        own = ids_ref[:, window - rows :]
        own_col = jnp.transpose(jnp.broadcast_to(own, (TILE, rows)))
        own_cols = jnp.concatenate([own_col] * (window // TILE), axis=1)
        r = lax.broadcasted_iota(jnp.int32, (rows, window), 0) + (window - rows)
        c = lax.broadcasted_iota(jnp.int32, (rows, window), 1)
        mask_ref[...] = jnp.where((own_cols == ids_ref[...]) & (c <= r), 0.0, MASKED)

    scaling = HEAD_WIDTH**-0.5
    lane = lax.broadcasted_iota(jnp.int32, (TILE, TILE), 1)
    reach = window - rows + TILE
    heads = q_ref.shape[1] // HEAD_WIDTH
    for first in range(0, rows, TILE):
        at = slice(first, first + TILE)
        keys = slice(first, first + reach)
        queries = []
        for h in range(heads):
            base = h * HEAD_WIDTH
            x = q_ref[at, base : base + TILE].astype(f32)
            swapped = jnp.where(
                lane < half, pltpu.roll(x, TILE - half, 1), pltpu.roll(x, half, 1)
            )
            rotated = ((x * cos_ref[at] + swapped * sin_ref[at]) * scaling).astype(bf16)
            tail = q_ref[at, base + TILE : base + HEAD_WIDTH] * jnp.asarray(scaling, bf16)
            queries.append(jnp.concatenate([rotated, tail], axis=1))
        scores = dot(jnp.concatenate(queries, axis=0), kt_ref[:, keys])
        weights = []
        totals = []
        for i in range(0, heads * TILE, FINE):
            row = first + i % TILE
            strip = scores[i : i + FINE] + mask_ref[row : row + FINE, keys]
            strip = jnp.exp(strip - jnp.max(strip, axis=1, keepdims=True))
            totals.append(1.0 / jnp.sum(strip, axis=1, keepdims=True))
            weights.append(strip.astype(bf16))
        mixed = dot(jnp.concatenate(weights, axis=0), v_ref[keys, :])
        for i, inverse in zip(range(0, heads * TILE, FINE), totals):
            rows_at = slice(first + i % TILE, first + i % TILE + FINE)
            cols = slice(i // TILE * HEAD_WIDTH, (i // TILE + 1) * HEAD_WIDTH)
            gate = sigmoid(gate_ref[rows_at, cols].astype(f32))
            out_ref[rows_at, cols] = (mixed[i : i + FINE] * inverse * gate).astype(bf16)


def attention_half(part, window_arrays, query, gate, partial_out=None):
    rows = query.shape[0]
    window = window_arrays[0].shape[1]
    heads = 4
    width = heads * HEAD_WIDTH
    steps = query.shape[1] // width // 2

    def at_part(i):
        return (0, part * steps + i)

    in_specs = [pl.BlockSpec(a.shape, lambda i: (0, 0)) for a in window_arrays]
    in_specs += [pl.BlockSpec((rows, width), at_part)] * 2
    args = [*window_arrays, query, gate]
    aliases = {}
    if partial_out is not None:
        aliases = {len(args): 0}
        in_specs.append(pl.BlockSpec(memory_space=pl.ANY))
        args.append(partial_out)
    return pl.pallas_call(
        attention_kernel,
        grid=(steps,),
        in_specs=in_specs,
        out_specs=pl.BlockSpec((rows, width), at_part),
        out_shape=jax.ShapeDtypeStruct(query.shape, bf16),
        scratch_shapes=[pltpu.VMEM((rows, window), f32)],
        input_output_aliases=aliases,
        compiler_params=params(28),
        cost_estimate=cost(5 * 10**9, 3 * 2**20, 10**6),
        name="attention",
    )(*args)


def up_chip(value, ranks):
    return lax.ppermute(value, "ctx", [(i, i + 2) for i in range(ranks - 2)])


def swap_cores(value, ranks):
    return lax.ppermute(value, "ctx", [(i, i ^ 1) for i in range(ranks)])


def per_device(
    segment_ids,
    attn_query,
    attention_keys,
    attention_values,
    attn_gate,
    delta_query,
    delta_key,
    update_rule_payload,
    delta_beta,
    delta_decay,
    delta_gate,
    norm_gain,
):
    ranks = lax.axis_size("ctx")
    rank = lax.axis_index("ctx")
    rows = segment_ids.shape[0]
    hops = ranks // 4
    core = rank % 2
    odd = core == 1

    ids = segment_ids.reshape(1, rows)

    (own,) = small_call(
        pack_kernel,
        "pack",
        [jax.ShapeDtypeStruct((rows + BLOCK, 2 * HEAD_WIDTH), bf16)],
        ids,
        attention_keys,
        attention_values,
        mib=60,
    )
    nearest = up_chip(own, ranks)

    keep_half = core.reshape(1).astype(jnp.int32)
    give_half = 1 - keep_half
    decay_rows = delta_decay.T
    local = partial(
        delta_local,
        seg_row=ids,
        key=delta_key,
        value=update_rule_payload,
        beta=delta_beta.T,
        decay=decay_rows,
    )
    reach = partial(
        delta_reach,
        seg_row=ids,
        query=delta_query,
        key=delta_key,
        decay=decay_rows,
        gate=delta_gate,
        gain=norm_gain.reshape(1, DV),
    )
    give_ma, give_solved = local(give_half, 20)
    other_ma = swap_cores(give_ma, ranks)
    nearest, give_ma = lax.optimization_barrier((nearest, give_ma))
    same = [nearest]
    for _ in range(hops - 1):
        same.append(up_chip(same[-1], ranks))
    keep_ma, keep_solved = local(keep_half, 20)
    give_solved, keep_ma = lax.optimization_barrier((give_solved, keep_ma))
    give_rows = reach(give_half, solved=give_solved)
    same, keep_ma, other_ma, give_rows = lax.optimization_barrier(
        (same, keep_ma, other_ma, give_rows)
    )
    chain = [own, *same]
    other = swap_cores(
        jnp.stack([jnp.where(odd, chain[i + 1], chain[i]) for i in range(hops)]), ranks
    )

    tall = keep_ma.shape[0]
    state_like = jax.ShapeDtypeStruct((tall, DV), bf16)
    chip_map, chip_add = small_call(
        compose_kernel, "compose", [state_like] * 2, keep_half, keep_ma, other_ma, scalars=1
    )
    state = up_chip(chip_add, ranks)

    window = (2 * hops + 1) * rows
    index = jnp.arange(ROTARY_ENTRIES // 2).astype(f32)
    freq = ROPE_THETA ** (-2.0 * index / ROTARY_ENTRIES)
    freq = jnp.broadcast_to(freq[:, None], (ROTARY_ENTRIES // 2, TILE))
    window_arrays = small_call(
        window_kernel,
        "window",
        [
            jax.ShapeDtypeStruct((HEAD_WIDTH, window), bf16),
            jax.ShapeDtypeStruct((window, HEAD_WIDTH), bf16),
            jax.ShapeDtypeStruct((1, window), f32),
            jax.ShapeDtypeStruct((rows, TILE), f32),
            jax.ShapeDtypeStruct((rows, TILE), f32),
        ],
        freq,
        own,
        *same,
        other,
    )
    kt, v_all, window_ids, cosine, sine = window_arrays
    window_arrays = (window_ids, cosine, sine, kt, v_all)
    attn_mixed = attention_half(0, window_arrays, attn_query, attn_gate)
    keep_solved, chip_add = lax.optimization_barrier((keep_solved, chip_add))
    keep_rows = reach(keep_half, solved=keep_solved)
    state, attn_mixed, keep_rows = lax.optimization_barrier((state, attn_mixed, keep_rows))
    leaving = chip_add
    for _ in range(hops - 1):
        (leaving,) = small_call(relay_kernel, "relay", [state_like], chip_map, chip_add, state)
        state = up_chip(leaving, ranks)
    attn_mixed, leaving = lax.optimization_barrier((attn_mixed, leaving))
    attn_mixed = attention_half(1, window_arrays, attn_query, attn_gate, attn_mixed)
    state, attn_mixed = lax.optimization_barrier((state, attn_mixed))

    final_like = jax.ShapeDtypeStruct((tall - BLOCK, DV), bf16)
    keep_state, pass_state = small_call(
        arrive_kernel, "arrive", [final_like] * 2, keep_half, keep_ma, other_ma, state, scalars=1
    )
    give_state = swap_cores(pass_state, ranks)

    delta_mixed = delta_out(keep_half, *keep_rows, keep_state)
    delta_mixed = delta_out(give_half, *give_rows, give_state, delta_mixed)
    return (attn_mixed, delta_mixed)


def solution(mesh):
    rows = P(("dp", "ctx"))
    wide = P(("dp", "ctx"), None)
    return jax.shard_map(
        per_device,
        mesh=mesh,
        in_specs=(rows,) + (wide,) * 10 + (P(),),
        out_specs=(wide, wide),
        check_vma=False,
    )
```

```python
from functools import partial

import jax
import jax.numpy as jnp
from jax import lax
from jax.experimental import pallas as pl
from jax.experimental.pallas import tpu as pltpu
from jax.sharding import PartitionSpec as P

HEAD_WIDTH = 256
ROTARY_ENTRIES = 64
DK = 128
DV = 128
DOCS = 8
ROPE_THETA = 10000000.0
LOG2E = 1.4426950408889634
MASKED = -1e30
EPS = 1e-6
TILE = 128
MIB = 1024 * 1024

f32 = jnp.float32
bf16 = jnp.bfloat16


def dot(a, b, precision=None):
    return jnp.dot(a, b, preferred_element_type=f32, precision=precision)


def params(mib=16):
    return pltpu.CompilerParams(vmem_limit_bytes=mib * MIB)


def sigmoid(x):
    return 0.5 * jnp.tanh(0.5 * x) + 0.5


def cost(flops, nbytes, exps=0):
    return pl.CostEstimate(flops=flops, bytes_accessed=nbytes, transcendentals=exps)


BLOCK = 16
MERGES = 3
STRIP = 32
FINE = 16
DONE = object()


def odd_rows(m, b):
    return jnp.concatenate([m[i + b : i + 2 * b] for i in range(0, TILE, 2 * b)], axis=0)


def interleave(even, odd, b):
    parts = []
    for i in range(0, TILE // 2, b):
        parts += [even[i : i + b], odd[i : i + b]]
    return jnp.concatenate(parts, axis=0)


def even_rows(m, b):
    return jnp.concatenate([m[i : i + b] for i in range(0, TILE, 2 * b)], axis=0)


def fold(m):
    row = lax.broadcasted_iota(jnp.int32, (BLOCK, TILE), 0)
    lane = lax.broadcasted_iota(jnp.int32, (BLOCK, TILE), 1)
    group = lane // BLOCK
    z = jnp.where(group == 0, m[:BLOCK], 0.0)
    for r in range(1, TILE // BLOCK):
        z = jnp.where(group == r, m[r * BLOCK : (r + 1) * BLOCK], z)
    return jnp.where(row > lax.rem(lane, BLOCK), z, 0.0).astype(bf16)


def fill_spread(spread_ref):
    row = lax.broadcasted_iota(jnp.int32, (TILE, TILE), 0)
    lane = lax.broadcasted_iota(jnp.int32, (TILE, TILE), 1)
    base = row - lane // BLOCK * BLOCK
    for k in range(BLOCK - 1):
        spread_ref[:, k * TILE : (k + 1) * TILE] = jnp.where(base == k, 1.0, 0.0).astype(bf16)


def block_inverses(folded, spread_ref):
    row = lax.broadcasted_iota(jnp.int32, (BLOCK, TILE), 0)
    lane = lax.broadcasted_iota(jnp.int32, (BLOCK, TILE), 1)
    group = lane // BLOCK
    within = lax.rem(lane, BLOCK)
    spread = dot(jnp.concatenate(folded, axis=0), spread_ref[...])
    unit = jnp.where(row == within, 1.0, 0.0)
    small = BLOCK // 2
    out = []
    tops = [unit[:small]] * len(folded)
    lows = [unit[small:]] * len(folded)
    for k in range(BLOCK - 1):
        at = slice(k * TILE, (k + 1) * TILE)
        for i in range(len(folded)):
            rows = spread[i * BLOCK : (i + 1) * BLOCK, at]
            source = tops[i][k : k + 1] if k < small else lows[i][k - small : k - small + 1]
            if k < small - 1:
                tops[i] = tops[i] + rows[:small] * source
            lows[i] = lows[i] + rows[small:] * source
    for top, low in zip(tops, lows):
        x = jnp.where(row > within, jnp.concatenate([top, low], axis=0), 0.0)
        out.append(
            jnp.concatenate(
                [jnp.where(group == r, x, 0.0) for r in range(TILE // BLOCK)], axis=0
            ).astype(bf16)
        )
    return out


def setup(half_ref, seg_ref, decay_ref, n, mask_ref, crow_ref, ccol_ref, first_ref, beta_ref=None):
    rows = seg_ref.shape[1]
    seg_row = seg_ref[...].astype(f32) + 1.0
    seg_col = jnp.transpose(jnp.broadcast_to(seg_row, (TILE, rows)))
    seg_cols = jnp.concatenate([seg_col] * (rows // TILE), axis=1)
    r = lax.broadcasted_iota(jnp.int32, (rows, rows), 0)
    c = lax.broadcasted_iota(jnp.int32, (rows, rows), 1)
    mask_ref[...] = jnp.where((seg_cols == seg_row) & (r >= c), 0.0, MASKED)
    first_ref[...] = jnp.where(seg_col == seg_row[:, :1], 1.0, 0.0)
    base = pl.multiple_of(half_ref[0] * n, n)
    decay = decay_ref[pl.ds(base, n), :] * LOG2E
    high = decay.astype(bf16)
    rest = decay - high.astype(f32)
    middle = rest.astype(bf16)
    parts = [high, middle, (rest - middle.astype(f32)).astype(bf16)]
    parts = jnp.concatenate([p.astype(f32) for p in parts], axis=0).astype(bf16)
    sums = dot(parts, jnp.where(r <= c, 1.0, 0.0).astype(bf16))
    cumulative = sums[:n] + sums[n : 2 * n] + sums[2 * n :]
    crow_ref[...] = cumulative
    beta = jnp.zeros((n, rows), f32) if beta_ref is None else beta_ref[pl.ds(base, n), :]
    fill = jnp.zeros((TILE - 2 * n, rows), f32)
    ccol_ref[...] = jnp.transpose(jnp.concatenate([cumulative, beta, fill], axis=0))
    return seg_row


def column(ref, at, lane, width):
    one = jnp.broadcast_to(ref[at, lane : lane + 1], (STRIP, TILE))
    return one if width == TILE else jnp.concatenate([one] * (width // TILE), axis=1)


def pipeline(phases, count):
    for slot in range(count + len(phases) - 1):
        running = [
            phase(slot - i) for i, phase in enumerate(phases) if 0 <= slot - i < count
        ]
        while running:
            running = [p for p in running if next(p, DONE) is not DONE]


def delta_local_kernel(
    half_ref,
    seg_ref,
    k_ref,
    v_ref,
    beta_ref,
    decay_ref,
    map_add_ref,
    solved_ref,
    mask_ref,
    level_ref,
    spread_ref,
    crow_ref,
    ccol_ref,
    first_ref,
):
    rows = k_ref.shape[0]
    n = v_ref.shape[1] // DV
    fill_spread(spread_ref)
    seg_row = setup(
        half_ref, seg_ref, decay_ref, n, mask_ref, crow_ref, ccol_ref, first_ref, beta_ref
    )
    map_add_ref[n * DK :, :] = jnp.broadcast_to(seg_row, (BLOCK, rows)).astype(bf16)
    r = lax.broadcasted_iota(jnp.int32, (TILE, TILE), 0)
    c = lax.broadcasted_iota(jnp.int32, (TILE, TILE), 1)
    eye = jnp.where(r == c, 1.0, 0.0)
    for level in range(MERGES):
        b = BLOCK << level
        sibling = jnp.where(r // b == c // b + 1, 1.0, 0.0)
        level_ref[level] = odd_rows(sibling, b).astype(bf16)
    strips = [slice(i, i + STRIP) for i in range(0, rows, STRIP)]
    pairs = [
        [dict(h=2 * kk + j, d=[], right=[]) for j in range(2)] for kk in range(n // 2)
    ]

    def elementwise(kk):
        pair = pairs[kk]
        k_raw = k_ref[:, kk * DK : (kk + 1) * DK]
        kt = jnp.transpose(k_raw.astype(f32))
        rk_row = lax.rsqrt(jnp.sum(kt * kt, axis=0, keepdims=True) + EPS)
        ktb = kt.astype(bf16)
        upper = dot(k_raw[:TILE], ktb[:, :TILE])
        lower = dot(k_raw[TILE:], ktb)
        yield
        for at in strips:
            raw, start = (upper, at.start) if at.start < TILE else (lower, at.start - TILE)
            width = raw.shape[1]
            kf = k_raw[at].astype(f32)
            rk = lax.rsqrt(jnp.sum(kf * kf, axis=1, keepdims=True) + EPS)
            kn = kf * rk
            gram = raw[start : start + STRIP] * rk_row[:, :width] * -rk
            for w in pair:
                h = w["h"]
                cc = column(ccol_ref, at, h, width)
                bt = column(ccol_ref, at, n + h, width)
                span = jnp.exp2(cc - crow_ref[h : h + 1, :width] + mask_ref[at, :width])
                w["d"].append(span * bt * gram)
                cc, bt = cc[:, :TILE], bt[:, :TILE]
                entry = jnp.exp2(cc) * first_ref[at]
                value = v_ref[at, h * DV : (h + 1) * DV].astype(f32)
                w["right"].append(
                    jnp.concatenate([bt * entry * kn, bt * value], axis=1).astype(bf16)
                )
                if at.stop == rows:
                    w["last"] = entry[STRIP - 1 :]
                    w["kd"] = (kt * (rk_row * span[STRIP - 1 :])).astype(bf16)
            yield
        top = TILE // STRIP
        for w in pair:
            d11 = jnp.concatenate(w["d"][:top], axis=0)
            d2 = jnp.concatenate(w["d"][top:], axis=0)
            blocks = [d11, d2[:, TILE:]]
            w["folded"] = [fold(m) for m in blocks]
            w["d"] = [m.astype(bf16) for m in blocks]
            w["d21"] = d2[:, :TILE].astype(bf16)
            w["right"] = jnp.concatenate(w["right"], axis=0)
        yield

    def invert():
        work = [w for pair in pairs for w in pair]
        mats = [m for w in work for m in w["d"]]
        inverses = block_inverses([z for w in work for z in w["folded"]], spread_ref)
        zeros = jnp.zeros((TILE // 2, TILE), bf16)
        for level in range(MERGES):
            b = BLOCK << level
            keep = level_ref[level]
            picked = [odd_rows(m, b) * keep for m in mats]
            ys = [(p.astype(f32) + dot(p, x)).astype(bf16) for p, x in zip(picked, inverses)]
            odds = [odd_rows(x, b) for x in inverses]
            odds = [
                x + (y.astype(f32) + dot(x, interleave(zeros, y, b))).astype(bf16)
                for x, y in zip(odds, ys)
            ]
            inverses = [interleave(even_rows(x, b), o, b) for x, o in zip(inverses, odds)]
        for i, w in enumerate(work):
            w["x"] = inverses[2 * i : 2 * i + 2]

    def finish(kk):
        pair = pairs[kk]
        for w in pair:
            w["u1"] = add_strips(w["right"][:TILE], dot(w["x"][0], w["right"][:TILE]))
        yield
        for w in pair:
            w["r2"] = add_strips(w["right"][TILE:], dot(w["d21"], w["u1"]))
        yield
        for w in pair:
            u2 = add_strips(w["r2"], dot(w["x"][1], w["r2"]))
            w["u"] = jnp.concatenate([w["u1"], u2], axis=0)
            solved_ref[w["h"] * rows : (w["h"] + 1) * rows, :] = w["u"]
        yield
        for w in pair:
            h = w["h"]
            ma = dot(w["kd"], w["u"])
            for start in range(0, DK, STRIP):
                part = ma[start : start + STRIP]
                kept = w["last"] * eye[start : start + STRIP]
                map_add_ref[h * DK + start : h * DK + start + STRIP, :] = jnp.concatenate(
                    [kept - part[:, :DK], part[:, DK:]], axis=1
                ).astype(bf16)
            yield

    pipeline([elementwise], n // 2)
    invert()
    pipeline([finish], n // 2)


def add_strips(a, b):
    return jnp.concatenate(
        [
            (a[i : i + STRIP].astype(f32) + b[i : i + STRIP]).astype(bf16)
            for i in range(0, a.shape[0], STRIP)
        ],
        axis=0,
    )


def delta_reach_kernel(
    half_ref,
    seg_ref,
    q_ref,
    k_ref,
    decay_ref,
    solved_ref,
    gate_ref,
    gain_ref,
    reach_ref,
    inner_ref,
    factor_ref,
    mask_ref,
    crow_ref,
    ccol_ref,
    first_ref,
):
    rows = k_ref.shape[0]
    n = reach_ref.shape[1] // DK
    setup(half_ref, seg_ref, decay_ref, n, mask_ref, crow_ref, ccol_ref, first_ref)
    strips = [slice(i, i + STRIP) for i in range(0, rows, STRIP)]
    pairs = [
        [dict(h=2 * kk + j, p=[], scaled=[]) for j in range(2)] for kk in range(n // 2)
    ]

    def elementwise(kk):
        pair = pairs[kk]
        cols = slice(kk * DK, (kk + 1) * DK)
        k_raw = k_ref[:, cols]
        q_raw = q_ref[:, cols]
        kt = jnp.transpose(k_raw.astype(f32))
        rk_row = lax.rsqrt(jnp.sum(kt * kt, axis=0, keepdims=True) + EPS)
        ktb = kt.astype(bf16)
        upper = dot(q_raw[:TILE], ktb[:, :TILE])
        lower = dot(q_raw[TILE:], ktb)
        yield
        for at in strips:
            raw, start = (upper, at.start) if at.start < TILE else (lower, at.start - TILE)
            width = raw.shape[1]
            qf = q_raw[at].astype(f32)
            rq = lax.rsqrt(jnp.sum(qf * qf, axis=1, keepdims=True) + EPS) * DK**-0.5
            qn = qf * rq
            probe = raw[start : start + STRIP] * rk_row[:, :width] * rq
            for w in pair:
                h = w["h"]
                cc = column(ccol_ref, at, h, width)
                span = jnp.exp2(cc - crow_ref[h : h + 1, :width] + mask_ref[at, :width])
                w["p"].append((span * probe).astype(bf16))
                entry = jnp.exp2(cc[:, :TILE]) * first_ref[at]
                w["scaled"].append((entry * qn).astype(bf16))
                cols = slice(h * DV, (h + 1) * DV)
                gate = gate_ref[at, cols].astype(f32)
                factor_ref[at, cols] = gate * sigmoid(gate) * gain_ref[...]
            yield

    def finish(kk):
        top = TILE // STRIP
        for w in pairs[kk]:
            h = w["h"]
            u = solved_ref[h * rows : (h + 1) * rows, :]
            upper = dot(jnp.concatenate(w["p"][:top], axis=0), u[:TILE])
            lower = dot(jnp.concatenate(w["p"][top:], axis=0), u)
            for at, scaled in zip(strips, w["scaled"]):
                pu = upper[at.start :] if at.start < TILE else lower[at.start - TILE :]
                pu = pu[:STRIP]
                reach_ref[at, h * DK : (h + 1) * DK] = (
                    scaled.astype(f32) - pu[:, :DK]
                ).astype(bf16)
                inner_ref[at, h * DV : (h + 1) * DV] = pu[:, DK:]
            yield

    pipeline([elementwise, finish], n // 2)


def half_call(kernel, name, mib, half, operands, outs, scratch):
    def at_half(i, s):
        return (0, s[0])

    def at_zero(i, s):
        return (0, 0)

    specs = []
    args = []
    for a in operands:
        if isinstance(a, tuple):
            (a,) = a
            specs.append(pl.BlockSpec((a.shape[0], a.shape[1] // 2), at_half))
        else:
            specs.append(pl.BlockSpec(a.shape, at_zero))
        args.append(a)
    return pl.pallas_call(
        kernel,
        grid_spec=pltpu.PrefetchScalarGridSpec(
            num_scalar_prefetch=1,
            grid=(1,),
            in_specs=specs,
            out_specs=[pl.BlockSpec(o.shape, at_zero) for o in outs],
            scratch_shapes=scratch,
        ),
        out_shape=outs,
        compiler_params=params(mib),
        cost_estimate=cost(4 * 10**9, 3 * 2**20),
        name=name,
    )(half, *args)


def setup_scratch(rows, n):
    return [
        pltpu.VMEM((rows, rows), f32),
        pltpu.VMEM((n, rows), f32),
        pltpu.VMEM((rows, TILE), f32),
        pltpu.VMEM((rows, TILE), f32),
    ]


def delta_local(half, mib, seg_row, key, value, beta, decay):
    rows = key.shape[0]
    n = value.shape[1] // DV // 2
    mask, *others = setup_scratch(rows, n)
    return half_call(
        delta_local_kernel,
        "delta_local",
        mib,
        half,
        [seg_row, (key,), (value,), beta, decay],
        [
            jax.ShapeDtypeStruct((n * DK + BLOCK, DK + DV), bf16),
            jax.ShapeDtypeStruct((n * rows, DK + DV), bf16),
        ],
        [
            mask,
            pltpu.VMEM((MERGES, TILE // 2, TILE), bf16),
            pltpu.VMEM((TILE, (BLOCK - 1) * TILE), bf16),
            *others,
        ],
    )


def delta_reach(half, seg_row, query, key, decay, gate, gain, solved):
    rows = key.shape[0]
    n = solved.shape[0] // rows
    return half_call(
        delta_reach_kernel,
        "delta_reach",
        20,
        half,
        [seg_row, (query,), (key,), decay, solved, (gate,), gain],
        [
            jax.ShapeDtypeStruct((rows, n * DK), bf16),
            jax.ShapeDtypeStruct((rows, n * DV), f32),
            jax.ShapeDtypeStruct((rows, n * DV), f32),
        ],
        setup_scratch(rows, n),
    )


def ids_of(ref):
    end = ref.shape[0] - BLOCK
    return ref[end : end + BLOCK, :].astype(f32)[:1]


def put_id(ref, value):
    end = ref.shape[0] - BLOCK
    ref[end:, :] = jnp.broadcast_to(value, (BLOCK, ref.shape[1])).astype(bf16)


def matching(a, b):
    return jnp.where(a == b, 1.0, 0.0)


def compose_kernel(core_ref, mine_ref, other_ref, map_ref, add_ref):
    odd = core_ref[0] == 1
    mine_ids, other_ids = ids_of(mine_ref), ids_of(other_ref)
    early_ids = jnp.where(odd, other_ids, mine_ids)
    late_ids = jnp.where(odd, mine_ids, other_ids)
    across = matching(early_ids[:, -1:], late_ids[:, :1])
    put_id(map_ref, early_ids[:, :1])
    put_id(add_ref, late_ids[:, -1:])
    for h in range(mine_ref.shape[0] // DK):
        at = slice(h * DK, (h + 1) * DK)
        mine, other = mine_ref[at], other_ref[at]
        early, late = jnp.where(odd, other, mine), jnp.where(odd, mine, other)
        both = dot(late[:, :DK], early) * across
        map_ref[at] = both[:, :DK].astype(bf16)
        add_ref[at] = (both[:, DK:] + late[:, DK:].astype(f32)).astype(bf16)


def relay_kernel(map_ref, add_ref, state_ref, out_ref):
    into = matching(ids_of(state_ref), ids_of(map_ref))
    put_id(out_ref, ids_of(add_ref))
    for h in range(map_ref.shape[0] // DK):
        at = slice(h * DK, (h + 1) * DK)
        out_ref[at] = (dot(map_ref[at], state_ref[at]) * into + add_ref[at].astype(f32)).astype(bf16)


def arrive_kernel(core_ref, mine_ref, other_ref, state_ref, keep_ref, give_ref):
    odd = core_ref[0] == 1
    mine_ids, other_ids = ids_of(mine_ref), ids_of(other_ref)
    early_ids = jnp.where(odd, other_ids, mine_ids)
    late_ids = jnp.where(odd, mine_ids, other_ids)
    across = matching(early_ids[:, -1:], late_ids[:, :1])
    into = matching(ids_of(state_ref), early_ids[:, :1])
    for h in range(keep_ref.shape[0] // DK):
        at = slice(h * DK, (h + 1) * DK)
        early = jnp.where(odd, other_ref[at], mine_ref[at])
        first = (state_ref[at].astype(f32) * into).astype(bf16)
        second = (
            (dot(early[:, :DK], first) + early[:, DK:].astype(f32)) * across
        ).astype(bf16)
        keep_ref[at] = jnp.where(odd, second, first)
        give_ref[at] = jnp.where(odd, first, second)


SMEM = pl.BlockSpec(memory_space=pltpu.SMEM)
VMEM = pl.BlockSpec(memory_space=pltpu.VMEM)


def small_call(kernel, name, outs, *args, scalars=0, mib=16):
    return pl.pallas_call(
        kernel,
        in_specs=[SMEM] * scalars + [VMEM] * (len(args) - scalars),
        out_specs=[VMEM] * len(outs),
        out_shape=outs,
        compiler_params=params(mib),
        cost_estimate=cost(10**8, 2**20),
        name=name,
    )(*args)


def delta_out_kernel(half_ref, reach_ref, inner_ref, factor_ref, state_ref, *rest):
    out_hbm, out_ref, sem = rest[-3:]
    n = state_ref.shape[0] // DK
    width = 2 * DV
    copies = []
    for h in range(n):
        cols = slice(h * DV, (h + 1) * DV)
        carried = dot(reach_ref[:, cols], state_ref[h * DK : (h + 1) * DK])
        for i in range(0, carried.shape[0], STRIP):
            at = slice(i, i + STRIP)
            out = inner_ref[at, cols] + carried[at]
            spread = lax.rsqrt(jnp.mean(out * out, axis=1, keepdims=True) + EPS)
            out_ref[at, cols] = (out * spread * factor_ref[at, cols]).astype(bf16)
        if h % 2 == 1:
            start = (h - 1) * DV
            target = pl.multiple_of(half_ref[0] * (n * DV) + start, width)
            copies.append(
                pltpu.make_async_copy(
                    out_ref.at[:, pl.ds(start, width)],
                    out_hbm.at[:, pl.ds(target, width)],
                    sem.at[h // 2],
                )
            )
            copies[-1].start()
    for copy in copies:
        copy.wait()


def delta_out(half, reach, inner, factor, state, partial_out=None):
    rows = reach.shape[0]
    n = state.shape[0] // DK
    in_specs = [SMEM] + [VMEM] * 4
    args = [half, reach, inner, factor, state]
    aliases = {}
    if partial_out is not None:
        aliases = {len(args): 0}
        in_specs.append(pl.BlockSpec(memory_space=pl.ANY))
        args.append(partial_out)
    return pl.pallas_call(
        delta_out_kernel,
        in_specs=in_specs,
        out_specs=pl.BlockSpec(memory_space=pl.ANY),
        out_shape=jax.ShapeDtypeStruct((rows, 2 * n * DV), bf16),
        scratch_shapes=[pltpu.VMEM((rows, n * DV), bf16), pltpu.SemaphoreType.DMA((n // 2,))],
        input_output_aliases=aliases,
        compiler_params=params(),
        cost_estimate=cost(10**8, 3 * 2**20),
        name="delta_out",
    )(*args)


def blocks_of(pieces):
    own, *same, other = pieces
    order = [(own, None)]
    for i, ref in enumerate(same):
        order += [(other, i), (ref, None)]
    return order[::-1]


def pack_kernel(seg_ref, key_ref, value_ref, out_ref):
    rows = key_ref.shape[0]
    ids = seg_ref[...].astype(f32) + 1.0
    out_ref[:rows, :HEAD_WIDTH] = key_ref[...]
    out_ref[:rows, HEAD_WIDTH:] = value_ref[...]
    out_ref[rows:, :rows] = jnp.broadcast_to(ids, (BLOCK, rows)).astype(bf16)
    out_ref[rows:, rows:] = jnp.zeros((BLOCK, 2 * HEAD_WIDTH - rows), bf16)


def window_kernel(freq_ref, *rest):
    *pieces, kt_ref, v_ref, ids_ref, cos_ref, sin_ref = rest
    rows = cos_ref.shape[0]
    window = ids_ref.shape[1]
    half = ROTARY_ENTRIES // 2
    blocks = [ref if index is None else ref.at[index] for ref, index in blocks_of(pieces)]
    row_ids = jnp.concatenate(
        [ref[rows : rows + BLOCK, :rows].astype(f32)[:1] for ref in blocks], axis=1
    )
    ids_ref[...] = row_ids
    ids = jnp.broadcast_to(row_ids, (DOCS, window))
    docs = lax.broadcasted_iota(jnp.int32, (DOCS, window), 0).astype(f32) + 1.0
    before = jnp.sum(jnp.where(ids < docs, 1.0, 0.0), axis=1, keepdims=True)
    start = jnp.sum(jnp.where(ids == docs, before, 0.0), axis=0, keepdims=True)
    place = lax.broadcasted_iota(jnp.int32, (1, window), 1).astype(f32)
    angle = freq_ref[:, :1] * (place - start)
    cosine = jnp.cos(angle)
    sine = jnp.sin(angle)
    for b, ref in enumerate(blocks):
        cols = slice(b * rows, (b + 1) * rows)
        kt = jnp.transpose(ref[:rows, :HEAD_WIDTH].astype(f32))
        one, two = kt[:half], kt[half:ROTARY_ENTRIES]
        cb, sb = cosine[:, cols], sine[:, cols]
        kt_ref[:half, cols] = (one * cb - two * sb).astype(bf16)
        kt_ref[half:ROTARY_ENTRIES, cols] = (two * cb + one * sb).astype(bf16)
        kt_ref[ROTARY_ENTRIES:, cols] = kt[ROTARY_ENTRIES:].astype(bf16)
        v_ref[cols, :] = ref[:rows, HEAD_WIDTH:]
    cq, sq = cosine[:, window - rows :], sine[:, window - rows :]
    rest_rows = TILE - ROTARY_ENTRIES
    cos_ref[...] = jnp.transpose(
        jnp.concatenate([cq, cq, jnp.ones((rest_rows, rows), f32)], axis=0)
    )
    sin_ref[...] = jnp.transpose(
        jnp.concatenate([-sq, sq, jnp.zeros((rest_rows, rows), f32)], axis=0)
    )


def attention_kernel(ids_ref, cos_ref, sin_ref, kt_ref, v_ref, q_ref, gate_ref, *rest):
    out_ref, mask_ref = rest[-2:]
    rows = q_ref.shape[0]
    window = ids_ref.shape[1]
    half = ROTARY_ENTRIES // 2

    @pl.when(pl.program_id(0) == 0)
    def _():
        own = ids_ref[:, window - rows :]
        own_col = jnp.transpose(jnp.broadcast_to(own, (TILE, rows)))
        own_cols = jnp.concatenate([own_col] * (window // TILE), axis=1)
        r = lax.broadcasted_iota(jnp.int32, (rows, window), 0) + (window - rows)
        c = lax.broadcasted_iota(jnp.int32, (rows, window), 1)
        mask_ref[...] = jnp.where((own_cols == ids_ref[...]) & (c <= r), 0.0, MASKED)

    scaling = HEAD_WIDTH**-0.5
    lane = lax.broadcasted_iota(jnp.int32, (TILE, TILE), 1)
    reach = window - rows + TILE
    heads = q_ref.shape[1] // HEAD_WIDTH
    for first in range(0, rows, TILE):
        at = slice(first, first + TILE)
        keys = slice(first, first + reach)
        queries = []
        for h in range(heads):
            base = h * HEAD_WIDTH
            x = q_ref[at, base : base + TILE].astype(f32)
            swapped = jnp.where(
                lane < half, pltpu.roll(x, TILE - half, 1), pltpu.roll(x, half, 1)
            )
            rotated = ((x * cos_ref[at] + swapped * sin_ref[at]) * scaling).astype(bf16)
            tail = q_ref[at, base + TILE : base + HEAD_WIDTH] * jnp.asarray(scaling, bf16)
            queries.append(jnp.concatenate([rotated, tail], axis=1))
        scores = dot(jnp.concatenate(queries, axis=0), kt_ref[:, keys])
        weights = []
        totals = []
        for i in range(0, heads * TILE, FINE):
            row = first + i % TILE
            strip = scores[i : i + FINE] + mask_ref[row : row + FINE, keys]
            strip = jnp.exp(strip - jnp.max(strip, axis=1, keepdims=True))
            totals.append(1.0 / jnp.sum(strip, axis=1, keepdims=True))
            weights.append(strip.astype(bf16))
        mixed = dot(jnp.concatenate(weights, axis=0), v_ref[keys, :])
        for i, inverse in zip(range(0, heads * TILE, FINE), totals):
            rows_at = slice(first + i % TILE, first + i % TILE + FINE)
            cols = slice(i // TILE * HEAD_WIDTH, (i // TILE + 1) * HEAD_WIDTH)
            gate = sigmoid(gate_ref[rows_at, cols].astype(f32))
            out_ref[rows_at, cols] = (mixed[i : i + FINE] * inverse * gate).astype(bf16)


def attention_half(part, window_arrays, query, gate, partial_out=None):
    rows = query.shape[0]
    window = window_arrays[0].shape[1]
    heads = 4
    width = heads * HEAD_WIDTH
    steps = query.shape[1] // width // 2

    def at_part(i):
        return (0, part * steps + i)

    in_specs = [pl.BlockSpec(a.shape, lambda i: (0, 0)) for a in window_arrays]
    in_specs += [pl.BlockSpec((rows, width), at_part)] * 2
    args = [*window_arrays, query, gate]
    aliases = {}
    if partial_out is not None:
        aliases = {len(args): 0}
        in_specs.append(pl.BlockSpec(memory_space=pl.ANY))
        args.append(partial_out)
    return pl.pallas_call(
        attention_kernel,
        grid=(steps,),
        in_specs=in_specs,
        out_specs=pl.BlockSpec((rows, width), at_part),
        out_shape=jax.ShapeDtypeStruct(query.shape, bf16),
        scratch_shapes=[pltpu.VMEM((rows, window), f32)],
        input_output_aliases=aliases,
        compiler_params=params(28),
        cost_estimate=cost(5 * 10**9, 3 * 2**20, 10**6),
        name="attention",
    )(*args)


def up_chip(value, ranks):
    return lax.ppermute(value, "ctx", [(i, i + 2) for i in range(ranks - 2)])


def swap_cores(value, ranks):
    return lax.ppermute(value, "ctx", [(i, i ^ 1) for i in range(ranks)])


def per_device(
    segment_ids,
    attn_query,
    attention_keys,
    attention_values,
    attn_gate,
    delta_query,
    delta_key,
    update_rule_payload,
    delta_beta,
    delta_decay,
    delta_gate,
    norm_gain,
):
    ranks = lax.axis_size("ctx")
    rank = lax.axis_index("ctx")
    rows = segment_ids.shape[0]
    hops = ranks // 4
    core = rank % 2
    odd = core == 1

    ids = segment_ids.reshape(1, rows)

    (own,) = small_call(
        pack_kernel,
        "pack",
        [jax.ShapeDtypeStruct((rows + BLOCK, 2 * HEAD_WIDTH), bf16)],
        ids,
        attention_keys,
        attention_values,
        mib=60,
    )
    nearest = up_chip(own, ranks)

    keep_half = core.reshape(1).astype(jnp.int32)
    give_half = 1 - keep_half
    decay_rows = delta_decay.T
    local = partial(
        delta_local,
        seg_row=ids,
        key=delta_key,
        value=update_rule_payload,
        beta=delta_beta.T,
        decay=decay_rows,
    )
    reach = partial(
        delta_reach,
        seg_row=ids,
        query=delta_query,
        key=delta_key,
        decay=decay_rows,
        gate=delta_gate,
        gain=norm_gain.reshape(1, DV),
    )
    give_ma, give_solved = local(give_half, 60)
    other_ma = swap_cores(give_ma, ranks)
    nearest, give_ma = lax.optimization_barrier((nearest, give_ma))
    same = [nearest]
    for _ in range(hops - 1):
        same.append(up_chip(same[-1], ranks))
    keep_ma, keep_solved = local(keep_half, 60)
    same, keep_ma, other_ma = lax.optimization_barrier((same, keep_ma, other_ma))
    chain = [own, *same]
    other = swap_cores(
        jnp.stack([jnp.where(odd, chain[i + 1], chain[i]) for i in range(hops)]), ranks
    )

    tall = keep_ma.shape[0]
    state_like = jax.ShapeDtypeStruct((tall, DV), bf16)
    chip_map, chip_add = small_call(
        compose_kernel, "compose", [state_like] * 2, keep_half, keep_ma, other_ma, scalars=1
    )
    state = up_chip(chip_add, ranks)

    window = (2 * hops + 1) * rows
    index = jnp.arange(ROTARY_ENTRIES // 2).astype(f32)
    freq = ROPE_THETA ** (-2.0 * index / ROTARY_ENTRIES)
    freq = jnp.broadcast_to(freq[:, None], (ROTARY_ENTRIES // 2, TILE))
    window_arrays = small_call(
        window_kernel,
        "window",
        [
            jax.ShapeDtypeStruct((HEAD_WIDTH, window), bf16),
            jax.ShapeDtypeStruct((window, HEAD_WIDTH), bf16),
            jax.ShapeDtypeStruct((1, window), f32),
            jax.ShapeDtypeStruct((rows, TILE), f32),
            jax.ShapeDtypeStruct((rows, TILE), f32),
        ],
        freq,
        own,
        *same,
        other,
    )
    kt, v_all, window_ids, cosine, sine = window_arrays
    window_arrays = (window_ids, cosine, sine, kt, v_all)
    attn_mixed = attention_half(0, window_arrays, attn_query, attn_gate)
    give_solved, chip_add = lax.optimization_barrier((give_solved, chip_add))
    give_rows = reach(give_half, solved=give_solved)
    state, attn_mixed, give_rows = lax.optimization_barrier((state, attn_mixed, give_rows))
    leaving = chip_add
    for _ in range(hops - 1):
        (leaving,) = small_call(relay_kernel, "relay", [state_like], chip_map, chip_add, state)
        state = up_chip(leaving, ranks)
    attn_mixed, keep_solved, leaving = lax.optimization_barrier((attn_mixed, keep_solved, leaving))
    attn_mixed = attention_half(1, window_arrays, attn_query, attn_gate, attn_mixed)
    keep_rows = reach(keep_half, solved=keep_solved)
    state, attn_mixed, keep_rows = lax.optimization_barrier((state, attn_mixed, keep_rows))

    final_like = jax.ShapeDtypeStruct((tall - BLOCK, DV), bf16)
    keep_state, pass_state = small_call(
        arrive_kernel, "arrive", [final_like] * 2, keep_half, keep_ma, other_ma, state, scalars=1
    )
    give_state = swap_cores(pass_state, ranks)

    delta_mixed = delta_out(keep_half, *keep_rows, keep_state)
    delta_mixed = delta_out(give_half, *give_rows, give_state, delta_mixed)
    return (attn_mixed, delta_mixed)


def solution(mesh):
    rows = P(("dp", "ctx"))
    wide = P(("dp", "ctx"), None)
    return jax.shard_map(
        per_device,
        mesh=mesh,
        in_specs=(rows,) + (wide,) * 10 + (P(),),
        out_specs=(wide, wide),
        check_vma=False,
    )
```
